32 devices in a mesh: tok: 8 (over z, x), hid: 4 (over y, core).
Axes of the slice: x: 2, y: 2, z: 4, core: 2. Of those that a mesh axis runs over, the one named last changes fastest.
Arguments:
- tokens: bfloat16 [8192, 1152], P('tok', 'hid'), may hold values from -6 to 6
- picture: int32 [8192], replicated, may hold values from -1 to 87, as said below
- cotangent: bfloat16 [8192, 1152], P('tok', 'hid'), may hold values from -6 to 6
- first_gain: float32 [2, 1152], P(None, 'hid'), may hold values from 0.25 to 1.75
- first_shift: float32 [2, 1152], P(None, 'hid'), may hold values from -1.5 to 1.5
- query_weight: bfloat16 [2, 1152, 1152], P(None, 'tok', 'hid'), may hold values from -0.1875 to 0.1875
- query_bias: float32 [2, 1152], P(None, 'hid'), may hold values from -1.5 to 1.5
- key_weight: bfloat16 [2, 1152, 1152], P(None, 'tok', 'hid'), may hold values from -0.1875 to 0.1875
- value_weight: bfloat16 [2, 1152, 1152], P(None, 'tok', 'hid'), may hold values from -0.1875 to 0.1875
- value_bias: float32 [2, 1152], P(None, 'hid'), may hold values from -1.5 to 1.5
- output_weight: bfloat16 [2, 1152, 1152], P(None, 'hid', 'tok'), may hold values from -0.75 to 0.75
- output_bias: float32 [2, 1152], P(None, 'hid'), may hold values from -1.5 to 1.5
- second_gain: float32 [2, 1152], P(None, 'hid'), may hold values from 0.25 to 1.75
- second_shift: float32 [2, 1152], P(None, 'hid'), may hold values from -1.5 to 1.5
- up_weight: bfloat16 [2, 1152, 4304], P(None, 'tok', 'hid'), may hold values from -0.1875 to 0.1875
- up_bias: float32 [2, 4304], P(None, 'hid'), may hold values from -1.5 to 1.5
- down_weight: bfloat16 [2, 4304, 1152], P(None, 'hid', 'tok'), may hold values from -0.09375 to 0.09375
- down_bias: float32 [2, 1152], P(None, 'hid'), may hold values from -1.5 to 1.5
Outputs:
- final_rows: float32 [8192, 1152], P('tok', 'hid')
- grad_tokens: float32 [8192, 1152], P('tok', 'hid')
- grad_first_gain: float32 [2, 1152], P(None, 'hid')
- grad_first_shift: float32 [2, 1152], P(None, 'hid')
- grad_query_weight: float32 [2, 1152, 1152], P(None, 'tok', 'hid')
- grad_query_bias: float32 [2, 1152], P(None, 'hid')
- grad_key_weight: float32 [2, 1152, 1152], P(None, 'tok', 'hid')
- grad_value_weight: float32 [2, 1152, 1152], P(None, 'tok', 'hid')
- grad_value_bias: float32 [2, 1152], P(None, 'hid')
- grad_output_weight: float32 [2, 1152, 1152], P(None, 'hid', 'tok')
- grad_output_bias: float32 [2, 1152], P(None, 'hid')
- grad_second_gain: float32 [2, 1152], P(None, 'hid')
- grad_second_shift: float32 [2, 1152], P(None, 'hid')
- grad_up_weight: float32 [2, 1152, 4304], P(None, 'tok', 'hid')
- grad_up_bias: float32 [2, 4304], P(None, 'hid')
- grad_down_weight: float32 [2, 4304, 1152], P(None, 'hid', 'tok')
- grad_down_bias: float32 [2, 1152], P(None, 'hid')
The draws below stay inside these ranges and needn't reach their ends.
Inputs may be any that keep to these rules, and one draw needn't show every extreme that they name: Tokens come in packed rows of 2048: tokens r * 2048 to (r + 1) * 2048 - 1 form row r. A row holds whole pictures of 100 to 1024 tokens in a row, each with its own number, then one or more padding tokens numbered -1 at its end. In every row one picture holds tokens on both sides of the row's middle.
All inputs are finite; a program needn't handle non-finite values.
Results may differ from the reference program's by a relative error of at most 0.03.
Values may be sent and summed in bfloat16 or wider, within the bound.
A program may use at most 192 MiB of HBM per device.

```python
import jax
import jax.numpy as jnp
from jax import lax

D = 1152
HEADS = 16
HEAD_DIM = 72
FF = 4304
LAYERS = 2
ROW = 2048
MINPIC = 100
TOK_DEV = 1024
TOKENS = 8192


def draw_picture(key, part):
    key = jax.random.fold_in(key, 7)
    row_total = TOKENS // ROW
    piece_count = ROW // MINPIC + 2
    first_key, cross_key, rest_key, pick_key = jax.random.split(key, 4)
    leading = jax.random.randint(first_key, (row_total, 1), MINPIC, TOK_DEV)
    crossing = jax.random.randint(cross_key, (row_total, 1), jnp.maximum(MINPIC, TOK_DEV + 1 - leading), TOK_DEV + 1)
    chosen = jax.random.randint(pick_key, (), 0, row_total)
    row_number = jnp.arange(row_total, dtype=jnp.int32)[:, None]
    crossing = jnp.where(row_number == chosen, TOK_DEV, crossing)
    trailing = jax.random.randint(rest_key, (row_total, piece_count - 2), MINPIC, TOK_DEV + 1)
    bounds = jnp.cumsum(jnp.concatenate([leading, crossing, trailing], axis=1), axis=1)
    position = jnp.arange(ROW, dtype=jnp.int32)
    within = jnp.sum((bounds[:, :, None] <= position[None, None, :]).astype(jnp.int32), axis=1)
    pad_start = jnp.max(jnp.where(bounds < ROW, bounds, 0), axis=1)
    number = (row_total - row_number) * piece_count - 1 - within
    picture = jnp.where(position[None, :] >= pad_start[:, None], -1, number)
    return picture.reshape(TOKENS).astype(jnp.int32)


def levels(rng, extent, cuts, least, largest):
    level = 1.0
    for dim, blocks in cuts:
        draws = jax.random.uniform(jax.random.fold_in(jax.random.fold_in(rng, 6), dim), (blocks,), jnp.float32, least / len(cuts), largest / len(cuts))
        level = level * jnp.repeat(jnp.exp(draws), extent[dim] // blocks).reshape((-1,) + (1,) * (len(extent) - 1 - dim))
    return level


def noise(key, extent, deviation, most, shards=(), kind=jnp.bfloat16):
    result = jax.random.normal(key, extent, jnp.float32) * deviation
    if len(shards) > 0:
        result = levels(key, extent, shards, -0.22, 0.18) * result
    return jnp.clip(result, min=-most, max=most).astype(kind)


def setup_inputs(seed: int = 0) -> dict:
    streams_of = jax.random.split(jax.random.key(seed), 19)
    return {
        "tokens": noise(streams_of[0], (TOKENS, D), 1.0, 6.0, ((0, 8), (1, 4))),
        "picture": draw_picture(jax.random.fold_in(streams_of[18], 71), 0),
        "cotangent": noise(streams_of[2], (TOKENS, D), 1.0, 6.0, ((0, 8), (1, 4))),
        "first_gain": jnp.clip(1.0 + 0.15 * jax.random.normal(streams_of[3], (LAYERS, D), jnp.float32), 0.25, 1.75),
        "first_shift": noise(streams_of[4], (LAYERS, D), 0.3, 1.5, ((1, 4),), jnp.float32),
        "query_weight": noise(streams_of[5], (LAYERS, D, D), D ** -0.5, 0.1875, ((1, 8), (2, 4))),
        "query_bias": noise(streams_of[6], (LAYERS, D), 0.3, 1.5, ((1, 4),), jnp.float32),
        "key_weight": noise(streams_of[7], (LAYERS, D, D), D ** -0.5, 0.1875, ((1, 8), (2, 4))),
        "value_weight": noise(streams_of[8], (LAYERS, D, D), D ** -0.5, 0.1875, ((1, 8), (2, 4))),
        "value_bias": noise(streams_of[9], (LAYERS, D), 0.3, 1.5, ((1, 4),), jnp.float32),
        "output_weight": noise(streams_of[10], (LAYERS, D, D), (D // 16) ** -0.5, 0.75, ((1, 4), (2, 8))),
        "output_bias": noise(streams_of[11], (LAYERS, D), 0.3, 1.5, ((1, 4),), jnp.float32),
        "second_gain": jnp.clip(1.0 + 0.15 * jax.random.normal(streams_of[12], (LAYERS, D), jnp.float32), 0.25, 1.75),
        "second_shift": noise(streams_of[13], (LAYERS, D), 0.3, 1.5, ((1, 4),), jnp.float32),
        "up_weight": noise(streams_of[14], (LAYERS, D, FF), D ** -0.5, 0.1875, ((1, 8), (2, 4))),
        "up_bias": noise(streams_of[15], (LAYERS, FF), 0.3, 1.5, ((1, 4),), jnp.float32),
        "down_weight": noise(streams_of[16], (LAYERS, FF, D), FF ** -0.5, 0.09375, ((1, 4), (2, 8))),
        "down_bias": noise(streams_of[17], (LAYERS, D), 0.3, 1.5, ((1, 4),), jnp.float32),
    }


@jax.custom_vjp
def low(v):
    return lax.optimization_barrier(v.astype(jnp.bfloat16)).astype(jnp.float32)

@jax.custom_vjp
def low_back(v):
    return v

def low_keep(v):
    return (low(v), None)

def low_pass(kept, grad):
    return (grad,)

def back_keep(v):
    return (v, None)

def back_low(kept, grad):
    return (low(grad),)
low.defvjp(low_keep, low_pass)
low_back.defvjp(back_keep, back_low)
eps_norm = 1e-06
gelu_factor = 0.7978845608028654
masked_fill = -1e+30

def gelu_tanh(hidden):
    return 0.5 * hidden * (1.0 + jnp.tanh(gelu_factor * (hidden + 0.044715 * hidden * hidden * hidden)))

def product(left, right):
    return jnp.dot(left, right, precision=lax.Precision.HIGHEST)

def layer_norm(residual, gain, shift):
    row_mean = lax.optimization_barrier(jnp.mean(residual, axis=-1, keepdims=True))
    centred = residual - row_mean
    inverse = lax.rsqrt(lax.optimization_barrier(jnp.mean(centred * centred, axis=-1, keepdims=True)) + eps_norm)
    return centred * inverse * gain + shift

def attend_row(queries, key_rows, value_rows, picture_row):
    shaped_query = queries.reshape(ROW, HEADS, HEAD_DIM)
    shaped_key = key_rows.reshape(ROW, HEADS, HEAD_DIM)
    shaped_value = value_rows.reshape(ROW, HEADS, HEAD_DIM)
    scores = jnp.einsum('qhd,khd->hqk', shaped_query, shaped_key, precision=lax.Precision.HIGHEST) * HEAD_DIM ** (-0.5)
    scores = low_back(scores)
    same_picture = picture_row[:, None] == picture_row[None, :]
    scores = jnp.where(same_picture[None], scores, masked_fill)
    highest = lax.optimization_barrier(jnp.max(scores, axis=-1, keepdims=True))
    powers = jnp.exp(scores - highest)
    probs = powers / lax.optimization_barrier(jnp.sum(powers, axis=-1, keepdims=True))
    mixture = jnp.einsum('hqk,khd->qhd', low(probs), shaped_value, precision=lax.Precision.HIGHEST)
    return mixture.reshape(ROW, D)
checked_row = jax.checkpoint(attend_row)

def attention(queries, key_rows, value_rows, picture):
    row_total = TOKENS // ROW
    mixture = lax.map(lambda pieces: checked_row(pieces[0], pieces[1], pieces[2], pieces[3]), (queries.reshape(row_total, ROW, D), key_rows.reshape(row_total, ROW, D), value_rows.reshape(row_total, ROW, D), picture.reshape(row_total, ROW)))
    return mixture.reshape(TOKENS, D)

def block(residual, params, picture):
    first_gain, first_shift, query_weight, query_bias, key_weight, value_weight, value_bias, output_weight, output_bias, second_gain, second_shift, up_weight, up_bias, down_weight, down_bias = params
    normed = low(layer_norm(residual, first_gain, first_shift))
    queries = low(low_back(product(normed, query_weight) + query_bias))
    key_rows = low(low_back(product(normed, key_weight)))
    value_rows = low(low_back(product(normed, value_weight) + value_bias))
    mixture = low(low_back(attention(queries, key_rows, value_rows, picture)))
    after = residual + low_back(product(mixture, output_weight) + output_bias)
    normed_two = low(layer_norm(after, second_gain, second_shift))
    hidden = low_back(product(normed_two, up_weight) + up_bias)
    active = low(gelu_tanh(hidden))
    return after + low_back(product(active, down_weight) + down_bias)

def reference(tokens, picture, cotangent, first_gain, first_shift, query_weight, query_bias, key_weight, value_weight, value_bias, output_weight, output_bias, second_gain, second_shift, up_weight, up_bias, down_weight, down_bias):
    params = tuple((weight_array.astype(jnp.float32) for weight_array in (first_gain, first_shift, query_weight, query_bias, key_weight, value_weight, value_bias, output_weight, output_bias, second_gain, second_shift, up_weight, up_bias, down_weight, down_bias)))

    def forward(initial, weights):
        residual = initial
        for layer_index in range(LAYERS):
            residual = block(residual, tuple((weight_array[layer_index] for weight_array in weights)), picture)
        return residual
    final_rows, pullback = jax.vjp(forward, tokens.astype(jnp.float32), params)
    grad_tokens, grads = pullback(cotangent.astype(jnp.float32))
    return (final_rows, grad_tokens, grads[0], grads[1], grads[2], grads[3], grads[4], grads[5], grads[6], grads[7], grads[8], grads[9], grads[10], grads[11], grads[12], grads[13], grads[14])
```

```python
import functools

import jax
import jax.numpy as jnp
from jax import lax
from jax.experimental import pallas as pl
from jax.experimental.pallas import tpu as pltpu
from jax.sharding import PartitionSpec as P

HEAD_DIM = 72
LANES = 128
KEYS = 256
EPS = 1e-06
GELU = 0.7978845608028654
CUBE = 0.044715
MASKED = -1e30
LOG2E = 1.4426950408889634
LN2 = 0.6931471805599453
NN = (((1,), (0,)), ((), ()))
NT = (((1,), (1,)), ((), ()))
TN = (((0,), (0,)), ((), ()))
MESH = pl.DeviceIdType.MESH
BF = jnp.bfloat16
F32 = jnp.float32
VMEM_LIMIT = 60 * 1024 * 1024


def dot(left, right, dims=NN):
    return lax.dot_general(left, right, dims, preferred_element_type=F32)


def micros(duration):
    return pl.CostEstimate(flops=duration * 10**9, bytes_accessed=0, transcendentals=0)


def flat(value):
    return value.reshape(value.shape[0] * value.shape[1], value.shape[2])


class Net:
    def __init__(self, send_sems, recv_sems):
        tok, hid = lax.axis_index("tok"), lax.axis_index("hid")
        near = hid + 1 - 2 * lax.rem(hid, 2)
        self.tok, self.hid = tok, hid
        self.core = (tok, near)
        self.far = (tok, lax.rem(hid + 2, 4))
        self.far_core = (tok, lax.rem(near + 2, 4))
        self.half = (tok + 1 - 2 * lax.rem(tok, 2), hid)
        self.low, self.high = lax.rem(tok, 2), lax.div(tok, 2)
        self.send_sems, self.recv_sems = send_sems, recv_sems
        self.copies = []

    def row(self, high):
        return (high * 2 + self.low, self.hid)

    def rows(self, count):
        return [self.row(lax.rem(self.high + step, count)) for step in range(1, count)]

    def barrier(self, devices):
        sem = pltpu.get_barrier_semaphore()
        for device in devices:
            pl.semaphore_signal(sem, inc=1, device_id=device, device_id_type=MESH)
        pl.semaphore_wait(sem, len(devices))

    def copy(self, source, target, device):
        index = len(self.copies)
        made = pltpu.make_async_remote_copy(
            src_ref=source,
            dst_ref=target,
            send_sem=self.send_sems.at[index],
            recv_sem=self.recv_sems.at[index],
            device_id=device,
            device_id_type=MESH,
        )
        self.copies.append(made)
        made.start()
        return made

    def finish(self, waited=()):
        done = [id(made) for made in waited]
        for made in self.copies:
            if id(made) not in done:
                made.wait_send()


def norm_parts(rows):
    centred = rows - jnp.mean(rows, axis=1, keepdims=True)
    inverse = lax.rsqrt(jnp.mean(centred * centred, axis=1, keepdims=True) + EPS)
    return centred * inverse, inverse


def norm_back(rows, gain, grad):
    scaled, inverse = norm_parts(rows)
    inner = grad * gain
    first = jnp.mean(inner, axis=1, keepdims=True)
    second = jnp.mean(inner * scaled, axis=1, keepdims=True)
    return (
        inverse * (inner - first - scaled * second),
        jnp.sum(grad * scaled, axis=0, keepdims=True),
        jnp.sum(grad, axis=0, keepdims=True),
    )


def gather_send(net, full, chunk):
    near = net.copy(full.at[0, chunk], full.at[1, chunk], net.core)
    far = net.copy(full.at[0, chunk], full.at[2, chunk], net.far)
    return near, far


def gather_pass(net, full, chunk, far):
    far.wait_recv()
    return net.copy(full.at[2, chunk], full.at[3, chunk], net.core)


def scatter_scratch(rows, width, chunks):
    return [
        pltpu.VMEM((rows, width), F32),
        pltpu.VMEM((rows, width), F32),
    ] + [pltpu.VMEM((rows, width), BF)] * 6


class Scatter:
    def __init__(self, net, scratch):
        self.net = net
        self.hold, self.total, self.cs0, self.cr0, self.ys, self.yr, self.cs1, self.cr1 = scratch
        self.first, self.second = {}, {}

    def far_part(self, key, chunk, partial):
        rows = partial.shape[0] // 2
        self.hold[chunk] = partial[:rows]
        self.cs0[chunk] = partial[rows:].astype(BF)
        self.first[key] = self.net.copy(self.cs0.at[chunk], self.cr0.at[chunk], self.net.core)

    def far_send(self, key, chunk):
        self.first[key].wait_recv()
        self.ys[chunk] = (self.hold[chunk] + self.cr0[chunk].astype(F32)).astype(BF)
        self.second[key] = self.net.copy(self.ys.at[chunk], self.yr.at[chunk], self.net.far)

    def near_part(self, partial):
        rows = partial.shape[0] // 2
        self.total[...] = partial[:rows]
        self.cs1[...] = partial[rows:].astype(BF)
        self.near = self.net.copy(self.cs1, self.cr1, self.net.core)

    def near_done(self):
        self.near.wait_recv()
        self.total[...] += self.cr1[...].astype(F32)

    def result(self, key, chunk):
        self.second[key].wait_recv()
        return self.total[chunk] + self.yr[chunk].astype(F32)


def chunks_of(rows, count):
    step = rows // count
    return [pl.ds(index * step, step) for index in range(count)]


def weight_grad(left, right, out):
    width = left.shape[2]
    tile = 384

    def one(index, carry):
        columns = pl.ds(pl.multiple_of(index * tile, tile), tile)
        out[columns, :] = dot(flat(left[:, :, columns]), flat(right[...]), TN).astype(out.dtype)
        return carry

    lax.fori_loop(0, width // tile, one, 0)


def project_kernel(
    x, vec, weight, bias, normed, queries, pairs, far_pairs, send_sems, recv_sems, *, factor
):
    net = Net(send_sems, recv_sems)
    rows, width = x.shape
    pair_cols = pairs.shape[2]
    all_cols = pair_cols + queries.shape[2]
    parts = chunks_of(rows, 2)
    net.barrier([net.core, net.far, net.half])
    scaled, _ = norm_parts(x[...])
    normed[0] = (scaled * vec[0:1] + vec[1:2]).astype(BF)
    sent = [gather_send(net, normed, chunk) for chunk in parts]
    arrived = []

    def project(slot):
        result = dot(normed[slot], weight[:, :all_cols]) + bias[...]
        pairs[slot] = result[:, :pair_cols].astype(BF)
        queries[slot] = (result[:, pair_cols:] * factor).astype(BF)
        arrived.append(net.copy(pairs.at[slot], far_pairs.at[slot], net.half))

    project(0)
    for near, _ in sent:
        near.wait_recv()
    project(1)
    passed = [gather_pass(net, normed, chunk, far) for chunk, (_, far) in zip(parts, sent)]
    project(2)
    for one in passed:
        one.wait_recv()
    project(3)
    for one in arrived:
        one.wait_recv()
    net.finish()


def project(x, vec, weight, bias, head_cols):
    rows, width = x.shape
    shapes = [
        jax.ShapeDtypeStruct((4, rows, width), BF),
        jax.ShapeDtypeStruct((4, rows, head_cols), BF),
        jax.ShapeDtypeStruct((4, rows, 2 * head_cols), BF),
        jax.ShapeDtypeStruct((4, rows, 2 * head_cols), BF),
    ]
    space = pl.BlockSpec(memory_space=pltpu.VMEM)
    return pl.pallas_call(
        functools.partial(project_kernel, factor=HEAD_DIM ** (-0.5) * LOG2E),
        name="project",
        cost_estimate=micros(44),
        out_shape=shapes,
        in_specs=[space] * 4,
        out_specs=[space] * 4,
        scratch_shapes=[pltpu.SemaphoreType.DMA((12,)), pltpu.SemaphoreType.DMA((12,))],
        compiler_params=pltpu.CompilerParams(
            collective_id=0, has_side_effects=True, vmem_limit_bytes=VMEM_LIMIT
        ),
    )(x, vec, weight, bias)


def head_pick(width, head):
    row = lax.broadcasted_iota(jnp.int32, (width, LANES), 0)
    lane = lax.broadcasted_iota(jnp.int32, (width, LANES), 1)
    return ((row == lane + head * HEAD_DIM) & (lane < HEAD_DIM)).astype(BF)


def as_rows(columns):
    rows = columns[0].shape[0]
    lane = lax.broadcasted_iota(jnp.int32, (rows, LANES), 1)
    together = jnp.zeros((rows, LANES), F32)
    for head, column in enumerate(columns):
        together = jnp.where(lane == head, column, together)
    return together.T[:8]


def load_pairs(meta, own_pairs, far_pairs, key_scratch, value_scratch, heads):
    rows = own_pairs.shape[1]
    head_cols = heads * HEAD_DIM
    hid, half = meta[0], meta[1]
    for which, source in ((0, own_pairs), (1, far_pairs)):
        for slot in range(4):
            block = jnp.bitwise_xor(hid, slot)
            place = jnp.bitwise_xor(half, which) * 4 + block
            start = pl.ds(pl.multiple_of(place * rows, rows), rows)
            both = source[slot]
            for head in range(heads):
                key = dot(both, head_pick(2 * head_cols, head))
                key_scratch[head, start, :] = key.astype(BF)
                value = dot(both, head_pick(2 * head_cols, head + heads))
                value_scratch[head, start, :] = value.astype(BF)


def attend_kernel(
    meta, queries, own_pairs, far_pairs, query_ids, key_ids, mixture, logsum,
    key_scratch, value_scratch, score_scratch, high_scratch, total_scratch, sum_scratch, query_scratch,
    *, heads
):
    rows = queries.shape[1]
    head_cols = heads * HEAD_DIM
    load_pairs(meta, own_pairs, far_pairs, key_scratch, value_scratch, heads)

    def one_block(block, carry):
        slot = jnp.bitwise_xor(meta[0], block)
        first, last = meta[2 + 2 * block], meta[3 + 2 * block]
        own = pl.ds(pl.multiple_of(block * rows, rows), rows)
        ids = query_ids[own, :]
        for head in range(heads):
            query_scratch[head] = dot(queries[slot], head_pick(head_cols, head)).astype(BF)
        high_scratch[...] = jnp.full_like(high_scratch, -3e38)
        sum_scratch[...] = jnp.zeros_like(sum_scratch)
        total_scratch[...] = jnp.zeros_like(total_scratch)

        def scores_of(key_block, inner):
            keys = pl.ds(pl.multiple_of(key_block * KEYS, KEYS), KEYS)
            same = ids == key_ids[:, keys]
            for head in range(heads):
                scores = dot(query_scratch[head], key_scratch[head, keys, :], NT)
                scores = jnp.where(same, scores, MASKED)
                score_scratch[head, :, keys] = scores
                high = high_scratch[head]
                for lane in range(0, KEYS, LANES):
                    high = jnp.maximum(high, scores[:, lane : lane + LANES])
                high_scratch[head] = high
            return inner

        lax.fori_loop(first, last, scores_of, 0)
        for head in range(heads):
            high_scratch[head] = jnp.broadcast_to(
                jnp.max(high_scratch[head], axis=1, keepdims=True), (rows, LANES)
            )

        def sums_of(key_block, inner):
            keys = pl.ds(pl.multiple_of(key_block * KEYS, KEYS), KEYS)
            for head in range(heads):
                high = high_scratch[head]
                high = jnp.concatenate([high] * (KEYS // LANES), axis=1)
                powers = jnp.exp2(score_scratch[head, :, keys] - high)
                total = total_scratch[head]
                for lane in range(0, KEYS, LANES):
                    total += powers[:, lane : lane + LANES]
                total_scratch[head] = total
                sum_scratch[head] += dot(powers.astype(BF), value_scratch[head, keys, :])
            return inner

        lax.fori_loop(first, last, sums_of, 0)
        result = jnp.zeros((rows, head_cols), F32)
        columns = []
        for head in range(heads):
            sums = sum_scratch[head]
            total = jnp.sum(total_scratch[head], axis=1, keepdims=True)
            columns.append(high_scratch[head][:, :1] + jnp.log2(total))
            mixed = (sums / total).astype(BF)
            result += dot(mixed, head_pick(head_cols, head), NT)
        mixture[slot] = result.astype(BF)
        logsum[:, own] = as_rows(columns)
        return carry

    lax.fori_loop(0, 4, one_block, 0)


def attend(meta, queries, own_pairs, far_pairs, query_ids, key_ids):
    _, rows, head_cols = queries.shape
    heads = head_cols // HEAD_DIM
    own, count = 4 * rows, 8 * rows
    space = pl.BlockSpec(memory_space=pltpu.VMEM)
    return pl.pallas_call(
        functools.partial(attend_kernel, heads=heads),
        name="attend",
        cost_estimate=micros(22),
        out_shape=[
            jax.ShapeDtypeStruct((4, rows, head_cols), BF),
            jax.ShapeDtypeStruct((8, own), F32),
        ],
        in_specs=[pl.BlockSpec(memory_space=pltpu.SMEM)] + [space] * 5,
        out_specs=[space] * 2,
        scratch_shapes=[
            pltpu.VMEM((heads, count, LANES), BF),
            pltpu.VMEM((heads, count, LANES), BF),
            pltpu.VMEM((heads, rows, count), F32),
            pltpu.VMEM((heads, rows, LANES), F32),
            pltpu.VMEM((heads, rows, LANES), F32),
            pltpu.VMEM((heads, rows, LANES), F32),
            pltpu.VMEM((heads, rows, LANES), BF),
        ],
        compiler_params=pltpu.CompilerParams(vmem_limit_bytes=VMEM_LIMIT),
    )(meta, queries, own_pairs, far_pairs, query_ids, key_ids)


def attend_back_kernel(
    meta, queries, own_pairs, far_pairs, query_ids, key_ids, grad_mixture, logsum,
    grad_queries, grad_own, grad_far,
    key_scratch, value_scratch, grad_key, grad_value, grad_query, query_scratch, grad_scratch,
    prob_scratch, grad_prob_scratch, delta_scratch,
    *, heads
):
    rows = queries.shape[1]
    head_cols = heads * HEAD_DIM
    load_pairs(meta, own_pairs, far_pairs, key_scratch, value_scratch, heads)
    grad_key[...] = jnp.zeros_like(grad_key)
    grad_value[...] = jnp.zeros_like(grad_value)

    def one_block(block, carry):
        slot = jnp.bitwise_xor(meta[0], block)
        first, last = meta[2 + 2 * block], meta[3 + 2 * block]
        own = pl.ds(pl.multiple_of(block * rows, rows), rows)
        ids = query_ids[:, own]
        for head in range(heads):
            pick = head_pick(head_cols, head)
            query_scratch[head] = dot(queries[slot], pick).astype(BF)
            grad_scratch[head] = dot(grad_mixture[slot], pick).astype(BF)
        logs = logsum[:, own]
        grad_query[...] = jnp.zeros_like(grad_query)
        delta_scratch[...] = jnp.zeros_like(delta_scratch)

        def probs_of(key_block, inner):
            keys = pl.ds(pl.multiple_of(key_block * KEYS, KEYS), KEYS)
            same = key_ids[keys, :] == ids
            for head in range(heads):
                grad = grad_scratch[head]
                scores = dot(key_scratch[head, keys, :], query_scratch[head], NT)
                probs = jnp.where(same, jnp.exp2(scores - logs[head : head + 1]), 0.0)
                grad_probs = dot(value_scratch[head, keys, :], grad, NT)
                prob_scratch[head, keys, :] = probs
                grad_prob_scratch[head, keys, :] = grad_probs
                delta_scratch[head] += jnp.sum((probs * grad_probs).reshape(KEYS // 8, 8, rows), axis=0)
                grad_value[head, keys, :] += dot(probs.astype(BF), grad)
            return inner

        lax.fori_loop(first, last, probs_of, 0)
        for head in range(heads):
            delta_scratch[head, 0:1] = jnp.sum(delta_scratch[head], axis=0, keepdims=True)

        def one_key(key_block, inner):
            keys = pl.ds(pl.multiple_of(key_block * KEYS, KEYS), KEYS)
            for head in range(heads):
                delta = delta_scratch[head, 0:1]
                grad_scores = prob_scratch[head, keys, :] * (grad_prob_scratch[head, keys, :] - delta)
                grad_scores = grad_scores.astype(BF)
                grad_key[head, keys, :] += dot(grad_scores, query_scratch[head])
                grad_query[head] += dot(grad_scores, key_scratch[head, keys, :], TN)
            return inner

        lax.fori_loop(first, last, one_key, 0)
        result = jnp.zeros((rows, head_cols), F32)
        for head in range(heads):
            scaled = (grad_query[head] * HEAD_DIM ** (-0.5)).astype(BF)
            result += dot(scaled, head_pick(head_cols, head), NT)
        grad_queries[slot] = result.astype(BF)
        return carry

    lax.fori_loop(0, 4, one_block, 0)
    hid, half = meta[0], meta[1]
    for which, target in ((0, grad_own), (1, grad_far)):
        for slot in range(4):
            place = jnp.bitwise_xor(half, which) * 4 + jnp.bitwise_xor(hid, slot)
            start = pl.ds(pl.multiple_of(place * rows, rows), rows)
            keys = jnp.zeros((rows, head_cols), F32)
            values = jnp.zeros((rows, head_cols), F32)
            for head in range(heads):
                pick = head_pick(head_cols, head)
                keys += dot((grad_key[head, start, :] * LN2).astype(BF), pick, NT)
                values += dot(grad_value[head, start, :].astype(BF), pick, NT)
            target[slot, :, :head_cols] = keys.astype(BF)
            target[slot, :, head_cols:] = values.astype(BF)


def attend_back(meta, queries, own_pairs, far_pairs, query_ids, key_ids, grad_mixture, logsum):
    _, rows, head_cols = queries.shape
    heads = head_cols // HEAD_DIM
    count = 8 * rows
    space = pl.BlockSpec(memory_space=pltpu.VMEM)
    return pl.pallas_call(
        functools.partial(attend_back_kernel, heads=heads),
        name="attend_back",
        cost_estimate=micros(37),
        out_shape=[
            jax.ShapeDtypeStruct((4, rows, head_cols), BF),
            jax.ShapeDtypeStruct((4, rows, 2 * head_cols), BF),
            jax.ShapeDtypeStruct((4, rows, 2 * head_cols), BF),
        ],
        in_specs=[pl.BlockSpec(memory_space=pltpu.SMEM)] + [space] * 7,
        out_specs=[space] * 3,
        scratch_shapes=[
            pltpu.VMEM((heads, count, LANES), BF),
            pltpu.VMEM((heads, count, LANES), BF),
            pltpu.VMEM((heads, count, LANES), F32),
            pltpu.VMEM((heads, count, LANES), F32),
            pltpu.VMEM((heads, rows, LANES), F32),
            pltpu.VMEM((heads, rows, LANES), BF),
            pltpu.VMEM((heads, rows, LANES), BF),
            pltpu.VMEM((heads, count, rows), F32),
            pltpu.VMEM((heads, count, rows), F32),
            pltpu.VMEM((heads, 8, rows), F32),
        ],
        compiler_params=pltpu.CompilerParams(vmem_limit_bytes=VMEM_LIMIT),
    )(meta, queries, own_pairs, far_pairs, query_ids, key_ids, grad_mixture, logsum)


def mlp_kernel(
    mixture, x, vec, out_weight, up_weight, up_bias, down_weight,
    x_next, after, normed, active, slope, *scratch
):
    net = Net(*scratch[16:])
    rows = x.shape[0]
    parts = chunks_of(rows, 2)
    net.barrier([net.core, net.far])
    out_bias, gain, shift, down_bias = vec[2:3], vec[3:4], vec[4:5], vec[5:6]

    def mixed(slots, chunk):
        return dot(flat(mixture[slots, chunk, :]), out_weight[...], NT)

    def up(slots, chunk):
        hidden = dot(flat(normed[slots, chunk, :]), up_weight[...]) + up_bias[...]
        square = hidden * hidden
        bend = jnp.tanh(GELU * hidden * (1.0 + CUBE * square))
        half = 0.5 * (1.0 + bend)
        value = hidden * half
        rise = half + 0.5 * hidden * (1.0 - bend * bend) * GELU * (1.0 + 3.0 * CUBE * square)
        shape = (2, hidden.shape[0] // 2, hidden.shape[1])
        active[slots, chunk, :] = value.astype(BF).reshape(shape)
        slope[slots, chunk, :] = rise.astype(BF).reshape(shape)

    def down(slots, chunk):
        return dot(flat(active[slots, chunk, :]), down_weight[...], NT)

    near, far, whole = pl.ds(0, 2), pl.ds(2, 2), pl.ds(0, rows)
    first = Scatter(net, scratch[0:8])
    for key, chunk in enumerate(parts):
        first.far_part(key, chunk, mixed(far, chunk))
    for key, chunk in enumerate(parts):
        first.far_send(key, chunk)
    first.near_part(mixed(near, whole))
    first.near_done()
    sent = []
    for key, chunk in enumerate(parts):
        residual = first.result(key, chunk) + x[chunk, :] + out_bias
        after[chunk, :] = residual
        normed[0, chunk, :] = (norm_parts(residual)[0] * gain + shift).astype(BF)
        sent.append(gather_send(net, normed, chunk))
    for one, _ in sent:
        one.wait_recv()
    up(near, whole)
    second = Scatter(net, scratch[8:16])
    for key, chunk in enumerate(parts):
        passed = gather_pass(net, normed, chunk, sent[key][1])
        passed.wait_recv()
        up(far, chunk)
        second.far_part(key, chunk, down(far, chunk))
        second.far_send(key, chunk)
    second.near_part(down(near, whole))
    second.near_done()
    for key, chunk in enumerate(parts):
        x_next[chunk, :] = second.result(key, chunk) + after[chunk, :] + down_bias
    net.finish()


def mlp(mixture, x, vec, out_weight, up_weight, up_bias, down_weight):
    rows, width = x.shape
    hidden = up_weight.shape[1]
    space = pl.BlockSpec(memory_space=pltpu.VMEM)
    return pl.pallas_call(
        mlp_kernel,
        name="mlp",
        cost_estimate=micros(51),
        out_shape=[
            jax.ShapeDtypeStruct((rows, width), F32),
            jax.ShapeDtypeStruct((rows, width), F32),
            jax.ShapeDtypeStruct((4, rows, width), BF),
            jax.ShapeDtypeStruct((4, rows, hidden), BF),
            jax.ShapeDtypeStruct((4, rows, hidden), BF),
        ],
        in_specs=[space] * 7,
        out_specs=[space] * 5,
        scratch_shapes=scatter_scratch(rows, width, 2) * 2
        + [pltpu.SemaphoreType.DMA((16,)), pltpu.SemaphoreType.DMA((16,))],
        compiler_params=pltpu.CompilerParams(
            collective_id=1, has_side_effects=True, vmem_limit_bytes=VMEM_LIMIT
        ),
    )(mixture, x, vec, out_weight, up_weight, up_bias, down_weight)


def mlp_back_kernel(
    gradient, after, vec, out_weight, up_weight, down_weight, mixture, normed, active, slope,
    grad_after, grad_mixture, grad_down, grad_up, grad_out, sums, hidden_sums, *scratch
):
    net = Net(*scratch[11:])
    grad_rows, grad_hidden, grad_mid = scratch[8:11]
    rows, width = gradient.shape
    parts = chunks_of(rows, 2)
    net.barrier([net.core, net.far])
    gain = vec[3:4]
    near, far, whole = pl.ds(0, 2), pl.ds(2, 2), pl.ds(0, rows)
    rounded = gradient[...].astype(BF)
    grad_rows[0] = rounded
    sent = [gather_send(net, grad_rows, chunk) for chunk in parts]
    sums[...] = jnp.zeros_like(sums)
    sums[5:6] = jnp.sum(rounded.astype(F32), axis=0, keepdims=True)

    def hidden_grad(slots, chunk):
        value = dot(flat(grad_rows[slots, chunk, :]), down_weight[...])
        value = value * flat(slope[slots, chunk, :]).astype(F32)
        shape = (2, value.shape[0] // 2, value.shape[1])
        grad_hidden[slots, chunk, :] = value.astype(BF).reshape(shape)

    def up_back(slots, chunk):
        return dot(flat(grad_hidden[slots, chunk, :]), up_weight[...], NT)

    for one, _ in sent:
        one.wait_recv()
    hidden_grad(near, whole)
    scatter = Scatter(net, scratch[0:8])
    for key, chunk in enumerate(parts):
        passed = gather_pass(net, grad_rows, chunk, sent[key][1])
        passed.wait_recv()
        hidden_grad(far, chunk)
        scatter.far_part(key, chunk, up_back(far, chunk))
        scatter.far_send(key, chunk)
    scatter.near_part(up_back(near, whole))
    weight_grad(grad_rows, active, grad_down)
    scatter.near_done()
    sent = []
    for key, chunk in enumerate(parts):
        back, gain_sum, shift_sum = norm_back(after[chunk, :], gain, scatter.result(key, chunk))
        total = gradient[chunk, :] + back
        grad_after[chunk, :] = total
        rounded = total.astype(BF)
        grad_mid[0, chunk, :] = rounded
        sent.append(gather_send(net, grad_mid, chunk))
        sums[3:4] += gain_sum
        sums[4:5] += shift_sum
        sums[2:3] += jnp.sum(rounded.astype(F32), axis=0, keepdims=True)
    weight_grad(normed, grad_hidden, grad_up)
    column = jnp.zeros((1, hidden_sums.shape[1]), F32)
    for slot in range(4):
        column += jnp.sum(grad_hidden[slot].astype(F32), axis=0, keepdims=True)
    hidden_sums[...] = column

    def mix_back(slots, chunk):
        value = dot(flat(grad_mid[slots, chunk, :]), out_weight[...])
        shape = (2, value.shape[0] // 2, value.shape[1])
        grad_mixture[slots, chunk, :] = value.astype(BF).reshape(shape)

    for one, _ in sent:
        one.wait_recv()
    mix_back(near, whole)
    for key, chunk in enumerate(parts):
        gather_pass(net, grad_mid, chunk, sent[key][1]).wait_recv()
    mix_back(far, whole)
    weight_grad(grad_mid, mixture, grad_out)
    net.finish()


def mlp_back(
    gradient, after, vec, out_weight, up_weight, down_weight, mixture, normed, active, slope
):
    rows, width = gradient.shape
    hidden = up_weight.shape[1]
    head_cols = out_weight.shape[1]
    space = pl.BlockSpec(memory_space=pltpu.VMEM)
    return pl.pallas_call(
        mlp_back_kernel,
        name="mlp_back",
        cost_estimate=micros(54),
        out_shape=[
            jax.ShapeDtypeStruct((rows, width), F32),
            jax.ShapeDtypeStruct((4, rows, head_cols), BF),
            jax.ShapeDtypeStruct((width, hidden), BF),
            jax.ShapeDtypeStruct((width, hidden), BF),
            jax.ShapeDtypeStruct((width, head_cols), BF),
            jax.ShapeDtypeStruct((8, width), F32),
            jax.ShapeDtypeStruct((1, hidden), F32),
        ],
        in_specs=[space] * 10,
        out_specs=[space] * 7,
        scratch_shapes=scatter_scratch(rows, width, 2)
        + [
            pltpu.VMEM((4, rows, width), BF),
            pltpu.VMEM((4, rows, hidden), BF),
            pltpu.VMEM((4, rows, width), BF),
            pltpu.SemaphoreType.DMA((20,)),
            pltpu.SemaphoreType.DMA((20,)),
        ],
        compiler_params=pltpu.CompilerParams(
            collective_id=2, has_side_effects=True, vmem_limit_bytes=VMEM_LIMIT
        ),
    )(gradient, after, vec, out_weight, up_weight, down_weight, mixture, normed, active, slope)


def project_back_kernel(
    grad_after, x, vec, weight, normed, grad_queries, grad_own, grad_far,
    gradient, grad_weight, sums, column_sums, *scratch
):
    net = Net(*scratch[10:])
    landed, together = scratch[8:10]
    rows, width = x.shape
    pair_cols = grad_own.shape[2]
    all_cols = together.shape[2]
    parts = chunks_of(rows, 2)
    near, far, whole = pl.ds(0, 2), pl.ds(2, 2), pl.ds(0, rows)
    net.barrier([net.core, net.far, net.half])
    arriving = {
        slot: net.copy(grad_far.at[slot], landed.at[slot], net.half) for slot in (3, 2, 1, 0)
    }
    together[:, :, pair_cols:] = grad_queries[...]

    def join(slot):
        arriving[slot].wait_recv()
        pair = grad_own[slot].astype(F32) + landed[slot].astype(F32)
        together[slot, :, :pair_cols] = pair.astype(BF)

    def back(slots, chunk):
        return dot(flat(together[slots, chunk, :]), weight[:, :all_cols], NT)

    scatter = Scatter(net, scratch[0:8])
    join(3)
    join(2)
    for key, chunk in enumerate(parts):
        scatter.far_part(key, chunk, back(far, chunk))
    for key, chunk in enumerate(parts):
        scatter.far_send(key, chunk)
    join(1)
    join(0)
    scatter.near_part(back(near, whole))
    weight_grad(normed, together, grad_weight)
    column = jnp.zeros((1, all_cols), F32)
    for slot in range(4):
        column += jnp.sum(together[slot].astype(F32), axis=0, keepdims=True)
    column_sums[...] = column
    scatter.near_done()
    sums[...] = jnp.zeros_like(sums)
    for key, chunk in enumerate(parts):
        grad, gain_sum, shift_sum = norm_back(x[chunk, :], vec[0:1], scatter.result(key, chunk))
        gradient[chunk, :] = grad_after[chunk, :] + grad
        sums[0:1] += gain_sum
        sums[1:2] += shift_sum
    net.finish()


def project_back(grad_after, x, vec, weight, normed, grad_queries, grad_own, grad_far):
    rows, width = x.shape
    all_cols = grad_queries.shape[2] + grad_own.shape[2]
    space = pl.BlockSpec(memory_space=pltpu.VMEM)
    return pl.pallas_call(
        project_back_kernel,
        name="project_back",
        cost_estimate=micros(44),
        out_shape=[
            jax.ShapeDtypeStruct((rows, width), F32),
            jax.ShapeDtypeStruct((width, all_cols), BF),
            jax.ShapeDtypeStruct((8, width), F32),
            jax.ShapeDtypeStruct((1, all_cols), F32),
        ],
        in_specs=[space] * 8,
        out_specs=[space] * 4,
        scratch_shapes=scatter_scratch(rows, width, 2)
        + [
            pltpu.VMEM(grad_far.shape, BF),
            pltpu.VMEM((4, rows, all_cols), BF),
            pltpu.SemaphoreType.DMA((12,)),
            pltpu.SemaphoreType.DMA((12,)),
        ],
        compiler_params=pltpu.CompilerParams(
            collective_id=3, has_side_effects=True, vmem_limit_bytes=VMEM_LIMIT
        ),
    )(grad_after, x, vec, weight, normed, grad_queries, grad_own, grad_far)


def entry_kernel(
    tokens, cotangent, vectors, shard, tokens_out, cotangent_out, vectors_out, weights,
    send_sems, recv_sems, local_sem,
):
    net = Net(send_sems, recv_sems)
    count = weights.shape[0] // 2
    others = [net.core, net.far, net.far_core]
    net.barrier(others + [net.half] + net.rows(count))
    mine = net.tok
    local = pltpu.make_async_copy(shard, weights.at[mine], local_sem)
    local.start()
    along = [net.copy(shard, weights.at[mine], device) for device in net.rows(count)]
    across = [net.copy(shard, weights.at[mine], net.half)]
    moved = []
    for source, target in ((tokens, tokens_out), (cotangent, cotangent_out)):
        for device in reversed(others):
            moved.append(net.copy(source.at[device[1]], target.at[net.hid], device))
        target[net.hid] = source[net.hid]
    for device in others:
        moved.append(net.copy(vectors, vectors_out.at[net.hid], device))
    vectors_out[net.hid] = vectors[...]
    for step, one in enumerate(along):
        one.wait_recv()
        place = lax.rem(net.high + count - step - 1, count) * 2 + net.low
        across.append(net.copy(weights.at[place], weights.at[place], net.half))
    for one in across + moved:
        one.wait_recv()
    local.wait()
    net.finish()


def entry(tokens, cotangent, vectors, shard, count):
    space = pl.BlockSpec(memory_space=pltpu.VMEM)
    whole = pl.BlockSpec(memory_space=pl.ANY)
    copies = 9 + count
    return pl.pallas_call(
        entry_kernel,
        name="entry",
        cost_estimate=micros(40),
        out_shape=[
            jax.ShapeDtypeStruct(tokens.shape, BF),
            jax.ShapeDtypeStruct(cotangent.shape, BF),
            jax.ShapeDtypeStruct((4,) + vectors.shape, F32),
            jax.ShapeDtypeStruct((count,) + shard.shape, BF),
        ],
        in_specs=[space] * 3 + [whole],
        out_specs=[space] * 3 + [whole],
        scratch_shapes=[
            pltpu.SemaphoreType.DMA((copies,)),
            pltpu.SemaphoreType.DMA((copies,)),
            pltpu.SemaphoreType.DMA(()),
        ],
        compiler_params=pltpu.CompilerParams(
            collective_id=4, has_side_effects=True, vmem_limit_bytes=VMEM_LIMIT
        ),
    )(tokens, cotangent, vectors, shard)


def finish_kernel(
    final, gradient, wide, narrow, grads, final_out, gradient_out, sums, total,
    wide_land, across_land, along_land, landed, passing, arrived, send_sems, recv_sems,
):
    net = Net(send_sems, recv_sems)
    count = grads.shape[0] // 2
    others = [net.core, net.far, net.far_core]
    net.barrier(others + [net.half] + net.rows(count))
    steps = list(range(1, count)) + [0]
    place = {step: lax.rem(net.high + step, count) for step in steps}
    summed = [net.copy(wide.at[device[1]], wide_land.at[net.hid], device) for device in others]
    across = {}
    for step in steps:
        source = grads.at[place[step] * 2 + 1 - net.low]
        across[step] = net.copy(source, landed.at[place[step]], net.half)
    moved = []
    for source, target in ((final, final_out), (gradient, gradient_out)):
        for device in reversed(others):
            moved.append(net.copy(source.at[device[1]], target.at[net.hid], device))
        target[net.hid] = source[net.hid]
    wide_land[net.hid] = wide[net.hid]
    for one in summed:
        one.wait_recv()
    top = wide.shape[1]
    sums[:top] = wide_land[0] + wide_land[1] + wide_land[2] + wide_land[3]
    sums[top:] = narrow[...]
    swap = net.copy(sums, across_land, net.half)
    swap.wait()
    sums[...] += across_land[...]
    spread = [
        net.copy(sums, along_land.at[step], device)
        for step, device in enumerate(net.rows(count))
    ]
    along = []
    for step in steps[:-1]:
        across[step].wait_recv()
        mine = grads[place[step] * 2 + net.low].astype(F32)
        passing[step] = (mine + landed[place[step]].astype(F32)).astype(BF)
        along.append(net.copy(passing.at[step], arrived.at[step], net.row(place[step])))
    across[0].wait_recv()
    total[...] = grads[net.tok].astype(F32) + landed[net.high].astype(F32)
    for step, one in enumerate(spread):
        one.wait()
    reduced = sums[...]
    for step in range(count - 1):
        reduced += along_land[step]
    sums[...] = reduced
    for step, one in zip(steps, along):
        one.wait_recv()
        total[...] += arrived[step].astype(F32)
    for one in moved:
        one.wait_recv()
    net.finish([swap] + spread)


def finish(final, gradient, wide, narrow, grads):
    count, shard, width = grads.shape
    count = count // 2
    space = pl.BlockSpec(memory_space=pltpu.VMEM)
    sum_rows = wide.shape[1] + narrow.shape[0]
    copies = 10 + 3 * count
    return pl.pallas_call(
        finish_kernel,
        name="finish",
        cost_estimate=micros(40),
        out_shape=[
            jax.ShapeDtypeStruct(final.shape, BF),
            jax.ShapeDtypeStruct(gradient.shape, BF),
            jax.ShapeDtypeStruct((sum_rows, wide.shape[2]), F32),
            jax.ShapeDtypeStruct((shard, width), F32),
        ],
        in_specs=[space] * 5,
        out_specs=[space] * 4,
        scratch_shapes=[
            pltpu.VMEM(wide.shape, F32),
            pltpu.VMEM((sum_rows, wide.shape[2]), F32),
            pltpu.VMEM((count, sum_rows, wide.shape[2]), F32),
            pltpu.VMEM((count, shard, width), BF),
            pltpu.VMEM((count, shard, width), BF),
            pltpu.VMEM((count, shard, width), BF),
            pltpu.SemaphoreType.DMA((copies,)),
            pltpu.SemaphoreType.DMA((copies,)),
        ],
        compiler_params=pltpu.CompilerParams(
            collective_id=5, has_side_effects=True, vmem_limit_bytes=VMEM_LIMIT
        ),
    )(final, gradient, wide, narrow, grads)


def key_ranges(own_ids, row_ids, rows):
    position = jnp.arange(row_ids.shape[0], dtype=jnp.int32)
    bounds = []
    for block in range(own_ids.shape[0] // rows):
        first = own_ids[block * rows]
        last = own_ids[(block + 1) * rows - 1]
        low = jnp.min(jnp.where(row_ids == first, position, row_ids.shape[0]))
        high = jnp.max(jnp.where(row_ids == last, position, -1)) + 1
        bounds += [low // KEYS, (high + KEYS - 1) // KEYS]
    return bounds


def body(
    tokens, picture, cotangent, first_gain, first_shift, query_weight, query_bias, key_weight,
    value_weight, value_bias, output_weight, output_bias, second_gain, second_shift, up_weight,
    up_bias, down_weight, down_bias,
):
    token_count = tokens.shape[0]
    rows = token_count // 4
    layers = query_weight.shape[0]
    head_cols = query_bias.shape[1]
    feed = up_bias.shape[1]
    feed_pad = -feed % LANES
    hid = lax.axis_index("hid")
    tok = lax.axis_index("tok")

    own_ids = lax.dynamic_slice_in_dim(picture, tok * token_count, token_count)
    row_ids = lax.dynamic_slice_in_dim(picture, (tok // 2) * 2 * token_count, 2 * token_count)
    meta = jnp.stack([hid, tok % 2] + key_ranges(own_ids, row_ids, rows)).astype(jnp.int32)

    def side_by_side(*parts):
        return jnp.concatenate(parts, axis=1)

    def padded(part):
        return jnp.pad(part, ((0, 0), (0, feed_pad)))

    def by_tokens(array):
        return array.transpose(1, 0, 2).reshape(rows, 4 * array.shape[2]).astype(F32)

    def by_features(array):
        return array.reshape(rows, 4, head_cols).transpose(1, 0, 2)

    count = lax.axis_size("tok")
    shard = query_weight.shape[1]
    shard_pad = -shard % 16
    layer_parts = []
    for layer in range(layers):
        mixed = side_by_side(
            key_weight[layer], value_weight[layer], query_weight[layer], output_weight[layer].T
        )
        layer_parts.append((mixed, padded(up_weight[layer]), padded(down_weight[layer].T)))
    vectors = jnp.stack(
        [first_gain, first_shift, output_bias, second_gain, second_shift, down_bias], axis=1
    )
    vectors = jnp.pad(vectors, ((0, 0), (0, 2), (0, 0))).reshape(layers * 8, head_cols)
    x, gradient, vectors, first_mixed = entry(
        tokens.reshape(4, rows, head_cols),
        cotangent.reshape(4, rows, head_cols),
        vectors,
        jnp.pad(layer_parts[0][0], ((0, shard_pad), (0, 0))),
        count,
    )
    x, gradient = by_tokens(x), by_tokens(gradient)
    vectors = vectors.transpose(1, 0, 2).reshape(layers, 8, 4 * head_cols)

    def gather(part):
        return lax.all_gather(part, "tok", axis=0, tiled=True)

    weights = []
    for layer in range(layers):
        mixed, up, down = layer_parts[layer]
        if layer == 0:
            mixed = first_mixed[:, :shard].reshape(count * shard, mixed.shape[1])
        else:
            mixed, _ = lax.optimization_barrier((mixed, both))
            mixed = gather(mixed)
            up, _ = lax.optimization_barrier((up, mixed))
        both = gather(side_by_side(up, down))
        up, down = jnp.split(both, 2, axis=1)
        weights.append((mixed, mixed[:, 3 * head_cols :], up, down))

    saved = []
    for layer in range(layers):
        mixed, out, up, down = weights[layer]
        bias = jnp.concatenate(
            [jnp.zeros_like(value_bias[layer]), value_bias[layer], query_bias[layer]]
        )[None]
        normed, queries, own_pairs, far_pairs = project(x, vectors[layer], mixed, bias, head_cols)
        mixture, logsum = attend(
            meta, queries, own_pairs, far_pairs, own_ids[:, None], row_ids[None, :]
        )
        hidden_bias = jnp.pad(up_bias[layer], (0, feed_pad))[None]
        x_next, after, normed_two, active, slope = mlp(
            mixture, x, vectors[layer], out, up, hidden_bias, down
        )
        saved.append(
            (x, normed, queries, own_pairs, far_pairs, mixture, logsum, after, normed_two, active, slope)
        )
        x = x_next
    final = x

    def scatter(part):
        mine = lax.psum_scatter(part, "tok", scatter_dimension=0, tiled=True)
        return lax.optimization_barrier(mine).astype(F32)

    grads = [None] * layers
    wide, narrow, broad = [None] * layers, [None] * layers, [None] * layers
    for layer in reversed(range(layers)):
        x, normed, queries, own_pairs, far_pairs, mixture, logsum, after, normed_two, active, slope = saved[layer]
        mixed, out, up, down = weights[layer]
        grad_after, grad_mixture, grad_down, grad_up, grad_out, sums_two, hidden_sums = mlp_back(
            gradient, after, vectors[layer], out, up, down, mixture, normed_two, active, slope
        )
        grad_queries, grad_own, grad_far = attend_back(
            meta, queries, own_pairs, far_pairs, own_ids[None, :], row_ids[:, None],
            grad_mixture, logsum,
        )
        if layer == 0:
            grad_after, grads[1][1] = lax.optimization_barrier((grad_after, grads[1][1]))
        gradient, grad_mixed, sums_one, column_sums = project_back(
            grad_after, x, vectors[layer], mixed, normed, grad_queries, grad_own, grad_far
        )
        grad_both = side_by_side(grad_up, grad_down)
        grad_mixed = side_by_side(grad_mixed, grad_out)
        grads[layer] = [grad_mixed, scatter(grad_both)]
        if layer > 0:
            grads[layer][0] = scatter(grad_mixed)
        wide[layer] = sums_one + sums_two
        narrow[layer] = column_sums[0]
        broad[layer] = hidden_sums[0]
    wide = jnp.concatenate(wide, axis=0)
    wide = wide.reshape(layers * 8, 4, head_cols).transpose(1, 0, 2)
    narrow = jnp.concatenate(narrow + broad)
    narrow_rows = -(-narrow.shape[0] // head_cols)
    narrow_rows += -narrow_rows % 8
    narrow = jnp.pad(narrow, (0, narrow_rows * head_cols - narrow.shape[0]))
    grad_mixed = grads[0][0].reshape(count, shard, 4 * head_cols)
    final, gradient, sums, first_grad = finish(
        by_features(final.astype(BF)),
        by_features(gradient.astype(BF)),
        wide,
        narrow.reshape(narrow_rows, head_cols),
        jnp.pad(grad_mixed, ((0, 0), (0, shard_pad), (0, 0))),
    )
    grads[0][0] = first_grad[:shard]
    wide = sums[: layers * 8].reshape(layers, 8, head_cols)
    narrow = sums[layers * 8 :].reshape(-1)
    cut = layers * 3 * head_cols
    broad = narrow[cut : cut + layers * (feed + feed_pad)].reshape(layers, feed + feed_pad)[:, :feed]
    narrow = narrow[:cut].reshape(layers, 3 * head_cols)

    def stacked(pick):
        return jnp.stack([pick(mixed, both) for mixed, both in grads])

    return (
        final.reshape(4 * rows, head_cols).astype(F32),
        gradient.reshape(4 * rows, head_cols).astype(F32),
        wide[:, 0],
        wide[:, 1],
        stacked(lambda mixed, both: mixed[:, 2 * head_cols : 3 * head_cols]),
        narrow[:, 2 * head_cols :],
        stacked(lambda mixed, both: mixed[:, :head_cols]),
        stacked(lambda mixed, both: mixed[:, head_cols : 2 * head_cols]),
        narrow[:, head_cols : 2 * head_cols],
        stacked(lambda mixed, both: mixed[:, 3 * head_cols :].T),
        wide[:, 2],
        wide[:, 3],
        wide[:, 4],
        stacked(lambda mixed, both: both[:, :feed]),
        broad,
        stacked(lambda mixed, both: both[:, feed + feed_pad : feed + feed_pad + feed].T),
        wide[:, 5],
    )


def solution(mesh):
    rows = P("tok", "hid")
    vector = P(None, "hid")
    inward = P(None, "tok", "hid")
    outward = P(None, "hid", "tok")
    in_specs = (
        rows, P(), rows, vector, vector, inward, vector, inward, inward, vector, outward, vector,
        vector, vector, inward, vector, outward, vector,
    )
    out_specs = (
        rows, rows, vector, vector, inward, vector, inward, inward, vector, outward, vector,
        vector, vector, inward, vector, outward, vector,
    )
    return jax.shard_map(body, mesh=mesh, in_specs=in_specs, out_specs=out_specs, check_vma=False)
```

```python
import functools

import jax
import jax.numpy as jnp
from jax import lax
from jax.experimental import pallas as pl
from jax.experimental.pallas import tpu as pltpu
from jax.sharding import PartitionSpec as P

HEAD_DIM = 72
LANES = 128
KEYS = 512
EPS = 1e-06
GELU = 0.7978845608028654
CUBE = 0.044715
MASKED = -1e30
LOG2E = 1.4426950408889634
LN2 = 0.6931471805599453
NN = (((1,), (0,)), ((), ()))
NT = (((1,), (1,)), ((), ()))
TN = (((0,), (0,)), ((), ()))
MESH = pl.DeviceIdType.MESH
BF = jnp.bfloat16
F32 = jnp.float32
VMEM_LIMIT = 60 * 1024 * 1024


def dot(left, right, dims=NN):
    return lax.dot_general(left, right, dims, preferred_element_type=F32)


def micros(duration):
    return pl.CostEstimate(flops=duration * 10**9, bytes_accessed=0, transcendentals=0)


def flat(value):
    return value.reshape(value.shape[0] * value.shape[1], value.shape[2])


class Net:
    def __init__(self, send_sems, recv_sems):
        tok, hid = lax.axis_index("tok"), lax.axis_index("hid")
        near = hid + 1 - 2 * lax.rem(hid, 2)
        self.tok, self.hid = tok, hid
        self.core = (tok, near)
        self.far = (tok, lax.rem(hid + 2, 4))
        self.far_core = (tok, lax.rem(near + 2, 4))
        self.half = (tok + 1 - 2 * lax.rem(tok, 2), hid)
        self.low, self.high = lax.rem(tok, 2), lax.div(tok, 2)
        self.send_sems, self.recv_sems = send_sems, recv_sems
        self.copies, self.count = [], 0

    def row(self, high):
        return (high * 2 + self.low, self.hid)

    def line(self, count):
        self.before, self.has_before = self.row(lax.max(self.high - 1, 0)), self.high > 0
        self.after = self.row(lax.min(self.high + 1, count - 1))
        self.has_after, self.last = self.high + 1 < count, count - 1

    def barrier(self, devices, line=False):
        sem = pltpu.get_barrier_semaphore()

        def signal(device):
            pl.semaphore_signal(sem, inc=1, device_id=device, device_id_type=MESH)

        for device in devices:
            signal(device)
        peers = len(devices)
        if line:
            pl.when(self.has_before)(lambda: signal(self.before))
            pl.when(self.has_after)(lambda: signal(self.after))
            peers = peers + lax.min(self.high, 1) + lax.min(self.last - self.high, 1)
        pl.semaphore_wait(sem, peers)

    def take(self, count):
        first = self.count
        self.count += count
        return first

    def make(self, index, source, target, device):
        return pltpu.make_async_remote_copy(
            src_ref=source,
            dst_ref=target,
            send_sem=self.send_sems.at[index],
            recv_sem=self.recv_sems.at[index],
            device_id=device,
            device_id_type=MESH,
        )

    def copy(self, source, target, device):
        made = self.make(self.take(1), source, target, device)
        self.copies.append(made)
        made.start()
        return made

    def finish(self, waited=()):
        done = [id(made) for made in waited]
        for made in self.copies:
            if id(made) not in done:
                made.wait_send()


class Moves:
    def __init__(self, sems):
        self.sems, self.count, self.stores = sems, 0, []

    def take(self, count):
        first = self.count
        self.count += count
        return first

    def make(self, index, source, target):
        return pltpu.make_async_copy(source, target, self.sems.at[index])

    def load(self, source, target):
        made = self.make(self.take(1), source, target)
        made.start()
        return made

    def store(self, source, target):
        self.stores.append(self.load(source, target))

    def finish(self):
        for made in self.stores:
            made.wait()


class Several:
    def __init__(self, copies):
        self.copies = copies

    def wait(self):
        for one in self.copies:
            one.wait()


def weight_loads(parts):
    return 1 if len(parts) == 1 else 2 * parts[0].shape[0]


def load_weight(net, moves, parts, columns, target):
    if len(parts) == 1:
        return moves.load(parts[0].at[:, columns], target)
    copies = []
    for part, low in zip(parts, (net.low, 1 - net.low)):
        shard = part.shape[1]
        for high in range(part.shape[0]):
            start = pl.multiple_of((high * 2 + low) * shard, 16)
            copies.append(moves.load(part.at[high, :, columns], target.at[pl.ds(start, shard)]))
    return Several(copies)


def spaced(arrays):
    return [(array, False) for array in arrays]


def job_copies(count):
    return 2 * count + 1


class GatherJob:
    def __init__(self, net, moves, shard, weights):
        self.net, self.weights = net, weights
        self.count = weights.shape[0] // 2
        self.across = net.take(2 * self.count - 1)
        self.up, self.down = net.take(self.count), net.take(self.count)
        own = weights.at[net.tok]
        moves.store(shard, own)
        first = self.swap(0, shard, own)
        pl.when(net.has_after)(lambda: net.make(self.up, shard, own, net.after).start())
        pl.when(net.has_before)(lambda: net.make(self.down, shard, own, net.before).start())
        first.start()

    def swap(self, index, source, target):
        return self.net.make(self.across + index, source, target, self.net.half)

    def arrive(self, step, above):
        net = self.net
        place = net.high + step if above else net.high - step
        block = self.weights.at[place * 2 + net.low]
        base, onward = (self.down, net.before) if above else (self.up, net.after)
        net.make(base + step - 1, block, block, onward).wait_recv()
        if step + 1 < self.count:
            go_on = net.has_before if above else net.has_after
            pl.when(go_on)(lambda: net.make(base + step, block, block, onward).start())
        self.swap(2 * step - int(above), block, block).start()

    def forward(self, point, points):
        net = self.net
        for step in range(1, self.count):
            if (step - 1) * points // (self.count - 1) == point:
                pl.when(net.high - step >= 0)(functools.partial(self.arrive, step, False))
                pl.when(net.high + step < self.count)(functools.partial(self.arrive, step, True))

    def finish(self):
        net = self.net
        own = self.weights.at[net.tok]
        self.swap(0, own, own).wait()
        for step in range(1, self.count):
            below, above = net.high - step >= 0, net.high + step < self.count
            pl.when(below)(lambda step=step: self.swap(2 * step, own, own).wait())
            pl.when(above)(lambda step=step: self.swap(2 * step - 1, own, own).wait())
        for step in range(self.count - 1):
            for base, device, has, there in (
                (self.up, net.after, net.has_after, net.high - step >= 0),
                (self.down, net.before, net.has_before, net.high + step < self.count),
            ):
                sent = net.make(base + step, own, own, device)
                pl.when(jnp.logical_and(has, there))(sent.wait_send)


class Line:
    def __init__(self, net, count, value, passing, arrived):
        self.net, self.count, self.value = net, count, value
        self.passing, self.arrived = passing, arrived
        self.up, self.down = net.take(count), net.take(count)

    def upward(self, place):
        source, target = self.passing.at[place], self.arrived.at[place + 1]
        return self.net.make(self.up + place, source, target, self.net.after)

    def downward(self, place):
        source, target = self.passing.at[place], self.arrived.at[place]
        return self.net.make(self.down + place, source, target, self.net.before)

    def send(self, place, above):
        net = self.net
        value = self.value(place)
        self.passing[place] = value.astype(BF)
        move = self.upward(place) if above else self.downward(place)

        def add():
            move.wait_recv()
            landed = self.arrived[place + 1 if above else place]
            self.passing[place] = (value + landed.astype(F32)).astype(BF)

        pl.when(net.has_before if above else net.has_after)(add)
        move.start()

    def forward(self, point, points):
        high, last = self.net.high, self.count - 1
        for slot in range(last):
            if slot * points // last == point:
                pl.when(high <= slot)(functools.partial(self.send, last - slot + high, True))
                pl.when(last - high <= slot)(functools.partial(self.send, slot - last + high, False))

    def finish(self, total):
        net = self.net
        total[...] = self.value(net.high)

        def add(move, place):
            move.wait_recv()
            total[...] += self.arrived[place].astype(F32)

        pl.when(net.has_before)(lambda: add(self.upward(net.high), net.high + 1))
        pl.when(net.has_after)(lambda: add(self.downward(net.high), net.high))

    def drain(self):
        for place in range(self.count):
            pl.when(self.net.high < place)(self.upward(place).wait_send)
            pl.when(self.net.high > place)(self.downward(place).wait_send)


def part_scratch(count, shard, width):
    half = count // 2
    return [pltpu.VMEM((half, shard, width), BF)] * 3 + [pltpu.VMEM((half + 1, shard, width), BF)]


class ScatterParts:
    def __init__(self, net, moves, grads, scratch):
        self.net, self.moves = net, moves
        self.own, self.landed, passing, arrived = scratch
        self.count = count = grads.shape[0] // 2
        ends = [[count - 1 - step, step] for step in range((count + 1) // 2)]
        order = list(dict.fromkeys(sum(ends, [])))
        self.across, self.loads = net.take(count), moves.take(count)
        for place in order:
            self.swap(place, grads.at[place * 2 + 1 - net.low]).start()
        for place in order:
            source = grads.at[place * 2 + net.low]
            moves.make(self.loads + place, source, self.own.at[place]).start()
        self.line = Line(net, count, self.pair, passing, arrived)
        self.forward = self.line.forward

    def swap(self, place, source=None):
        target = self.landed.at[place]
        source = target if source is None else source
        return self.net.make(self.across + place, source, target, self.net.half)

    def pair(self, place):
        own = self.own.at[place]
        self.moves.make(self.loads + place, own, own).wait()
        self.swap(place).wait_recv()
        return self.own[place].astype(F32) + self.landed[place].astype(F32)

    def finish(self, total):
        self.line.finish(total)
        self.line.drain()
        for place in range(self.count):
            self.swap(place).wait_send()


def run(kernel, name, duration, inputs, outputs, scratch, identity, copies, moves):
    def space(near):
        return pl.BlockSpec(memory_space=pltpu.VMEM if near else pl.ANY)

    return pl.pallas_call(
        kernel,
        name=name,
        cost_estimate=micros(duration),
        out_shape=[jax.ShapeDtypeStruct(shape, dtype) for shape, dtype, _ in outputs],
        in_specs=[space(near) for _, near in inputs],
        out_specs=[space(near) for _, _, near in outputs],
        scratch_shapes=list(scratch)
        + [
            pltpu.SemaphoreType.DMA((copies,)),
            pltpu.SemaphoreType.DMA((copies,)),
            pltpu.SemaphoreType.DMA((moves,)),
        ],
        compiler_params=pltpu.CompilerParams(
            collective_id=identity, has_side_effects=True, vmem_limit_bytes=VMEM_LIMIT
        ),
    )(*[array for array, _ in inputs])


def split_refs(refs, inputs, outputs):
    return refs[:inputs], refs[inputs : inputs + outputs], refs[inputs + outputs :]


def norm_parts(rows):
    centred = rows - jnp.mean(rows, axis=1, keepdims=True)
    inverse = lax.rsqrt(jnp.mean(centred * centred, axis=1, keepdims=True) + EPS)
    return centred * inverse, inverse


def norm_back(rows, gain, grad):
    scaled, inverse = norm_parts(rows)
    inner = grad * gain
    first = jnp.mean(inner, axis=1, keepdims=True)
    second = jnp.mean(inner * scaled, axis=1, keepdims=True)
    return (
        inverse * (inner - first - scaled * second),
        jnp.sum(grad * scaled, axis=0, keepdims=True),
        jnp.sum(grad, axis=0, keepdims=True),
    )


def gather_send(net, full, chunk):
    near = net.copy(full.at[0, chunk], full.at[1, chunk], net.core)
    far = net.copy(full.at[0, chunk], full.at[2, chunk], net.far)
    return near, far


def gather_pass(net, full, chunk, far):
    far.wait_recv()
    return net.copy(full.at[2, chunk], full.at[3, chunk], net.core)


def scatter_scratch(rows, width):
    return [
        pltpu.VMEM((rows, width), F32),
        pltpu.VMEM((rows, width), F32),
    ] + [pltpu.VMEM((rows, width), BF)] * 6


class Scatter:
    def __init__(self, net, scratch):
        self.net = net
        self.hold, self.total, self.cs0, self.cr0, self.ys, self.yr, self.cs1, self.cr1 = scratch
        self.first, self.second = {}, {}

    def far_part(self, key, chunk, partial):
        rows = partial.shape[0] // 2
        self.hold[chunk] = partial[:rows]
        self.cs0[chunk] = partial[rows:].astype(BF)
        self.first[key] = self.net.copy(self.cs0.at[chunk], self.cr0.at[chunk], self.net.core)

    def far_send(self, key, chunk):
        self.first[key].wait_recv()
        self.ys[chunk] = (self.hold[chunk] + self.cr0[chunk].astype(F32)).astype(BF)
        self.second[key] = self.net.copy(self.ys.at[chunk], self.yr.at[chunk], self.net.far)

    def near_part(self, partial):
        rows = partial.shape[0] // 2
        self.total[...] = partial[:rows]
        self.cs1[...] = partial[rows:].astype(BF)
        self.near = self.net.copy(self.cs1, self.cr1, self.net.core)

    def near_done(self):
        self.near.wait_recv()
        self.total[...] += self.cr1[...].astype(F32)

    def result(self, key, chunk):
        self.second[key].wait_recv()
        return self.total[chunk] + self.yr[chunk].astype(F32)


def blocked(value):
    return value.astype(BF).reshape(2, value.shape[0] // 2, value.shape[1])


def chunks_of(rows, count):
    step = rows // count
    return [pl.ds(index * step, step) for index in range(count)]


def weight_grad(left, right, out, extra=None):
    width = left.shape[2]
    tile = 384

    def one(index, carry):
        columns = pl.ds(pl.multiple_of(index * tile, tile), tile)
        result = dot(flat(left[:, :, columns]), flat(right[...]), TN)
        if extra is None:
            out[columns, :] = result.astype(out.dtype)
        else:
            start = out.shape[1] - extra.shape[1]
            join = result.shape[1] - start
            added = extra[columns, :]
            out[columns, :start] = result[:, :start].astype(out.dtype)
            both = result[:, start:] + added[:, :join].astype(F32)
            out[columns, start : start + join] = both.astype(out.dtype)
            out[columns, start + join :] = added[:, join:]
        return carry

    lax.fori_loop(0, width // tile, one, 0)


def project_kernel(*refs, layer, head_cols, factor, parts):
    (x_hbm, vec, bias, *mixed_hbm), outs, scratch = split_refs(refs, 3 + parts, 4)
    normed_out, queries_out, pairs_out, far_out = outs
    x, weight, normed, queries, pairs, far_pairs, send_sems, recv_sems, move_sems = scratch
    net, moves = Net(send_sems, recv_sems), Moves(move_sems)
    rows = x.shape[0]
    pair_cols = 2 * head_cols
    chunks = chunks_of(rows, 2)
    x_load = moves.load(x_hbm, x)
    columns = pl.ds(0, weight.shape[1])
    weight_load = load_weight(net, moves, mixed_hbm, columns, weight)
    net.barrier([net.core, net.far, net.half])
    x_load.wait()
    sent = []
    for chunk in chunks:
        scaled, _ = norm_parts(x[chunk, :])
        normed[0, chunk, :] = (scaled * vec[layer, 0:1] + vec[layer, 1:2]).astype(BF)
        sent.append(gather_send(net, normed, chunk))
    arrived = []
    weight_load.wait()

    def project(slots, chunk):
        result = dot(flat(normed[slots, chunk, :]), weight[...]) + bias[layer : layer + 1]
        shape = (slots.size, chunk.size, -1)
        pairs[slots, chunk, :] = result[:, :pair_cols].astype(BF).reshape(shape)
        own = result[:, pair_cols : pair_cols + head_cols] * factor
        queries[slots, chunk, :] = own.astype(BF).reshape(shape)
        source, target = pairs.at[slots, chunk], far_pairs.at[slots, chunk]
        arrived.append(net.copy(source, target, net.half))

    whole = pl.ds(0, rows)
    project(pl.ds(0, 1), whole)
    for near, _ in sent:
        near.wait_recv()
    project(pl.ds(1, 1), whole)
    for chunk, (_, far) in zip(chunks, sent):
        gather_pass(net, normed, chunk, far).wait_recv()
        project(pl.ds(2, 2), chunk)
    moves.store(normed, normed_out)
    moves.store(queries, queries_out)
    moves.store(pairs, pairs_out)
    for one in arrived:
        one.wait_recv()
    moves.store(far_pairs, far_out)
    net.finish()
    moves.finish()


def project(layer, x, vec, bias, mixed, head_cols):
    rows, width = x.shape
    used = bias.shape[1]
    outputs = [
        ((4, rows, width), BF, False),
        ((4, rows, head_cols), BF, False),
        ((4, rows, 2 * head_cols), BF, False),
        ((4, rows, 2 * head_cols), BF, False),
    ]
    scratch = [pltpu.VMEM((rows, width), F32), pltpu.VMEM((width, used), BF)]
    scratch += [pltpu.VMEM(shape, dtype) for shape, dtype, _ in outputs]
    kernel = functools.partial(
        project_kernel,
        layer=layer,
        head_cols=head_cols,
        factor=HEAD_DIM ** (-0.5) * LOG2E,
        parts=len(mixed),
    )
    inputs = [(x, False), (vec, True), (bias, True)] + spaced(mixed)
    return run(kernel, "project", 40, inputs, outputs, scratch, 8 * layer, 12, 6 + weight_loads(mixed))


def pair_windows(width, lead=0):
    windows = []
    for first in range(lead, width - HEAD_DIM, 2 * HEAD_DIM):
        start = first // LANES * LANES
        size = min(2 * LANES, width - start)
        row = lax.broadcasted_iota(jnp.int32, (size, 2 * LANES), 0) + (start - first)
        lane = lax.broadcasted_iota(jnp.int32, (size, 2 * LANES), 1)
        second = lane >= LANES
        lane = jnp.where(second, lane - LANES, lane)
        match = row == jnp.where(second, lane + HEAD_DIM, lane)
        windows.append((start, size, jnp.logical_and(match, lane < HEAD_DIM).astype(BF)))
    return windows


def spread_heads(value, windows):
    heads = []
    for start, size, pick in windows:
        both = dot(value[:, start : start + size], pick).astype(BF)
        heads += [both[:, :LANES], both[:, LANES:]]
    return heads


def join_heads(heads, windows, width):
    tiles = [None] * (-(-width // LANES))
    for index, (start, size, pick) in enumerate(windows):
        both = jnp.concatenate(heads[2 * index : 2 * index + 2], axis=1)
        part = dot(both, pick, NT)
        for lane in range(0, size, LANES):
            tile, piece = (start + lane) // LANES, part[:, lane : lane + LANES]
            tiles[tile] = piece if tiles[tile] is None else tiles[tile] + piece
    return jnp.concatenate(tiles, axis=1)


def as_rows(columns):
    rows = columns[0].shape[0]
    lane = lax.broadcasted_iota(jnp.int32, (rows, LANES), 1)
    together = jnp.zeros((rows, LANES), F32)
    for head, column in enumerate(columns):
        together = jnp.where(lane == head, column, together)
    return together.T[:8]


def load_pairs(meta, own_pairs, far_pairs, key_scratch, value_scratch, heads):
    rows = own_pairs.shape[1]
    hid, half = meta[0], meta[1]
    windows = pair_windows(own_pairs.shape[2])
    for which, source in ((0, own_pairs), (1, far_pairs)):
        for slot in range(4):
            place = jnp.bitwise_xor(half, which) * 4 + jnp.bitwise_xor(hid, slot)
            start = pl.ds(pl.multiple_of(place * rows, rows), rows)
            spread = spread_heads(source[slot], windows)
            for head in range(heads):
                key_scratch[head, start, :] = spread[head]
                value_scratch[head, start, :] = spread[heads + head]


def attend_kernel(
    meta, queries, own_pairs, far_pairs, query_ids, key_ids, mixture, logsum,
    key_scratch, value_scratch, score_scratch, high_scratch, total_scratch, sum_scratch, query_scratch,
    *, heads
):
    rows = queries.shape[1]
    head_cols = heads * HEAD_DIM
    load_pairs(meta, own_pairs, far_pairs, key_scratch, value_scratch, heads)
    query_windows = pair_windows(head_cols)
    mixed_windows = pair_windows(mixture.shape[2], mixture.shape[2] - head_cols)

    def one_block(block, carry):
        slot = jnp.bitwise_xor(meta[0], block)
        first, last = meta[2 + 2 * block], meta[3 + 2 * block]
        own = pl.ds(pl.multiple_of(block * rows, rows), rows)
        ids = query_ids[own, :]
        for head, query in enumerate(spread_heads(queries[slot], query_windows)):
            query_scratch[head] = query
        high_scratch[...] = jnp.full_like(high_scratch, -3e38)
        sum_scratch[...] = jnp.zeros_like(sum_scratch)
        total_scratch[...] = jnp.zeros_like(total_scratch)

        def scores_of(key_block, inner):
            keys = pl.ds(pl.multiple_of(key_block * KEYS, KEYS), KEYS)
            same = ids == key_ids[:, keys]
            for head in range(heads):
                scores = dot(query_scratch[head], key_scratch[head, keys, :], NT)
                scores = jnp.where(same, scores, MASKED)
                score_scratch[head, :, keys] = scores
                high = high_scratch[head]
                for lane in range(0, KEYS, LANES):
                    high = jnp.maximum(high, scores[:, lane : lane + LANES])
                high_scratch[head] = high
            return inner

        lax.fori_loop(first, last, scores_of, 0)
        for head in range(heads):
            high_scratch[head] = jnp.broadcast_to(
                jnp.max(high_scratch[head], axis=1, keepdims=True), (rows, LANES)
            )

        def sums_of(key_block, inner):
            keys = pl.ds(pl.multiple_of(key_block * KEYS, KEYS), KEYS)
            for head in range(heads):
                high = high_scratch[head]
                high = jnp.concatenate([high] * (KEYS // LANES), axis=1)
                powers = jnp.exp2(score_scratch[head, :, keys] - high)
                total = total_scratch[head]
                for lane in range(0, KEYS, LANES):
                    total += powers[:, lane : lane + LANES]
                total_scratch[head] = total
                sum_scratch[head] += dot(powers.astype(BF), value_scratch[head, keys, :])
            return inner

        lax.fori_loop(first, last, sums_of, 0)
        mixed, columns = [], []
        for head in range(heads):
            total = jnp.sum(total_scratch[head], axis=1, keepdims=True)
            columns.append(high_scratch[head][:, :1] + jnp.log2(total))
            mixed.append((sum_scratch[head] / total).astype(BF))
        mixture[slot] = join_heads(mixed, mixed_windows, mixture.shape[2]).astype(BF)
        logsum[:, own] = as_rows(columns)
        return carry

    lax.fori_loop(0, 4, one_block, 0)


def attend(meta, queries, own_pairs, far_pairs, query_ids, key_ids, lead):
    _, rows, head_cols = queries.shape
    heads = head_cols // HEAD_DIM
    own, count = 4 * rows, 8 * rows
    space = pl.BlockSpec(memory_space=pltpu.VMEM)
    return pl.pallas_call(
        functools.partial(attend_kernel, heads=heads),
        name="attend",
        cost_estimate=micros(22),
        out_shape=[
            jax.ShapeDtypeStruct((4, rows, lead + head_cols), BF),
            jax.ShapeDtypeStruct((8, own), F32),
        ],
        in_specs=[pl.BlockSpec(memory_space=pltpu.SMEM)] + [space] * 5,
        out_specs=[space] * 2,
        scratch_shapes=[
            pltpu.VMEM((heads, count, LANES), BF),
            pltpu.VMEM((heads, count, LANES), BF),
            pltpu.VMEM((heads, rows, count), F32),
            pltpu.VMEM((heads, rows, LANES), F32),
            pltpu.VMEM((heads, rows, LANES), F32),
            pltpu.VMEM((heads, rows, LANES), F32),
            pltpu.VMEM((heads, rows, LANES), BF),
        ],
        compiler_params=pltpu.CompilerParams(vmem_limit_bytes=VMEM_LIMIT),
    )(meta, queries, own_pairs, far_pairs, query_ids, key_ids)


def attend_back_kernel(
    meta, queries, own_pairs, far_pairs, query_ids, key_ids, grad_mixture, logsum,
    grad_queries, grad_own, grad_far,
    key_scratch, value_scratch, grad_key, grad_value, grad_query, query_scratch, grad_scratch,
    prob_scratch, grad_prob_scratch, delta_scratch,
    *, heads
):
    rows = queries.shape[1]
    head_cols = heads * HEAD_DIM
    load_pairs(meta, own_pairs, far_pairs, key_scratch, value_scratch, heads)
    query_windows = pair_windows(head_cols)
    mixed_windows = pair_windows(grad_mixture.shape[2], grad_mixture.shape[2] - head_cols)
    grad_key[...] = jnp.zeros_like(grad_key)
    grad_value[...] = jnp.zeros_like(grad_value)

    def one_block(block, carry):
        slot = jnp.bitwise_xor(meta[0], block)
        first, last = meta[2 + 2 * block], meta[3 + 2 * block]
        own = pl.ds(pl.multiple_of(block * rows, rows), rows)
        ids = query_ids[:, own]
        for head, query in enumerate(spread_heads(queries[slot], query_windows)):
            query_scratch[head] = query
        for head, grad in enumerate(spread_heads(grad_mixture[slot], mixed_windows)):
            grad_scratch[head] = grad
        logs = logsum[:, own]
        grad_query[...] = jnp.zeros_like(grad_query)
        delta_scratch[...] = jnp.zeros_like(delta_scratch)

        def probs_of(key_block, inner):
            keys = pl.ds(pl.multiple_of(key_block * KEYS, KEYS), KEYS)
            same = key_ids[keys, :] == ids
            for head in range(heads):
                grad = grad_scratch[head]
                scores = dot(key_scratch[head, keys, :], query_scratch[head], NT)
                probs = jnp.where(same, jnp.exp2(scores - logs[head : head + 1]), 0.0)
                grad_probs = dot(value_scratch[head, keys, :], grad, NT)
                prob_scratch[head, keys, :] = probs
                grad_prob_scratch[head, keys, :] = grad_probs
                delta_scratch[head] += jnp.sum((probs * grad_probs).reshape(KEYS // 8, 8, rows), axis=0)
                grad_value[head, keys, :] += dot(probs.astype(BF), grad)
            return inner

        lax.fori_loop(first, last, probs_of, 0)
        for head in range(heads):
            delta_scratch[head, 0:1] = jnp.sum(delta_scratch[head], axis=0, keepdims=True)

        def one_key(key_block, inner):
            keys = pl.ds(pl.multiple_of(key_block * KEYS, KEYS), KEYS)
            for head in range(heads):
                delta = delta_scratch[head, 0:1]
                grad_scores = prob_scratch[head, keys, :] * (grad_prob_scratch[head, keys, :] - delta)
                grad_scores = grad_scores.astype(BF)
                grad_key[head, keys, :] += dot(grad_scores, query_scratch[head])
                grad_query[head] += dot(grad_scores, key_scratch[head, keys, :], TN)
            return inner

        lax.fori_loop(first, last, one_key, 0)
        scaled = [(grad_query[head] * HEAD_DIM ** (-0.5)).astype(BF) for head in range(heads)]
        grad_queries[slot] = join_heads(scaled, query_windows, head_cols).astype(BF)
        return carry

    lax.fori_loop(0, 4, one_block, 0)
    hid, half = meta[0], meta[1]
    for which, target in ((0, grad_own), (1, grad_far)):
        for slot in range(4):
            place = jnp.bitwise_xor(half, which) * 4 + jnp.bitwise_xor(hid, slot)
            start = pl.ds(pl.multiple_of(place * rows, rows), rows)
            parts = [(grad_key[head, start, :] * LN2).astype(BF) for head in range(heads)]
            parts += [grad_value[head, start, :].astype(BF) for head in range(heads)]
            target[slot] = join_heads(parts, pair_windows(2 * head_cols), 2 * head_cols).astype(BF)


def attend_back(meta, queries, own_pairs, far_pairs, query_ids, key_ids, grad_mixture, logsum):
    _, rows, head_cols = queries.shape
    heads = head_cols // HEAD_DIM
    count = 8 * rows
    space = pl.BlockSpec(memory_space=pltpu.VMEM)
    return pl.pallas_call(
        functools.partial(attend_back_kernel, heads=heads),
        name="attend_back",
        cost_estimate=micros(37),
        out_shape=[
            jax.ShapeDtypeStruct((4, rows, head_cols), BF),
            jax.ShapeDtypeStruct((4, rows, 2 * head_cols), BF),
            jax.ShapeDtypeStruct((4, rows, 2 * head_cols), BF),
        ],
        in_specs=[pl.BlockSpec(memory_space=pltpu.SMEM)] + [space] * 7,
        out_specs=[space] * 3,
        scratch_shapes=[
            pltpu.VMEM((heads, count, LANES), BF),
            pltpu.VMEM((heads, count, LANES), BF),
            pltpu.VMEM((heads, count, LANES), F32),
            pltpu.VMEM((heads, count, LANES), F32),
            pltpu.VMEM((heads, rows, LANES), F32),
            pltpu.VMEM((heads, rows, LANES), BF),
            pltpu.VMEM((heads, rows, LANES), BF),
            pltpu.VMEM((heads, count, rows), F32),
            pltpu.VMEM((heads, count, rows), F32),
            pltpu.VMEM((heads, 8, rows), F32),
        ],
        compiler_params=pltpu.CompilerParams(vmem_limit_bytes=VMEM_LIMIT),
    )(meta, queries, own_pairs, far_pairs, query_ids, key_ids, grad_mixture, logsum)


def mlp_kernel(*refs, layer, parts):
    ins, outs, scratch = split_refs(refs, 4 + sum(parts), 5)
    mixture_hbm, x_hbm, vec, up_bias = ins[:4]
    mixed_hbm, up_hbm, down_hbm = split_refs(ins[4:], parts[0], parts[1])
    x_out, after_out, normed_out, active_out, slope_out = outs
    mixture, x, out_weight, up_weight, down_weight, x_next, after, normed, active, slope = scratch[:10]
    first_scratch, second_scratch = scratch[10:18], scratch[18:26]
    send_sems, recv_sems, move_sems = scratch[26:]
    net, moves = Net(send_sems, recv_sems), Moves(move_sems)
    rows = x.shape[0]
    hidden_cols = up_weight.shape[1]
    out_cols = out_weight.shape[1]
    chunks = chunks_of(rows, 2)
    out_part = pl.ds(x.shape[1] - out_cols, out_cols)
    loads = [
        moves.load(mixture_hbm, mixture), load_weight(net, moves, mixed_hbm, out_part, out_weight),
    ]
    x_load = moves.load(x_hbm, x)
    up_load = load_weight(net, moves, up_hbm, pl.ds(0, hidden_cols), up_weight)
    down_load = load_weight(net, moves, down_hbm, pl.ds(0, hidden_cols), down_weight)
    net.barrier([net.core, net.far])
    out_bias, gain = vec[layer, 2:3], vec[layer, 3:4]
    shift, down_bias = vec[layer, 4:5], vec[layer, 5:6]

    def mixed(slots, chunk):
        return dot(flat(mixture[slots, chunk, :]), out_weight[...], NT)

    def up(slots, chunk):
        hidden = dot(flat(normed[slots, chunk, :]), up_weight[...]) + up_bias[layer : layer + 1]
        square = hidden * hidden
        bend = jnp.tanh(GELU * hidden * (1.0 + CUBE * square))
        half = 0.5 * (1.0 + bend)
        value = hidden * half
        rise = half + 0.5 * hidden * (1.0 - bend * bend) * GELU * (1.0 + 3.0 * CUBE * square)
        active[slots, chunk, :] = blocked(value)
        slope[slots, chunk, :] = blocked(rise)

    def down(slots, chunk):
        return dot(flat(active[slots, chunk, :]), down_weight[...], NT)

    near, far, whole = pl.ds(0, 2), pl.ds(2, 2), pl.ds(0, rows)
    for load in loads:
        load.wait()
    first = Scatter(net, first_scratch)
    for key, chunk in enumerate(chunks):
        first.far_part(key, chunk, mixed(far, chunk))
    for key, chunk in enumerate(chunks):
        first.far_send(key, chunk)
    first.near_part(mixed(near, whole))
    first.near_done()
    x_load.wait()
    sent = []
    for key, chunk in enumerate(chunks):
        residual = first.result(key, chunk) + x[chunk, :] + out_bias
        after[chunk, :] = residual
        normed[0, chunk, :] = (norm_parts(residual)[0] * gain + shift).astype(BF)
        sent.append(gather_send(net, normed, chunk))
    moves.store(after, after_out)
    for one, _ in sent:
        one.wait_recv()
    up_load.wait()
    up(near, whole)
    down_load.wait()
    second = Scatter(net, second_scratch)
    for key, chunk in enumerate(chunks):
        passed = gather_pass(net, normed, chunk, sent[key][1])
        passed.wait_recv()
        up(far, chunk)
        second.far_part(key, chunk, down(far, chunk))
        second.far_send(key, chunk)
    moves.store(normed, normed_out)
    moves.store(active, active_out)
    moves.store(slope, slope_out)
    second.near_part(down(near, whole))
    second.near_done()
    for key, chunk in enumerate(chunks):
        x_next[chunk, :] = second.result(key, chunk) + after[chunk, :] + down_bias
    moves.store(x_next, x_out)
    net.finish()
    moves.finish()


def mlp(layer, mixture, x, vec, up_bias, mixed, up, down):
    rows, width = x.shape
    hidden = up_bias.shape[1]
    outputs = [
        ((rows, width), F32, False),
        ((rows, width), F32, False),
        ((4, rows, width), BF, False),
        ((4, rows, hidden), BF, False),
        ((4, rows, hidden), BF, False),
    ]
    scratch = [
        pltpu.VMEM(mixture.shape, BF),
        pltpu.VMEM((rows, width), F32),
        pltpu.VMEM((width, mixture.shape[2]), BF),
        pltpu.VMEM((width, hidden), BF),
        pltpu.VMEM((width, hidden), BF),
    ]
    scratch += [pltpu.VMEM(shape, dtype) for shape, dtype, _ in outputs]
    scratch += scatter_scratch(rows, width) * 2
    inputs = [(mixture, False), (x, False), (vec, True), (up_bias, True)]
    inputs += spaced(mixed + up + down)
    parts = (len(mixed), len(up), len(down))
    kernel = functools.partial(mlp_kernel, layer=layer, parts=parts)
    moves = 8 + weight_loads(mixed) + weight_loads(up) + weight_loads(down)
    return run(kernel, "mlp", 48, inputs, outputs, scratch, 8 * layer + 1, 18, moves)


def mlp_back_kernel(*refs, layer, parts):
    ins, outs, scratch = split_refs(refs, 7 + sum(parts), 7)
    gradient_hbm, after_hbm, vec, mixture_hbm, normed_hbm, active_hbm, slope_hbm = ins[:7]
    mixed_hbm, up_hbm, down_hbm = split_refs(ins[7:], parts[0], parts[1])
    after_out, mixture_out, up_out, down_out, out_out, sums, hidden_sums = outs
    gradient, after, out_weight, up_weight, down_weight, mixture, normed, active, slope = scratch[:9]
    grad_after, grad_mixture, grad_down, grad_up, grad_out = scratch[9:14]
    grad_rows, grad_hidden, grad_mid = scratch[14:17]
    scatter_refs = scratch[17:25]
    send_sems, recv_sems, move_sems = scratch[25:]
    net, moves = Net(send_sems, recv_sems), Moves(move_sems)
    rows, width = gradient.shape
    hidden_cols = up_weight.shape[1]
    out_cols = out_weight.shape[1]
    chunks = chunks_of(rows, 2)
    out_part = pl.ds(width - out_cols, out_cols)
    load_gradient = moves.load(gradient_hbm, gradient)
    load_down = load_weight(net, moves, down_hbm, pl.ds(0, hidden_cols), down_weight)
    load_slope = moves.load(slope_hbm, slope)
    load_up = load_weight(net, moves, up_hbm, pl.ds(0, hidden_cols), up_weight)
    load_active = moves.load(active_hbm, active)
    load_after = moves.load(after_hbm, after)
    load_normed = moves.load(normed_hbm, normed)
    load_out = load_weight(net, moves, mixed_hbm, out_part, out_weight)
    load_mixture = moves.load(mixture_hbm, mixture)
    net.barrier([net.core, net.far])
    gain = vec[layer, 3:4]
    near, far, whole = pl.ds(0, 2), pl.ds(2, 2), pl.ds(0, rows)
    load_gradient.wait()
    rounded = gradient[...].astype(BF)
    grad_rows[0] = rounded
    sent = [gather_send(net, grad_rows, chunk) for chunk in chunks]
    sums[...] = jnp.zeros_like(sums)
    sums[5:6] = jnp.sum(rounded.astype(F32), axis=0, keepdims=True)

    def hidden_grad(slots, chunk):
        value = dot(flat(grad_rows[slots, chunk, :]), down_weight[...])
        value = value * flat(slope[slots, chunk, :]).astype(F32)
        grad_hidden[slots, chunk, :] = blocked(value)

    def up_back(slots, chunk):
        return dot(flat(grad_hidden[slots, chunk, :]), up_weight[...], NT)

    for one, _ in sent:
        one.wait_recv()
    load_down.wait()
    load_slope.wait()
    hidden_grad(near, whole)
    load_up.wait()
    scatter = Scatter(net, scatter_refs)
    for key, chunk in enumerate(chunks):
        passed = gather_pass(net, grad_rows, chunk, sent[key][1])
        passed.wait_recv()
        hidden_grad(far, chunk)
        scatter.far_part(key, chunk, up_back(far, chunk))
        scatter.far_send(key, chunk)
    scatter.near_part(up_back(near, whole))
    load_active.wait()
    weight_grad(grad_rows, active, grad_down)
    moves.store(grad_down, down_out)
    scatter.near_done()
    load_after.wait()
    sent = []
    for key, chunk in enumerate(chunks):
        back, gain_sum, shift_sum = norm_back(after[chunk, :], gain, scatter.result(key, chunk))
        total = gradient[chunk, :] + back
        grad_after[chunk, :] = total
        rounded = total.astype(BF)
        grad_mid[0, chunk, :] = rounded
        sent.append(gather_send(net, grad_mid, chunk))
        sums[3:4] += gain_sum
        sums[4:5] += shift_sum
        sums[2:3] += jnp.sum(rounded.astype(F32), axis=0, keepdims=True)
    moves.store(grad_after, after_out)
    load_normed.wait()
    weight_grad(normed, grad_hidden, grad_up)
    moves.store(grad_up, up_out)
    column = jnp.zeros((1, hidden_cols), F32)
    for slot in range(4):
        column += jnp.sum(grad_hidden[slot].astype(F32), axis=0, keepdims=True)
    hidden_sums[...] = column

    def mix_back(slots, chunk):
        value = dot(flat(grad_mid[slots, chunk, :]), out_weight[...])
        grad_mixture[slots, chunk, :] = blocked(value)

    for one, _ in sent:
        one.wait_recv()
    load_out.wait()
    mix_back(near, whole)
    for key, chunk in enumerate(chunks):
        gather_pass(net, grad_mid, chunk, sent[key][1]).wait_recv()
    mix_back(far, whole)
    moves.store(grad_mixture, mixture_out)
    load_mixture.wait()
    weight_grad(grad_mid, mixture, grad_out)
    moves.store(grad_out, out_out)
    net.finish()
    moves.finish()


def mlp_back(layer, gradient, after, vec, mixed, up, down, mixture, normed, active, slope):
    rows, width = gradient.shape
    hidden = active.shape[2]
    out_cols = mixture.shape[2]
    outputs = [
        ((rows, width), F32, False),
        ((4, rows, out_cols), BF, False),
        ((width, hidden), BF, False),
        ((width, hidden), BF, False),
        ((width, out_cols), BF, False),
        ((8, width), F32, True),
        ((1, hidden), F32, True),
    ]
    shapes = [
        ((rows, width), F32),
        ((rows, width), F32),
        ((width, out_cols), BF),
        ((width, hidden), BF),
        ((width, hidden), BF),
        ((4, rows, out_cols), BF),
        ((4, rows, width), BF),
        ((4, rows, hidden), BF),
        ((4, rows, hidden), BF),
        ((rows, width), F32),
        ((4, rows, out_cols), BF),
        ((width, hidden), BF),
        ((width, hidden), BF),
        ((width, out_cols), BF),
        ((4, rows, width), BF),
        ((4, rows, hidden), BF),
        ((4, rows, width), BF),
    ]
    scratch = [pltpu.VMEM(shape, dtype) for shape, dtype in shapes] + scatter_scratch(rows, width)
    inputs = [
        (gradient, False), (after, False), (vec, True), (mixture, False), (normed, False),
        (active, False), (slope, False),
    ] + spaced(mixed + up + down)
    parts = (len(mixed), len(up), len(down))
    kernel = functools.partial(mlp_back_kernel, layer=layer, parts=parts)
    moves = 12 + weight_loads(mixed) + weight_loads(up) + weight_loads(down)
    return run(kernel, "mlp_back", 48, inputs, outputs, scratch, 8 * layer + 2, 20, moves)


def project_back_kernel(*refs, layer, parts):
    ins, outs, scratch = split_refs(refs, 8 + parts, 4)
    after_hbm, x_hbm, vec, normed_hbm, queries_hbm, own_hbm, far_hbm, out_hbm = ins[:8]
    mixed_hbm = ins[8:]
    gradient_out, weight_out, sums, column_sums = outs
    grad_after, x, weight, normed, grad_queries, grad_own, grad_out = scratch[:7]
    landed, together, gradient, grad_weight = scratch[7:11]
    scatter_refs = scratch[11:19]
    send_sems, recv_sems, move_sems = scratch[19:]
    net, moves = Net(send_sems, recv_sems), Moves(move_sems)
    rows, width = x.shape
    pair_cols = grad_own.shape[2]
    used_cols = pair_cols + grad_queries.shape[2]
    all_cols = together.shape[2]
    chunks = chunks_of(rows, 2)
    near, far, whole = pl.ds(0, 2), pl.ds(2, 2), pl.ds(0, rows)
    load_own = moves.load(own_hbm, grad_own)
    load_queries = moves.load(queries_hbm, grad_queries)
    loading = load_weight(net, moves, mixed_hbm, pl.ds(0, all_cols), weight)
    load_normed = moves.load(normed_hbm, normed)
    load_out = moves.load(out_hbm, grad_out)
    load_x = moves.load(x_hbm, x)
    load_after = moves.load(after_hbm, grad_after)
    net.barrier([net.core, net.far, net.half])
    arriving = {
        slot: net.copy(far_hbm.at[slot], landed.at[slot], net.half) for slot in (3, 2, 1, 0)
    }
    load_queries.wait()
    together[:, :, pair_cols:used_cols] = grad_queries[...]
    together[:, :, used_cols:] = jnp.zeros((4, rows, all_cols - used_cols), BF)
    load_own.wait()
    loading.wait()

    def join(slot):
        arriving[slot].wait_recv()
        pair = grad_own[slot].astype(F32) + landed[slot].astype(F32)
        together[slot, :, :pair_cols] = pair.astype(BF)

    def back(slots, chunk):
        return dot(flat(together[slots, chunk, :]), weight[...], NT)

    scatter = Scatter(net, scatter_refs)
    join(3)
    join(2)
    for key, chunk in enumerate(chunks):
        scatter.far_part(key, chunk, back(far, chunk))
    for key, chunk in enumerate(chunks):
        scatter.far_send(key, chunk)
    join(1)
    join(0)
    scatter.near_part(back(near, whole))
    load_normed.wait()
    load_out.wait()
    weight_grad(normed, together, grad_weight, grad_out)
    moves.store(grad_weight, weight_out)
    column = jnp.zeros((1, all_cols), F32)
    for slot in range(4):
        column += jnp.sum(together[slot].astype(F32), axis=0, keepdims=True)
    column_sums[...] = column
    scatter.near_done()
    sums[...] = jnp.zeros_like(sums)
    load_x.wait()
    load_after.wait()
    for key, chunk in enumerate(chunks):
        grad, gain_sum, shift_sum = norm_back(
            x[chunk, :], vec[layer, 0:1], scatter.result(key, chunk)
        )
        gradient[chunk, :] = grad_after[chunk, :] + grad
        sums[0:1] += gain_sum
        sums[1:2] += shift_sum
    moves.store(gradient, gradient_out)
    net.finish()
    moves.finish()


def project_back(
    layer, grad_after, x, vec, mixed, normed, grad_queries, grad_own, grad_far, grad_out, all_cols
):
    rows, width = x.shape
    outputs = [
        ((rows, width), F32, False),
        ((width, width), BF, False),
        ((8, width), F32, True),
        ((1, all_cols), F32, True),
    ]
    shapes = [
        ((rows, width), F32),
        ((rows, width), F32),
        ((width, all_cols), BF),
        (normed.shape, BF),
        (grad_queries.shape, BF),
        (grad_own.shape, BF),
        (grad_out.shape, BF),
        (grad_far.shape, BF),
        ((4, rows, all_cols), BF),
        ((rows, width), F32),
        ((width, width), BF),
    ]
    scratch = [pltpu.VMEM(shape, dtype) for shape, dtype in shapes] + scatter_scratch(rows, width)
    inputs = [
        (grad_after, False), (x, False), (vec, True), (normed, False), (grad_queries, False),
        (grad_own, False), (grad_far, False), (grad_out, False),
    ] + spaced(mixed)
    kernel = functools.partial(project_back_kernel, layer=layer, parts=len(mixed))
    return run(kernel, "project_back", 42, inputs, outputs, scratch, 8 * layer + 3, 12, 9 + weight_loads(mixed))


def entry_kernel(*refs):
    (tokens, cotangent, vectors, shard), outs, scratch = split_refs(refs, 4, 4)
    tokens_out, cotangent_out, vectors_out, weights = outs
    send_sems, recv_sems, move_sems = scratch
    net, moves = Net(send_sems, recv_sems), Moves(move_sems)
    others = [net.core, net.far, net.far_core]
    net.line(weights.shape[0] // 2)
    net.barrier(others + [net.half], True)
    gathering = GatherJob(net, moves, shard, weights)
    moved = []
    for source, target in ((tokens, tokens_out), (cotangent, cotangent_out)):
        for device in reversed(others):
            moved.append(net.copy(source.at[device[1]], target.at[net.hid], device))
        target[net.hid] = source[net.hid]
    for device in others:
        moved.append(net.copy(vectors, vectors_out.at[net.hid], device))
    vectors_out[net.hid] = vectors[...]
    gathering.forward(0, 1)
    gathering.finish()
    for one in moved:
        one.wait_recv()
    net.finish()
    moves.finish()


def entry(tokens, cotangent, vectors, shard, count):
    inputs = [(tokens, True), (cotangent, True), (vectors, True), (shard, False)]
    outputs = [
        (tokens.shape, BF, True),
        (cotangent.shape, BF, True),
        ((4,) + vectors.shape, F32, True),
        ((count,) + shard.shape, BF, False),
    ]
    return run(entry_kernel, "entry", 40, inputs, outputs, [], 4, 9 + job_copies(count), 1)


def finish_kernel(*refs):
    (final, gradient, wide, narrow, broad, grads), outs, scratch = split_refs(refs, 6, 5)
    final_out, gradient_out, sums, hidden_sums, total = outs
    final_land, gradient_land, wide_land, across_land, along_land = scratch[:5]
    across_hidden, along_hidden = scratch[5:7]
    job_refs = scratch[7:11]
    send_sems, recv_sems, move_sems = scratch[11:]
    net, moves = Net(send_sems, recv_sems), Moves(move_sems)
    count = grads.shape[0] // 2
    others = [net.core, net.far, net.far_core]
    net.line(count)
    net.barrier(others + [net.half], True)
    summed = [net.copy(wide.at[device[1]], wide_land.at[net.hid], device) for device in others]
    scattering = ScatterParts(net, moves, grads, job_refs)
    moved = []
    for source, target in ((final, final_land), (gradient, gradient_land)):
        for device in reversed(others):
            moved.append(net.copy(source.at[device[1]], target.at[net.hid], device))
        target[net.hid] = source[net.hid]
    wide_land[net.hid] = wide[net.hid]
    last = count - 1
    pairs = ((sums, across_land, along_land), (hidden_sums, across_hidden, along_hidden))
    bases = [(net.take(count), net.take(count)) for _ in pairs]

    def send_sums():
        for one in summed:
            one.wait_recv()
        top = wide.shape[1]
        sums[:top] = wide_land[0] + wide_land[1] + wide_land[2] + wide_land[3]
        sums[top:] = narrow[...]
        hidden_sums[...] = broad[...]
        return [net.copy(value, across, net.half) for value, across, _ in pairs]

    def spread_sums(swaps):
        for one in swaps:
            one.wait()
        for (value, across, along), base in zip(pairs, bases):
            value[...] += across[...]
            own = along.at[net.high]
            along[net.high] = value[...]
            pl.when(net.has_after)(net.make(base[0], own, own, net.after).start)
            pl.when(net.has_before)(net.make(base[1], own, own, net.before).start)

    def pass_sums(step):
        for (_, _, along), base in zip(pairs, bases):
            below, above = along.at[net.high - step], along.at[net.high + step]

            def pass_on(index, block, device, has):
                net.make(index, block, block, device).wait_recv()
                if step < last:
                    pl.when(has)(net.make(index + 1, block, block, device).start)

            pl.when(net.high >= step)(
                functools.partial(pass_on, base[0] + step - 1, below, net.after, net.has_after)
            )
            pl.when(net.high + step < count)(
                functools.partial(pass_on, base[1] + step - 1, above, net.before, net.has_before)
            )

    swaps = send_sums()
    scattering.forward(0, 3)
    scattering.forward(1, 3)
    spread_sums(swaps)
    scattering.forward(2, 3)
    for step in range(1, count):
        pass_sums(step)
    for (value, _, along), base in zip(pairs, bases):
        total_value = along[0]
        for place in range(1, count):
            total_value += along[place]
        value[...] = total_value
        own = along.at[net.high]
        for step in range(count - 1):
            up = jnp.logical_and(net.has_after, net.high >= step)
            down = jnp.logical_and(net.has_before, net.high + step < count)
            pl.when(up)(net.make(base[0] + step, own, own, net.after).wait_send)
            pl.when(down)(net.make(base[1] + step, own, own, net.before).wait_send)
    for one in moved:
        one.wait_recv()
    for source, target in ((final_land, final_out), (gradient_land, gradient_out)):
        target[...] = flat(source[...]).astype(F32)
    scattering.finish(total)
    net.finish(swaps)


def finish(final, gradient, wide, narrow, broad, grads):
    count = grads.shape[0] // 2
    sums = (wide.shape[1] + narrow.shape[0], wide.shape[2])
    rows = (final.shape[0] * final.shape[1], final.shape[2])
    outputs = [
        (rows, F32, True),
        (rows, F32, True),
        (sums, F32, True),
        (broad.shape, F32, True),
        (grads.shape[1:], F32, True),
    ]
    scratch = [
        pltpu.VMEM(final.shape, BF),
        pltpu.VMEM(final.shape, BF),
        pltpu.VMEM(wide.shape, F32),
        pltpu.VMEM(sums, F32),
        pltpu.VMEM((count,) + sums, F32),
        pltpu.VMEM(broad.shape, F32),
        pltpu.VMEM((count,) + broad.shape, F32),
    ] + part_scratch(*grads.shape)
    inputs = [
        (final, True), (gradient, True), (wide, True), (narrow, True), (broad, True), (grads, False),
    ]
    return run(
        finish_kernel, "finish", 40, inputs, outputs, scratch, 5, 12 + 7 * count, 1 + count
    )


def key_ranges(own_ids, row_ids, rows):
    blocks = own_ids.reshape(-1, rows)
    position = jnp.arange(row_ids.shape[0], dtype=jnp.int32)
    low = jnp.min(jnp.where(row_ids == blocks[:, :1], position, row_ids.shape[0]), axis=1)
    high = jnp.max(jnp.where(row_ids == blocks[:, -1:], position, -1), axis=1)
    return jnp.stack([low // KEYS, high // KEYS + 1], axis=1).reshape(-1)


def body(
    tokens, picture, cotangent, first_gain, first_shift, query_weight, query_bias, key_weight,
    value_weight, value_bias, output_weight, output_bias, second_gain, second_shift, up_weight,
    up_bias, down_weight, down_bias,
):
    token_count = tokens.shape[0]
    rows = token_count // 4
    layers = query_weight.shape[0]
    head_cols = query_bias.shape[1]
    feed = up_bias.shape[1]
    feed_pad = -feed % LANES
    feed_cols = feed + feed_pad
    hid = lax.axis_index("hid")
    tok = lax.axis_index("tok")
    count = lax.axis_size("tok")
    shard = query_weight.shape[1]
    shard_pad = -shard % 16
    width = count * shard
    lead = 3 * head_cols % LANES
    used_cols = 3 * head_cols + -3 * head_cols % LANES

    own_ids = lax.dynamic_slice_in_dim(picture, tok * token_count, token_count)
    row_ids = lax.dynamic_slice_in_dim(picture, (tok // 2) * 2 * token_count, 2 * token_count)
    place = jnp.stack([hid, tok % 2]).astype(jnp.int32)
    meta = jnp.concatenate([place, key_ranges(own_ids, row_ids, rows)])

    def side_by_side(*parts):
        return jnp.concatenate(parts, axis=1)

    def padded(part):
        return jnp.pad(part, ((0, 0), (0, feed_pad)))

    def shards(part):
        return jnp.pad(part, ((0, shard_pad), (0, 0)))

    def by_tokens(array):
        return array.transpose(1, 0, 2).reshape(rows, 4 * array.shape[2]).astype(F32)

    def by_features(array):
        return array.reshape(rows, 4, head_cols).transpose(1, 0, 2)

    def joined(gathered):
        return gathered[:, :shard].reshape(width, gathered.shape[2])

    def separate(grads):
        grads = grads.reshape(count, shard, grads.shape[1])
        return jnp.pad(grads, ((0, 0), (0, shard_pad), (0, 0)))

    mixed_parts = [
        shards(
            side_by_side(
                key_weight[layer], value_weight[layer], query_weight[layer], output_weight[layer].T
            )
        )
        for layer in range(layers)
    ]
    vectors = jnp.stack(
        [first_gain, first_shift, output_bias, second_gain, second_shift, down_bias], axis=1
    )
    vectors = jnp.pad(vectors, ((0, 0), (0, 2), (0, 0))).reshape(layers * 8, head_cols)
    x, gradient, vectors, mixed = entry(
        tokens.reshape(4, rows, head_cols),
        cotangent.reshape(4, rows, head_cols),
        vectors,
        mixed_parts[0],
        count,
    )
    x, gradient = by_tokens(x), by_tokens(gradient)
    vectors = vectors.transpose(1, 0, 2).reshape(layers, 8, width)
    bias = side_by_side(jnp.zeros_like(value_bias), value_bias, query_bias)
    bias = jnp.pad(bias, ((0, 0), (0, used_cols - 3 * head_cols)))
    up_bias = padded(up_bias)

    halves = [(place, place ^ 1) for place in range(count)]
    lines = [[place * 2 + low for place in range(count // 2)] for low in range(2)]

    def swap(part):
        return lax.ppermute(part, "tok", halves)

    def both_halves(own, other):
        first = tok % 2 == 0
        return jnp.stack([jnp.where(first, own, other), jnp.where(first, other, own)])

    def along(part):
        return lax.all_gather(part, "tok", axis=0, tiled=True, axis_index_groups=lines)

    def along_first(part):
        own = along(part)
        other = swap(own)
        parts = [rows_of.reshape(count // 2, shard, part.shape[1]) for rows_of in (own, other)]
        if shard % 16 == 0:
            return parts
        return [both_halves(*parts).transpose(1, 0, 2, 3).reshape(width, part.shape[1])]

    def across_first(part):
        pair = both_halves(part, swap(part)).reshape(2 * shard, part.shape[1])
        return along(pair)

    def up_part(layer):
        return padded(up_weight[layer])

    def down_part(layer):
        return padded(down_weight[layer].T)

    weights = [[[joined(mixed)], along_first(up_part(0)), [across_first(down_part(0))]]]
    for layer in range(1, layers):
        mixed = along_first(mixed_parts[layer][:shard])
        weights.append([mixed, [across_first(up_part(layer))], [across_first(down_part(layer))]])
    saved = []
    for layer in range(layers):
        mixed, up, down = weights[layer]
        normed, queries, own_pairs, far_pairs = project(layer, x, vectors, bias, mixed, head_cols)
        mixture, logsum = attend(
            meta, queries, own_pairs, far_pairs, own_ids[:, None], row_ids[None, :], lead
        )
        x_next, after, normed_two, active, slope = mlp(
            layer, mixture, x, vectors, up_bias, mixed, up, down
        )
        saved.append(
            (x, normed, queries, own_pairs, far_pairs, mixture, logsum, after, normed_two, active, slope)
        )
        x = x_next
    final = x

    def by_halves(part):
        own = lax.dynamic_index_in_dim(part, tok % 2, 1, keepdims=False)
        other = lax.dynamic_index_in_dim(part, 1 - tok % 2, 1, keepdims=False)
        return own, other

    def sum_along(part):
        return lax.psum_scatter(
            part, "tok", scatter_dimension=0, tiled=True, axis_index_groups=lines
        )

    def hold(*values):
        return lax.optimization_barrier(values)

    def halves_of(part):
        part = part.reshape(-1, 2, shard, part.shape[1])
        own, other = by_halves(part)
        return own, swap(other)

    def added(own, other):
        return (own.astype(F32) + other.astype(F32)).astype(BF)

    def in_rows(part):
        return part.reshape(-1, part.shape[-1])

    mixed_grads, up_grads, down_grads = [None] * layers, [None] * layers, [None] * layers
    wide, narrow, broad = [None] * layers, [None] * layers, [None] * layers
    grads = None
    for layer in reversed(range(layers)):
        x, normed, queries, own_pairs, far_pairs, mixture, logsum, after, normed_two, active, slope = saved[layer]
        mixed, up, down = weights[layer]
        last = layer + 1
        if last < layers:
            gradient, down_grad, up_grad = hold(gradient, down_grads[last], up_grads[last])
            up_grads[last] = sum_along(in_rows(up_grad))
            mixed_own, mixed_other = halves_of(grads)
            down_own, down_other = halves_of(down_grad)
        grad_after, grad_mixture, grad_up, grad_down, grad_out, sums_two, hidden_sums = mlp_back(
            layer, gradient, after, vectors, mixed, up, down, mixture, normed_two, active, slope
        )
        if last < layers:
            mixed_other, down_other, grad_mixture = hold(mixed_other, down_other, grad_mixture)
            down_grads[last] = added(down_own, down_other)[0]
            mixed_grad = added(mixed_own, mixed_other)
            grad_mixture, up_grads[last], mixed_grad = hold(grad_mixture, up_grads[last], mixed_grad)
            down_rows = grad_down.reshape(count // 2, 2 * shard, feed_cols)
            together = jnp.concatenate([mixed_grad, down_rows], axis=1)
            together = sum_along(in_rows(together))
        else:
            down_grads[layer] = sum_along(grad_down)
        up_own, up_other = halves_of(grad_up)
        grad_queries, grad_own, grad_far = attend_back(
            meta, queries, own_pairs, far_pairs, own_ids[None, :], row_ids[:, None],
            grad_mixture, logsum,
        )
        up_other, grad_far = hold(up_other, grad_far)
        up_grads[layer] = added(up_own, up_other)
        gradient, grads, sums_one, column_sums = project_back(
            layer, grad_after, x, vectors, mixed, normed, grad_queries, grad_own, grad_far,
            grad_out, used_cols,
        )
        if last < layers:
            grads, together = hold(grads, together)
            mixed_grads[last], down_grads[layer] = together[:shard], together[shard:]
        wide[layer] = sums_one + sums_two
        narrow[layer] = column_sums[0, : 3 * head_cols].reshape(3, head_cols)
        broad[layer] = hidden_sums
    up_grad, down_grads[0] = hold(up_grads[0], down_grads[0])
    up_grads[0] = sum_along(in_rows(up_grad))
    down_own, down_other = halves_of(down_grads[0])
    grads = separate(grads)
    wide = jnp.concatenate(wide, axis=0)
    wide = wide.reshape(layers * 8, 4, head_cols).transpose(1, 0, 2)

    def tall(parts):
        rows_of = jnp.concatenate(parts, axis=0)
        return jnp.pad(rows_of, ((0, -rows_of.shape[0] % 8), (0, 0)))

    final, gradient, sums, broad, first_grad = finish(
        by_features(final.astype(BF)),
        by_features(gradient.astype(BF)),
        wide,
        tall(narrow),
        tall(broad),
        grads,
    )
    mixed_grads[0] = first_grad[:shard]
    down_other, up_grads[0], final, gradient, sums, broad, mixed_grads[0] = hold(
        down_other, up_grads[0], final, gradient, sums, broad, mixed_grads[0]
    )
    down_grads[0] = added(down_own, down_other)[0]
    wide = sums[: layers * 8].reshape(layers, 8, head_cols)
    narrow = sums[layers * 8 : layers * 11].reshape(layers, 3, head_cols)

    def mixed_columns(start):
        columns = slice(start * head_cols, (start + 1) * head_cols)
        return jnp.stack([part[:, columns].astype(F32) for part in mixed_grads])

    def hidden_columns(parts):
        return jnp.stack([part[:, :feed].astype(F32) for part in parts])

    return (
        final,
        gradient,
        wide[:, 0],
        wide[:, 1],
        mixed_columns(2),
        narrow[:, 2],
        mixed_columns(0),
        mixed_columns(1),
        narrow[:, 1],
        mixed_columns(3).transpose(0, 2, 1),
        wide[:, 2],
        wide[:, 3],
        wide[:, 4],
        hidden_columns(up_grads),
        broad[:layers, :feed],
        hidden_columns(down_grads).transpose(0, 2, 1),
        wide[:, 5],
    )


def solution(mesh):
    rows = P("tok", "hid")
    vector = P(None, "hid")
    inward = P(None, "tok", "hid")
    outward = P(None, "hid", "tok")
    in_specs = (
        rows, P(), rows, vector, vector, inward, vector, inward, inward, vector, outward, vector,
        vector, vector, inward, vector, outward, vector,
    )
    out_specs = (
        rows, rows, vector, vector, inward, vector, inward, inward, vector, outward, vector,
        vector, vector, inward, vector, outward, vector,
    )
    return jax.shard_map(body, mesh=mesh, in_specs=in_specs, out_specs=out_specs, check_vma=False)
```

```python
import functools

import jax
import jax.numpy as jnp
from jax import lax
from jax.experimental import pallas as pl
from jax.experimental.pallas import tpu as pltpu
from jax.sharding import PartitionSpec as P

HEAD_DIM = 72
LANES = 128
KEYS = 512
EPS = 1e-06
GELU = 0.7978845608028654
CUBE = 0.044715
MASKED = -1e30
LOG2E = 1.4426950408889634
LN2 = 0.6931471805599453
NN = (((1,), (0,)), ((), ()))
NT = (((1,), (1,)), ((), ()))
TN = (((0,), (0,)), ((), ()))
MESH = pl.DeviceIdType.MESH
BF = jnp.bfloat16
F32 = jnp.float32
VMEM_LIMIT = 60 * 1024 * 1024


def dot(left, right, dims=NN):
    return lax.dot_general(left, right, dims, preferred_element_type=F32)


def micros(duration):
    return pl.CostEstimate(flops=duration * 10**9, bytes_accessed=0, transcendentals=0)


def flat(value):
    return value.reshape(value.shape[0] * value.shape[1], value.shape[2])


class Net:
    def __init__(self, send_sems, recv_sems):
        tok, hid = lax.axis_index("tok"), lax.axis_index("hid")
        near = hid + 1 - 2 * lax.rem(hid, 2)
        self.tok, self.hid = tok, hid
        self.core = (tok, near)
        self.far = (tok, lax.rem(hid + 2, 4))
        self.far_core = (tok, lax.rem(near + 2, 4))
        self.half = (tok + 1 - 2 * lax.rem(tok, 2), hid)
        self.low, self.high = lax.rem(tok, 2), lax.div(tok, 2)
        self.send_sems, self.recv_sems = send_sems, recv_sems
        self.copies, self.count = [], 0

    def row(self, high):
        return (high * 2 + self.low, self.hid)

    def line(self, count):
        self.before, self.has_before = self.row(lax.max(self.high - 1, 0)), self.high > 0
        self.after = self.row(lax.min(self.high + 1, count - 1))
        self.has_after, self.last = self.high + 1 < count, count - 1

    def barrier(self, devices, line=False):
        sem = pltpu.get_barrier_semaphore()

        def signal(device):
            pl.semaphore_signal(sem, inc=1, device_id=device, device_id_type=MESH)

        for device in devices:
            signal(device)
        peers = len(devices)
        if line:
            pl.when(self.has_before)(lambda: signal(self.before))
            pl.when(self.has_after)(lambda: signal(self.after))
            peers = peers + lax.min(self.high, 1) + lax.min(self.last - self.high, 1)
        pl.semaphore_wait(sem, peers)

    def take(self, count):
        first = self.count
        self.count += count
        return first

    def make(self, index, source, target, device):
        return pltpu.make_async_remote_copy(
            src_ref=source,
            dst_ref=target,
            send_sem=self.send_sems.at[index],
            recv_sem=self.recv_sems.at[index],
            device_id=device,
            device_id_type=MESH,
        )

    def copy(self, source, target, device):
        made = self.make(self.take(1), source, target, device)
        self.copies.append(made)
        made.start()
        return made

    def finish(self, waited=()):
        done = [id(made) for made in waited]
        for made in self.copies:
            if id(made) not in done:
                made.wait_send()


class Moves:
    def __init__(self, sems):
        self.sems, self.count, self.stores = sems, 0, []

    def take(self, count):
        first = self.count
        self.count += count
        return first

    def make(self, index, source, target):
        return pltpu.make_async_copy(source, target, self.sems.at[index])

    def load(self, source, target):
        made = self.make(self.take(1), source, target)
        made.start()
        return made

    def store(self, source, target):
        self.stores.append(self.load(source, target))

    def finish(self):
        for made in self.stores:
            made.wait()


class Several:
    def __init__(self, copies):
        self.copies = copies

    def wait(self):
        for one in self.copies:
            one.wait()


def weight_loads(parts):
    return 1 if len(parts) == 1 else 2 * parts[0].shape[0]


def load_weight(net, moves, parts, columns, target):
    if len(parts) == 1:
        return moves.load(parts[0].at[:, columns], target)
    copies = []
    for part, low in zip(parts, (net.low, 1 - net.low)):
        shard = part.shape[1]
        for high in range(part.shape[0]):
            start = pl.multiple_of((high * 2 + low) * shard, 16)
            copies.append(moves.load(part.at[high, :, columns], target.at[pl.ds(start, shard)]))
    return Several(copies)


def store_halves(net, moves, grad, outs, shard):
    if not shard:
        moves.store(grad, outs[0])
        return
    for out, low in zip(outs, (net.low, 1 - net.low)):
        for place in range(out.shape[0]):
            start = pl.multiple_of((place * 2 + low) * shard, 16)
            moves.store(grad.at[pl.ds(start, shard)], out.at[place])


def half_outputs(rows, columns, shard):
    if not shard:
        return [((rows, columns), BF, False)]
    return [((rows // (2 * shard), shard, columns), BF, False)] * 2


def spaced(arrays):
    return [(array, False) for array in arrays]


def job_copies(count):
    return 2 * count + 1


class GatherJob:
    def __init__(self, net, moves, shard, weights):
        self.net, self.weights = net, weights
        self.count = weights.shape[0] // 2
        self.across = net.take(2 * self.count - 1)
        self.up, self.down = net.take(self.count), net.take(self.count)
        own = weights.at[net.tok]
        moves.store(shard, own)
        first = self.swap(0, shard, own)
        pl.when(net.has_after)(lambda: net.make(self.up, shard, own, net.after).start())
        pl.when(net.has_before)(lambda: net.make(self.down, shard, own, net.before).start())
        first.start()

    def swap(self, index, source, target):
        return self.net.make(self.across + index, source, target, self.net.half)

    def arrive(self, step, above):
        net = self.net
        place = net.high + step if above else net.high - step
        block = self.weights.at[place * 2 + net.low]
        base, onward = (self.down, net.before) if above else (self.up, net.after)
        net.make(base + step - 1, block, block, onward).wait_recv()
        if step + 1 < self.count:
            go_on = net.has_before if above else net.has_after
            pl.when(go_on)(lambda: net.make(base + step, block, block, onward).start())
        self.swap(2 * step - int(above), block, block).start()

    def forward(self, point, points):
        net = self.net
        for step in range(1, self.count):
            if (step - 1) * points // (self.count - 1) == point:
                pl.when(net.high - step >= 0)(functools.partial(self.arrive, step, False))
                pl.when(net.high + step < self.count)(functools.partial(self.arrive, step, True))

    def finish(self):
        net = self.net
        own = self.weights.at[net.tok]
        self.swap(0, own, own).wait()
        for step in range(1, self.count):
            below, above = net.high - step >= 0, net.high + step < self.count
            pl.when(below)(lambda step=step: self.swap(2 * step, own, own).wait())
            pl.when(above)(lambda step=step: self.swap(2 * step - 1, own, own).wait())
        for step in range(self.count - 1):
            for base, device, has, there in (
                (self.up, net.after, net.has_after, net.high - step >= 0),
                (self.down, net.before, net.has_before, net.high + step < self.count),
            ):
                sent = net.make(base + step, own, own, device)
                pl.when(jnp.logical_and(has, there))(sent.wait_send)


class Line:
    def __init__(self, net, count, value, passing, arrived):
        self.net, self.count, self.value = net, count, value
        self.passing, self.arrived = passing, arrived
        self.up, self.down = net.take(count), net.take(count)

    def upward(self, place):
        source, target = self.passing.at[place], self.arrived.at[place + 1]
        return self.net.make(self.up + place, source, target, self.net.after)

    def downward(self, place):
        source, target = self.passing.at[place], self.arrived.at[place]
        return self.net.make(self.down + place, source, target, self.net.before)

    def send(self, place, above):
        net = self.net
        value = self.value(place)
        self.passing[place] = value.astype(BF)
        move = self.upward(place) if above else self.downward(place)

        def add():
            move.wait_recv()
            landed = self.arrived[place + 1 if above else place]
            self.passing[place] = (value + landed.astype(F32)).astype(BF)

        pl.when(net.has_before if above else net.has_after)(add)
        move.start()

    def forward(self, point, points):
        high, last = self.net.high, self.count - 1
        for slot in range(last):
            if slot * points // last == point:
                pl.when(high <= slot)(functools.partial(self.send, last - slot + high, True))
                pl.when(last - high <= slot)(functools.partial(self.send, slot - last + high, False))

    def finish(self, total):
        net = self.net
        total[...] = self.value(net.high)

        def add(move, place):
            move.wait_recv()
            total[...] += self.arrived[place].astype(F32)

        pl.when(net.has_before)(lambda: add(self.upward(net.high), net.high + 1))
        pl.when(net.has_after)(lambda: add(self.downward(net.high), net.high))

    def drain(self):
        for place in range(self.count):
            pl.when(self.net.high < place)(self.upward(place).wait_send)
            pl.when(self.net.high > place)(self.downward(place).wait_send)


def part_scratch(count, shard, width):
    half = count // 2
    return [pltpu.VMEM((half, shard, width), BF)] * 3 + [pltpu.VMEM((half + 1, shard, width), BF)]


class ScatterParts:
    def __init__(self, net, moves, grads, scratch):
        self.net, self.moves = net, moves
        self.own, self.landed, passing, arrived = scratch
        self.count = count = grads.shape[0] // 2
        self.across, self.loads = net.take(count), moves.take(count)
        high, last = net.high, count - 1

        def start(place):
            self.swap(place, grads.at[place * 2 + 1 - net.low]).start()

        for slot in range(last):
            pl.when(high <= slot)(functools.partial(start, last - slot + high))
            pl.when(last - high <= slot)(functools.partial(start, slot - last + high))
        start(high)
        for place in range(count):
            source = grads.at[place * 2 + net.low]
            moves.make(self.loads + place, source, self.own.at[place]).start()
        self.line = Line(net, count, self.pair, passing, arrived)
        self.forward = self.line.forward

    def swap(self, place, source=None):
        target = self.landed.at[place]
        source = target if source is None else source
        return self.net.make(self.across + place, source, target, self.net.half)

    def pair(self, place):
        own = self.own.at[place]
        self.moves.make(self.loads + place, own, own).wait()
        self.swap(place).wait_recv()
        return self.own[place].astype(F32) + self.landed[place].astype(F32)

    def finish(self, total):
        self.line.finish(total)
        self.line.drain()
        for place in range(self.count):
            self.swap(place).wait_send()


def run(kernel, name, duration, inputs, outputs, scratch, identity, copies, moves):
    def space(near):
        return pl.BlockSpec(memory_space=pltpu.VMEM if near else pl.ANY)

    return pl.pallas_call(
        kernel,
        name=name,
        cost_estimate=micros(duration),
        out_shape=[jax.ShapeDtypeStruct(shape, dtype) for shape, dtype, _ in outputs],
        in_specs=[space(near) for _, near in inputs],
        out_specs=[space(near) for _, _, near in outputs],
        scratch_shapes=list(scratch)
        + [
            pltpu.SemaphoreType.DMA((copies,)),
            pltpu.SemaphoreType.DMA((copies,)),
            pltpu.SemaphoreType.DMA((moves,)),
        ],
        compiler_params=pltpu.CompilerParams(
            collective_id=identity, has_side_effects=True, vmem_limit_bytes=VMEM_LIMIT
        ),
    )(*[array for array, _ in inputs])


def split_refs(refs, inputs, outputs):
    return refs[:inputs], refs[inputs : inputs + outputs], refs[inputs + outputs :]


def norm_parts(rows):
    centred = rows - jnp.mean(rows, axis=1, keepdims=True)
    inverse = lax.rsqrt(jnp.mean(centred * centred, axis=1, keepdims=True) + EPS)
    return centred * inverse, inverse


def norm_back(rows, gain, grad):
    scaled, inverse = norm_parts(rows)
    inner = grad * gain
    first = jnp.mean(inner, axis=1, keepdims=True)
    second = jnp.mean(inner * scaled, axis=1, keepdims=True)
    return (
        inverse * (inner - first - scaled * second),
        jnp.sum(grad * scaled, axis=0, keepdims=True),
        jnp.sum(grad, axis=0, keepdims=True),
    )


def gather_send(net, full, chunk):
    near = net.copy(full.at[0, chunk], full.at[1, chunk], net.core)
    far = net.copy(full.at[0, chunk], full.at[2, chunk], net.far)
    return near, far


def gather_pass(net, full, chunk, far):
    far.wait_recv()
    return net.copy(full.at[2, chunk], full.at[3, chunk], net.core)


def scatter_scratch(rows, width):
    return [
        pltpu.VMEM((rows, width), F32),
        pltpu.VMEM((rows, width), F32),
    ] + [pltpu.VMEM((rows, width), BF)] * 6


class Scatter:
    def __init__(self, net, scratch):
        self.net = net
        self.hold, self.total, self.cs0, self.cr0, self.ys, self.yr, self.cs1, self.cr1 = scratch
        self.first, self.second = {}, {}

    def far_part(self, key, chunk, partial):
        rows = partial.shape[0] // 2
        self.hold[chunk] = partial[:rows]
        self.cs0[chunk] = partial[rows:].astype(BF)
        self.first[key] = self.net.copy(self.cs0.at[chunk], self.cr0.at[chunk], self.net.core)

    def far_send(self, key, chunk):
        self.first[key].wait_recv()
        self.ys[chunk] = (self.hold[chunk] + self.cr0[chunk].astype(F32)).astype(BF)
        self.second[key] = self.net.copy(self.ys.at[chunk], self.yr.at[chunk], self.net.far)

    def near_part(self, partial):
        rows = partial.shape[0] // 2
        self.total[...] = partial[:rows]
        self.cs1[...] = partial[rows:].astype(BF)
        self.near = self.net.copy(self.cs1, self.cr1, self.net.core)

    def near_done(self):
        self.near.wait_recv()
        self.total[...] += self.cr1[...].astype(F32)

    def result(self, key, chunk):
        self.second[key].wait_recv()
        return self.total[chunk] + self.yr[chunk].astype(F32)


def blocked(value):
    return value.astype(BF).reshape(2, value.shape[0] // 2, value.shape[1])


def chunks_of(rows, count):
    step = rows // count
    return [pl.ds(index * step, step) for index in range(count)]


def weight_grad(left, right, out, extra=None):
    width = left.shape[2]
    tile = 384

    def one(index, carry):
        columns = pl.ds(pl.multiple_of(index * tile, tile), tile)
        result = dot(flat(left[:, :, columns]), flat(right[...]), TN)
        if extra is None:
            out[columns, :] = result.astype(out.dtype)
        else:
            start = out.shape[1] - extra.shape[1]
            join = result.shape[1] - start
            added = extra[columns, :]
            out[columns, :start] = result[:, :start].astype(out.dtype)
            both = result[:, start:] + added[:, :join].astype(F32)
            out[columns, start : start + join] = both.astype(out.dtype)
            out[columns, start + join :] = added[:, join:]
        return carry

    lax.fori_loop(0, width // tile, one, 0)


def project_kernel(*refs, layer, head_cols, factor, parts):
    (x_hbm, vec, bias, *mixed_hbm), outs, scratch = split_refs(refs, 3 + parts, 4)
    normed_out, queries_out, pairs_out, far_out = outs
    x, weight, normed, queries, pairs, far_pairs, send_sems, recv_sems, move_sems = scratch
    net, moves = Net(send_sems, recv_sems), Moves(move_sems)
    rows = x.shape[0]
    pair_cols = 2 * head_cols
    chunks = chunks_of(rows, 2)
    x_load = moves.load(x_hbm, x)
    columns = pl.ds(0, weight.shape[1])
    weight_load = load_weight(net, moves, mixed_hbm, columns, weight)
    net.barrier([net.core, net.far, net.half])
    x_load.wait()
    sent = []
    for chunk in chunks:
        scaled, _ = norm_parts(x[chunk, :])
        normed[0, chunk, :] = (scaled * vec[layer, 0:1] + vec[layer, 1:2]).astype(BF)
        sent.append(gather_send(net, normed, chunk))
    arrived = []
    weight_load.wait()

    def project(slots, chunk):
        result = dot(flat(normed[slots, chunk, :]), weight[...]) + bias[layer : layer + 1]
        shape = (slots.size, chunk.size, -1)
        pairs[slots, chunk, :] = result[:, :pair_cols].astype(BF).reshape(shape)
        own = result[:, pair_cols : pair_cols + head_cols] * factor
        queries[slots, chunk, :] = own.astype(BF).reshape(shape)
        source, target = pairs.at[slots, chunk], far_pairs.at[slots, chunk]
        arrived.append(net.copy(source, target, net.half))

    whole = pl.ds(0, rows)
    project(pl.ds(0, 1), whole)
    for near, _ in sent:
        near.wait_recv()
    project(pl.ds(1, 1), whole)
    for chunk, (_, far) in zip(chunks, sent):
        gather_pass(net, normed, chunk, far).wait_recv()
        project(pl.ds(2, 2), chunk)
    moves.store(normed, normed_out)
    moves.store(queries, queries_out)
    moves.store(pairs, pairs_out)
    for one in arrived:
        one.wait_recv()
    moves.store(far_pairs, far_out)
    net.finish()
    moves.finish()


def project(layer, x, vec, bias, mixed, head_cols):
    rows, width = x.shape
    used = bias.shape[1]
    outputs = [
        ((4, rows, width), BF, False),
        ((4, rows, head_cols), BF, False),
        ((4, rows, 2 * head_cols), BF, False),
        ((4, rows, 2 * head_cols), BF, False),
    ]
    scratch = [pltpu.VMEM((rows, width), F32), pltpu.VMEM((width, used), BF)]
    scratch += [pltpu.VMEM(shape, dtype) for shape, dtype, _ in outputs]
    kernel = functools.partial(
        project_kernel,
        layer=layer,
        head_cols=head_cols,
        factor=HEAD_DIM ** (-0.5) * LOG2E,
        parts=len(mixed),
    )
    inputs = [(x, False), (vec, True), (bias, True)] + spaced(mixed)
    return run(kernel, "project", 40, inputs, outputs, scratch, 8 * layer, 12, 6 + weight_loads(mixed))


def pair_windows(width, lead=0):
    windows = []
    for first in range(lead, width - HEAD_DIM, 2 * HEAD_DIM):
        start = first // LANES * LANES
        size = min(2 * LANES, width - start)
        row = lax.broadcasted_iota(jnp.int32, (size, 2 * LANES), 0) + (start - first)
        lane = lax.broadcasted_iota(jnp.int32, (size, 2 * LANES), 1)
        second = lane >= LANES
        lane = jnp.where(second, lane - LANES, lane)
        match = row == jnp.where(second, lane + HEAD_DIM, lane)
        windows.append((start, size, jnp.logical_and(match, lane < HEAD_DIM).astype(BF)))
    return windows


def spread_heads(value, windows):
    heads = []
    for start, size, pick in windows:
        both = dot(value[:, start : start + size], pick).astype(BF)
        heads += [both[:, :LANES], both[:, LANES:]]
    return heads


def join_heads(heads, windows, width):
    tiles = [None] * (-(-width // LANES))
    for index, (start, size, pick) in enumerate(windows):
        both = jnp.concatenate(heads[2 * index : 2 * index + 2], axis=1)
        part = dot(both, pick, NT)
        for lane in range(0, size, LANES):
            tile, piece = (start + lane) // LANES, part[:, lane : lane + LANES]
            tiles[tile] = piece if tiles[tile] is None else tiles[tile] + piece
    return jnp.concatenate(tiles, axis=1)


def as_rows(columns):
    rows = columns[0].shape[0]
    lane = lax.broadcasted_iota(jnp.int32, (rows, LANES), 1)
    together = jnp.zeros((rows, LANES), F32)
    for head, column in enumerate(columns):
        together = jnp.where(lane == head, column, together)
    return together.T[:8]


def load_pairs(meta, own_pairs, far_pairs, key_scratch, value_scratch, heads):
    rows = own_pairs.shape[1]
    hid, half = meta[0], meta[1]
    windows = pair_windows(own_pairs.shape[2])
    for which, source in ((0, own_pairs), (1, far_pairs)):
        for slot in range(4):
            place = jnp.bitwise_xor(half, which) * 4 + jnp.bitwise_xor(hid, slot)
            start = pl.ds(pl.multiple_of(place * rows, rows), rows)
            spread = spread_heads(source[slot], windows)
            for head in range(heads):
                key_scratch[head, start, :] = spread[head]
                value_scratch[head, start, :] = spread[heads + head]


def attend_kernel(
    meta, queries, own_pairs, far_pairs, query_ids, key_ids, mixture, logsum,
    key_scratch, value_scratch, score_scratch, high_scratch, total_scratch, sum_scratch, query_scratch,
    *, heads
):
    rows = queries.shape[1]
    head_cols = heads * HEAD_DIM
    load_pairs(meta, own_pairs, far_pairs, key_scratch, value_scratch, heads)
    query_windows = pair_windows(head_cols)
    mixed_windows = pair_windows(mixture.shape[2], mixture.shape[2] - head_cols)

    def one_block(block, carry):
        slot = jnp.bitwise_xor(meta[0], block)
        first, last = meta[2 + 2 * block], meta[3 + 2 * block]
        own = pl.ds(pl.multiple_of(block * rows, rows), rows)
        ids = query_ids[own, :]
        for head, query in enumerate(spread_heads(queries[slot], query_windows)):
            query_scratch[head] = query
        high_scratch[...] = jnp.full_like(high_scratch, -3e38)
        sum_scratch[...] = jnp.zeros_like(sum_scratch)
        total_scratch[...] = jnp.zeros_like(total_scratch)

        def scores_of(key_block, inner):
            keys = pl.ds(pl.multiple_of(key_block * KEYS, KEYS), KEYS)
            same = ids == key_ids[:, keys]
            for head in range(heads):
                scores = dot(query_scratch[head], key_scratch[head, keys, :], NT)
                scores = jnp.where(same, scores, MASKED)
                score_scratch[head, :, keys] = scores
                high = high_scratch[head]
                for lane in range(0, KEYS, LANES):
                    high = jnp.maximum(high, scores[:, lane : lane + LANES])
                high_scratch[head] = high
            return inner

        lax.fori_loop(first, last, scores_of, 0)
        for head in range(heads):
            high_scratch[head] = jnp.broadcast_to(
                jnp.max(high_scratch[head], axis=1, keepdims=True), (rows, LANES)
            )

        def sums_of(key_block, inner):
            keys = pl.ds(pl.multiple_of(key_block * KEYS, KEYS), KEYS)
            for head in range(heads):
                high = high_scratch[head]
                high = jnp.concatenate([high] * (KEYS // LANES), axis=1)
                powers = jnp.exp2(score_scratch[head, :, keys] - high)
                total = total_scratch[head]
                for lane in range(0, KEYS, LANES):
                    total += powers[:, lane : lane + LANES]
                total_scratch[head] = total
                sum_scratch[head] += dot(powers.astype(BF), value_scratch[head, keys, :])
            return inner

        lax.fori_loop(first, last, sums_of, 0)
        mixed, columns = [], []
        for head in range(heads):
            total = jnp.sum(total_scratch[head], axis=1, keepdims=True)
            columns.append(high_scratch[head][:, :1] + jnp.log2(total))
            mixed.append((sum_scratch[head] / total).astype(BF))
        mixture[slot] = join_heads(mixed, mixed_windows, mixture.shape[2]).astype(BF)
        logsum[:, own] = as_rows(columns)
        return carry

    lax.fori_loop(0, 4, one_block, 0)


def attend(meta, queries, own_pairs, far_pairs, query_ids, key_ids, lead):
    _, rows, head_cols = queries.shape
    heads = head_cols // HEAD_DIM
    own, count = 4 * rows, 8 * rows
    space = pl.BlockSpec(memory_space=pltpu.VMEM)
    return pl.pallas_call(
        functools.partial(attend_kernel, heads=heads),
        name="attend",
        cost_estimate=micros(22),
        out_shape=[
            jax.ShapeDtypeStruct((4, rows, lead + head_cols), BF),
            jax.ShapeDtypeStruct((8, own), F32),
        ],
        in_specs=[pl.BlockSpec(memory_space=pltpu.SMEM)] + [space] * 5,
        out_specs=[space] * 2,
        scratch_shapes=[
            pltpu.VMEM((heads, count, LANES), BF),
            pltpu.VMEM((heads, count, LANES), BF),
            pltpu.VMEM((heads, rows, count), F32),
            pltpu.VMEM((heads, rows, LANES), F32),
            pltpu.VMEM((heads, rows, LANES), F32),
            pltpu.VMEM((heads, rows, LANES), F32),
            pltpu.VMEM((heads, rows, LANES), BF),
        ],
        compiler_params=pltpu.CompilerParams(vmem_limit_bytes=VMEM_LIMIT),
    )(meta, queries, own_pairs, far_pairs, query_ids, key_ids)


def attend_back_kernel(
    meta, queries, own_pairs, far_pairs, query_ids, key_ids, grad_mixture, logsum,
    grad_queries, grad_own, grad_far,
    key_scratch, value_scratch, grad_key, grad_value, grad_query, query_scratch, grad_scratch,
    prob_scratch, grad_prob_scratch, delta_scratch,
    *, heads
):
    rows = queries.shape[1]
    head_cols = heads * HEAD_DIM
    load_pairs(meta, own_pairs, far_pairs, key_scratch, value_scratch, heads)
    query_windows = pair_windows(head_cols)
    mixed_windows = pair_windows(grad_mixture.shape[2], grad_mixture.shape[2] - head_cols)
    grad_key[...] = jnp.zeros_like(grad_key)
    grad_value[...] = jnp.zeros_like(grad_value)

    def one_block(block, carry):
        slot = jnp.bitwise_xor(meta[0], block)
        first, last = meta[2 + 2 * block], meta[3 + 2 * block]
        own = pl.ds(pl.multiple_of(block * rows, rows), rows)
        ids = query_ids[:, own]
        for head, query in enumerate(spread_heads(queries[slot], query_windows)):
            query_scratch[head] = query
        for head, grad in enumerate(spread_heads(grad_mixture[slot], mixed_windows)):
            grad_scratch[head] = grad
        logs = logsum[:, own]
        grad_query[...] = jnp.zeros_like(grad_query)
        delta_scratch[...] = jnp.zeros_like(delta_scratch)

        def probs_of(key_block, inner):
            keys = pl.ds(pl.multiple_of(key_block * KEYS, KEYS), KEYS)
            same = key_ids[keys, :] == ids
            for head in range(heads):
                grad = grad_scratch[head]
                scores = dot(key_scratch[head, keys, :], query_scratch[head], NT)
                probs = jnp.where(same, jnp.exp2(scores - logs[head : head + 1]), 0.0)
                grad_probs = dot(value_scratch[head, keys, :], grad, NT)
                prob_scratch[head, keys, :] = probs
                grad_prob_scratch[head, keys, :] = grad_probs
                delta_scratch[head] += jnp.sum((probs * grad_probs).reshape(KEYS // 8, 8, rows), axis=0)
                grad_value[head, keys, :] += dot(probs.astype(BF), grad)
            return inner

        lax.fori_loop(first, last, probs_of, 0)
        for head in range(heads):
            delta_scratch[head, 0:1] = jnp.sum(delta_scratch[head], axis=0, keepdims=True)

        def one_key(key_block, inner):
            keys = pl.ds(pl.multiple_of(key_block * KEYS, KEYS), KEYS)
            for head in range(heads):
                delta = delta_scratch[head, 0:1]
                grad_scores = prob_scratch[head, keys, :] * (grad_prob_scratch[head, keys, :] - delta)
                grad_scores = grad_scores.astype(BF)
                grad_key[head, keys, :] += dot(grad_scores, query_scratch[head])
                grad_query[head] += dot(grad_scores, key_scratch[head, keys, :], TN)
            return inner

        lax.fori_loop(first, last, one_key, 0)
        scaled = [(grad_query[head] * HEAD_DIM ** (-0.5)).astype(BF) for head in range(heads)]
        grad_queries[slot] = join_heads(scaled, query_windows, head_cols).astype(BF)
        return carry

    lax.fori_loop(0, 4, one_block, 0)
    hid, half = meta[0], meta[1]
    for which, target in ((0, grad_own), (1, grad_far)):
        for slot in range(4):
            place = jnp.bitwise_xor(half, which) * 4 + jnp.bitwise_xor(hid, slot)
            start = pl.ds(pl.multiple_of(place * rows, rows), rows)
            parts = [(grad_key[head, start, :] * LN2).astype(BF) for head in range(heads)]
            parts += [grad_value[head, start, :].astype(BF) for head in range(heads)]
            target[slot] = join_heads(parts, pair_windows(2 * head_cols), 2 * head_cols).astype(BF)


def attend_back(meta, queries, own_pairs, far_pairs, query_ids, key_ids, grad_mixture, logsum):
    _, rows, head_cols = queries.shape
    heads = head_cols // HEAD_DIM
    count = 8 * rows
    space = pl.BlockSpec(memory_space=pltpu.VMEM)
    return pl.pallas_call(
        functools.partial(attend_back_kernel, heads=heads),
        name="attend_back",
        cost_estimate=micros(37),
        out_shape=[
            jax.ShapeDtypeStruct((4, rows, head_cols), BF),
            jax.ShapeDtypeStruct((4, rows, 2 * head_cols), BF),
            jax.ShapeDtypeStruct((4, rows, 2 * head_cols), BF),
        ],
        in_specs=[pl.BlockSpec(memory_space=pltpu.SMEM)] + [space] * 7,
        out_specs=[space] * 3,
        scratch_shapes=[
            pltpu.VMEM((heads, count, LANES), BF),
            pltpu.VMEM((heads, count, LANES), BF),
            pltpu.VMEM((heads, count, LANES), F32),
            pltpu.VMEM((heads, count, LANES), F32),
            pltpu.VMEM((heads, rows, LANES), F32),
            pltpu.VMEM((heads, rows, LANES), BF),
            pltpu.VMEM((heads, rows, LANES), BF),
            pltpu.VMEM((heads, count, rows), F32),
            pltpu.VMEM((heads, count, rows), F32),
            pltpu.VMEM((heads, 8, rows), F32),
        ],
        compiler_params=pltpu.CompilerParams(vmem_limit_bytes=VMEM_LIMIT),
    )(meta, queries, own_pairs, far_pairs, query_ids, key_ids, grad_mixture, logsum)


def mlp_kernel(*refs, layer, parts, last):
    ins, outs, scratch = split_refs(refs, 4 + sum(parts), 5 - last)
    mixture_hbm, x_hbm, vec, up_bias = ins[:4]
    mixed_hbm, up_hbm, down_hbm = split_refs(ins[4:], parts[0], parts[1])
    after_out, normed_out, active_out, slope_out = outs[:4]
    mixture, x, out_weight, up_weight, down_weight, after, normed, active, slope, x_next = scratch[:10]
    first_scratch, second_scratch = scratch[10:18], scratch[18:26]
    send_sems, recv_sems, move_sems = scratch[26:]
    net, moves = Net(send_sems, recv_sems), Moves(move_sems)
    rows = x.shape[0]
    hidden_cols = up_weight.shape[1]
    out_cols = out_weight.shape[1]
    chunks = chunks_of(rows, 2)
    out_part = pl.ds(x.shape[1] - out_cols, out_cols)
    loads = [
        moves.load(mixture_hbm, mixture), load_weight(net, moves, mixed_hbm, out_part, out_weight),
    ]
    x_load = moves.load(x_hbm, x)
    up_load = load_weight(net, moves, up_hbm, pl.ds(0, hidden_cols), up_weight)
    if not last:
        down_load = load_weight(net, moves, down_hbm, pl.ds(0, hidden_cols), down_weight)
    net.barrier([net.core, net.far])
    out_bias, gain = vec[layer, 2:3], vec[layer, 3:4]
    shift, down_bias = vec[layer, 4:5], vec[layer, 5:6]

    def mixed(slots, chunk):
        return dot(flat(mixture[slots, chunk, :]), out_weight[...], NT)

    def up(slots, chunk):
        hidden = dot(flat(normed[slots, chunk, :]), up_weight[...]) + up_bias[layer : layer + 1]
        square = hidden * hidden
        bend = jnp.tanh(GELU * hidden * (1.0 + CUBE * square))
        half = 0.5 * (1.0 + bend)
        value = hidden * half
        rise = half + 0.5 * hidden * (1.0 - bend * bend) * GELU * (1.0 + 3.0 * CUBE * square)
        active[slots, chunk, :] = blocked(value)
        slope[slots, chunk, :] = blocked(rise)

    def down(slots, chunk):
        return dot(flat(active[slots, chunk, :]), down_weight[...], NT)

    near, far, whole = pl.ds(0, 2), pl.ds(2, 2), pl.ds(0, rows)
    for load in loads:
        load.wait()
    first = Scatter(net, first_scratch)
    for key, chunk in enumerate(chunks):
        first.far_part(key, chunk, mixed(far, chunk))
    for key, chunk in enumerate(chunks):
        first.far_send(key, chunk)
    first.near_part(mixed(near, whole))
    first.near_done()
    x_load.wait()
    sent = []
    for key, chunk in enumerate(chunks):
        residual = first.result(key, chunk) + x[chunk, :] + out_bias
        after[chunk, :] = residual
        normed[0, chunk, :] = (norm_parts(residual)[0] * gain + shift).astype(BF)
        sent.append(gather_send(net, normed, chunk))
    moves.store(after, after_out)
    for one, _ in sent:
        one.wait_recv()
    up_load.wait()
    up(near, whole)
    if not last:
        down_load.wait()
    second = Scatter(net, second_scratch)
    for key, chunk in enumerate(chunks):
        passed = gather_pass(net, normed, chunk, sent[key][1])
        passed.wait_recv()
        up(far, chunk)
        if not last:
            second.far_part(key, chunk, down(far, chunk))
            second.far_send(key, chunk)
    moves.store(normed, normed_out)
    moves.store(active, active_out)
    moves.store(slope, slope_out)
    if not last:
        second.near_part(down(near, whole))
        second.near_done()
        for key, chunk in enumerate(chunks):
            x_next[chunk, :] = second.result(key, chunk) + after[chunk, :] + down_bias
        moves.store(x_next, outs[4])
    net.finish()
    moves.finish()


def mlp(layer, mixture, x, vec, up_bias, mixed, up, down, last):
    rows, width = x.shape
    hidden = up_bias.shape[1]
    outputs = [
        ((rows, width), F32, False),
        ((4, rows, width), BF, False),
        ((4, rows, hidden), BF, False),
        ((4, rows, hidden), BF, False),
        ((rows, width), F32, False),
    ]
    scratch = [
        pltpu.VMEM(mixture.shape, BF),
        pltpu.VMEM((rows, width), F32),
        pltpu.VMEM((width, mixture.shape[2]), BF),
        pltpu.VMEM((width, hidden), BF),
        pltpu.VMEM((width, hidden), BF),
    ]
    scratch += [pltpu.VMEM(shape, dtype) for shape, dtype, _ in outputs]
    scratch += scatter_scratch(rows, width) * 2
    outputs = outputs[: 5 - last]
    down = () if last else down
    inputs = [(mixture, False), (x, False), (vec, True), (up_bias, True)]
    inputs += spaced([*mixed, *up, *down])
    parts = (len(mixed), len(up), len(down))
    kernel = functools.partial(mlp_kernel, layer=layer, parts=parts, last=last)
    moves = 8 + sum(weight_loads(part) for part in (mixed, up, down) if part)
    return run(kernel, "mlp", 48, inputs, outputs, scratch, 8 * layer + 1, 18, moves)


def mlp_back_kernel(*refs, layer, parts, given, shard):
    ins, outs, scratch = split_refs(refs, 7 + given + sum(parts), 7 + (shard > 0))
    gradient_hbm, after_hbm, vec, mixture_hbm, normed_hbm, active_hbm, slope_hbm = ins[:7]
    mixed_hbm, up_hbm, down_hbm = split_refs(ins[7 + given :], parts[0], parts[1])
    after_out, mixture_out, down_out, out_out, sums, hidden_sums = outs[:6]
    up_outs = outs[6:]
    gradient, after, out_weight, up_weight, down_weight, mixture, normed, active, slope = scratch[:9]
    grad_after, grad_mixture, grad_down, grad_up, grad_out = scratch[9:14]
    grad_rows, grad_hidden, grad_mid = scratch[14:17]
    scatter_refs = scratch[17:25]
    send_sems, recv_sems, move_sems = scratch[25:]
    net, moves = Net(send_sems, recv_sems), Moves(move_sems)
    rows, width = gradient.shape
    hidden_cols = up_weight.shape[1]
    out_cols = out_weight.shape[1]
    chunks = chunks_of(rows, 2)
    out_part = pl.ds(width - out_cols, out_cols)
    load_gradient = moves.load(ins[7] if given else gradient_hbm, grad_rows if given else gradient)
    load_down = load_weight(net, moves, down_hbm, pl.ds(0, hidden_cols), down_weight)
    load_slope = moves.load(slope_hbm, slope)
    load_up = load_weight(net, moves, up_hbm, pl.ds(0, hidden_cols), up_weight)
    load_active = moves.load(active_hbm, active)
    load_after = moves.load(after_hbm, after)
    load_normed = moves.load(normed_hbm, normed)
    load_out = load_weight(net, moves, mixed_hbm, out_part, out_weight)
    load_mixture = moves.load(mixture_hbm, mixture)
    if given:
        load_own = moves.load(gradient_hbm, gradient)
    net.barrier([net.core, net.far])
    gain = vec[layer, 3:4]
    near, far, whole = pl.ds(0, 2), pl.ds(2, 2), pl.ds(0, rows)
    load_gradient.wait()
    if not given:
        grad_rows[0] = gradient[...].astype(BF)
        sent = [gather_send(net, grad_rows, chunk) for chunk in chunks]
    sums[...] = jnp.zeros_like(sums)
    sums[5:6] = jnp.sum(grad_rows[0].astype(F32), axis=0, keepdims=True)

    def hidden_grad(slots, chunk):
        value = dot(flat(grad_rows[slots, chunk, :]), down_weight[...])
        value = value * flat(slope[slots, chunk, :]).astype(F32)
        grad_hidden[slots, chunk, :] = blocked(value)

    def up_back(slots, chunk):
        return dot(flat(grad_hidden[slots, chunk, :]), up_weight[...], NT)

    if not given:
        for one, _ in sent:
            one.wait_recv()
    load_down.wait()
    load_slope.wait()
    scatter = Scatter(net, scatter_refs)
    if given:
        for key, chunk in enumerate(chunks):
            hidden_grad(far, chunk)
            if key == 0:
                load_up.wait()
            scatter.far_part(key, chunk, up_back(far, chunk))
        for key, chunk in enumerate(chunks):
            scatter.far_send(key, chunk)
        hidden_grad(near, whole)
    else:
        hidden_grad(near, whole)
        load_up.wait()
        for key, chunk in enumerate(chunks):
            passed = gather_pass(net, grad_rows, chunk, sent[key][1])
            passed.wait_recv()
            hidden_grad(far, chunk)
            scatter.far_part(key, chunk, up_back(far, chunk))
            scatter.far_send(key, chunk)
    scatter.near_part(up_back(near, whole))
    load_active.wait()
    weight_grad(grad_rows, active, grad_down)
    moves.store(grad_down, down_out)
    scatter.near_done()
    load_after.wait()
    if given:
        load_own.wait()
    sent = []
    for key, chunk in enumerate(chunks):
        back, gain_sum, shift_sum = norm_back(after[chunk, :], gain, scatter.result(key, chunk))
        total = gradient[chunk, :] + back
        grad_after[chunk, :] = total
        rounded = total.astype(BF)
        grad_mid[0, chunk, :] = rounded
        sent.append(gather_send(net, grad_mid, chunk))
        sums[3:4] += gain_sum
        sums[4:5] += shift_sum
        sums[2:3] += jnp.sum(rounded.astype(F32), axis=0, keepdims=True)
    moves.store(grad_after, after_out)
    load_normed.wait()
    weight_grad(normed, grad_hidden, grad_up)
    store_halves(net, moves, grad_up, up_outs, shard)
    column = jnp.zeros((1, hidden_cols), F32)
    for slot in range(4):
        column += jnp.sum(grad_hidden[slot].astype(F32), axis=0, keepdims=True)
    hidden_sums[...] = column

    def mix_back(slots, chunk):
        value = dot(flat(grad_mid[slots, chunk, :]), out_weight[...])
        grad_mixture[slots, chunk, :] = blocked(value)

    for one, _ in sent:
        one.wait_recv()
    load_out.wait()
    mix_back(near, whole)
    for key, chunk in enumerate(chunks):
        gather_pass(net, grad_mid, chunk, sent[key][1]).wait_recv()
    mix_back(far, whole)
    moves.store(grad_mixture, mixture_out)
    load_mixture.wait()
    weight_grad(grad_mid, mixture, grad_out)
    moves.store(grad_out, out_out)
    net.finish()
    moves.finish()


def mlp_back(
    layer, gradient, after, vec, mixed, up, down, mixture, normed, active, slope, given=(),
    shard=0,
):
    rows, width = gradient.shape
    hidden = active.shape[2]
    out_cols = mixture.shape[2]
    outputs = [
        ((rows, width), F32, False),
        ((4, rows, out_cols), BF, False),
        ((width, hidden), BF, False),
        ((width, out_cols), BF, False),
        ((8, width), F32, True),
        ((1, hidden), F32, True),
    ]
    shapes = [
        ((rows, width), F32),
        ((rows, width), F32),
        ((width, out_cols), BF),
        ((width, hidden), BF),
        ((width, hidden), BF),
        ((4, rows, out_cols), BF),
        ((4, rows, width), BF),
        ((4, rows, hidden), BF),
        ((4, rows, hidden), BF),
        ((rows, width), F32),
        ((4, rows, out_cols), BF),
        ((width, hidden), BF),
        ((width, hidden), BF),
        ((width, out_cols), BF),
        ((4, rows, width), BF),
        ((4, rows, hidden), BF),
        ((4, rows, width), BF),
    ]
    outputs += half_outputs(width, hidden, shard)
    scratch = [pltpu.VMEM(shape, dtype) for shape, dtype in shapes] + scatter_scratch(rows, width)
    inputs = [
        (gradient, False), (after, False), (vec, True), (mixture, False), (normed, False),
        (active, False), (slope, False),
    ] + spaced([*given, *mixed, *up, *down])
    parts = (len(mixed), len(up), len(down))
    kernel = functools.partial(
        mlp_back_kernel, layer=layer, parts=parts, given=len(given), shard=shard
    )
    moves = 13 + (3 * width // (2 * shard) if shard else 0)
    moves += weight_loads(mixed) + weight_loads(up) + weight_loads(down)
    return run(kernel, "mlp_back", 48, inputs, outputs, scratch, 8 * layer + 2, 20, moves)


def project_back_kernel(*refs, layer, parts, closing):
    ins, outs, scratch = split_refs(refs, 8 + parts + closing, 4 + (closing > 0))
    after_hbm, x_hbm, vec, normed_hbm, queries_hbm, own_hbm, far_hbm, out_hbm = ins[:8]
    mixed_hbm, closing_ins = ins[8 : 8 + parts], ins[8 + parts :]
    gradient_out, sums, column_sums, weight_out = outs[:4]
    grad_after, x, weight, normed, grad_queries, grad_own, grad_out = scratch[:7]
    landed, together, gradient, grad_weight = scratch[7:11]
    scatter_refs, closing_refs = scratch[11:19], scratch[19:-3]
    send_sems, recv_sems, move_sems = scratch[-3:]
    net, moves = Net(send_sems, recv_sems), Moves(move_sems)
    rows, width = x.shape
    pair_cols = grad_own.shape[2]
    used_cols = pair_cols + grad_queries.shape[2]
    all_cols = together.shape[2]
    chunks = chunks_of(rows, 2)
    near, far, whole = pl.ds(0, 2), pl.ds(2, 2), pl.ds(0, rows)
    load_own = moves.load(own_hbm, grad_own)
    load_queries = moves.load(queries_hbm, grad_queries)
    loading = load_weight(net, moves, mixed_hbm, pl.ds(0, all_cols), weight)
    load_normed = moves.load(normed_hbm, normed)
    load_out = moves.load(out_hbm, grad_out)
    load_x = moves.load(x_hbm, x)
    load_after = moves.load(after_hbm, grad_after)
    if closing:
        active, down_weight, after, final = closing_refs[:4]
        load_active = moves.load(closing_ins[0], active)
        load_after_two = moves.load(closing_ins[1], after)
        columns = pl.ds(0, down_weight.shape[1])
        load_down = load_weight(net, moves, closing_ins[2:], columns, down_weight)
    net.barrier([net.core, net.far, net.half])
    arriving = {
        slot: net.copy(far_hbm.at[slot], landed.at[slot], net.half) for slot in (3, 2, 1, 0)
    }
    load_queries.wait()
    together[:, :, pair_cols:used_cols] = grad_queries[...]
    together[:, :, used_cols:] = jnp.zeros((4, rows, all_cols - used_cols), BF)
    load_own.wait()
    loading.wait()

    def join(slot):
        arriving[slot].wait_recv()
        pair = grad_own[slot].astype(F32) + landed[slot].astype(F32)
        together[slot, :, :pair_cols] = pair.astype(BF)

    def back(slots, chunk):
        return dot(flat(together[slots, chunk, :]), weight[...], NT)

    if closing:

        def down(slots, chunk):
            return dot(flat(active[slots, chunk, :]), down_weight[...], NT)

        load_active.wait()
        load_down.wait()
        last = Scatter(net, closing_refs[4:])
        for key, chunk in enumerate(chunks):
            last.far_part(key, chunk, down(far, chunk))
        for key, chunk in enumerate(chunks):
            last.far_send(key, chunk)
        last.near_part(down(near, whole))
        last.near_done()
    scatter = Scatter(net, scatter_refs)
    join(3)
    join(2)
    for key, chunk in enumerate(chunks):
        scatter.far_part(key, chunk, back(far, chunk))
    for key, chunk in enumerate(chunks):
        scatter.far_send(key, chunk)
    join(1)
    join(0)
    scatter.near_part(back(near, whole))
    load_normed.wait()
    load_out.wait()
    weight_grad(normed, together, grad_weight, grad_out)
    moves.store(grad_weight, weight_out)
    column = jnp.zeros((1, all_cols), F32)
    for slot in range(4):
        column += jnp.sum(together[slot].astype(F32), axis=0, keepdims=True)
    column_sums[...] = column
    scatter.near_done()
    sums[...] = jnp.zeros_like(sums)
    load_x.wait()
    load_after.wait()
    for key, chunk in enumerate(chunks):
        grad, gain_sum, shift_sum = norm_back(
            x[chunk, :], vec[layer, 0:1], scatter.result(key, chunk)
        )
        gradient[chunk, :] = grad_after[chunk, :] + grad
        sums[0:1] += gain_sum
        sums[1:2] += shift_sum
    moves.store(gradient, gradient_out)
    if closing:
        load_after_two.wait()
        for key, chunk in enumerate(chunks):
            final[chunk, :] = last.result(key, chunk) + after[chunk, :] + vec[layer, 5:6]
        moves.store(final, outs[-1])
    net.finish()
    moves.finish()


def project_back(
    layer, grad_after, x, vec, mixed, normed, grad_queries, grad_own, grad_far, grad_out, all_cols,
    closing=(),
):
    rows, width = x.shape
    outputs = [
        ((rows, width), F32, False),
        ((8, width), F32, True),
        ((1, all_cols), F32, True),
        ((width, width), BF, False),
    ]
    shapes = [
        ((rows, width), F32),
        ((rows, width), F32),
        ((width, all_cols), BF),
        (normed.shape, BF),
        (grad_queries.shape, BF),
        (grad_own.shape, BF),
        (grad_out.shape, BF),
        (grad_far.shape, BF),
        ((4, rows, all_cols), BF),
        ((rows, width), F32),
        ((width, width), BF),
    ]
    scratch = [pltpu.VMEM(shape, dtype) for shape, dtype in shapes] + scatter_scratch(rows, width)
    copies, moves = 12, 9 + weight_loads(mixed)
    if closing:
        active, after, *down = closing
        outputs.append(((rows, width), F32, False))
        shapes = [
            (active.shape, BF), ((width, active.shape[2]), BF), ((rows, width), F32), ((rows, width), F32),
        ]
        scratch += [pltpu.VMEM(shape, dtype) for shape, dtype in shapes] + scatter_scratch(rows, width)
        copies, moves = 18, moves + 3 + weight_loads(down)
    inputs = [
        (grad_after, False), (x, False), (vec, True), (normed, False), (grad_queries, False),
        (grad_own, False), (grad_far, False), (grad_out, False),
    ] + spaced([*mixed, *closing])
    kernel = functools.partial(
        project_back_kernel, layer=layer, parts=len(mixed), closing=len(closing)
    )
    return run(kernel, "project_back", 42, inputs, outputs, scratch, 8 * layer + 3, copies, moves)


def entry_kernel(*refs):
    ins, outs, scratch = split_refs(refs, 12, 7)
    tokens, cotangent, value_bias, query_bias, up_bias, shard = ins[:6]
    x, gradient, grad_rows, vec, bias, hidden_bias, weights = outs
    vectors, token_land, cotangent_land, vector_land, send_sems, recv_sems, move_sems = scratch
    net, moves = Net(send_sems, recv_sems), Moves(move_sems)
    rows, cols = x.shape[0], tokens.shape[0]
    layers = vec.shape[0]
    others = [net.core, net.far, net.far_core]
    vectors[...] = jnp.zeros_like(vectors)
    for index, one in enumerate(ins[6:]):
        for layer in range(layers):
            vectors[layer * 8 + index : layer * 8 + index + 1] = one[layer : layer + 1]
    net.line(weights.shape[0] // 2)
    net.barrier(others + [net.half], True)
    gathering = GatherJob(net, moves, shard, weights)

    def block(hid):
        return pl.ds(pl.multiple_of(hid * rows, rows), rows)

    moved = [
        net.copy(tokens.at[:, block(device[1])], token_land.at[net.hid], device)
        for device in reversed(others)
    ]
    moved += [net.copy(vectors, vector_land.at[net.hid], device) for device in others]
    sent = []
    for chunk in chunks_of(4 * rows, 2):
        source, own = cotangent.at[:, chunk], cotangent_land.at[net.hid, :, chunk]
        moved.append(net.copy(source, own, net.core))
        sent.append((net.copy(source, own, net.far), cotangent_land.at[net.far[1], :, chunk]))
    token_land[net.hid] = tokens[:, block(net.hid)]
    cotangent_land[net.hid] = cotangent[...]
    vector_land[net.hid] = vectors[...]
    bias[...] = jnp.zeros_like(bias)
    bias[:, cols : 2 * cols] = value_bias[...]
    bias[:, 2 * cols : 3 * cols] = query_bias[...]
    hidden_bias[...] = jnp.zeros_like(hidden_bias)
    hidden_bias[:, : up_bias.shape[1]] = up_bias[...]
    gathering.forward(0, 3)
    for point, (one, landed) in enumerate(sent):
        one.wait_recv()
        moved.append(net.copy(landed, landed, net.core))
        gathering.forward(point + 1, 3)
    for one in moved:
        one.wait_recv()
    for place in range(4):
        columns = slice(place * cols, (place + 1) * cols)
        for layer in range(layers):
            vec[layer, :, columns] = vector_land[place, layer * 8 : layer * 8 + 8]
    x[...] = flat(token_land[...]).astype(F32).T
    for slot, device in enumerate([(net.tok, net.hid)] + others):
        whole = flat(cotangent_land[:, :, block(device[1])])
        grad_rows[slot] = whole.astype(F32).T.astype(BF)
    gradient[...] = grad_rows[0].astype(F32)
    gathering.finish()
    net.finish()
    moves.finish()


def entry(tokens, cotangent, value_bias, query_bias, up_bias, shard, vectors, count, used_cols):
    cols, rows = tokens.shape[0], tokens.shape[1] // 4
    layers, feed = up_bias.shape
    inputs = [
        (tokens, True), (cotangent, True), (value_bias, True), (query_bias, True), (up_bias, True),
        (shard, False),
    ] + [(one, True) for one in vectors]
    outputs = [
        ((rows, 4 * cols), F32, True),
        ((rows, 4 * cols), F32, True),
        ((4, rows, 4 * cols), BF, True),
        ((layers, 8, 4 * cols), F32, True),
        ((layers, used_cols), F32, True),
        ((layers, feed + -feed % LANES), F32, True),
        ((count,) + shard.shape, BF, False),
    ]
    scratch = [
        pltpu.VMEM((layers * 8, cols), F32),
        pltpu.VMEM((4, cols, rows), BF),
        pltpu.VMEM((4,) + cotangent.shape, BF),
        pltpu.VMEM((4, layers * 8, cols), F32),
    ]
    return run(entry_kernel, "entry", 50, inputs, outputs, scratch, 4, 12 + job_copies(count), 1)


def finish_kernel(*refs, layers):
    ins, outs, scratch = split_refs(refs, 3 + 4 * layers, 12)
    final_rows, gradient_rows, grads = ins[:3]
    layer_sums = [ins[3 + 4 * layer : 7 + 4 * layer] for layer in range(layers)]
    final_out, gradient_out, total = outs[:3]
    wide_outs, query_out, value_out, hidden_out = outs[3:9], outs[9], outs[10], outs[11]
    final, gradient, wide, sums, hidden_sums = scratch[:5]
    final_land, gradient_land, wide_land, across_land, along_land = scratch[5:10]
    across_hidden, along_hidden = scratch[10:12]
    job_refs = scratch[12:16]
    send_sems, recv_sems, move_sems = scratch[16:]
    net, moves = Net(send_sems, recv_sems), Moves(move_sems)
    count = grads.shape[0] // 2
    others = [net.core, net.far, net.far_core]
    net.line(count)
    net.barrier(others + [net.half], True)
    scattering = ScatterParts(net, moves, grads, job_refs)
    cols, rows = wide.shape[2], final_rows.shape[0]
    for layer, (one, two, _, _) in enumerate(layer_sums):
        both = one[...] + two[...]
        for place in range(4):
            columns = slice(place * cols, (place + 1) * cols)
            wide[place, layer * 8 : layer * 8 + 8] = both[:, columns]
    summed = [net.copy(wide.at[device[1]], wide_land.at[net.hid], device) for device in others]
    for target, source in ((final, final_rows), (gradient, gradient_rows)):
        target[...] = source[...].T.astype(BF).reshape(target.shape)
    moved = []
    for source, target in ((final, final_land), (gradient, gradient_land)):
        for device in reversed(others):
            moved.append(net.copy(source.at[device[1]], target.at[net.hid], device))
        target[net.hid] = source[net.hid]
    wide_land[net.hid] = wide[net.hid]
    last = count - 1
    pairs = ((sums, across_land, along_land), (hidden_sums, across_hidden, along_hidden))
    bases = [(net.take(count), net.take(count)) for _ in pairs]

    def send_sums():
        for one in summed:
            one.wait_recv()
        top = wide.shape[1]
        sums[:top] = wide_land[0] + wide_land[1] + wide_land[2] + wide_land[3]
        sums[top:] = jnp.zeros((sums.shape[0] - top, cols), F32)
        hidden_sums[...] = jnp.zeros_like(hidden_sums)
        for layer, (_, _, column_sums, hidden) in enumerate(layer_sums):
            for place in range(3):
                row = top + layer * 3 + place
                sums[row : row + 1] = column_sums[:, place * cols : (place + 1) * cols]
            hidden_sums[layer : layer + 1] = hidden[...]
        return [net.copy(value, across, net.half) for value, across, _ in pairs]

    def spread_sums(swaps):
        for one in swaps:
            one.wait()
        for (value, across, along), base in zip(pairs, bases):
            value[...] += across[...]
            own = along.at[net.high]
            along[net.high] = value[...]
            pl.when(net.has_after)(net.make(base[0], own, own, net.after).start)
            pl.when(net.has_before)(net.make(base[1], own, own, net.before).start)

    def pass_sums(step):
        for (_, _, along), base in zip(pairs, bases):
            below, above = along.at[net.high - step], along.at[net.high + step]

            def pass_on(index, block, device, has):
                net.make(index, block, block, device).wait_recv()
                if step < last:
                    pl.when(has)(net.make(index + 1, block, block, device).start)

            pl.when(net.high >= step)(
                functools.partial(pass_on, base[0] + step - 1, below, net.after, net.has_after)
            )
            pl.when(net.high + step < count)(
                functools.partial(pass_on, base[1] + step - 1, above, net.before, net.has_before)
            )

    swaps = send_sums()
    scattering.forward(0, 3)
    scattering.forward(1, 3)
    spread_sums(swaps)
    scattering.forward(2, 3)
    for step in range(1, count):
        pass_sums(step)
    for (value, _, along), base in zip(pairs, bases):
        total_value = along[0]
        for place in range(1, count):
            total_value += along[place]
        value[...] = total_value
        own = along.at[net.high]
        for step in range(count - 1):
            up = jnp.logical_and(net.has_after, net.high >= step)
            down = jnp.logical_and(net.has_before, net.high + step < count)
            pl.when(up)(net.make(base[0] + step, own, own, net.after).wait_send)
            pl.when(down)(net.make(base[1] + step, own, own, net.before).wait_send)
    for one in moved:
        one.wait_recv()
    for source, target in ((final_land, final_out), (gradient_land, gradient_out)):
        for place in range(4):
            target[:, place * rows : (place + 1) * rows] = source[place].astype(F32)
    for layer in range(layers):
        one = slice(layer, layer + 1)
        for index, out in enumerate(wide_outs):
            out[one, :] = sums[layer * 8 + index : layer * 8 + index + 1]
        row = layers * 8 + layer * 3
        value_out[one, :] = sums[row + 1 : row + 2]
        query_out[one, :] = sums[row + 2 : row + 3]
        hidden_out[one, :] = hidden_sums[one, : hidden_out.shape[1]]
    scattering.finish(total)
    net.finish(swaps)


def finish(final, gradient, grads, layer_sums, head_cols, feed):
    count, layers = grads.shape[0] // 2, len(layer_sums)
    rows = final.shape[0]
    sums = (layers * 11 + -layers * 11 % 8, head_cols)
    hidden = (layers + -layers % 8, layer_sums[0][3].shape[1])
    vector = ((layers, head_cols), F32, True)
    outputs = [
        ((head_cols, 4 * rows), F32, True),
        ((head_cols, 4 * rows), F32, True),
        (grads.shape[1:], F32, True),
    ] + [vector] * 8
    outputs.append(((layers, feed), F32, True))
    blocks, wide = (4, head_cols, rows), (4, layers * 8, head_cols)
    scratch = [
        pltpu.VMEM(blocks, BF),
        pltpu.VMEM(blocks, BF),
        pltpu.VMEM(wide, F32),
        pltpu.VMEM(sums, F32),
        pltpu.VMEM(hidden, F32),
        pltpu.VMEM(blocks, BF),
        pltpu.VMEM(blocks, BF),
        pltpu.VMEM(wide, F32),
        pltpu.VMEM(sums, F32),
        pltpu.VMEM((count,) + sums, F32),
        pltpu.VMEM(hidden, F32),
        pltpu.VMEM((count,) + hidden, F32),
    ] + part_scratch(*grads.shape)
    inputs = [(final, True), (gradient, True), (grads, False)]
    inputs += [(one, True) for four in layer_sums for one in four]
    kernel = functools.partial(finish_kernel, layers=layers)
    return run(kernel, "finish", 40, inputs, outputs, scratch, 5, 12 + 7 * count, 1 + count)


def key_ranges(own_ids, row_ids, rows):
    blocks = own_ids.reshape(-1, rows)
    position = jnp.arange(row_ids.shape[0], dtype=jnp.int32)
    low = jnp.min(jnp.where(row_ids == blocks[:, :1], position, row_ids.shape[0]), axis=1)
    high = jnp.max(jnp.where(row_ids == blocks[:, -1:], position, -1), axis=1)
    return jnp.stack([low // KEYS, high // KEYS + 1], axis=1).reshape(-1)


def body(
    tokens, picture, cotangent, first_gain, first_shift, query_weight, query_bias, key_weight,
    value_weight, value_bias, output_weight, output_bias, second_gain, second_shift, up_weight,
    up_bias, down_weight, down_bias,
):
    token_count = tokens.shape[0]
    rows = token_count // 4
    layers = query_weight.shape[0]
    head_cols = query_bias.shape[1]
    feed = up_bias.shape[1]
    feed_pad = -feed % LANES
    feed_cols = feed + feed_pad
    hid = lax.axis_index("hid")
    tok = lax.axis_index("tok")
    count = lax.axis_size("tok")
    shard = query_weight.shape[1]
    shard_pad = -shard % 16
    width = count * shard
    lead = 3 * head_cols % LANES
    used_cols = 3 * head_cols + -3 * head_cols % LANES

    own_ids = lax.dynamic_slice_in_dim(picture, tok * token_count, token_count)
    row_ids = lax.dynamic_slice_in_dim(picture, (tok // 2) * 2 * token_count, 2 * token_count)
    place = jnp.stack([hid, tok % 2]).astype(jnp.int32)
    meta = jnp.concatenate([place, key_ranges(own_ids, row_ids, rows)])

    def side_by_side(*parts):
        return jnp.concatenate(parts, axis=1)

    def padded(part):
        return jnp.pad(part, ((0, 0), (0, feed_pad)))

    def shards(part):
        return jnp.pad(part, ((0, shard_pad), (0, 0)))

    def joined(gathered):
        return gathered[:, :shard].reshape(width, gathered.shape[2])

    def separate(grads):
        grads = grads.reshape(count, shard, grads.shape[1])
        return jnp.pad(grads, ((0, 0), (0, shard_pad), (0, 0)))

    mixed_parts = [
        shards(
            side_by_side(
                key_weight[layer], value_weight[layer], query_weight[layer], output_weight[layer].T
            )
        )
        for layer in range(layers)
    ]
    vectors = (first_gain, first_shift, output_bias, second_gain, second_shift, down_bias)
    x, gradient, grad_rows, vectors, bias, up_bias, mixed = entry(
        tokens.T, cotangent.T, value_bias, query_bias, up_bias, mixed_parts[0], vectors, count, used_cols
    )

    halves = [(place, place ^ 1) for place in range(count)]
    lines = [[place * 2 + low for place in range(count // 2)] for low in range(2)]

    def swap(part):
        return lax.ppermute(part, "tok", halves)

    def both_halves(own, other):
        first = tok % 2 == 0
        return jnp.stack([jnp.where(first, own, other), jnp.where(first, other, own)])

    def along(part):
        return lax.all_gather(part, "tok", axis=0, tiled=True, axis_index_groups=lines)

    def along_first(part):
        own = along(part)
        other = swap(own)
        parts = [rows_of.reshape(count // 2, shard, part.shape[1]) for rows_of in (own, other)]
        if shard % 16 == 0:
            return parts
        return [both_halves(*parts).transpose(1, 0, 2, 3).reshape(width, part.shape[1])]

    def hold(*values):
        return lax.optimization_barrier(values)

    def pair_rows(part, other):
        return both_halves(part, other).reshape(2 * shard, part.shape[1])

    def up_part(layer):
        return padded(up_weight[layer])

    def down_part(layer):
        return padded(down_weight[layer].T)

    ups, weights = [along_first(up_part(0))], [[joined(mixed)]]
    early = down_part(0)
    early, early_other, x = hold(early, swap(early), x)
    downs = [[along(pair_rows(early, early_other))]]
    for layer in range(1, layers):
        weights.append(along_first(mixed_parts[layer][:shard]))
        coming = up_part(layer)
        ups.append([along(pair_rows(coming, swap(coming)))])
    saved = []
    for layer in range(layers):
        mixed, up = weights[layer], ups[layer]
        more = layer + 1 < layers
        normed, queries, own_pairs, far_pairs = project(layer, x, vectors, bias, mixed, head_cols)
        if layer > 0:
            queries, coming, coming_other = hold(queries, coming, coming_other)
            downs.append([along(pair_rows(coming, coming_other))])
        mixture, logsum = attend(
            meta, queries, own_pairs, far_pairs, own_ids[:, None], row_ids[None, :], lead
        )
        if more:
            coming, mixture = hold(down_part(layer + 1), mixture)
            coming_other = swap(coming)
        after, normed_two, active, slope, *x_next = mlp(
            layer, mixture, x, vectors, up_bias, mixed, up, downs[layer], not more
        )
        saved.append(
            (x, normed, queries, own_pairs, far_pairs, mixture, logsum, after, normed_two, active, slope)
        )
        x = x_next[0] if x_next else None

    def by_halves(part):
        own = lax.dynamic_index_in_dim(part, tok % 2, 1, keepdims=False)
        other = lax.dynamic_index_in_dim(part, 1 - tok % 2, 1, keepdims=False)
        return own, other

    def sum_along(part):
        return lax.psum_scatter(
            part, "tok", scatter_dimension=0, tiled=True, axis_index_groups=lines
        )

    def halves_of(parts):
        if len(parts) == 1:
            part = parts[0].reshape(-1, 2, shard, parts[0].shape[1])
            parts = by_halves(part)
        return parts[0], swap(parts[1])

    def added(own, other):
        return (own.astype(F32) + other.astype(F32)).astype(BF)

    def in_rows(part):
        return part.reshape(-1, part.shape[-1])

    split = shard if shard % 16 == 0 else 0
    mixed_grads, up_grads, down_grads = [None] * layers, [None] * layers, [None] * layers
    layer_sums = [None] * layers
    grads = final = None
    for layer in reversed(range(layers)):
        x, normed, queries, own_pairs, far_pairs, mixture, logsum, after, normed_two, active, slope = saved[layer]
        mixed, up, down = weights[layer], ups[layer], downs[layer]
        last = layer + 1
        if last < layers:
            gradient, down_grads[last] = hold(gradient, down_grads[last])
            down_own, down_other = halves_of([down_grads[last]])
        grad_after, grad_mixture, grad_down, grad_out, sums_two, hidden_sums, *grad_up = mlp_back(
            layer, gradient, after, vectors, mixed, up, down, mixture, normed_two, active, slope,
            () if last < layers else (grad_rows,), split,
        )
        if last < layers:
            down_other, up_grads[last], grad_mixture = hold(
                down_other, up_grads[last], grad_mixture
            )
            down_grads[last] = added(down_own, down_other)[0]
            grad_down, up_grads[last] = hold(grad_down, up_grads[last])
        down_grads[layer] = sum_along(grad_down)
        up_own, up_other = halves_of(grad_up)
        grad_queries, grad_own, grad_far = attend_back(
            meta, queries, own_pairs, far_pairs, own_ids[None, :], row_ids[:, None],
            grad_mixture, logsum,
        )
        up_other, grad_far = hold(up_other, grad_far)
        up_grad = added(up_own, up_other)
        if last < layers:
            grad_after, mixed_grads[last] = hold(grad_after, mixed_grads[last])
            mixed_own, mixed_other = halves_of([mixed_grads[last]])
        grad_after, up_grad = hold(grad_after, up_grad)
        up_grads[layer] = sum_along(in_rows(up_grad))
        gradient, sums_one, column_sums, grads, *closed = project_back(
            layer, grad_after, x, vectors, mixed, normed, grad_queries, grad_own, grad_far,
            grad_out, used_cols, () if last < layers else (active, after, *down),
        )
        final = closed[0] if closed else final
        if last < layers:
            mixed_other, gradient = hold(mixed_other, gradient)
            mixed_grads[last] = added(mixed_own, mixed_other)[0]
        if layer > 0:
            mixed_grads[layer] = sum_along(grads)
        layer_sums[layer] = (sums_one, sums_two, column_sums, hidden_sums)
    gradient, down_grads[0] = hold(gradient, down_grads[0])
    down_own, down_other = halves_of([down_grads[0]])
    final, gradient, mixed_grad, *small = finish(
        final, gradient, separate(grads), layer_sums, head_cols, feed
    )
    down_other, up_grads[0], final, gradient, mixed_grad, *small = hold(
        down_other, up_grads[0], final, gradient, mixed_grad, *small
    )
    mixed_grads[0] = mixed_grad[:shard]
    down_grads[0] = added(down_own, down_other)[0]
    first_gain, first_shift, output_bias, second_gain, second_shift, down_bias = small[:6]
    query_bias, value_bias, up_bias = small[6:]

    def mixed_columns(start):
        columns = slice(start * head_cols, (start + 1) * head_cols)
        return jnp.stack([part[:, columns].astype(F32) for part in mixed_grads])

    def hidden_columns(parts):
        return jnp.stack([part[:, :feed].astype(F32) for part in parts])

    return (
        final.T,
        gradient.T,
        first_gain,
        first_shift,
        mixed_columns(2),
        query_bias,
        mixed_columns(0),
        mixed_columns(1),
        value_bias,
        mixed_columns(3).transpose(0, 2, 1),
        output_bias,
        second_gain,
        second_shift,
        hidden_columns(up_grads),
        up_bias,
        hidden_columns(down_grads).transpose(0, 2, 1),
        down_bias,
    )


def solution(mesh):
    rows = P("tok", "hid")
    vector = P(None, "hid")
    inward = P(None, "tok", "hid")
    outward = P(None, "hid", "tok")
    in_specs = (
        rows, P(), rows, vector, vector, inward, vector, inward, inward, vector, outward, vector,
        vector, vector, inward, vector, outward, vector,
    )
    out_specs = (
        rows, rows, vector, vector, inward, vector, inward, inward, vector, outward, vector,
        vector, vector, inward, vector, outward, vector,
    )
    return jax.shard_map(body, mesh=mesh, in_specs=in_specs, out_specs=out_specs, check_vma=False)
```

```python
import functools

import jax
import jax.numpy as jnp
from jax import lax
from jax.experimental import pallas as pl
from jax.experimental.pallas import tpu as pltpu
from jax.sharding import PartitionSpec as P

HEAD_DIM = 72
LANES = 128
KEYS = 512
EPS = 1e-06
GELU = 0.7978845608028654
CUBE = 0.044715
MASKED = -1e30
LOG2E = 1.4426950408889634
LN2 = 0.6931471805599453
NN = (((1,), (0,)), ((), ()))
NT = (((1,), (1,)), ((), ()))
TN = (((0,), (0,)), ((), ()))
MESH = pl.DeviceIdType.MESH
BF = jnp.bfloat16
F32 = jnp.float32
VMEM_LIMIT = 60 * 1024 * 1024


def dot(left, right, dims=NN):
    return lax.dot_general(left, right, dims, preferred_element_type=F32)


def micros(duration):
    return pl.CostEstimate(flops=duration * 10**9, bytes_accessed=0, transcendentals=0)


def flat(value):
    return value.reshape(value.shape[0] * value.shape[1], value.shape[2])


class Net:
    def __init__(self, send_sems, recv_sems):
        tok, hid = lax.axis_index("tok"), lax.axis_index("hid")
        near = hid + 1 - 2 * lax.rem(hid, 2)
        self.tok, self.hid = tok, hid
        self.core = (tok, near)
        self.far = (tok, lax.rem(hid + 2, 4))
        self.far_core = (tok, lax.rem(near + 2, 4))
        self.half = (tok + 1 - 2 * lax.rem(tok, 2), hid)
        self.low, self.high = lax.rem(tok, 2), lax.div(tok, 2)
        self.send_sems, self.recv_sems = send_sems, recv_sems
        self.copies, self.count = [], 0

    def row(self, high):
        return (high * 2 + self.low, self.hid)

    def line(self, count):
        self.before, self.has_before = self.row(lax.max(self.high - 1, 0)), self.high > 0
        self.after = self.row(lax.min(self.high + 1, count - 1))
        self.has_after, self.last = self.high + 1 < count, count - 1

    def barrier(self, devices, line=False):
        sem = pltpu.get_barrier_semaphore()

        def signal(device):
            pl.semaphore_signal(sem, inc=1, device_id=device, device_id_type=MESH)

        for device in devices:
            signal(device)
        peers = len(devices)
        if line:
            pl.when(self.has_before)(lambda: signal(self.before))
            pl.when(self.has_after)(lambda: signal(self.after))
            peers = peers + lax.min(self.high, 1) + lax.min(self.last - self.high, 1)
        pl.semaphore_wait(sem, peers)

    def take(self, count):
        first = self.count
        self.count += count
        return first

    def make(self, index, source, target, device):
        return pltpu.make_async_remote_copy(
            src_ref=source,
            dst_ref=target,
            send_sem=self.send_sems.at[index],
            recv_sem=self.recv_sems.at[index],
            device_id=device,
            device_id_type=MESH,
        )

    def copy(self, source, target, device):
        made = self.make(self.take(1), source, target, device)
        self.copies.append(made)
        made.start()
        return made

    def finish(self, waited=()):
        done = [id(made) for made in waited]
        for made in self.copies:
            if id(made) not in done:
                made.wait_send()


class Moves:
    def __init__(self, sems):
        self.sems, self.count, self.stores = sems, 0, []

    def take(self, count):
        first = self.count
        self.count += count
        return first

    def make(self, index, source, target):
        return pltpu.make_async_copy(source, target, self.sems.at[index])

    def load(self, source, target):
        made = self.make(self.take(1), source, target)
        made.start()
        return made

    def store(self, source, target):
        self.stores.append(self.load(source, target))

    def finish(self):
        for made in self.stores:
            made.wait()


class Several:
    def __init__(self, copies):
        self.copies = copies

    def wait(self):
        for one in self.copies:
            one.wait()


def weight_loads(parts):
    return 1 if len(parts) == 1 else 2 * parts[0].shape[0]


def load_weight(net, moves, parts, columns, target):
    if len(parts) == 1:
        return moves.load(parts[0].at[:, columns], target)
    copies = []
    for part, low in zip(parts, (net.low, 1 - net.low)):
        shard = part.shape[1]
        for high in range(part.shape[0]):
            start = pl.multiple_of((high * 2 + low) * shard, 16)
            copies.append(moves.load(part.at[high, :, columns], target.at[pl.ds(start, shard)]))
    return Several(copies)


def store_halves(net, moves, grad, outs, shard):
    if not shard:
        moves.store(grad, outs[0])
        return
    for out, low in zip(outs, (net.low, 1 - net.low)):
        for place in range(out.shape[0]):
            start = pl.multiple_of((place * 2 + low) * shard, 16)
            moves.store(grad.at[pl.ds(start, shard)], out.at[place])


def half_outputs(rows, columns, shard):
    if not shard:
        return [((rows, columns), BF, False)]
    return [((rows // (2 * shard), shard, columns), BF, False)] * 2


def spaced(arrays):
    return [(array, False) for array in arrays]


def job_copies(count):
    return 2 * count + 1


class GatherJob:
    def __init__(self, net, moves, shard, weights):
        self.net, self.weights = net, weights
        self.count = weights.shape[0] // 2
        self.across = net.take(2 * self.count - 1)
        self.up, self.down = net.take(self.count), net.take(self.count)
        own = weights.at[net.tok]
        moves.store(shard, own)
        first = self.swap(0, shard, own)
        pl.when(net.has_after)(lambda: net.make(self.up, shard, own, net.after).start())
        pl.when(net.has_before)(lambda: net.make(self.down, shard, own, net.before).start())
        first.start()

    def swap(self, index, source, target):
        return self.net.make(self.across + index, source, target, self.net.half)

    def arrive(self, step, above):
        net = self.net
        place = net.high + step if above else net.high - step
        block = self.weights.at[place * 2 + net.low]
        base, onward = (self.down, net.before) if above else (self.up, net.after)
        net.make(base + step - 1, block, block, onward).wait_recv()
        if step + 1 < self.count:
            go_on = net.has_before if above else net.has_after
            pl.when(go_on)(lambda: net.make(base + step, block, block, onward).start())
        self.swap(2 * step - int(above), block, block).start()

    def forward(self, point, points):
        net = self.net
        for step in range(1, self.count):
            if (step - 1) * points // (self.count - 1) == point:
                pl.when(net.high - step >= 0)(functools.partial(self.arrive, step, False))
                pl.when(net.high + step < self.count)(functools.partial(self.arrive, step, True))

    def finish(self):
        net = self.net
        own = self.weights.at[net.tok]
        self.swap(0, own, own).wait()
        for step in range(1, self.count):
            below, above = net.high - step >= 0, net.high + step < self.count
            pl.when(below)(lambda step=step: self.swap(2 * step, own, own).wait())
            pl.when(above)(lambda step=step: self.swap(2 * step - 1, own, own).wait())
        for step in range(self.count - 1):
            for base, device, has, there in (
                (self.up, net.after, net.has_after, net.high - step >= 0),
                (self.down, net.before, net.has_before, net.high + step < self.count),
            ):
                sent = net.make(base + step, own, own, device)
                pl.when(jnp.logical_and(has, there))(sent.wait_send)


class Line:
    def __init__(self, net, count, value, passing, arrived):
        self.net, self.count, self.value = net, count, value
        self.passing, self.arrived = passing, arrived
        self.up, self.down = net.take(count), net.take(count)

    def upward(self, place):
        source, target = self.passing.at[place], self.arrived.at[place + 1]
        return self.net.make(self.up + place, source, target, self.net.after)

    def downward(self, place):
        source, target = self.passing.at[place], self.arrived.at[place]
        return self.net.make(self.down + place, source, target, self.net.before)

    def send(self, place, above):
        net = self.net
        value = self.value(place)
        self.passing[place] = value.astype(BF)
        move = self.upward(place) if above else self.downward(place)

        def add():
            move.wait_recv()
            landed = self.arrived[place + 1 if above else place]
            self.passing[place] = (value + landed.astype(F32)).astype(BF)

        pl.when(net.has_before if above else net.has_after)(add)
        move.start()

    def forward(self, point, points):
        high, last = self.net.high, self.count - 1
        for slot in range(last):
            if slot * points // last == point:
                pl.when(high <= slot)(functools.partial(self.send, last - slot + high, True))
                pl.when(last - high <= slot)(functools.partial(self.send, slot - last + high, False))

    def finish(self, total):
        net = self.net
        total[...] = self.value(net.high)

        def add(move, place):
            move.wait_recv()
            total[...] += self.arrived[place].astype(F32)

        pl.when(net.has_before)(lambda: add(self.upward(net.high), net.high + 1))
        pl.when(net.has_after)(lambda: add(self.downward(net.high), net.high))

    def drain(self):
        for place in range(self.count):
            pl.when(self.net.high < place)(self.upward(place).wait_send)
            pl.when(self.net.high > place)(self.downward(place).wait_send)


def part_scratch(count, shard, width):
    half = count // 2
    return [pltpu.VMEM((half, shard, width), BF)] * 3 + [pltpu.VMEM((half + 1, shard, width), BF)]


class ScatterParts:
    def __init__(self, net, moves, grads, scratch):
        self.net, self.moves = net, moves
        self.own, self.landed, passing, arrived = scratch
        self.count = count = grads.shape[0] // 2
        self.across, self.loads = net.take(count), moves.take(count)
        high, last = net.high, count - 1

        def start(place):
            self.swap(place, grads.at[place * 2 + 1 - net.low]).start()

        for slot in range(last):
            pl.when(high <= slot)(functools.partial(start, last - slot + high))
            pl.when(last - high <= slot)(functools.partial(start, slot - last + high))
        start(high)
        for place in range(count):
            source = grads.at[place * 2 + net.low]
            moves.make(self.loads + place, source, self.own.at[place]).start()
        self.line = Line(net, count, self.pair, passing, arrived)
        self.forward = self.line.forward

    def swap(self, place, source=None):
        target = self.landed.at[place]
        source = target if source is None else source
        return self.net.make(self.across + place, source, target, self.net.half)

    def pair(self, place):
        own = self.own.at[place]
        self.moves.make(self.loads + place, own, own).wait()
        self.swap(place).wait_recv()
        return self.own[place].astype(F32) + self.landed[place].astype(F32)

    def finish(self, total):
        self.line.finish(total)
        self.line.drain()
        for place in range(self.count):
            self.swap(place).wait_send()


class Across:
    def __init__(self, net, moves, part, scratch):
        self.net, self.part = net, part
        self.own, self.landed = scratch
        self.load = moves.load(part.at[net.low], self.own)

    def start(self):
        self.copy = self.net.copy(self.part.at[1 - self.net.low], self.landed, self.net.half)

    def finish(self, total):
        self.load.wait()
        self.copy.wait_recv()
        total[...] = self.own[...].astype(F32) + self.landed[...].astype(F32)


def across_scratch(part):
    return [pltpu.VMEM(part.shape[1:], BF)] * 2


def run(kernel, name, duration, inputs, outputs, scratch, identity, copies, moves):
    def space(near):
        return pl.BlockSpec(memory_space=pltpu.VMEM if near else pl.ANY)

    return pl.pallas_call(
        kernel,
        name=name,
        cost_estimate=micros(duration),
        out_shape=[jax.ShapeDtypeStruct(shape, dtype) for shape, dtype, _ in outputs],
        in_specs=[space(near) for _, near in inputs],
        out_specs=[space(near) for _, _, near in outputs],
        scratch_shapes=list(scratch)
        + [
            pltpu.SemaphoreType.DMA((copies,)),
            pltpu.SemaphoreType.DMA((copies,)),
            pltpu.SemaphoreType.DMA((moves,)),
        ],
        compiler_params=pltpu.CompilerParams(
            collective_id=identity, has_side_effects=True, vmem_limit_bytes=VMEM_LIMIT
        ),
    )(*[array for array, _ in inputs])


def split_refs(refs, inputs, outputs):
    return refs[:inputs], refs[inputs : inputs + outputs], refs[inputs + outputs :]


def norm_parts(rows):
    centred = rows - jnp.mean(rows, axis=1, keepdims=True)
    inverse = lax.rsqrt(jnp.mean(centred * centred, axis=1, keepdims=True) + EPS)
    return centred * inverse, inverse


def norm_back(rows, gain, grad):
    scaled, inverse = norm_parts(rows)
    inner = grad * gain
    first = jnp.mean(inner, axis=1, keepdims=True)
    second = jnp.mean(inner * scaled, axis=1, keepdims=True)
    return (
        inverse * (inner - first - scaled * second),
        jnp.sum(grad * scaled, axis=0, keepdims=True),
        jnp.sum(grad, axis=0, keepdims=True),
    )


def gather_send(net, full, chunk):
    near = net.copy(full.at[0, chunk], full.at[1, chunk], net.core)
    far = net.copy(full.at[0, chunk], full.at[2, chunk], net.far)
    return near, far


def gather_pass(net, full, chunk, far):
    far.wait_recv()
    return net.copy(full.at[2, chunk], full.at[3, chunk], net.core)


def scatter_scratch(rows, width):
    return [
        pltpu.VMEM((rows, width), F32),
        pltpu.VMEM((rows, width), F32),
    ] + [pltpu.VMEM((rows, width), BF)] * 6


class Scatter:
    def __init__(self, net, scratch):
        self.net = net
        self.hold, self.total, self.cs0, self.cr0, self.ys, self.yr, self.cs1, self.cr1 = scratch
        self.first, self.second = {}, {}

    def far_part(self, key, chunk, partial):
        rows = partial.shape[0] // 2
        self.hold[chunk] = partial[:rows]
        self.cs0[chunk] = partial[rows:].astype(BF)
        self.first[key] = self.net.copy(self.cs0.at[chunk], self.cr0.at[chunk], self.net.core)

    def far_send(self, key, chunk):
        self.first[key].wait_recv()
        self.ys[chunk] = (self.hold[chunk] + self.cr0[chunk].astype(F32)).astype(BF)
        self.second[key] = self.net.copy(self.ys.at[chunk], self.yr.at[chunk], self.net.far)

    def near_part(self, partial):
        rows = partial.shape[0] // 2
        self.total[...] = partial[:rows]
        self.cs1[...] = partial[rows:].astype(BF)
        self.near = self.net.copy(self.cs1, self.cr1, self.net.core)

    def near_done(self):
        self.near.wait_recv()
        self.total[...] += self.cr1[...].astype(F32)

    def result(self, key, chunk):
        self.second[key].wait_recv()
        return self.total[chunk] + self.yr[chunk].astype(F32)


def blocked(value):
    return value.astype(BF).reshape(2, value.shape[0] // 2, value.shape[1])


def chunks_of(rows, count):
    step = rows // count
    return [pl.ds(index * step, step) for index in range(count)]


def weight_grad(left, right, out, extra=None):
    width = left.shape[2]
    tile = 384

    def one(index, carry):
        columns = pl.ds(pl.multiple_of(index * tile, tile), tile)
        result = dot(flat(left[:, :, columns]), flat(right[...]), TN)
        if extra is None:
            out[columns, :] = result.astype(out.dtype)
        else:
            start = out.shape[1] - extra.shape[1]
            join = result.shape[1] - start
            added = extra[columns, :]
            out[columns, :start] = result[:, :start].astype(out.dtype)
            both = result[:, start:] + added[:, :join].astype(F32)
            out[columns, start : start + join] = both.astype(out.dtype)
            out[columns, start + join :] = added[:, join:]
        return carry

    lax.fori_loop(0, width // tile, one, 0)


def packed_shape(rows, columns):
    return (2, rows // 2 * columns // LANES, LANES)


def pack_half(tiles, target):
    rows = tiles[0].shape[0]
    for index, tile in enumerate(tiles[:-1]):
        target[index * rows : (index + 1) * rows, :] = tile.astype(BF)
    tail = tiles[-1][:, : LANES // 2]
    both = jnp.concatenate([tail[: rows // 2], tail[rows // 2 :]], axis=1)
    target[(len(tiles) - 1) * rows :, :] = both.astype(BF)


def unpack_half(packed, rows):
    full = packed.shape[0] // rows
    tiles = [packed[index * rows : (index + 1) * rows] for index in range(full)]
    tail = packed[full * rows :]
    return tiles + [jnp.concatenate([tail[:, : LANES // 2], tail[:, LANES // 2 :]], axis=0)]


def project_kernel(*refs, layer, head_cols, factor, parts):
    (x_hbm, vec, bias, *mixed_hbm), outs, scratch = split_refs(refs, 3 + parts, 4)
    normed_out, queries_out, pairs_out, far_out = outs
    x, weight, normed, queries, pairs, far_pairs, send_sems, recv_sems, move_sems = scratch
    net, moves = Net(send_sems, recv_sems), Moves(move_sems)
    rows = x.shape[0]
    pair_cols = 2 * head_cols
    chunks = chunks_of(rows, 2)
    x_load = moves.load(x_hbm, x)
    columns = pl.ds(0, weight.shape[1])
    weight_load = load_weight(net, moves, mixed_hbm, columns, weight)
    net.barrier([net.core, net.far, net.half])
    x_load.wait()
    sent = []
    for chunk in chunks:
        scaled, _ = norm_parts(x[chunk, :])
        normed[0, chunk, :] = (scaled * vec[layer, 0:1] + vec[layer, 1:2]).astype(BF)
        sent.append(gather_send(net, normed, chunk))
    arrived = []
    weight_load.wait()

    def project(slots, chunk):
        result = dot(flat(normed[slots, chunk, :]), weight[...]) + bias[layer : layer + 1]
        shape = (slots.size, chunk.size, -1)
        halves = range(len(chunks)) if chunk.size == rows else [chunk.start // chunk.size]
        step = rows // len(chunks)
        for index in range(slots.size):
            for place, half in enumerate(halves):
                start = (index * len(halves) + place) * step
                part = result[start : start + step]
                tiles = [part[:, lane : lane + LANES] for lane in range(0, pair_cols, LANES)]
                pack_half(tiles, pairs.at[slots.start + index, half])
        halves = pl.ds(halves[0], len(halves))
        own = result[:, pair_cols : pair_cols + head_cols] * factor
        queries[slots, chunk, :] = own.astype(BF).reshape(shape)
        source, target = pairs.at[slots, halves], far_pairs.at[slots, halves]
        arrived.append(net.copy(source, target, net.half))

    whole = pl.ds(0, rows)
    project(pl.ds(0, 1), whole)
    for near, _ in sent:
        near.wait_recv()
    project(pl.ds(1, 1), whole)
    for chunk, (_, far) in zip(chunks, sent):
        gather_pass(net, normed, chunk, far).wait_recv()
        project(pl.ds(2, 2), chunk)
    moves.store(normed, normed_out)
    moves.store(queries, queries_out)
    moves.store(pairs, pairs_out)
    for one in arrived:
        one.wait_recv()
    moves.store(far_pairs, far_out)
    net.finish()
    moves.finish()


def project(layer, x, vec, bias, mixed, head_cols):
    rows, width = x.shape
    used = bias.shape[1]
    outputs = [
        ((4, rows, width), BF, False),
        ((4, rows, head_cols), BF, False),
        ((4,) + packed_shape(rows, 2 * head_cols), BF, False),
        ((4,) + packed_shape(rows, 2 * head_cols), BF, False),
    ]
    scratch = [pltpu.VMEM((rows, width), F32), pltpu.VMEM((width, used), BF)]
    scratch += [pltpu.VMEM(shape, dtype) for shape, dtype, _ in outputs]
    kernel = functools.partial(
        project_kernel,
        layer=layer,
        head_cols=head_cols,
        factor=HEAD_DIM ** (-0.5) * LOG2E,
        parts=len(mixed),
    )
    inputs = [(x, False), (vec, True), (bias, True)] + spaced(mixed)
    return run(kernel, "project", 40, inputs, outputs, scratch, 8 * layer, 12, 6 + weight_loads(mixed))


def pair_windows(width, lead=0):
    windows = []
    for first in range(lead, width - HEAD_DIM, 2 * HEAD_DIM):
        start = first // LANES * LANES
        size = min(2 * LANES, width - start)
        row = lax.broadcasted_iota(jnp.int32, (size, 2 * LANES), 0) + (start - first)
        lane = lax.broadcasted_iota(jnp.int32, (size, 2 * LANES), 1)
        second = lane >= LANES
        lane = jnp.where(second, lane - LANES, lane)
        match = row == jnp.where(second, lane + HEAD_DIM, lane)
        windows.append((start, size, jnp.logical_and(match, lane < HEAD_DIM).astype(BF)))
    return windows


def spread_heads(value, windows):
    heads = []
    for start, size, pick in windows:
        both = dot(value[:, start : start + size], pick).astype(BF)
        heads += [both[:, :LANES], both[:, LANES:]]
    return heads


def join_heads(heads, windows, width):
    tiles = [None] * (-(-width // LANES))
    for index, (start, size, pick) in enumerate(windows):
        both = jnp.concatenate(heads[2 * index : 2 * index + 2], axis=1)
        part = dot(both, pick, NT)
        for lane in range(0, size, LANES):
            tile, piece = (start + lane) // LANES, part[:, lane : lane + LANES]
            tiles[tile] = piece if tiles[tile] is None else tiles[tile] + piece
    return jnp.concatenate(tiles, axis=1)


def as_rows(columns):
    rows = columns[0].shape[0]
    lane = lax.broadcasted_iota(jnp.int32, (rows, LANES), 1)
    together = jnp.zeros((rows, LANES), F32)
    for head, column in enumerate(columns):
        together = jnp.where(lane == head, column, together)
    return together.T[:8]


def load_pairs(meta, own_pairs, far_pairs, key_scratch, value_scratch, heads):
    rows = 2 * (own_pairs.shape[2] * LANES // (2 * heads * HEAD_DIM))
    hid, half = meta[0], meta[1]
    windows = pair_windows(2 * heads * HEAD_DIM)
    for which, source in ((0, own_pairs), (1, far_pairs)):
        for slot in range(4):
            place = jnp.bitwise_xor(half, which) * 4 + jnp.bitwise_xor(hid, slot)
            start = pl.ds(pl.multiple_of(place * rows, rows), rows)
            halves = [unpack_half(source[slot, index], rows // 2) for index in range(2)]
            tiles = [jnp.concatenate(both, axis=0) for both in zip(*halves)]
            spread = spread_heads(jnp.concatenate(tiles, axis=1), windows)
            for head in range(heads):
                key_scratch[head, start, :] = spread[head]
                value_scratch[head, start, :] = spread[heads + head]


def attend_kernel(
    meta, queries, own_pairs, far_pairs, query_ids, key_ids, mixture, logsum,
    key_scratch, value_scratch, score_scratch, high_scratch, total_scratch, sum_scratch, query_scratch,
    *, heads
):
    rows = queries.shape[1]
    head_cols = heads * HEAD_DIM
    load_pairs(meta, own_pairs, far_pairs, key_scratch, value_scratch, heads)
    query_windows = pair_windows(head_cols)
    mixed_windows = pair_windows(mixture.shape[2], mixture.shape[2] - head_cols)

    def one_block(block, carry):
        slot = jnp.bitwise_xor(meta[0], block)
        first, last = meta[2 + 2 * block], meta[3 + 2 * block]
        own = pl.ds(pl.multiple_of(block * rows, rows), rows)
        ids = query_ids[own, :]
        for head, query in enumerate(spread_heads(queries[slot], query_windows)):
            query_scratch[head] = query
        high_scratch[...] = jnp.full_like(high_scratch, -3e38)
        sum_scratch[...] = jnp.zeros_like(sum_scratch)
        total_scratch[...] = jnp.zeros_like(total_scratch)

        def scores_of(key_block, inner):
            keys = pl.ds(pl.multiple_of(key_block * KEYS, KEYS), KEYS)
            same = ids == key_ids[:, keys]
            for head in range(heads):
                scores = dot(query_scratch[head], key_scratch[head, keys, :], NT)
                scores = jnp.where(same, scores, MASKED)
                score_scratch[head, :, keys] = scores
                high = high_scratch[head]
                for lane in range(0, KEYS, LANES):
                    high = jnp.maximum(high, scores[:, lane : lane + LANES])
                high_scratch[head] = high
            return inner

        lax.fori_loop(first, last, scores_of, 0)
        for head in range(heads):
            high_scratch[head] = jnp.broadcast_to(
                jnp.max(high_scratch[head], axis=1, keepdims=True), (rows, LANES)
            )

        def sums_of(key_block, inner):
            keys = pl.ds(pl.multiple_of(key_block * KEYS, KEYS), KEYS)
            for head in range(heads):
                high = high_scratch[head]
                high = jnp.concatenate([high] * (KEYS // LANES), axis=1)
                powers = jnp.exp2(score_scratch[head, :, keys] - high)
                total = total_scratch[head]
                for lane in range(0, KEYS, LANES):
                    total += powers[:, lane : lane + LANES]
                total_scratch[head] = total
                sum_scratch[head] += dot(powers.astype(BF), value_scratch[head, keys, :])
            return inner

        lax.fori_loop(first, last, sums_of, 0)
        mixed, columns = [], []
        for head in range(heads):
            total = jnp.sum(total_scratch[head], axis=1, keepdims=True)
            columns.append(high_scratch[head][:, :1] + jnp.log2(total))
            mixed.append((sum_scratch[head] / total).astype(BF))
        mixture[slot] = join_heads(mixed, mixed_windows, mixture.shape[2]).astype(BF)
        logsum[:, own] = as_rows(columns)
        return carry

    lax.fori_loop(0, 4, one_block, 0)


def attend(meta, queries, own_pairs, far_pairs, query_ids, key_ids, lead):
    _, rows, head_cols = queries.shape
    heads = head_cols // HEAD_DIM
    own, count = 4 * rows, 8 * rows
    space = pl.BlockSpec(memory_space=pltpu.VMEM)
    return pl.pallas_call(
        functools.partial(attend_kernel, heads=heads),
        name="attend",
        cost_estimate=micros(22),
        out_shape=[
            jax.ShapeDtypeStruct((4, rows, lead + head_cols), BF),
            jax.ShapeDtypeStruct((8, own), F32),
        ],
        in_specs=[pl.BlockSpec(memory_space=pltpu.SMEM)] + [space] * 5,
        out_specs=[space] * 2,
        scratch_shapes=[
            pltpu.VMEM((heads, count, LANES), BF),
            pltpu.VMEM((heads, count, LANES), BF),
            pltpu.VMEM((heads, rows, count), F32),
            pltpu.VMEM((heads, rows, LANES), F32),
            pltpu.VMEM((heads, rows, LANES), F32),
            pltpu.VMEM((heads, rows, LANES), F32),
            pltpu.VMEM((heads, rows, LANES), BF),
        ],
        compiler_params=pltpu.CompilerParams(vmem_limit_bytes=VMEM_LIMIT),
    )(meta, queries, own_pairs, far_pairs, query_ids, key_ids)


def attend_back_kernel(
    meta, queries, own_pairs, far_pairs, query_ids, key_ids, grad_mixture, logsum,
    grad_queries, grad_own, grad_far,
    key_scratch, value_scratch, grad_key, grad_value, grad_query, query_scratch, grad_scratch,
    prob_scratch, grad_prob_scratch, delta_scratch,
    *, heads
):
    rows = queries.shape[1]
    head_cols = heads * HEAD_DIM
    load_pairs(meta, own_pairs, far_pairs, key_scratch, value_scratch, heads)
    query_windows = pair_windows(head_cols)
    mixed_windows = pair_windows(grad_mixture.shape[2], grad_mixture.shape[2] - head_cols)
    grad_key[...] = jnp.zeros_like(grad_key)
    grad_value[...] = jnp.zeros_like(grad_value)

    def one_block(block, carry):
        slot = jnp.bitwise_xor(meta[0], block)
        first, last = meta[2 + 2 * block], meta[3 + 2 * block]
        own = pl.ds(pl.multiple_of(block * rows, rows), rows)
        ids = query_ids[:, own]
        for head, query in enumerate(spread_heads(queries[slot], query_windows)):
            query_scratch[head] = query
        for head, grad in enumerate(spread_heads(grad_mixture[slot], mixed_windows)):
            grad_scratch[head] = grad
        logs = logsum[:, own]
        grad_query[...] = jnp.zeros_like(grad_query)
        delta_scratch[...] = jnp.zeros_like(delta_scratch)

        def probs_of(key_block, inner):
            keys = pl.ds(pl.multiple_of(key_block * KEYS, KEYS), KEYS)
            same = key_ids[keys, :] == ids
            for head in range(heads):
                grad = grad_scratch[head]
                scores = dot(key_scratch[head, keys, :], query_scratch[head], NT)
                probs = jnp.where(same, jnp.exp2(scores - logs[head : head + 1]), 0.0)
                grad_probs = dot(value_scratch[head, keys, :], grad, NT)
                prob_scratch[head, keys, :] = probs
                grad_prob_scratch[head, keys, :] = grad_probs
                delta_scratch[head] += jnp.sum((probs * grad_probs).reshape(KEYS // 8, 8, rows), axis=0)
                grad_value[head, keys, :] += dot(probs.astype(BF), grad)
            return inner

        lax.fori_loop(first, last, probs_of, 0)
        for head in range(heads):
            delta_scratch[head, 0:1] = jnp.sum(delta_scratch[head], axis=0, keepdims=True)

        def one_key(key_block, inner):
            keys = pl.ds(pl.multiple_of(key_block * KEYS, KEYS), KEYS)
            for head in range(heads):
                delta = delta_scratch[head, 0:1]
                grad_scores = prob_scratch[head, keys, :] * (grad_prob_scratch[head, keys, :] - delta)
                grad_scores = grad_scores.astype(BF)
                grad_key[head, keys, :] += dot(grad_scores, query_scratch[head])
                grad_query[head] += dot(grad_scores, key_scratch[head, keys, :], TN)
            return inner

        lax.fori_loop(first, last, one_key, 0)
        scaled = [(grad_query[head] * HEAD_DIM ** (-0.5)).astype(BF) for head in range(heads)]
        grad_queries[slot] = join_heads(scaled, query_windows, head_cols).astype(BF)
        return carry

    lax.fori_loop(0, 4, one_block, 0)
    hid, half = meta[0], meta[1]
    for which, target in ((0, grad_own), (1, grad_far)):
        for slot in range(4):
            place = jnp.bitwise_xor(half, which) * 4 + jnp.bitwise_xor(hid, slot)
            start = pl.ds(pl.multiple_of(place * rows, rows), rows)
            parts = [(grad_key[head, start, :] * LN2).astype(BF) for head in range(heads)]
            parts += [grad_value[head, start, :].astype(BF) for head in range(heads)]
            joined = join_heads(parts, pair_windows(2 * head_cols), 2 * head_cols)
            for index in range(2):
                part = joined[index * (rows // 2) : (index + 1) * (rows // 2)]
                tiles = [part[:, lane : lane + LANES] for lane in range(0, 2 * head_cols, LANES)]
                pack_half(tiles, target.at[slot, index])


def attend_back(meta, queries, own_pairs, far_pairs, query_ids, key_ids, grad_mixture, logsum):
    _, rows, head_cols = queries.shape
    heads = head_cols // HEAD_DIM
    count = 8 * rows
    space = pl.BlockSpec(memory_space=pltpu.VMEM)
    return pl.pallas_call(
        functools.partial(attend_back_kernel, heads=heads),
        name="attend_back",
        cost_estimate=micros(37),
        out_shape=[
            jax.ShapeDtypeStruct((4, rows, head_cols), BF),
            jax.ShapeDtypeStruct(own_pairs.shape, BF),
            jax.ShapeDtypeStruct(own_pairs.shape, BF),
        ],
        in_specs=[pl.BlockSpec(memory_space=pltpu.SMEM)] + [space] * 7,
        out_specs=[space] * 3,
        scratch_shapes=[
            pltpu.VMEM((heads, count, LANES), BF),
            pltpu.VMEM((heads, count, LANES), BF),
            pltpu.VMEM((heads, count, LANES), F32),
            pltpu.VMEM((heads, count, LANES), F32),
            pltpu.VMEM((heads, rows, LANES), F32),
            pltpu.VMEM((heads, rows, LANES), BF),
            pltpu.VMEM((heads, rows, LANES), BF),
            pltpu.VMEM((heads, count, rows), F32),
            pltpu.VMEM((heads, count, rows), F32),
            pltpu.VMEM((heads, 8, rows), F32),
        ],
        compiler_params=pltpu.CompilerParams(vmem_limit_bytes=VMEM_LIMIT),
    )(meta, queries, own_pairs, far_pairs, query_ids, key_ids, grad_mixture, logsum)


def mlp_kernel(*refs, layer, parts, last):
    ins, outs, scratch = split_refs(refs, 4 + sum(parts), 5 - last)
    mixture_hbm, x_hbm, vec, up_bias = ins[:4]
    mixed_hbm, up_hbm, down_hbm = split_refs(ins[4:], parts[0], parts[1])
    after_out, normed_out, active_out, slope_out = outs[:4]
    mixture, x, out_weight, up_weight, down_weight, after, normed, active, slope, x_next = scratch[:10]
    first_scratch, second_scratch = scratch[10:18], scratch[18:26]
    send_sems, recv_sems, move_sems = scratch[26:]
    net, moves = Net(send_sems, recv_sems), Moves(move_sems)
    rows = x.shape[0]
    hidden_cols = up_weight.shape[1]
    out_cols = out_weight.shape[1]
    chunks = chunks_of(rows, 2)
    out_part = pl.ds(x.shape[1] - out_cols, out_cols)
    loads = [
        moves.load(mixture_hbm, mixture), load_weight(net, moves, mixed_hbm, out_part, out_weight),
    ]
    x_load = moves.load(x_hbm, x)
    up_load = load_weight(net, moves, up_hbm, pl.ds(0, hidden_cols), up_weight)
    if not last:
        down_load = load_weight(net, moves, down_hbm, pl.ds(0, hidden_cols), down_weight)
    net.barrier([net.core, net.far])
    out_bias, gain = vec[layer, 2:3], vec[layer, 3:4]
    shift, down_bias = vec[layer, 4:5], vec[layer, 5:6]

    def mixed(slots, chunk):
        return dot(flat(mixture[slots, chunk, :]), out_weight[...], NT)

    def up(slots, chunk):
        hidden = dot(flat(normed[slots, chunk, :]), up_weight[...]) + up_bias[layer : layer + 1]
        square = hidden * hidden
        bend = jnp.tanh(GELU * hidden * (1.0 + CUBE * square))
        half = 0.5 * (1.0 + bend)
        value = hidden * half
        rise = half + 0.5 * hidden * (1.0 - bend * bend) * GELU * (1.0 + 3.0 * CUBE * square)
        active[slots, chunk, :] = blocked(value)
        slope[slots, chunk, :] = blocked(rise)

    def down(slots, chunk):
        return dot(flat(active[slots, chunk, :]), down_weight[...], NT)

    near, far, whole = pl.ds(0, 2), pl.ds(2, 2), pl.ds(0, rows)
    for load in loads:
        load.wait()
    first = Scatter(net, first_scratch)
    for key, chunk in enumerate(chunks):
        first.far_part(key, chunk, mixed(far, chunk))
    for key, chunk in enumerate(chunks):
        first.far_send(key, chunk)
    first.near_part(mixed(near, whole))
    first.near_done()
    x_load.wait()
    sent = []
    for key, chunk in enumerate(chunks):
        residual = first.result(key, chunk) + x[chunk, :] + out_bias
        after[chunk, :] = residual
        normed[0, chunk, :] = (norm_parts(residual)[0] * gain + shift).astype(BF)
        sent.append(gather_send(net, normed, chunk))
    moves.store(after, after_out)
    for one, _ in sent:
        one.wait_recv()
    up_load.wait()
    up(near, whole)
    if not last:
        down_load.wait()
    second = Scatter(net, second_scratch)
    for key, chunk in enumerate(chunks):
        passed = gather_pass(net, normed, chunk, sent[key][1])
        passed.wait_recv()
        up(far, chunk)
        if not last:
            second.far_part(key, chunk, down(far, chunk))
            second.far_send(key, chunk)
    moves.store(normed, normed_out)
    moves.store(active, active_out)
    moves.store(slope, slope_out)
    if not last:
        second.near_part(down(near, whole))
        second.near_done()
        for key, chunk in enumerate(chunks):
            x_next[chunk, :] = second.result(key, chunk) + after[chunk, :] + down_bias
        moves.store(x_next, outs[4])
    net.finish()
    moves.finish()


def mlp(layer, mixture, x, vec, up_bias, mixed, up, down, last):
    rows, width = x.shape
    hidden = up_bias.shape[1]
    outputs = [
        ((rows, width), F32, False),
        ((4, rows, width), BF, False),
        ((4, rows, hidden), BF, False),
        ((4, rows, hidden), BF, False),
        ((rows, width), F32, False),
    ]
    scratch = [
        pltpu.VMEM(mixture.shape, BF),
        pltpu.VMEM((rows, width), F32),
        pltpu.VMEM((width, mixture.shape[2]), BF),
        pltpu.VMEM((width, hidden), BF),
        pltpu.VMEM((width, hidden), BF),
    ]
    scratch += [pltpu.VMEM(shape, dtype) for shape, dtype, _ in outputs]
    scratch += scatter_scratch(rows, width) * 2
    outputs = outputs[: 5 - last]
    down = () if last else down
    inputs = [(mixture, False), (x, False), (vec, True), (up_bias, True)]
    inputs += spaced([*mixed, *up, *down])
    parts = (len(mixed), len(up), len(down))
    kernel = functools.partial(mlp_kernel, layer=layer, parts=parts, last=last)
    moves = 8 + sum(weight_loads(part) for part in (mixed, up, down) if part)
    return run(kernel, "mlp", 48, inputs, outputs, scratch, 8 * layer + 1, 18, moves)


def mlp_back_kernel(*refs, layer, parts, given, shard, crossing):
    ins, outs, scratch = split_refs(
        refs, 7 + given + sum(parts) + crossing, 7 + (shard > 0) + crossing
    )
    gradient_hbm, after_hbm, vec, mixture_hbm, normed_hbm, active_hbm, slope_hbm = ins[:7]
    weights = ins[7 + given : 7 + given + sum(parts)]
    mixed_hbm, up_hbm, down_hbm = split_refs(weights, parts[0], parts[1])
    after_out, mixture_out, down_out, out_out, sums, hidden_sums = outs[:6]
    up_outs = outs[6 : 7 + (shard > 0)]
    gradient, after, out_weight, up_weight, down_weight, mixture, normed, active, slope = scratch[:9]
    grad_after, grad_mixture, grad_down, grad_up, grad_out = scratch[9:14]
    grad_rows, grad_hidden, grad_mid = scratch[14:17]
    scatter_refs, across_refs = scratch[17:25], scratch[25:-3]
    send_sems, recv_sems, move_sems = scratch[-3:]
    net, moves = Net(send_sems, recv_sems), Moves(move_sems)
    rows, width = gradient.shape
    hidden_cols = up_weight.shape[1]
    out_cols = out_weight.shape[1]
    chunks = chunks_of(rows, 2)
    out_part = pl.ds(width - out_cols, out_cols)
    load_gradient = moves.load(ins[7] if given else gradient_hbm, grad_rows if given else gradient)
    load_down = load_weight(net, moves, down_hbm, pl.ds(0, hidden_cols), down_weight)
    load_slope = moves.load(slope_hbm, slope)
    load_up = load_weight(net, moves, up_hbm, pl.ds(0, hidden_cols), up_weight)
    load_active = moves.load(active_hbm, active)
    load_after = moves.load(after_hbm, after)
    load_normed = moves.load(normed_hbm, normed)
    load_out = load_weight(net, moves, mixed_hbm, out_part, out_weight)
    load_mixture = moves.load(mixture_hbm, mixture)
    if given:
        load_own = moves.load(gradient_hbm, gradient)
    across = Across(net, moves, ins[-1], across_refs) if crossing else None
    net.barrier([net.core, net.far] + ([net.half] if crossing else []))
    if crossing:
        across.start()
    gain = vec[layer, 3:4]
    near, far, whole = pl.ds(0, 2), pl.ds(2, 2), pl.ds(0, rows)
    load_gradient.wait()
    if not given:
        grad_rows[0] = gradient[...].astype(BF)
        sent = [gather_send(net, grad_rows, chunk) for chunk in chunks]
    sums[...] = jnp.zeros_like(sums)
    sums[5:6] = jnp.sum(grad_rows[0].astype(F32), axis=0, keepdims=True)

    def hidden_grad(slots, chunk):
        value = dot(flat(grad_rows[slots, chunk, :]), down_weight[...])
        value = value * flat(slope[slots, chunk, :]).astype(F32)
        grad_hidden[slots, chunk, :] = blocked(value)

    def up_back(slots, chunk):
        return dot(flat(grad_hidden[slots, chunk, :]), up_weight[...], NT)

    if not given:
        for one, _ in sent:
            one.wait_recv()
    load_down.wait()
    load_slope.wait()
    scatter = Scatter(net, scatter_refs)
    if given:
        for key, chunk in enumerate(chunks):
            hidden_grad(far, chunk)
            if key == 0:
                load_up.wait()
            scatter.far_part(key, chunk, up_back(far, chunk))
        for key, chunk in enumerate(chunks):
            scatter.far_send(key, chunk)
        hidden_grad(near, whole)
    else:
        hidden_grad(near, whole)
        load_up.wait()
        for key, chunk in enumerate(chunks):
            passed = gather_pass(net, grad_rows, chunk, sent[key][1])
            passed.wait_recv()
            hidden_grad(far, chunk)
            scatter.far_part(key, chunk, up_back(far, chunk))
            scatter.far_send(key, chunk)
    scatter.near_part(up_back(near, whole))
    load_active.wait()
    weight_grad(grad_rows, active, grad_down)
    moves.store(grad_down, down_out)
    scatter.near_done()
    load_after.wait()
    if given:
        load_own.wait()
    sent = []
    for key, chunk in enumerate(chunks):
        back, gain_sum, shift_sum = norm_back(after[chunk, :], gain, scatter.result(key, chunk))
        total = gradient[chunk, :] + back
        grad_after[chunk, :] = total
        rounded = total.astype(BF)
        grad_mid[0, chunk, :] = rounded
        sent.append(gather_send(net, grad_mid, chunk))
        sums[3:4] += gain_sum
        sums[4:5] += shift_sum
        sums[2:3] += jnp.sum(rounded.astype(F32), axis=0, keepdims=True)
    moves.store(grad_after, after_out)
    load_normed.wait()
    weight_grad(normed, grad_hidden, grad_up)
    store_halves(net, moves, grad_up, up_outs, shard)
    column = jnp.zeros((1, hidden_cols), F32)
    for slot in range(4):
        column += jnp.sum(grad_hidden[slot].astype(F32), axis=0, keepdims=True)
    hidden_sums[...] = column

    def mix_back(slots, chunk):
        value = dot(flat(grad_mid[slots, chunk, :]), out_weight[...])
        grad_mixture[slots, chunk, :] = blocked(value)

    for one, _ in sent:
        one.wait_recv()
    load_out.wait()
    mix_back(near, whole)
    for key, chunk in enumerate(chunks):
        gather_pass(net, grad_mid, chunk, sent[key][1]).wait_recv()
    mix_back(far, whole)
    moves.store(grad_mixture, mixture_out)
    load_mixture.wait()
    weight_grad(grad_mid, mixture, grad_out)
    moves.store(grad_out, out_out)
    if crossing:
        across.finish(outs[-1])
    net.finish()
    moves.finish()


def mlp_back(
    layer, gradient, after, vec, mixed, up, down, mixture, normed, active, slope, given=(),
    shard=0, crossing=(),
):
    rows, width = gradient.shape
    hidden = active.shape[2]
    out_cols = mixture.shape[2]
    outputs = [
        ((rows, width), F32, False),
        ((4, rows, out_cols), BF, False),
        ((width, hidden), BF, False),
        ((width, out_cols), BF, False),
        ((8, width), F32, True),
        ((1, hidden), F32, True),
    ]
    shapes = [
        ((rows, width), F32),
        ((rows, width), F32),
        ((width, out_cols), BF),
        ((width, hidden), BF),
        ((width, hidden), BF),
        ((4, rows, out_cols), BF),
        ((4, rows, width), BF),
        ((4, rows, hidden), BF),
        ((4, rows, hidden), BF),
        ((rows, width), F32),
        ((4, rows, out_cols), BF),
        ((width, hidden), BF),
        ((width, hidden), BF),
        ((width, out_cols), BF),
        ((4, rows, width), BF),
        ((4, rows, hidden), BF),
        ((4, rows, width), BF),
    ]
    outputs += half_outputs(width, hidden, shard)
    scratch = [pltpu.VMEM(shape, dtype) for shape, dtype in shapes] + scatter_scratch(rows, width)
    for part in crossing:
        outputs.append((part.shape[1:], F32, True))
        scratch += across_scratch(part)
    inputs = [
        (gradient, False), (after, False), (vec, True), (mixture, False), (normed, False),
        (active, False), (slope, False),
    ] + spaced([*given, *mixed, *up, *down, *crossing])
    parts = (len(mixed), len(up), len(down))
    kernel = functools.partial(
        mlp_back_kernel,
        layer=layer,
        parts=parts,
        given=len(given),
        shard=shard,
        crossing=len(crossing),
    )
    moves = 14 + (3 * width // (2 * shard) if shard else 0)
    moves += weight_loads(mixed) + weight_loads(up) + weight_loads(down)
    return run(kernel, "mlp_back", 48, inputs, outputs, scratch, 8 * layer + 2, 21, moves)


def project_back_kernel(*refs, layer, parts, closing, crossing):
    ins, outs, scratch = split_refs(
        refs, 8 + parts + closing + crossing, 4 + (closing > 0) + crossing
    )
    after_hbm, x_hbm, vec, normed_hbm, queries_hbm, own_hbm, far_hbm, out_hbm = ins[:8]
    mixed_hbm, closing_ins = ins[8 : 8 + parts], ins[8 + parts : 8 + parts + closing]
    gradient_out, sums, column_sums, weight_out = outs[:4]
    grad_after, x, weight, normed, grad_queries, grad_own, grad_out = scratch[:7]
    landed, together, gradient, grad_weight = scratch[7:11]
    scatter_refs, closing_refs = scratch[11:19], scratch[19 : -3 - 2 * crossing]
    across_refs = scratch[-3 - 2 * crossing : -3]
    send_sems, recv_sems, move_sems = scratch[-3:]
    net, moves = Net(send_sems, recv_sems), Moves(move_sems)
    rows, width = x.shape
    pair_cols = 2 * grad_queries.shape[2]
    used_cols = pair_cols + grad_queries.shape[2]
    all_cols = together.shape[2]
    chunks = chunks_of(rows, 2)
    near, far, whole = pl.ds(0, 2), pl.ds(2, 2), pl.ds(0, rows)
    load_own = moves.load(own_hbm, grad_own)
    load_queries = moves.load(queries_hbm, grad_queries)
    loading = load_weight(net, moves, mixed_hbm, pl.ds(0, all_cols), weight)
    load_normed = moves.load(normed_hbm, normed)
    load_out = moves.load(out_hbm, grad_out)
    load_x = moves.load(x_hbm, x)
    load_after = moves.load(after_hbm, grad_after)
    if closing:
        active, down_weight, after, final = closing_refs[:4]
        load_active = moves.load(closing_ins[0], active)
        load_after_two = moves.load(closing_ins[1], after)
        columns = pl.ds(0, down_weight.shape[1])
        load_down = load_weight(net, moves, closing_ins[2:], columns, down_weight)
    across = Across(net, moves, ins[-1], across_refs) if crossing else None
    net.barrier([net.core, net.far, net.half])
    arriving = {
        slot: net.copy(far_hbm.at[slot], landed.at[slot], net.half) for slot in (3, 2, 1, 0)
    }
    load_queries.wait()
    together[:, :, pair_cols:used_cols] = grad_queries[...]
    together[:, :, used_cols:] = jnp.zeros((4, rows, all_cols - used_cols), BF)
    load_own.wait()
    loading.wait()

    def join(slot):
        arriving[slot].wait_recv()
        for index in range(2):
            pair = grad_own[slot, index].astype(F32) + landed[slot, index].astype(F32)
            part = pl.ds(index * (rows // 2), rows // 2)
            for place, tile in enumerate(unpack_half(pair.astype(BF), rows // 2)):
                columns = pl.ds(place * LANES, tile.shape[1])
                together[slot, part, columns] = tile

    def back(slots, chunk):
        return dot(flat(together[slots, chunk, :]), weight[...], NT)

    if closing:

        def down(slots, chunk):
            return dot(flat(active[slots, chunk, :]), down_weight[...], NT)

        load_active.wait()
        load_down.wait()
        last = Scatter(net, closing_refs[4:])
        for key, chunk in enumerate(chunks):
            last.far_part(key, chunk, down(far, chunk))
        for key, chunk in enumerate(chunks):
            last.far_send(key, chunk)
        last.near_part(down(near, whole))
        last.near_done()
    scatter = Scatter(net, scatter_refs)
    join(3)
    join(2)
    for key, chunk in enumerate(chunks):
        scatter.far_part(key, chunk, back(far, chunk))
    for key, chunk in enumerate(chunks):
        scatter.far_send(key, chunk)
    join(1)
    join(0)
    if crossing:
        across.start()
    scatter.near_part(back(near, whole))
    load_normed.wait()
    load_out.wait()
    weight_grad(normed, together, grad_weight, grad_out)
    moves.store(grad_weight, weight_out)
    column = jnp.zeros((1, all_cols), F32)
    for slot in range(4):
        column += jnp.sum(together[slot].astype(F32), axis=0, keepdims=True)
    column_sums[...] = column
    scatter.near_done()
    sums[...] = jnp.zeros_like(sums)
    load_x.wait()
    load_after.wait()
    for key, chunk in enumerate(chunks):
        grad, gain_sum, shift_sum = norm_back(
            x[chunk, :], vec[layer, 0:1], scatter.result(key, chunk)
        )
        gradient[chunk, :] = grad_after[chunk, :] + grad
        sums[0:1] += gain_sum
        sums[1:2] += shift_sum
    moves.store(gradient, gradient_out)
    if closing:
        load_after_two.wait()
        for key, chunk in enumerate(chunks):
            final[chunk, :] = last.result(key, chunk) + after[chunk, :] + vec[layer, 5:6]
        moves.store(final, outs[4])
    if crossing:
        across.finish(outs[-1])
    net.finish()
    moves.finish()


def project_back(
    layer, grad_after, x, vec, mixed, normed, grad_queries, grad_own, grad_far, grad_out, all_cols,
    closing=(), crossing=(),
):
    rows, width = x.shape
    outputs = [
        ((rows, width), F32, False),
        ((8, width), F32, True),
        ((1, all_cols), F32, True),
        ((width, width), BF, False),
    ]
    shapes = [
        ((rows, width), F32),
        ((rows, width), F32),
        ((width, all_cols), BF),
        (normed.shape, BF),
        (grad_queries.shape, BF),
        (grad_own.shape, BF),
        (grad_out.shape, BF),
        (grad_far.shape, BF),
        ((4, rows, all_cols), BF),
        ((rows, width), F32),
        ((width, width), BF),
    ]
    scratch = [pltpu.VMEM(shape, dtype) for shape, dtype in shapes] + scatter_scratch(rows, width)
    copies, moves = 12, 9 + weight_loads(mixed)
    if closing:
        active, after, *down = closing
        outputs.append(((rows, width), F32, False))
        shapes = [
            (active.shape, BF), ((width, active.shape[2]), BF), ((rows, width), F32), ((rows, width), F32),
        ]
        scratch += [pltpu.VMEM(shape, dtype) for shape, dtype in shapes] + scatter_scratch(rows, width)
        copies, moves = 18, moves + 3 + weight_loads(down)
    for part in crossing:
        outputs.append((part.shape[1:], F32, True))
        scratch += across_scratch(part)
        copies, moves = copies + 1, moves + 1
    inputs = [
        (grad_after, False), (x, False), (vec, True), (normed, False), (grad_queries, False),
        (grad_own, False), (grad_far, False), (grad_out, False),
    ] + spaced([*mixed, *closing, *crossing])
    kernel = functools.partial(
        project_back_kernel, layer=layer, parts=len(mixed), closing=len(closing),
        crossing=len(crossing),
    )
    return run(kernel, "project_back", 42, inputs, outputs, scratch, 8 * layer + 3, copies, moves)


def entry_kernel(*refs):
    ins, outs, scratch = split_refs(refs, 12, 7)
    tokens, cotangent, value_bias, query_bias, up_bias, shard = ins[:6]
    x, gradient, grad_rows, vec, bias, hidden_bias, weights = outs
    vectors, token_land, cotangent_land, vector_land, send_sems, recv_sems, move_sems = scratch
    net, moves = Net(send_sems, recv_sems), Moves(move_sems)
    rows, cols = x.shape[0], tokens.shape[0]
    layers = vec.shape[0]
    others = [net.core, net.far, net.far_core]
    vectors[...] = jnp.zeros_like(vectors)
    for index, one in enumerate(ins[6:]):
        for layer in range(layers):
            vectors[layer * 8 + index : layer * 8 + index + 1] = one[layer : layer + 1]
    net.line(weights.shape[0] // 2)
    net.barrier(others + [net.half], True)
    gathering = GatherJob(net, moves, shard, weights)

    def block(hid):
        return pl.ds(pl.multiple_of(hid * rows, rows), rows)

    moved = [
        net.copy(tokens.at[:, block(device[1])], token_land.at[net.hid], device)
        for device in reversed(others)
    ]
    moved += [net.copy(vectors, vector_land.at[net.hid], device) for device in others]
    sent = []
    for chunk in chunks_of(4 * rows, 2):
        source, own = cotangent.at[:, chunk], cotangent_land.at[net.hid, :, chunk]
        moved.append(net.copy(source, own, net.core))
        sent.append((net.copy(source, own, net.far), cotangent_land.at[net.far[1], :, chunk]))
    token_land[net.hid] = tokens[:, block(net.hid)]
    cotangent_land[net.hid] = cotangent[...]
    vector_land[net.hid] = vectors[...]
    bias[...] = jnp.zeros_like(bias)
    bias[:, cols : 2 * cols] = value_bias[...]
    bias[:, 2 * cols : 3 * cols] = query_bias[...]
    hidden_bias[...] = jnp.zeros_like(hidden_bias)
    hidden_bias[:, : up_bias.shape[1]] = up_bias[...]
    gathering.forward(0, 3)
    for point, (one, landed) in enumerate(sent):
        one.wait_recv()
        moved.append(net.copy(landed, landed, net.core))
        gathering.forward(point + 1, 3)
    for one in moved:
        one.wait_recv()
    for place in range(4):
        columns = slice(place * cols, (place + 1) * cols)
        for layer in range(layers):
            vec[layer, :, columns] = vector_land[place, layer * 8 : layer * 8 + 8]
    x[...] = flat(token_land[...]).astype(F32).T
    for slot, device in enumerate([(net.tok, net.hid)] + others):
        whole = flat(cotangent_land[:, :, block(device[1])])
        grad_rows[slot] = whole.astype(F32).T.astype(BF)
    gradient[...] = grad_rows[0].astype(F32)
    gathering.finish()
    net.finish()
    moves.finish()


def entry(tokens, cotangent, value_bias, query_bias, up_bias, shard, vectors, count, used_cols):
    cols, rows = tokens.shape[0], tokens.shape[1] // 4
    layers, feed = up_bias.shape
    inputs = [
        (tokens, True), (cotangent, True), (value_bias, True), (query_bias, True), (up_bias, True),
        (shard, False),
    ] + [(one, True) for one in vectors]
    outputs = [
        ((rows, 4 * cols), F32, True),
        ((rows, 4 * cols), F32, True),
        ((4, rows, 4 * cols), BF, True),
        ((layers, 8, 4 * cols), F32, True),
        ((layers, used_cols), F32, True),
        ((layers, feed + -feed % LANES), F32, True),
        ((count,) + shard.shape, BF, False),
    ]
    scratch = [
        pltpu.VMEM((layers * 8, cols), F32),
        pltpu.VMEM((4, cols, rows), BF),
        pltpu.VMEM((4,) + cotangent.shape, BF),
        pltpu.VMEM((4, layers * 8, cols), F32),
    ]
    return run(entry_kernel, "entry", 50, inputs, outputs, scratch, 4, 12 + job_copies(count), 1)


def finish_kernel(*refs, layers):
    ins, outs, scratch = split_refs(refs, 4 + 4 * layers, 13)
    final_rows, gradient_rows, grads, down_grads = ins[:4]
    layer_sums = [ins[4 + 4 * layer : 8 + 4 * layer] for layer in range(layers)]
    final_out, gradient_out, total = outs[:3]
    wide_outs, query_out, value_out, hidden_out = outs[3:9], outs[9], outs[10], outs[11]
    down_total = outs[12]
    final, gradient, final_land, gradient_land = scratch[:4]
    sums, across_land, along, wide, wide_land = scratch[4:9]
    job_refs, across_refs = scratch[9:13], scratch[13:15]
    send_sems, recv_sems, move_sems = scratch[15:]
    net, moves = Net(send_sems, recv_sems), Moves(move_sems)
    count = grads.shape[0] // 2
    rows, cols, last = final_rows.shape[0], wide.shape[2], count - 1
    others = [net.core, net.far, net.far_core]
    top = layers * 8
    sums[top:] = jnp.zeros((sums.shape[0] - top, sums.shape[1]), F32)
    for layer, (one, two, column_sums, hidden) in enumerate(layer_sums):
        sums[layer * 8 : layer * 8 + 8] = one[...] + two[...]
        sums[top + layer : top + layer + 1, : column_sums.shape[1]] = column_sums[...]
        sums[top + layers + layer : top + layers + layer + 1, : hidden.shape[1]] = hidden[...]
    net.line(count)
    net.barrier(others + [net.half], True)
    swap = net.copy(sums, across_land, net.half)
    scattering = ScatterParts(net, moves, grads, job_refs)
    across = Across(net, moves, down_grads, across_refs)
    for target, source in ((final, final_rows), (gradient, gradient_rows)):
        target[...] = source[...].T.astype(BF).reshape(target.shape)
    moved = []
    for source, target in ((final, final_land), (gradient, gradient_land)):
        for device in reversed(others):
            moved.append(net.copy(source.at[device[1]], target.at[net.hid], device))
        target[net.hid] = source[net.hid]
    up, down = net.take(count), net.take(count)
    own = along.at[net.high]
    swap.wait()
    along[net.high] = sums[...] + across_land[...]
    pl.when(net.has_after)(net.make(up, own, own, net.after).start)
    pl.when(net.has_before)(net.make(down, own, own, net.before).start)

    def pass_on(step, place, base, device, has):
        block = along.at[place]
        net.make(base + step - 1, block, block, device).wait_recv()
        if step < last:
            pl.when(has)(net.make(base + step, block, block, device).start)

    def pass_sums(step):
        pl.when(net.high >= step)(
            functools.partial(pass_on, step, net.high - step, up, net.after, net.has_after)
        )
        pl.when(net.high + step < count)(
            functools.partial(pass_on, step, net.high + step, down, net.before, net.has_before)
        )

    for point in range(3):
        scattering.forward(point, 3)
        for step in range(1, count):
            if (step - 1) * 3 // last == point:
                pass_sums(step)
    across.start()
    reduced = along[0]
    for place in range(1, count):
        reduced += along[place]
    sums[...] = reduced
    for place in range(4):
        wide[place] = sums[:top, place * cols : (place + 1) * cols]
    wide_land[net.hid] = wide[net.hid]
    summed = [net.copy(wide.at[device[1]], wide_land.at[net.hid], device) for device in others]
    for one in moved:
        one.wait_recv()
    for source, target in ((final_land, final_out), (gradient_land, gradient_out)):
        for place in range(4):
            target[:, place * rows : (place + 1) * rows] = source[place].astype(F32)
    for one in summed:
        one.wait_recv()
    narrow = wide_land[0] + wide_land[1] + wide_land[2] + wide_land[3]
    for layer in range(layers):
        one = slice(layer, layer + 1)
        for index, out in enumerate(wide_outs):
            out[one, :] = narrow[layer * 8 + index : layer * 8 + index + 1]
        row = slice(top + layer, top + layer + 1)
        value_out[one, :] = sums[row, cols : 2 * cols]
        query_out[one, :] = sums[row, 2 * cols : 3 * cols]
        row = slice(top + layers + layer, top + layers + layer + 1)
        hidden_out[one, :] = sums[row, : hidden_out.shape[1]]
    for step in range(last):
        sent_up = jnp.logical_and(net.has_after, net.high >= step)
        sent_down = jnp.logical_and(net.has_before, net.high + step < count)
        pl.when(sent_up)(net.make(up + step, own, own, net.after).wait_send)
        pl.when(sent_down)(net.make(down + step, own, own, net.before).wait_send)
    scattering.finish(total)
    across.finish(down_total)
    net.finish([swap])


def finish(final, gradient, grads, down_grads, layer_sums, head_cols, feed):
    count, layers = grads.shape[0] // 2, len(layer_sums)
    rows, width = final.shape
    sum_cols = max(width, layer_sums[0][2].shape[1], layer_sums[0][3].shape[1])
    sums = (layers * 10 + -layers * 10 % 8, sum_cols)
    vector = ((layers, head_cols), F32, True)
    outputs = [
        ((head_cols, 4 * rows), F32, True),
        ((head_cols, 4 * rows), F32, True),
        (grads.shape[1:], F32, True),
    ] + [vector] * 8
    outputs += [((layers, feed), F32, True), (down_grads.shape[1:], F32, True)]
    blocks, wide = (4, head_cols, rows), (4, layers * 8, head_cols)
    scratch = [pltpu.VMEM(blocks, BF)] * 4 + [
        pltpu.VMEM(sums, F32),
        pltpu.VMEM(sums, F32),
        pltpu.VMEM((count,) + sums, F32),
        pltpu.VMEM(wide, F32),
        pltpu.VMEM(wide, F32),
    ]
    scratch += part_scratch(*grads.shape) + across_scratch(down_grads)
    inputs = [(final, True), (gradient, True), (grads, False), (down_grads, False)]
    inputs += [(one, True) for four in layer_sums for one in four]
    kernel = functools.partial(finish_kernel, layers=layers)
    return run(kernel, "finish", 2, inputs, outputs, scratch, 5, 13 + 5 * count, 2 + count)


def key_ranges(own_ids, row_ids, rows):
    blocks = own_ids.reshape(-1, rows)
    position = jnp.arange(row_ids.shape[0], dtype=jnp.int32)
    low = jnp.min(jnp.where(row_ids == blocks[:, :1], position, row_ids.shape[0]), axis=1)
    high = jnp.max(jnp.where(row_ids == blocks[:, -1:], position, -1), axis=1)
    return jnp.stack([low // KEYS, high // KEYS + 1], axis=1).reshape(-1)


def body(
    tokens, picture, cotangent, first_gain, first_shift, query_weight, query_bias, key_weight,
    value_weight, value_bias, output_weight, output_bias, second_gain, second_shift, up_weight,
    up_bias, down_weight, down_bias,
):
    token_count = tokens.shape[0]
    rows = token_count // 4
    layers = query_weight.shape[0]
    head_cols = query_bias.shape[1]
    feed = up_bias.shape[1]
    feed_pad = -feed % LANES
    feed_cols = feed + feed_pad
    hid = lax.axis_index("hid")
    tok = lax.axis_index("tok")
    count = lax.axis_size("tok")
    shard = query_weight.shape[1]
    shard_pad = -shard % 16
    width = count * shard
    lead = 3 * head_cols % LANES
    used_cols = 3 * head_cols + -3 * head_cols % LANES

    own_ids = lax.dynamic_slice_in_dim(picture, tok * token_count, token_count)
    row_ids = lax.dynamic_slice_in_dim(picture, (tok // 2) * 2 * token_count, 2 * token_count)
    place = jnp.stack([hid, tok % 2]).astype(jnp.int32)
    meta = jnp.concatenate([place, key_ranges(own_ids, row_ids, rows)])

    def side_by_side(*parts):
        return jnp.concatenate(parts, axis=1)

    def padded(part):
        return jnp.pad(part, ((0, 0), (0, feed_pad)))

    def shards(part):
        return jnp.pad(part, ((0, shard_pad), (0, 0)))

    def joined(gathered):
        return gathered[:, :shard].reshape(width, gathered.shape[2])

    def separate(grads):
        grads = grads.reshape(count, shard, grads.shape[1])
        return jnp.pad(grads, ((0, 0), (0, shard_pad), (0, 0)))

    mixed_parts = [
        shards(
            side_by_side(
                key_weight[layer], value_weight[layer], query_weight[layer], output_weight[layer].T
            )
        )
        for layer in range(layers)
    ]
    vectors = (first_gain, first_shift, output_bias, second_gain, second_shift, down_bias)
    x, gradient, grad_rows, vectors, bias, up_bias, mixed = entry(
        tokens.T, cotangent.T, value_bias, query_bias, up_bias, mixed_parts[0], vectors, count, used_cols
    )

    halves = [(place, place ^ 1) for place in range(count)]
    lines = [[place * 2 + low for place in range(count // 2)] for low in range(2)]

    def swap(part):
        return lax.ppermute(part, "tok", halves)

    def both_halves(own, other):
        first = tok % 2 == 0
        return jnp.stack([jnp.where(first, own, other), jnp.where(first, other, own)])

    def along(part):
        return lax.all_gather(part, "tok", axis=0, tiled=True, axis_index_groups=lines)

    def along_first(part):
        own = along(part)
        other = swap(own)
        parts = [rows_of.reshape(count // 2, shard, part.shape[1]) for rows_of in (own, other)]
        if shard % 16 == 0:
            return parts
        return [both_halves(*parts).transpose(1, 0, 2, 3).reshape(width, part.shape[1])]

    def hold(*values):
        return lax.optimization_barrier(values)

    def pair_rows(part, other):
        return both_halves(part, other).reshape(2 * shard, part.shape[1])

    def up_part(layer):
        return padded(up_weight[layer])

    def down_part(layer):
        return padded(down_weight[layer].T)

    ups, weights = [along_first(up_part(0))], [[joined(mixed)]]
    early = down_part(0)
    early, early_other, x = hold(early, swap(early), x)
    downs = [[along(pair_rows(early, early_other))]]
    for layer in range(1, layers):
        weights.append(along_first(mixed_parts[layer][:shard]))
        coming = up_part(layer)
        ups.append([along(pair_rows(coming, swap(coming)))])
    saved = []
    for layer in range(layers):
        mixed, up = weights[layer], ups[layer]
        more = layer + 1 < layers
        normed, queries, own_pairs, far_pairs = project(layer, x, vectors, bias, mixed, head_cols)
        if layer > 0:
            queries, coming, coming_other = hold(queries, coming, coming_other)
            downs.append([along(pair_rows(coming, coming_other))])
        mixture, logsum = attend(
            meta, queries, own_pairs, far_pairs, own_ids[:, None], row_ids[None, :], lead
        )
        if more:
            coming, mixture = hold(down_part(layer + 1), mixture)
            coming_other = swap(coming)
        after, normed_two, active, slope, *x_next = mlp(
            layer, mixture, x, vectors, up_bias, mixed, up, downs[layer], not more
        )
        saved.append(
            (x, normed, queries, own_pairs, far_pairs, mixture, logsum, after, normed_two, active, slope)
        )
        x = x_next[0] if x_next else None

    def by_halves(part):
        own = lax.dynamic_index_in_dim(part, tok % 2, 1, keepdims=False)
        other = lax.dynamic_index_in_dim(part, 1 - tok % 2, 1, keepdims=False)
        return own, other

    def sum_along(part):
        return lax.psum_scatter(
            part, "tok", scatter_dimension=0, tiled=True, axis_index_groups=lines
        )

    def halves_of(parts):
        if len(parts) == 1:
            part = parts[0].reshape(-1, 2, shard, parts[0].shape[1])
            parts = by_halves(part)
        return parts[0], swap(parts[1])

    def by_half(part):
        return jnp.pad(part.reshape(2, shard, part.shape[1]), ((0, 0), (0, shard_pad), (0, 0)))

    def added(own, other):
        return (own.astype(F32) + other.astype(F32)).astype(BF)

    def in_rows(part):
        return part.reshape(-1, part.shape[-1])

    split = shard if shard % 16 == 0 else 0
    mixed_grads, up_grads, down_grads = [None] * layers, [None] * layers, [None] * layers
    layer_sums = [None] * layers
    grads = final = None
    for layer in reversed(range(layers)):
        x, normed, queries, own_pairs, far_pairs, mixture, logsum, after, normed_two, active, slope = saved[layer]
        mixed, up, down = weights[layer], ups[layer], downs[layer]
        last = layer + 1
        crossing = ()
        if last < layers:
            gradient, down_grads[last] = hold(gradient, down_grads[last])
            crossing = (by_half(down_grads[last]),)
        grad_after, grad_mixture, grad_down, grad_out, sums_two, hidden_sums, *grad_up = mlp_back(
            layer, gradient, after, vectors, mixed, up, down, mixture, normed_two, active, slope,
            () if last < layers else (grad_rows,), split, crossing,
        )
        if last < layers:
            down_grads[last] = grad_up.pop()
            grad_down, up_grads[last] = hold(grad_down, up_grads[last])
        down_grads[layer] = sum_along(grad_down)
        up_own, up_other = halves_of(grad_up)
        grad_queries, grad_own, grad_far = attend_back(
            meta, queries, own_pairs, far_pairs, own_ids[None, :], row_ids[:, None],
            grad_mixture, logsum,
        )
        up_other, grad_far = hold(up_other, grad_far)
        up_grad = added(up_own, up_other)
        crossing = ()
        if last < layers:
            grad_after, mixed_grads[last] = hold(grad_after, mixed_grads[last])
            crossing = (by_half(mixed_grads[last]),)
        grad_after, up_grad = hold(grad_after, up_grad)
        up_grads[layer] = sum_along(in_rows(up_grad))
        gradient, sums_one, column_sums, grads, *closed = project_back(
            layer, grad_after, x, vectors, mixed, normed, grad_queries, grad_own, grad_far,
            grad_out, used_cols, () if last < layers else (active, after, *down), crossing,
        )
        if last < layers:
            mixed_grads[last] = closed.pop()
        final = closed[0] if closed else final
        if layer > 0:
            mixed_grads[layer] = sum_along(grads)
        layer_sums[layer] = (sums_one, sums_two, column_sums, hidden_sums)
    gradient, down_grads[0] = hold(gradient, down_grads[0])
    final, gradient, mixed_grads[0], *small = finish(
        final, gradient, separate(grads), by_half(down_grads[0]), layer_sums, head_cols, feed
    )
    up_grads[0], final, gradient, mixed_grads[0], *small = hold(
        up_grads[0], final, gradient, mixed_grads[0], *small
    )
    down_grads[0] = small.pop()
    first_gain, first_shift, output_bias, second_gain, second_shift, down_bias = small[:6]
    query_bias, value_bias, up_bias = small[6:]

    def mixed_columns(start):
        columns = slice(start * head_cols, (start + 1) * head_cols)
        return jnp.stack([part[:shard, columns].astype(F32) for part in mixed_grads])

    def hidden_columns(parts):
        return jnp.stack([part[:shard, :feed].astype(F32) for part in parts])

    return (
        final.T,
        gradient.T,
        first_gain,
        first_shift,
        mixed_columns(2),
        query_bias,
        mixed_columns(0),
        mixed_columns(1),
        value_bias,
        mixed_columns(3).transpose(0, 2, 1),
        output_bias,
        second_gain,
        second_shift,
        hidden_columns(up_grads),
        up_bias,
        hidden_columns(down_grads).transpose(0, 2, 1),
        down_bias,
    )


def solution(mesh):
    rows = P("tok", "hid")
    vector = P(None, "hid")
    inward = P(None, "tok", "hid")
    outward = P(None, "hid", "tok")
    in_specs = (
        rows, P(), rows, vector, vector, inward, vector, inward, inward, vector, outward, vector,
        vector, vector, inward, vector, outward, vector,
    )
    out_specs = (
        rows, rows, vector, vector, inward, vector, inward, inward, vector, outward, vector,
        vector, vector, inward, vector, outward, vector,
    )
    return jax.shard_map(body, mesh=mesh, in_specs=in_specs, out_specs=out_specs, check_vma=False)
```

```python
import functools

import jax
import jax.numpy as jnp
from jax import lax
from jax.experimental import pallas as pl
from jax.experimental.pallas import tpu as pltpu
from jax.sharding import PartitionSpec as P

HEAD_DIM = 72
LANES = 128
KEYS = 512
EPS = 1e-06
GELU = 0.7978845608028654
CUBE = 0.044715
MASKED = -1e30
LOG2E = 1.4426950408889634
LN2 = 0.6931471805599453
NN = (((1,), (0,)), ((), ()))
NT = (((1,), (1,)), ((), ()))
TN = (((0,), (0,)), ((), ()))
MESH = pl.DeviceIdType.MESH
BF = jnp.bfloat16
F32 = jnp.float32
VMEM_LIMIT = 60 * 1024 * 1024


def dot(left, right, dims=NN):
    return lax.dot_general(left, right, dims, preferred_element_type=F32)


def micros(duration):
    return pl.CostEstimate(flops=duration * 10**9, bytes_accessed=0, transcendentals=0)


def flat(value):
    return value.reshape(value.shape[0] * value.shape[1], value.shape[2])


class Net:
    def __init__(self, send_sems, recv_sems):
        tok, hid = lax.axis_index("tok"), lax.axis_index("hid")
        near = hid + 1 - 2 * lax.rem(hid, 2)
        self.tok, self.hid = tok, hid
        self.core = (tok, near)
        self.far = (tok, lax.rem(hid + 2, 4))
        self.far_core = (tok, lax.rem(near + 2, 4))
        self.half = (tok + 1 - 2 * lax.rem(tok, 2), hid)
        self.low, self.high = lax.rem(tok, 2), lax.div(tok, 2)
        self.send_sems, self.recv_sems = send_sems, recv_sems
        self.copies, self.count = [], 0

    def row(self, high):
        return (high * 2 + self.low, self.hid)

    def line(self, count):
        self.before, self.has_before = self.row(lax.max(self.high - 1, 0)), self.high > 0
        self.after = self.row(lax.min(self.high + 1, count - 1))
        self.has_after, self.last = self.high + 1 < count, count - 1

    def barrier(self, devices, line=False):
        sem = pltpu.get_barrier_semaphore()

        def signal(device):
            pl.semaphore_signal(sem, inc=1, device_id=device, device_id_type=MESH)

        for device in devices:
            signal(device)
        peers = len(devices)
        if line:
            pl.when(self.has_before)(lambda: signal(self.before))
            pl.when(self.has_after)(lambda: signal(self.after))
            peers = peers + lax.min(self.high, 1) + lax.min(self.last - self.high, 1)
        pl.semaphore_wait(sem, peers)

    def take(self, count):
        first = self.count
        self.count += count
        return first

    def make(self, index, source, target, device):
        return pltpu.make_async_remote_copy(
            src_ref=source,
            dst_ref=target,
            send_sem=self.send_sems.at[index],
            recv_sem=self.recv_sems.at[index],
            device_id=device,
            device_id_type=MESH,
        )

    def copy(self, source, target, device):
        made = self.make(self.take(1), source, target, device)
        self.copies.append(made)
        made.start()
        return made

    def finish(self, waited=()):
        done = [id(made) for made in waited]
        for made in self.copies:
            if id(made) not in done:
                made.wait_send()


class Moves:
    def __init__(self, sems):
        self.sems, self.count, self.stores = sems, 0, []

    def take(self, count):
        first = self.count
        self.count += count
        return first

    def make(self, index, source, target):
        return pltpu.make_async_copy(source, target, self.sems.at[index])

    def load(self, source, target):
        made = self.make(self.take(1), source, target)
        made.start()
        return made

    def store(self, source, target):
        self.stores.append(self.load(source, target))

    def finish(self):
        for made in self.stores:
            made.wait()


class Several:
    def __init__(self, copies):
        self.copies = copies

    def wait(self):
        for one in self.copies:
            one.wait()


def weight_loads(parts):
    return 1 if len(parts) == 1 else 2 * parts[0].shape[0]


def load_weight(net, moves, parts, columns, target):
    if len(parts) == 1:
        return moves.load(parts[0].at[:, columns], target)
    copies = []
    for part, low in zip(parts, (net.low, 1 - net.low)):
        shard = part.shape[1]
        for high in range(part.shape[0]):
            start = pl.multiple_of((high * 2 + low) * shard, 16)
            copies.append(moves.load(part.at[high, :, columns], target.at[pl.ds(start, shard)]))
    return Several(copies)


def store_halves(net, moves, grad, outs, shard):
    if not shard:
        moves.store(grad, outs[0])
        return
    for out, low in zip(outs, (net.low, 1 - net.low)):
        for place in range(out.shape[0]):
            start = pl.multiple_of((place * 2 + low) * shard, 16)
            moves.store(grad.at[pl.ds(start, shard)], out.at[place])


def half_outputs(rows, columns, shard):
    if not shard:
        return [((rows, columns), BF, False)]
    return [((rows // (2 * shard), shard, columns), BF, False)] * 2


def spaced(arrays):
    return [(array, False) for array in arrays]


def job_copies(count):
    return 2 * count + 1


class GatherJob:
    def __init__(self, net, moves, shard, weights):
        self.net, self.weights = net, weights
        self.count = weights.shape[0] // 2
        self.across = net.take(2 * self.count - 1)
        self.up, self.down = net.take(self.count), net.take(self.count)
        own = weights.at[net.tok]
        moves.store(shard, own)
        first = self.swap(0, shard, own)
        pl.when(net.has_after)(lambda: net.make(self.up, shard, own, net.after).start())
        pl.when(net.has_before)(lambda: net.make(self.down, shard, own, net.before).start())
        first.start()

    def swap(self, index, source, target):
        return self.net.make(self.across + index, source, target, self.net.half)

    def arrive(self, step, above):
        net = self.net
        place = net.high + step if above else net.high - step
        block = self.weights.at[place * 2 + net.low]
        base, onward = (self.down, net.before) if above else (self.up, net.after)
        net.make(base + step - 1, block, block, onward).wait_recv()
        if step + 1 < self.count:
            go_on = net.has_before if above else net.has_after
            pl.when(go_on)(lambda: net.make(base + step, block, block, onward).start())
        self.swap(2 * step - int(above), block, block).start()

    def forward(self, point, points):
        net = self.net
        for step in range(1, self.count):
            if (step - 1) * points // (self.count - 1) == point:
                pl.when(net.high - step >= 0)(functools.partial(self.arrive, step, False))
                pl.when(net.high + step < self.count)(functools.partial(self.arrive, step, True))

    def finish(self):
        net = self.net
        own = self.weights.at[net.tok]
        self.swap(0, own, own).wait()
        for step in range(1, self.count):
            below, above = net.high - step >= 0, net.high + step < self.count
            pl.when(below)(lambda step=step: self.swap(2 * step, own, own).wait())
            pl.when(above)(lambda step=step: self.swap(2 * step - 1, own, own).wait())
        for step in range(self.count - 1):
            for base, device, has, there in (
                (self.up, net.after, net.has_after, net.high - step >= 0),
                (self.down, net.before, net.has_before, net.high + step < self.count),
            ):
                sent = net.make(base + step, own, own, device)
                pl.when(jnp.logical_and(has, there))(sent.wait_send)


class Line:
    def __init__(self, net, count, value, passing, arrived):
        self.net, self.count, self.value = net, count, value
        self.passing, self.arrived = passing, arrived
        self.up, self.down = net.take(count), net.take(count)

    def upward(self, place):
        source, target = self.passing.at[place], self.arrived.at[place + 1]
        return self.net.make(self.up + place, source, target, self.net.after)

    def downward(self, place):
        source, target = self.passing.at[place], self.arrived.at[place]
        return self.net.make(self.down + place, source, target, self.net.before)

    def send(self, place, above):
        net = self.net
        value = self.value(place)
        self.passing[place] = value.astype(BF)
        move = self.upward(place) if above else self.downward(place)

        def add():
            move.wait_recv()
            landed = self.arrived[place + 1 if above else place]
            self.passing[place] = (value + landed.astype(F32)).astype(BF)

        pl.when(net.has_before if above else net.has_after)(add)
        move.start()

    def forward(self, point, points):
        high, last = self.net.high, self.count - 1
        for slot in range(last):
            if slot * points // last == point:
                pl.when(high <= slot)(functools.partial(self.send, last - slot + high, True))
                pl.when(last - high <= slot)(functools.partial(self.send, slot - last + high, False))

    def finish(self, total):
        net = self.net
        total[...] = self.value(net.high)

        def add(move, place):
            move.wait_recv()
            total[...] += self.arrived[place].astype(F32)

        pl.when(net.has_before)(lambda: add(self.upward(net.high), net.high + 1))
        pl.when(net.has_after)(lambda: add(self.downward(net.high), net.high))

    def drain(self):
        for place in range(self.count):
            pl.when(self.net.high < place)(self.upward(place).wait_send)
            pl.when(self.net.high > place)(self.downward(place).wait_send)


def part_scratch(count, shard, width):
    half = count // 2
    return [pltpu.VMEM((half, shard, width), BF)] * 3 + [pltpu.VMEM((half + 1, shard, width), BF)]


class ScatterParts:
    def __init__(self, net, moves, grads, scratch):
        self.net, self.moves = net, moves
        self.own, self.landed, passing, arrived = scratch
        self.count = count = grads.shape[0] // 2
        self.across, self.loads = net.take(count), moves.take(count)
        high, last = net.high, count - 1

        def start(place):
            self.swap(place, grads.at[place * 2 + 1 - net.low]).start()

        for slot in range(last):
            pl.when(high <= slot)(functools.partial(start, last - slot + high))
            pl.when(last - high <= slot)(functools.partial(start, slot - last + high))
        start(high)
        for place in range(count):
            source = grads.at[place * 2 + net.low]
            moves.make(self.loads + place, source, self.own.at[place]).start()
        self.line = Line(net, count, self.pair, passing, arrived)
        self.forward = self.line.forward

    def swap(self, place, source=None):
        target = self.landed.at[place]
        source = target if source is None else source
        return self.net.make(self.across + place, source, target, self.net.half)

    def pair(self, place):
        own = self.own.at[place]
        self.moves.make(self.loads + place, own, own).wait()
        self.swap(place).wait_recv()
        return self.own[place].astype(F32) + self.landed[place].astype(F32)

    def finish(self, total):
        self.line.finish(total)
        self.line.drain()
        for place in range(self.count):
            self.swap(place).wait_send()


class Across:
    def __init__(self, net, moves, part, scratch):
        self.net, self.part = net, part
        self.own, self.landed = scratch
        self.load = moves.load(part.at[net.low], self.own)

    def start(self):
        self.copy = self.net.copy(self.part.at[1 - self.net.low], self.landed, self.net.half)

    def finish(self, total):
        self.load.wait()
        self.copy.wait_recv()
        total[...] = self.own[...].astype(F32) + self.landed[...].astype(F32)


def across_scratch(part):
    return [pltpu.VMEM(part.shape[1:], BF)] * 2


def run(kernel, name, duration, inputs, outputs, scratch, identity, copies, moves):
    def space(near):
        return pl.BlockSpec(memory_space=pltpu.VMEM if near else pl.ANY)

    return pl.pallas_call(
        kernel,
        name=name,
        cost_estimate=micros(duration),
        out_shape=[jax.ShapeDtypeStruct(shape, dtype) for shape, dtype, _ in outputs],
        in_specs=[space(near) for _, near in inputs],
        out_specs=[space(near) for _, _, near in outputs],
        scratch_shapes=list(scratch)
        + [
            pltpu.SemaphoreType.DMA((copies,)),
            pltpu.SemaphoreType.DMA((copies,)),
            pltpu.SemaphoreType.DMA((moves,)),
        ],
        compiler_params=pltpu.CompilerParams(
            collective_id=identity, has_side_effects=True, vmem_limit_bytes=VMEM_LIMIT
        ),
    )(*[array for array, _ in inputs])


def split_refs(refs, inputs, outputs):
    return refs[:inputs], refs[inputs : inputs + outputs], refs[inputs + outputs :]


def norm_parts(rows):
    centred = rows - jnp.mean(rows, axis=1, keepdims=True)
    inverse = lax.rsqrt(jnp.mean(centred * centred, axis=1, keepdims=True) + EPS)
    return centred * inverse, inverse


def norm_back(rows, gain, grad):
    scaled, inverse = norm_parts(rows)
    inner = grad * gain
    first = jnp.mean(inner, axis=1, keepdims=True)
    second = jnp.mean(inner * scaled, axis=1, keepdims=True)
    return (
        inverse * (inner - first - scaled * second),
        jnp.sum(grad * scaled, axis=0, keepdims=True),
        jnp.sum(grad, axis=0, keepdims=True),
    )


def gather_send(net, full, chunk):
    near = net.copy(full.at[0, chunk], full.at[1, chunk], net.core)
    far = net.copy(full.at[0, chunk], full.at[2, chunk], net.far)
    return near, far


def gather_pass(net, full, chunk, far):
    far.wait_recv()
    return net.copy(full.at[2, chunk], full.at[3, chunk], net.core)


def scatter_scratch(rows, width):
    return [
        pltpu.VMEM((rows, width), F32),
        pltpu.VMEM((rows, width), F32),
    ] + [pltpu.VMEM((rows, width), BF)] * 6


class Scatter:
    def __init__(self, net, scratch):
        self.net = net
        self.hold, self.total, self.cs0, self.cr0, self.ys, self.yr, self.cs1, self.cr1 = scratch
        self.first, self.second = {}, {}

    def far_part(self, key, chunk, partial):
        rows = partial.shape[0] // 2
        self.hold[chunk] = partial[:rows]
        self.cs0[chunk] = partial[rows:].astype(BF)
        self.first[key] = self.net.copy(self.cs0.at[chunk], self.cr0.at[chunk], self.net.core)

    def far_send(self, key, chunk):
        self.first[key].wait_recv()
        self.ys[chunk] = (self.hold[chunk] + self.cr0[chunk].astype(F32)).astype(BF)
        self.second[key] = self.net.copy(self.ys.at[chunk], self.yr.at[chunk], self.net.far)

    def near_part(self, partial):
        rows = partial.shape[0] // 2
        self.total[...] = partial[:rows]
        self.cs1[...] = partial[rows:].astype(BF)
        self.near = self.net.copy(self.cs1, self.cr1, self.net.core)

    def near_done(self):
        self.near.wait_recv()
        self.total[...] += self.cr1[...].astype(F32)

    def result(self, key, chunk):
        self.second[key].wait_recv()
        return self.total[chunk] + self.yr[chunk].astype(F32)


def blocked(value):
    return value.astype(BF).reshape(2, value.shape[0] // 2, value.shape[1])


def chunks_of(rows, count):
    step = rows // count
    return [pl.ds(index * step, step) for index in range(count)]


def weight_grad(left, right, out, extra=None):
    width = left.shape[2]
    tile = 384

    def one(index, carry):
        columns = pl.ds(pl.multiple_of(index * tile, tile), tile)
        result = dot(flat(left[:, :, columns]), flat(right[...]), TN)
        if extra is None:
            out[columns, :] = result.astype(out.dtype)
        else:
            start = out.shape[1] - extra.shape[1]
            join = result.shape[1] - start
            added = extra[columns, :]
            out[columns, :start] = result[:, :start].astype(out.dtype)
            both = result[:, start:] + added[:, :join].astype(F32)
            out[columns, start : start + join] = both.astype(out.dtype)
            out[columns, start + join :] = added[:, join:]
        return carry

    lax.fori_loop(0, width // tile, one, 0)


def packed_shape(rows, columns):
    return (2, rows // 2 * columns // LANES, LANES)


def pack_half(tiles, target):
    rows = tiles[0].shape[0]
    for index, tile in enumerate(tiles[:-1]):
        target[index * rows : (index + 1) * rows, :] = tile.astype(BF)
    tail = tiles[-1][:, : LANES // 2]
    both = jnp.concatenate([tail[: rows // 2], tail[rows // 2 :]], axis=1)
    target[(len(tiles) - 1) * rows :, :] = both.astype(BF)


def unpack_half(packed, rows):
    full = packed.shape[0] // rows
    tiles = [packed[index * rows : (index + 1) * rows] for index in range(full)]
    tail = packed[full * rows :]
    return tiles + [jnp.concatenate([tail[:, : LANES // 2], tail[:, LANES // 2 :]], axis=0)]


def project_kernel(*refs, layer, head_cols, factor, parts):
    (x_hbm, vec, bias, *mixed_hbm), outs, scratch = split_refs(refs, 3 + parts, 4)
    normed_out, queries_out, pairs_out, far_out = outs
    x, weight, normed, queries, pairs, far_pairs, send_sems, recv_sems, move_sems = scratch
    net, moves = Net(send_sems, recv_sems), Moves(move_sems)
    rows = x.shape[0]
    pair_cols = 2 * head_cols
    chunks = chunks_of(rows, 2)
    x_load = moves.load(x_hbm, x)
    columns = pl.ds(0, weight.shape[1])
    weight_load = load_weight(net, moves, mixed_hbm, columns, weight)
    net.barrier([net.core, net.far, net.half])
    x_load.wait()
    sent = []
    for chunk in chunks:
        scaled, _ = norm_parts(x[chunk, :])
        normed[0, chunk, :] = (scaled * vec[layer, 0:1] + vec[layer, 1:2]).astype(BF)
        sent.append(gather_send(net, normed, chunk))
    arrived = []
    weight_load.wait()

    def project(slots, chunk):
        result = dot(flat(normed[slots, chunk, :]), weight[...]) + bias[layer : layer + 1]
        shape = (slots.size, chunk.size, -1)
        halves = range(len(chunks)) if chunk.size == rows else [chunk.start // chunk.size]
        step = rows // len(chunks)
        for index in range(slots.size):
            for place, half in enumerate(halves):
                start = (index * len(halves) + place) * step
                part = result[start : start + step]
                tiles = [part[:, lane : lane + LANES] for lane in range(0, pair_cols, LANES)]
                pack_half(tiles, pairs.at[slots.start + index, half])
        halves = pl.ds(halves[0], len(halves))
        own = result[:, pair_cols : pair_cols + head_cols] * factor
        queries[slots, chunk, :] = own.astype(BF).reshape(shape)
        source, target = pairs.at[slots, halves], far_pairs.at[slots, halves]
        arrived.append(net.copy(source, target, net.half))

    whole = pl.ds(0, rows)
    project(pl.ds(0, 1), whole)
    for near, _ in sent:
        near.wait_recv()
    project(pl.ds(1, 1), whole)
    for chunk, (_, far) in zip(chunks, sent):
        gather_pass(net, normed, chunk, far).wait_recv()
        project(pl.ds(2, 2), chunk)
    moves.store(normed, normed_out)
    moves.store(queries, queries_out)
    moves.store(pairs, pairs_out)
    for one in arrived:
        one.wait_recv()
    moves.store(far_pairs, far_out)
    net.finish()
    moves.finish()


def project(layer, x, vec, bias, mixed, head_cols):
    rows, width = x.shape
    used = bias.shape[1]
    outputs = [
        ((4, rows, width), BF, False),
        ((4, rows, head_cols), BF, False),
        ((4,) + packed_shape(rows, 2 * head_cols), BF, False),
        ((4,) + packed_shape(rows, 2 * head_cols), BF, False),
    ]
    scratch = [pltpu.VMEM((rows, width), F32), pltpu.VMEM((width, used), BF)]
    scratch += [pltpu.VMEM(shape, dtype) for shape, dtype, _ in outputs]
    kernel = functools.partial(
        project_kernel,
        layer=layer,
        head_cols=head_cols,
        factor=HEAD_DIM ** (-0.5) * LOG2E,
        parts=len(mixed),
    )
    inputs = [(x, False), (vec, True), (bias, True)] + spaced(mixed)
    return run(kernel, "project", 40, inputs, outputs, scratch, 8 * layer, 12, 6 + weight_loads(mixed))


def pair_windows(width, lead=0):
    windows = []
    for first in range(lead, width - HEAD_DIM, 2 * HEAD_DIM):
        start = first // LANES * LANES
        size = min(2 * LANES, width - start)
        row = lax.broadcasted_iota(jnp.int32, (size, 2 * LANES), 0) + (start - first)
        lane = lax.broadcasted_iota(jnp.int32, (size, 2 * LANES), 1)
        second = lane >= LANES
        lane = jnp.where(second, lane - LANES, lane)
        match = row == jnp.where(second, lane + HEAD_DIM, lane)
        windows.append((start, size, jnp.logical_and(match, lane < HEAD_DIM).astype(BF)))
    return windows


def spread_heads(value, windows):
    heads = []
    for start, size, pick in windows:
        both = dot(value[:, start : start + size], pick).astype(BF)
        heads += [both[:, :LANES], both[:, LANES:]]
    return heads


def join_heads(heads, windows, width):
    tiles = [None] * (-(-width // LANES))
    for index, (start, size, pick) in enumerate(windows):
        both = jnp.concatenate(heads[2 * index : 2 * index + 2], axis=1)
        part = dot(both, pick, NT)
        for lane in range(0, size, LANES):
            tile, piece = (start + lane) // LANES, part[:, lane : lane + LANES]
            tiles[tile] = piece if tiles[tile] is None else tiles[tile] + piece
    return jnp.concatenate(tiles, axis=1)


def as_rows(columns):
    rows = columns[0].shape[0]
    lane = lax.broadcasted_iota(jnp.int32, (rows, LANES), 1)
    together = jnp.zeros((rows, LANES), F32)
    for head, column in enumerate(columns):
        together = jnp.where(lane == head, column, together)
    return together.T[:8]


def load_pairs(meta, own_pairs, far_pairs, key_marks, key_scratch, value_scratch, heads):
    rows = 2 * (own_pairs.shape[2] * LANES // (2 * heads * HEAD_DIM))
    hid, half = meta[0], meta[1]
    windows = pair_windows(2 * heads * HEAD_DIM)
    for which, source in ((0, own_pairs), (1, far_pairs)):
        for slot in range(4):
            place = jnp.bitwise_xor(half, which) * 4 + jnp.bitwise_xor(hid, slot)
            start = pl.ds(pl.multiple_of(place * rows, rows), rows)
            marks = key_marks[start, :]
            halves = [unpack_half(source[slot, index], rows // 2) for index in range(2)]
            tiles = [jnp.concatenate(both, axis=0) for both in zip(*halves)]
            spread = spread_heads(jnp.concatenate(tiles, axis=1), windows)
            for head in range(heads):
                key_scratch[head, start, :] = spread[head] + marks
                value_scratch[head, start, :] = spread[heads + head]


def attend_kernel(
    meta, queries, own_pairs, far_pairs, query_marks, key_marks, mixture, logsum,
    key_scratch, value_scratch, score_scratch, high_scratch, total_scratch, sum_scratch, query_scratch,
    *, heads
):
    rows = queries.shape[1]
    head_cols = heads * HEAD_DIM
    load_pairs(meta, own_pairs, far_pairs, key_marks, key_scratch, value_scratch, heads)
    query_windows = pair_windows(head_cols)
    mixed_windows = pair_windows(mixture.shape[2], mixture.shape[2] - head_cols)

    def one_block(block, carry):
        slot = jnp.bitwise_xor(meta[0], block)
        first, last = meta[2 + 2 * block], meta[3 + 2 * block]
        own = pl.ds(pl.multiple_of(block * rows, rows), rows)
        marks = query_marks[own, :]
        for head, query in enumerate(spread_heads(queries[slot], query_windows)):
            query_scratch[head] = query + marks
        high_scratch[...] = jnp.full_like(high_scratch, -3e38)
        sum_scratch[...] = jnp.zeros_like(sum_scratch)
        total_scratch[...] = jnp.zeros_like(total_scratch)

        def scores_of(key_block, inner):
            keys = pl.ds(pl.multiple_of(key_block * KEYS, KEYS), KEYS)
            for head in range(heads):
                scores = dot(query_scratch[head], key_scratch[head, keys, :], NT)
                score_scratch[head, :, keys] = scores
                high = high_scratch[head]
                for lane in range(0, KEYS, LANES):
                    high = jnp.maximum(high, scores[:, lane : lane + LANES])
                high_scratch[head] = high
            return inner

        lax.fori_loop(first, last, scores_of, 0)
        for head in range(heads):
            high_scratch[head] = jnp.broadcast_to(
                jnp.max(high_scratch[head], axis=1, keepdims=True), (rows, LANES)
            )

        def sums_of(key_block, inner):
            keys = pl.ds(pl.multiple_of(key_block * KEYS, KEYS), KEYS)
            for head in range(heads):
                high = high_scratch[head]
                high = jnp.concatenate([high] * (KEYS // LANES), axis=1)
                powers = jnp.exp2(score_scratch[head, :, keys] - high)
                total = total_scratch[head]
                for lane in range(0, KEYS, LANES):
                    total += powers[:, lane : lane + LANES]
                total_scratch[head] = total
                sum_scratch[head] += dot(powers.astype(BF), value_scratch[head, keys, :])
            return inner

        lax.fori_loop(first, last, sums_of, 0)
        mixed, columns = [], []
        for head in range(heads):
            total = jnp.sum(total_scratch[head], axis=1, keepdims=True)
            columns.append(high_scratch[head][:, :1] + jnp.log2(total))
            mixed.append((sum_scratch[head] / total).astype(BF))
        mixture[slot] = join_heads(mixed, mixed_windows, mixture.shape[2]).astype(BF)
        logsum[:, own] = as_rows(columns)
        return carry

    lax.fori_loop(0, 4, one_block, 0)


def attend(meta, queries, own_pairs, far_pairs, query_marks, key_marks, lead):
    _, rows, head_cols = queries.shape
    heads = head_cols // HEAD_DIM
    own, count = 4 * rows, 8 * rows
    space = pl.BlockSpec(memory_space=pltpu.VMEM)
    return pl.pallas_call(
        functools.partial(attend_kernel, heads=heads),
        name="attend",
        cost_estimate=micros(22),
        out_shape=[
            jax.ShapeDtypeStruct((4, rows, lead + head_cols), BF),
            jax.ShapeDtypeStruct((8, own), F32),
        ],
        in_specs=[pl.BlockSpec(memory_space=pltpu.SMEM)] + [space] * 5,
        out_specs=[space] * 2,
        scratch_shapes=[
            pltpu.VMEM((heads, count, LANES), BF),
            pltpu.VMEM((heads, count, LANES), BF),
            pltpu.VMEM((heads, rows, count), F32),
            pltpu.VMEM((heads, rows, LANES), F32),
            pltpu.VMEM((heads, rows, LANES), F32),
            pltpu.VMEM((heads, rows, LANES), F32),
            pltpu.VMEM((heads, rows, LANES), BF),
        ],
        compiler_params=pltpu.CompilerParams(vmem_limit_bytes=VMEM_LIMIT),
    )(meta, queries, own_pairs, far_pairs, query_marks, key_marks)


def attend_back_kernel(
    meta, queries, own_pairs, far_pairs, query_marks, key_marks, grad_mixture, logsum,
    grad_queries, grad_own, grad_far,
    key_scratch, value_scratch, grad_key, grad_value, grad_query, query_scratch, grad_scratch,
    prob_scratch, grad_prob_scratch, delta_scratch,
    *, heads
):
    rows = queries.shape[1]
    head_cols = heads * HEAD_DIM
    load_pairs(meta, own_pairs, far_pairs, key_marks, key_scratch, value_scratch, heads)
    query_windows = pair_windows(head_cols)
    mixed_windows = pair_windows(grad_mixture.shape[2], grad_mixture.shape[2] - head_cols)
    grad_key[...] = jnp.zeros_like(grad_key)
    grad_value[...] = jnp.zeros_like(grad_value)

    def one_block(block, carry):
        slot = jnp.bitwise_xor(meta[0], block)
        first, last = meta[2 + 2 * block], meta[3 + 2 * block]
        own = pl.ds(pl.multiple_of(block * rows, rows), rows)
        marks = query_marks[own, :]
        for head, query in enumerate(spread_heads(queries[slot], query_windows)):
            query_scratch[head] = query + marks
        for head, grad in enumerate(spread_heads(grad_mixture[slot], mixed_windows)):
            grad_scratch[head] = grad
        logs = logsum[:, own]
        grad_query[...] = jnp.zeros_like(grad_query)
        delta_scratch[...] = jnp.zeros_like(delta_scratch)

        def probs_of(key_block, inner):
            keys = pl.ds(pl.multiple_of(key_block * KEYS, KEYS), KEYS)
            for head in range(heads):
                grad = grad_scratch[head]
                scores = dot(key_scratch[head, keys, :], query_scratch[head], NT)
                probs = jnp.exp2(scores - logs[head : head + 1])
                grad_probs = dot(value_scratch[head, keys, :], grad, NT)
                prob_scratch[head, keys, :] = probs
                grad_prob_scratch[head, keys, :] = grad_probs
                delta_scratch[head] += jnp.sum((probs * grad_probs).reshape(KEYS // 8, 8, rows), axis=0)
                grad_value[head, keys, :] += dot(probs.astype(BF), grad)
            return inner

        lax.fori_loop(first, last, probs_of, 0)
        for head in range(heads):
            delta_scratch[head, 0:1] = jnp.sum(delta_scratch[head], axis=0, keepdims=True)

        def one_key(key_block, inner):
            keys = pl.ds(pl.multiple_of(key_block * KEYS, KEYS), KEYS)
            for head in range(heads):
                delta = delta_scratch[head, 0:1]
                grad_scores = prob_scratch[head, keys, :] * (grad_prob_scratch[head, keys, :] - delta)
                grad_scores = grad_scores.astype(BF)
                grad_key[head, keys, :] += dot(grad_scores, query_scratch[head])
                grad_query[head] += dot(grad_scores, key_scratch[head, keys, :], TN)
            return inner

        lax.fori_loop(first, last, one_key, 0)
        real = lax.broadcasted_iota(jnp.int32, (rows, LANES), 1) < HEAD_DIM
        scaled = [
            jnp.where(real, grad_query[head] * HEAD_DIM ** (-0.5), 0.0).astype(BF)
            for head in range(heads)
        ]
        grad_queries[slot] = join_heads(scaled, query_windows, head_cols).astype(BF)
        return carry

    lax.fori_loop(0, 4, one_block, 0)
    hid, half = meta[0], meta[1]
    for which, target in ((0, grad_own), (1, grad_far)):
        for slot in range(4):
            place = jnp.bitwise_xor(half, which) * 4 + jnp.bitwise_xor(hid, slot)
            start = pl.ds(pl.multiple_of(place * rows, rows), rows)
            parts = [(grad_key[head, start, :] * LN2).astype(BF) for head in range(heads)]
            parts += [grad_value[head, start, :].astype(BF) for head in range(heads)]
            joined = join_heads(parts, pair_windows(2 * head_cols), 2 * head_cols)
            for index in range(2):
                part = joined[index * (rows // 2) : (index + 1) * (rows // 2)]
                tiles = [part[:, lane : lane + LANES] for lane in range(0, 2 * head_cols, LANES)]
                pack_half(tiles, target.at[slot, index])


def attend_back(
    meta, queries, own_pairs, far_pairs, query_marks, key_marks, grad_mixture, logsum
):
    _, rows, head_cols = queries.shape
    heads = head_cols // HEAD_DIM
    count = 8 * rows
    space = pl.BlockSpec(memory_space=pltpu.VMEM)
    return pl.pallas_call(
        functools.partial(attend_back_kernel, heads=heads),
        name="attend_back",
        cost_estimate=micros(37),
        out_shape=[
            jax.ShapeDtypeStruct((4, rows, head_cols), BF),
            jax.ShapeDtypeStruct(own_pairs.shape, BF),
            jax.ShapeDtypeStruct(own_pairs.shape, BF),
        ],
        in_specs=[pl.BlockSpec(memory_space=pltpu.SMEM)] + [space] * 7,
        out_specs=[space] * 3,
        scratch_shapes=[
            pltpu.VMEM((heads, count, LANES), BF),
            pltpu.VMEM((heads, count, LANES), BF),
            pltpu.VMEM((heads, count, LANES), F32),
            pltpu.VMEM((heads, count, LANES), F32),
            pltpu.VMEM((heads, rows, LANES), F32),
            pltpu.VMEM((heads, rows, LANES), BF),
            pltpu.VMEM((heads, rows, LANES), BF),
            pltpu.VMEM((heads, count, rows), F32),
            pltpu.VMEM((heads, count, rows), F32),
            pltpu.VMEM((heads, 8, rows), F32),
        ],
        compiler_params=pltpu.CompilerParams(vmem_limit_bytes=VMEM_LIMIT),
    )(meta, queries, own_pairs, far_pairs, query_marks, key_marks, grad_mixture, logsum)


def mlp_kernel(*refs, layer, parts, last):
    ins, outs, scratch = split_refs(refs, 4 + sum(parts), 5 - last)
    mixture_hbm, x_hbm, vec, up_bias = ins[:4]
    mixed_hbm, up_hbm, down_hbm = split_refs(ins[4:], parts[0], parts[1])
    after_out, normed_out, active_out, slope_out = outs[:4]
    mixture, x, out_weight, up_weight, down_weight, after, normed, active, slope, x_next = scratch[:10]
    first_scratch, second_scratch = scratch[10:18], scratch[18:26]
    send_sems, recv_sems, move_sems = scratch[26:]
    net, moves = Net(send_sems, recv_sems), Moves(move_sems)
    rows = x.shape[0]
    hidden_cols = up_weight.shape[1]
    out_cols = out_weight.shape[1]
    chunks = chunks_of(rows, 4)
    out_part = pl.ds(x.shape[1] - out_cols, out_cols)
    loads = [
        moves.load(mixture_hbm, mixture), load_weight(net, moves, mixed_hbm, out_part, out_weight),
    ]
    x_load = moves.load(x_hbm, x)
    up_load = load_weight(net, moves, up_hbm, pl.ds(0, hidden_cols), up_weight)
    if not last:
        down_load = load_weight(net, moves, down_hbm, pl.ds(0, hidden_cols), down_weight)
    net.barrier([net.core, net.far])
    out_bias, gain = vec[layer, 2:3], vec[layer, 3:4]
    shift, down_bias = vec[layer, 4:5], vec[layer, 5:6]

    def mixed(slots, chunk):
        return dot(flat(mixture[slots, chunk, :]), out_weight[...], NT)

    def up(slots, chunk):
        hidden = dot(flat(normed[slots, chunk, :]), up_weight[...]) + up_bias[layer : layer + 1]
        square = hidden * hidden
        bend = jnp.tanh(GELU * hidden * (1.0 + CUBE * square))
        half = 0.5 * (1.0 + bend)
        value = hidden * half
        rise = half + 0.5 * hidden * (1.0 - bend * bend) * GELU * (1.0 + 3.0 * CUBE * square)
        active[slots, chunk, :] = blocked(value)
        slope[slots, chunk, :] = blocked(rise)

    def down(slots, chunk):
        return dot(flat(active[slots, chunk, :]), down_weight[...], NT)

    near, far, whole = pl.ds(0, 2), pl.ds(2, 2), pl.ds(0, rows)
    for load in loads:
        load.wait()
    first = Scatter(net, first_scratch)
    for key, chunk in enumerate(chunks):
        first.far_part(key, chunk, mixed(far, chunk))
    for key, chunk in enumerate(chunks):
        first.far_send(key, chunk)
    first.near_part(mixed(near, whole))
    first.near_done()
    x_load.wait()
    sent = []
    for key, chunk in enumerate(chunks):
        residual = first.result(key, chunk) + x[chunk, :] + out_bias
        after[chunk, :] = residual
        normed[0, chunk, :] = (norm_parts(residual)[0] * gain + shift).astype(BF)
        sent.append(gather_send(net, normed, chunk))
    moves.store(after, after_out)
    for one, _ in sent:
        one.wait_recv()
    up_load.wait()
    up(near, whole)
    if not last:
        down_load.wait()
    second = Scatter(net, second_scratch)
    for key, chunk in enumerate(chunks):
        passed = gather_pass(net, normed, chunk, sent[key][1])
        passed.wait_recv()
        up(far, chunk)
        if not last:
            second.far_part(key, chunk, down(far, chunk))
            second.far_send(key, chunk)
    moves.store(normed, normed_out)
    moves.store(active, active_out)
    moves.store(slope, slope_out)
    if not last:
        second.near_part(down(near, whole))
        second.near_done()
        for key, chunk in enumerate(chunks):
            x_next[chunk, :] = second.result(key, chunk) + after[chunk, :] + down_bias
        moves.store(x_next, outs[4])
    net.finish()
    moves.finish()


def mlp(layer, mixture, x, vec, up_bias, mixed, up, down, last):
    rows, width = x.shape
    hidden = up_bias.shape[1]
    outputs = [
        ((rows, width), F32, False),
        ((4, rows, width), BF, False),
        ((4, rows, hidden), BF, False),
        ((4, rows, hidden), BF, False),
        ((rows, width), F32, False),
    ]
    scratch = [
        pltpu.VMEM(mixture.shape, BF),
        pltpu.VMEM((rows, width), F32),
        pltpu.VMEM((width, mixture.shape[2]), BF),
        pltpu.VMEM((width, hidden), BF),
        pltpu.VMEM((width, hidden), BF),
    ]
    scratch += [pltpu.VMEM(shape, dtype) for shape, dtype, _ in outputs]
    scratch += scatter_scratch(rows, width) * 2
    outputs = outputs[: 5 - last]
    down = () if last else down
    inputs = [(mixture, False), (x, False), (vec, True), (up_bias, True)]
    inputs += spaced([*mixed, *up, *down])
    parts = (len(mixed), len(up), len(down))
    kernel = functools.partial(mlp_kernel, layer=layer, parts=parts, last=last)
    moves = 8 + sum(weight_loads(part) for part in (mixed, up, down) if part)
    return run(kernel, "mlp", 48, inputs, outputs, scratch, 8 * layer + 1, 32, moves)


def mlp_back_kernel(*refs, layer, parts, given, shard, crossing):
    ins, outs, scratch = split_refs(
        refs, 7 + given + sum(parts) + crossing, 7 + (shard > 0) + crossing
    )
    gradient_hbm, after_hbm, vec, mixture_hbm, normed_hbm, active_hbm, slope_hbm = ins[:7]
    weights = ins[7 + given : 7 + given + sum(parts)]
    mixed_hbm, up_hbm, down_hbm = split_refs(weights, parts[0], parts[1])
    after_out, mixture_out, down_out, out_out, sums, hidden_sums = outs[:6]
    up_outs = outs[6 : 7 + (shard > 0)]
    gradient, after, out_weight, up_weight, down_weight, mixture, normed, active, slope = scratch[:9]
    grad_after, grad_mixture, grad_down, grad_up, grad_out = scratch[9:14]
    grad_rows, grad_hidden, grad_mid = scratch[14:17]
    scatter_refs, across_refs = scratch[17:25], scratch[25:-3]
    send_sems, recv_sems, move_sems = scratch[-3:]
    net, moves = Net(send_sems, recv_sems), Moves(move_sems)
    rows, width = gradient.shape
    hidden_cols = up_weight.shape[1]
    out_cols = out_weight.shape[1]
    chunks = chunks_of(rows, 2)
    out_part = pl.ds(width - out_cols, out_cols)
    load_gradient = moves.load(ins[7] if given else gradient_hbm, grad_rows if given else gradient)
    load_down = load_weight(net, moves, down_hbm, pl.ds(0, hidden_cols), down_weight)
    load_slope = moves.load(slope_hbm, slope)
    load_up = load_weight(net, moves, up_hbm, pl.ds(0, hidden_cols), up_weight)
    load_active = moves.load(active_hbm, active)
    load_after = moves.load(after_hbm, after)
    load_normed = moves.load(normed_hbm, normed)
    load_out = load_weight(net, moves, mixed_hbm, out_part, out_weight)
    load_mixture = moves.load(mixture_hbm, mixture)
    if given:
        load_own = moves.load(gradient_hbm, gradient)
    across = Across(net, moves, ins[-1], across_refs) if crossing else None
    net.barrier([net.core, net.far] + ([net.half] if crossing else []))
    if crossing:
        across.start()
    gain = vec[layer, 3:4]
    near, far, whole = pl.ds(0, 2), pl.ds(2, 2), pl.ds(0, rows)
    load_gradient.wait()
    if not given:
        grad_rows[0] = gradient[...].astype(BF)
        sent = [gather_send(net, grad_rows, chunk) for chunk in chunks]
    sums[...] = jnp.zeros_like(sums)
    sums[5:6] = jnp.sum(grad_rows[0].astype(F32), axis=0, keepdims=True)

    def hidden_grad(slots, chunk):
        value = dot(flat(grad_rows[slots, chunk, :]), down_weight[...])
        value = value * flat(slope[slots, chunk, :]).astype(F32)
        grad_hidden[slots, chunk, :] = blocked(value)

    def up_back(slots, chunk):
        return dot(flat(grad_hidden[slots, chunk, :]), up_weight[...], NT)

    if not given:
        for one, _ in sent:
            one.wait_recv()
    load_down.wait()
    load_slope.wait()
    scatter = Scatter(net, scatter_refs)
    if given:
        for key, chunk in enumerate(chunks):
            hidden_grad(far, chunk)
            if key == 0:
                load_up.wait()
            scatter.far_part(key, chunk, up_back(far, chunk))
        for key, chunk in enumerate(chunks):
            scatter.far_send(key, chunk)
        hidden_grad(near, whole)
    else:
        hidden_grad(near, whole)
        load_up.wait()
        for key, chunk in enumerate(chunks):
            passed = gather_pass(net, grad_rows, chunk, sent[key][1])
            passed.wait_recv()
            hidden_grad(far, chunk)
            scatter.far_part(key, chunk, up_back(far, chunk))
            scatter.far_send(key, chunk)
    scatter.near_part(up_back(near, whole))
    load_active.wait()
    weight_grad(grad_rows, active, grad_down)
    moves.store(grad_down, down_out)
    scatter.near_done()
    load_after.wait()
    if given:
        load_own.wait()
    sent = []
    for key, chunk in enumerate(chunks):
        back, gain_sum, shift_sum = norm_back(after[chunk, :], gain, scatter.result(key, chunk))
        total = gradient[chunk, :] + back
        grad_after[chunk, :] = total
        rounded = total.astype(BF)
        grad_mid[0, chunk, :] = rounded
        sent.append(gather_send(net, grad_mid, chunk))
        sums[3:4] += gain_sum
        sums[4:5] += shift_sum
        sums[2:3] += jnp.sum(rounded.astype(F32), axis=0, keepdims=True)
    moves.store(grad_after, after_out)
    load_normed.wait()
    weight_grad(normed, grad_hidden, grad_up)
    store_halves(net, moves, grad_up, up_outs, shard)
    column = jnp.zeros((1, hidden_cols), F32)
    for slot in range(4):
        column += jnp.sum(grad_hidden[slot].astype(F32), axis=0, keepdims=True)
    hidden_sums[...] = column

    def mix_back(slots, chunk):
        value = dot(flat(grad_mid[slots, chunk, :]), out_weight[...])
        grad_mixture[slots, chunk, :] = blocked(value)

    for one, _ in sent:
        one.wait_recv()
    load_out.wait()
    mix_back(near, whole)
    for key, chunk in enumerate(chunks):
        gather_pass(net, grad_mid, chunk, sent[key][1]).wait_recv()
    mix_back(far, whole)
    moves.store(grad_mixture, mixture_out)
    load_mixture.wait()
    weight_grad(grad_mid, mixture, grad_out)
    moves.store(grad_out, out_out)
    if crossing:
        across.finish(outs[-1])
    net.finish()
    moves.finish()


def mlp_back(
    layer, gradient, after, vec, mixed, up, down, mixture, normed, active, slope, given=(),
    shard=0, crossing=(),
):
    rows, width = gradient.shape
    hidden = active.shape[2]
    out_cols = mixture.shape[2]
    outputs = [
        ((rows, width), F32, False),
        ((4, rows, out_cols), BF, False),
        ((width, hidden), BF, False),
        ((width, out_cols), BF, False),
        ((8, width), F32, True),
        ((1, hidden), F32, True),
    ]
    shapes = [
        ((rows, width), F32),
        ((rows, width), F32),
        ((width, out_cols), BF),
        ((width, hidden), BF),
        ((width, hidden), BF),
        ((4, rows, out_cols), BF),
        ((4, rows, width), BF),
        ((4, rows, hidden), BF),
        ((4, rows, hidden), BF),
        ((rows, width), F32),
        ((4, rows, out_cols), BF),
        ((width, hidden), BF),
        ((width, hidden), BF),
        ((width, out_cols), BF),
        ((4, rows, width), BF),
        ((4, rows, hidden), BF),
        ((4, rows, width), BF),
    ]
    outputs += half_outputs(width, hidden, shard)
    scratch = [pltpu.VMEM(shape, dtype) for shape, dtype in shapes] + scatter_scratch(rows, width)
    for part in crossing:
        outputs.append((part.shape[1:], F32, True))
        scratch += across_scratch(part)
    inputs = [
        (gradient, False), (after, False), (vec, True), (mixture, False), (normed, False),
        (active, False), (slope, False),
    ] + spaced([*given, *mixed, *up, *down, *crossing])
    parts = (len(mixed), len(up), len(down))
    kernel = functools.partial(
        mlp_back_kernel,
        layer=layer,
        parts=parts,
        given=len(given),
        shard=shard,
        crossing=len(crossing),
    )
    moves = 14 + (3 * width // (2 * shard) if shard else 0)
    moves += weight_loads(mixed) + weight_loads(up) + weight_loads(down)
    return run(kernel, "mlp_back", 48, inputs, outputs, scratch, 8 * layer + 2, 21, moves)


def project_back_kernel(*refs, layer, parts, closing, crossing):
    ins, outs, scratch = split_refs(
        refs, 8 + parts + closing + crossing, 4 + (closing > 0) + crossing
    )
    after_hbm, x_hbm, vec, normed_hbm, queries_hbm, own_hbm, far_hbm, out_hbm = ins[:8]
    mixed_hbm, closing_ins = ins[8 : 8 + parts], ins[8 + parts : 8 + parts + closing]
    gradient_out, sums, column_sums, weight_out = outs[:4]
    grad_after, x, weight, normed, grad_queries, grad_own, grad_out = scratch[:7]
    landed, together, gradient, grad_weight = scratch[7:11]
    scatter_refs, closing_refs = scratch[11:19], scratch[19 : -3 - 2 * crossing]
    across_refs = scratch[-3 - 2 * crossing : -3]
    send_sems, recv_sems, move_sems = scratch[-3:]
    net, moves = Net(send_sems, recv_sems), Moves(move_sems)
    rows, width = x.shape
    pair_cols = 2 * grad_queries.shape[2]
    used_cols = pair_cols + grad_queries.shape[2]
    all_cols = together.shape[2]
    chunks = chunks_of(rows, 2)
    near, far, whole = pl.ds(0, 2), pl.ds(2, 2), pl.ds(0, rows)
    load_own = moves.load(own_hbm, grad_own)
    load_queries = moves.load(queries_hbm, grad_queries)
    loading = load_weight(net, moves, mixed_hbm, pl.ds(0, all_cols), weight)
    load_normed = moves.load(normed_hbm, normed)
    load_out = moves.load(out_hbm, grad_out)
    load_x = moves.load(x_hbm, x)
    load_after = moves.load(after_hbm, grad_after)
    if closing:
        active, down_weight, after, final = closing_refs[:4]
        load_active = moves.load(closing_ins[0], active)
        load_after_two = moves.load(closing_ins[1], after)
        columns = pl.ds(0, down_weight.shape[1])
        load_down = load_weight(net, moves, closing_ins[2:], columns, down_weight)
    across = Across(net, moves, ins[-1], across_refs) if crossing else None
    net.barrier([net.core, net.far, net.half])
    arriving = {
        slot: net.copy(far_hbm.at[slot], landed.at[slot], net.half) for slot in (3, 2, 1, 0)
    }
    load_queries.wait()
    together[:, :, pair_cols:used_cols] = grad_queries[...]
    together[:, :, used_cols:] = jnp.zeros((4, rows, all_cols - used_cols), BF)
    load_own.wait()
    loading.wait()

    def join(slot):
        arriving[slot].wait_recv()
        for index in range(2):
            pair = grad_own[slot, index].astype(F32) + landed[slot, index].astype(F32)
            part = pl.ds(index * (rows // 2), rows // 2)
            for place, tile in enumerate(unpack_half(pair.astype(BF), rows // 2)):
                columns = pl.ds(place * LANES, tile.shape[1])
                together[slot, part, columns] = tile

    def back(slots, chunk):
        return dot(flat(together[slots, chunk, :]), weight[...], NT)

    if closing:

        def down(slots, chunk):
            return dot(flat(active[slots, chunk, :]), down_weight[...], NT)

        load_active.wait()
        load_down.wait()
        last = Scatter(net, closing_refs[4:])
        for key, chunk in enumerate(chunks):
            last.far_part(key, chunk, down(far, chunk))
        for key, chunk in enumerate(chunks):
            last.far_send(key, chunk)
        last.near_part(down(near, whole))
        last.near_done()
    scatter = Scatter(net, scatter_refs)
    join(3)
    join(2)
    for key, chunk in enumerate(chunks):
        scatter.far_part(key, chunk, back(far, chunk))
    for key, chunk in enumerate(chunks):
        scatter.far_send(key, chunk)
    join(1)
    join(0)
    if crossing:
        across.start()
    scatter.near_part(back(near, whole))
    load_normed.wait()
    load_out.wait()
    weight_grad(normed, together, grad_weight, grad_out)
    moves.store(grad_weight, weight_out)
    column = jnp.zeros((1, all_cols), F32)
    for slot in range(4):
        column += jnp.sum(together[slot].astype(F32), axis=0, keepdims=True)
    column_sums[...] = column
    scatter.near_done()
    sums[...] = jnp.zeros_like(sums)
    load_x.wait()
    load_after.wait()
    for key, chunk in enumerate(chunks):
        grad, gain_sum, shift_sum = norm_back(
            x[chunk, :], vec[layer, 0:1], scatter.result(key, chunk)
        )
        gradient[chunk, :] = grad_after[chunk, :] + grad
        sums[0:1] += gain_sum
        sums[1:2] += shift_sum
    moves.store(gradient, gradient_out)
    if closing:
        load_after_two.wait()
        for key, chunk in enumerate(chunks):
            final[chunk, :] = last.result(key, chunk) + after[chunk, :] + vec[layer, 5:6]
        moves.store(final, outs[4])
    if crossing:
        across.finish(outs[-1])
    net.finish()
    moves.finish()


def project_back(
    layer, grad_after, x, vec, mixed, normed, grad_queries, grad_own, grad_far, grad_out, all_cols,
    closing=(), crossing=(),
):
    rows, width = x.shape
    outputs = [
        ((rows, width), F32, False),
        ((8, width), F32, True),
        ((1, all_cols), F32, True),
        ((width, width), BF, False),
    ]
    shapes = [
        ((rows, width), F32),
        ((rows, width), F32),
        ((width, all_cols), BF),
        (normed.shape, BF),
        (grad_queries.shape, BF),
        (grad_own.shape, BF),
        (grad_out.shape, BF),
        (grad_far.shape, BF),
        ((4, rows, all_cols), BF),
        ((rows, width), F32),
        ((width, width), BF),
    ]
    scratch = [pltpu.VMEM(shape, dtype) for shape, dtype in shapes] + scatter_scratch(rows, width)
    copies, moves = 12, 9 + weight_loads(mixed)
    if closing:
        active, after, *down = closing
        outputs.append(((rows, width), F32, False))
        shapes = [
            (active.shape, BF), ((width, active.shape[2]), BF), ((rows, width), F32), ((rows, width), F32),
        ]
        scratch += [pltpu.VMEM(shape, dtype) for shape, dtype in shapes] + scatter_scratch(rows, width)
        copies, moves = 18, moves + 3 + weight_loads(down)
    for part in crossing:
        outputs.append((part.shape[1:], F32, True))
        scratch += across_scratch(part)
        copies, moves = copies + 1, moves + 1
    inputs = [
        (grad_after, False), (x, False), (vec, True), (normed, False), (grad_queries, False),
        (grad_own, False), (grad_far, False), (grad_out, False),
    ] + spaced([*mixed, *closing, *crossing])
    kernel = functools.partial(
        project_back_kernel, layer=layer, parts=len(mixed), closing=len(closing),
        crossing=len(crossing),
    )
    return run(kernel, "project_back", 42, inputs, outputs, scratch, 8 * layer + 3, copies, moves)


def entry_kernel(*refs):
    ins, outs, scratch = split_refs(refs, 12, 7)
    tokens, cotangent, value_bias, query_bias, up_bias, shard = ins[:6]
    x, gradient, grad_rows, vec, bias, hidden_bias, weights = outs
    vectors, token_land, cotangent_land, vector_land, send_sems, recv_sems, move_sems = scratch
    net, moves = Net(send_sems, recv_sems), Moves(move_sems)
    rows, cols = x.shape[0], tokens.shape[0]
    layers = vec.shape[0]
    others = [net.core, net.far, net.far_core]
    vectors[...] = jnp.zeros_like(vectors)
    for index, one in enumerate(ins[6:]):
        for layer in range(layers):
            vectors[layer * 8 + index : layer * 8 + index + 1] = one[layer : layer + 1]
    net.line(weights.shape[0] // 2)
    net.barrier(others + [net.half], True)
    gathering = GatherJob(net, moves, shard, weights)

    def block(hid):
        return pl.ds(pl.multiple_of(hid * rows, rows), rows)

    moved = [
        net.copy(tokens.at[:, block(device[1])], token_land.at[net.hid], device)
        for device in reversed(others)
    ]
    moved += [net.copy(vectors, vector_land.at[net.hid], device) for device in others]
    sent = []
    for chunk in chunks_of(4 * rows, 2):
        source, own = cotangent.at[:, chunk], cotangent_land.at[net.hid, :, chunk]
        moved.append(net.copy(source, own, net.core))
        sent.append((net.copy(source, own, net.far), cotangent_land.at[net.far[1], :, chunk]))
    token_land[net.hid] = tokens[:, block(net.hid)]
    cotangent_land[net.hid] = cotangent[...]
    vector_land[net.hid] = vectors[...]
    bias[...] = jnp.zeros_like(bias)
    bias[:, cols : 2 * cols] = value_bias[...]
    bias[:, 2 * cols : 3 * cols] = query_bias[...]
    hidden_bias[...] = jnp.zeros_like(hidden_bias)
    hidden_bias[:, : up_bias.shape[1]] = up_bias[...]
    gathering.forward(0, 3)
    for point, (one, landed) in enumerate(sent):
        one.wait_recv()
        moved.append(net.copy(landed, landed, net.core))
        gathering.forward(point + 1, 3)
    for one in moved:
        one.wait_recv()
    for place in range(4):
        columns = slice(place * cols, (place + 1) * cols)
        for layer in range(layers):
            vec[layer, :, columns] = vector_land[place, layer * 8 : layer * 8 + 8]
    x[...] = flat(token_land[...]).astype(F32).T
    for slot, device in enumerate([(net.tok, net.hid)] + others):
        whole = flat(cotangent_land[:, :, block(device[1])])
        grad_rows[slot] = whole.astype(F32).T.astype(BF)
    gradient[...] = grad_rows[0].astype(F32)
    gathering.finish()
    net.finish()
    moves.finish()


def entry(tokens, cotangent, value_bias, query_bias, up_bias, shard, vectors, count, used_cols):
    cols, rows = tokens.shape[0], tokens.shape[1] // 4
    layers, feed = up_bias.shape
    inputs = [
        (tokens, True), (cotangent, True), (value_bias, True), (query_bias, True), (up_bias, True),
        (shard, False),
    ] + [(one, True) for one in vectors]
    outputs = [
        ((rows, 4 * cols), F32, True),
        ((rows, 4 * cols), F32, True),
        ((4, rows, 4 * cols), BF, True),
        ((layers, 8, 4 * cols), F32, True),
        ((layers, used_cols), F32, True),
        ((layers, feed + -feed % LANES), F32, True),
        ((count,) + shard.shape, BF, False),
    ]
    scratch = [
        pltpu.VMEM((layers * 8, cols), F32),
        pltpu.VMEM((4, cols, rows), BF),
        pltpu.VMEM((4,) + cotangent.shape, BF),
        pltpu.VMEM((4, layers * 8, cols), F32),
    ]
    return run(entry_kernel, "entry", 50, inputs, outputs, scratch, 4, 12 + job_copies(count), 1)


def finish_kernel(*refs, layers):
    ins, outs, scratch = split_refs(refs, 4 + 4 * layers, 13)
    final_rows, gradient_rows, grads, down_grads = ins[:4]
    layer_sums = [ins[4 + 4 * layer : 8 + 4 * layer] for layer in range(layers)]
    final_out, gradient_out, total = outs[:3]
    wide_outs, query_out, value_out, hidden_out = outs[3:9], outs[9], outs[10], outs[11]
    down_total = outs[12]
    final, gradient, final_land, gradient_land = scratch[:4]
    sums, across_land, along, wide, wide_land = scratch[4:9]
    job_refs, across_refs = scratch[9:13], scratch[13:15]
    send_sems, recv_sems, move_sems = scratch[15:]
    net, moves = Net(send_sems, recv_sems), Moves(move_sems)
    count = grads.shape[0] // 2
    rows, cols, last = final_rows.shape[0], wide.shape[2], count - 1
    others = [net.core, net.far, net.far_core]
    top = layers * 8
    sums[top:] = jnp.zeros((sums.shape[0] - top, sums.shape[1]), F32)
    for layer, (one, two, column_sums, hidden) in enumerate(layer_sums):
        sums[layer * 8 : layer * 8 + 8] = one[...] + two[...]
        sums[top + layer : top + layer + 1, : column_sums.shape[1]] = column_sums[...]
        sums[top + layers + layer : top + layers + layer + 1, : hidden.shape[1]] = hidden[...]
    net.line(count)
    net.barrier(others + [net.half], True)
    swap = net.copy(sums, across_land, net.half)
    scattering = ScatterParts(net, moves, grads, job_refs)
    across = Across(net, moves, down_grads, across_refs)
    for target, source in ((final, final_rows), (gradient, gradient_rows)):
        target[...] = source[...].T.astype(BF).reshape(target.shape)
    moved = []
    for source, target in ((final, final_land), (gradient, gradient_land)):
        for device in reversed(others):
            moved.append(net.copy(source.at[device[1]], target.at[net.hid], device))
        target[net.hid] = source[net.hid]
    up, down = net.take(count), net.take(count)
    own = along.at[net.high]
    swap.wait()
    along[net.high] = sums[...] + across_land[...]
    pl.when(net.has_after)(net.make(up, own, own, net.after).start)
    pl.when(net.has_before)(net.make(down, own, own, net.before).start)

    def pass_on(step, place, base, device, has):
        block = along.at[place]
        net.make(base + step - 1, block, block, device).wait_recv()
        if step < last:
            pl.when(has)(net.make(base + step, block, block, device).start)

    def pass_sums(step):
        pl.when(net.high >= step)(
            functools.partial(pass_on, step, net.high - step, up, net.after, net.has_after)
        )
        pl.when(net.high + step < count)(
            functools.partial(pass_on, step, net.high + step, down, net.before, net.has_before)
        )

    for point in range(3):
        scattering.forward(point, 3)
        for step in range(1, count):
            if (step - 1) * 3 // last == point:
                pass_sums(step)
    across.start()
    reduced = along[0]
    for place in range(1, count):
        reduced += along[place]
    sums[...] = reduced
    for place in range(4):
        wide[place] = sums[:top, place * cols : (place + 1) * cols]
    wide_land[net.hid] = wide[net.hid]
    summed = [net.copy(wide.at[device[1]], wide_land.at[net.hid], device) for device in others]
    for one in moved:
        one.wait_recv()
    for source, target in ((final_land, final_out), (gradient_land, gradient_out)):
        for place in range(4):
            target[:, place * rows : (place + 1) * rows] = source[place].astype(F32)
    for one in summed:
        one.wait_recv()
    narrow = wide_land[0] + wide_land[1] + wide_land[2] + wide_land[3]
    for layer in range(layers):
        one = slice(layer, layer + 1)
        for index, out in enumerate(wide_outs):
            out[one, :] = narrow[layer * 8 + index : layer * 8 + index + 1]
        row = slice(top + layer, top + layer + 1)
        value_out[one, :] = sums[row, cols : 2 * cols]
        query_out[one, :] = sums[row, 2 * cols : 3 * cols]
        row = slice(top + layers + layer, top + layers + layer + 1)
        hidden_out[one, :] = sums[row, : hidden_out.shape[1]]
    for step in range(last):
        sent_up = jnp.logical_and(net.has_after, net.high >= step)
        sent_down = jnp.logical_and(net.has_before, net.high + step < count)
        pl.when(sent_up)(net.make(up + step, own, own, net.after).wait_send)
        pl.when(sent_down)(net.make(down + step, own, own, net.before).wait_send)
    scattering.finish(total)
    across.finish(down_total)
    net.finish([swap])


def finish(final, gradient, grads, down_grads, layer_sums, head_cols, feed):
    count, layers = grads.shape[0] // 2, len(layer_sums)
    rows, width = final.shape
    sum_cols = max(width, layer_sums[0][2].shape[1], layer_sums[0][3].shape[1])
    sums = (layers * 10 + -layers * 10 % 8, sum_cols)
    vector = ((layers, head_cols), F32, True)
    outputs = [
        ((head_cols, 4 * rows), F32, True),
        ((head_cols, 4 * rows), F32, True),
        (grads.shape[1:], F32, True),
    ] + [vector] * 8
    outputs += [((layers, feed), F32, True), (down_grads.shape[1:], F32, True)]
    blocks, wide = (4, head_cols, rows), (4, layers * 8, head_cols)
    scratch = [pltpu.VMEM(blocks, BF)] * 4 + [
        pltpu.VMEM(sums, F32),
        pltpu.VMEM(sums, F32),
        pltpu.VMEM((count,) + sums, F32),
        pltpu.VMEM(wide, F32),
        pltpu.VMEM(wide, F32),
    ]
    scratch += part_scratch(*grads.shape) + across_scratch(down_grads)
    inputs = [(final, True), (gradient, True), (grads, False), (down_grads, False)]
    inputs += [(one, True) for four in layer_sums for one in four]
    kernel = functools.partial(finish_kernel, layers=layers)
    return run(kernel, "finish", 2, inputs, outputs, scratch, 5, 13 + 5 * count, 2 + count)


def key_ranges(own_ids, row_ids, rows):
    blocks = own_ids.reshape(-1, rows)
    position = jnp.arange(row_ids.shape[0], dtype=jnp.int32)
    low = jnp.min(jnp.where(row_ids == blocks[:, :1], position, row_ids.shape[0]), axis=1)
    high = jnp.max(jnp.where(row_ids == blocks[:, -1:], position, -1), axis=1)
    return jnp.stack([low // KEYS, high // KEYS + 1], axis=1).reshape(-1)


def body(
    tokens, picture, cotangent, first_gain, first_shift, query_weight, query_bias, key_weight,
    value_weight, value_bias, output_weight, output_bias, second_gain, second_shift, up_weight,
    up_bias, down_weight, down_bias,
):
    token_count = tokens.shape[0]
    rows = token_count // 4
    layers = query_weight.shape[0]
    head_cols = query_bias.shape[1]
    feed = up_bias.shape[1]
    feed_pad = -feed % LANES
    feed_cols = feed + feed_pad
    hid = lax.axis_index("hid")
    tok = lax.axis_index("tok")
    count = lax.axis_size("tok")
    shard = query_weight.shape[1]
    shard_pad = -shard % 16
    width = count * shard
    lead = 3 * head_cols % LANES
    used_cols = 3 * head_cols + -3 * head_cols % LANES

    own_ids = lax.dynamic_slice_in_dim(picture, tok * token_count, token_count)
    row_ids = lax.dynamic_slice_in_dim(picture, (tok // 2) * 2 * token_count, 2 * token_count)
    place = jnp.stack([hid, tok % 2]).astype(jnp.int32)
    meta = jnp.concatenate([place, key_ranges(own_ids, row_ids, rows)])

    starts = jnp.concatenate([jnp.zeros(1, jnp.int32), (row_ids[1:] != row_ids[:-1]).astype(jnp.int32)])
    number = jnp.cumsum(starts)[:, None] + HEAD_DIM
    lane = lax.broadcasted_iota(jnp.int32, (row_ids.shape[0], LANES), 1)
    key_marks = jnp.where((lane == number) | (lane < HEAD_DIM), 0.0, MASKED).astype(BF)
    own_number = lax.dynamic_slice_in_dim(number, tok % 2 * token_count, token_count)
    query_marks = (lane[:token_count] == own_number).astype(BF)

    def side_by_side(*parts):
        return jnp.concatenate(parts, axis=1)

    def padded(part):
        return jnp.pad(part, ((0, 0), (0, feed_pad)))

    def shards(part):
        return jnp.pad(part, ((0, shard_pad), (0, 0)))

    def joined(gathered):
        return gathered[:, :shard].reshape(width, gathered.shape[2])

    def separate(grads):
        grads = grads.reshape(count, shard, grads.shape[1])
        return jnp.pad(grads, ((0, 0), (0, shard_pad), (0, 0)))

    mixed_parts = [
        shards(
            side_by_side(
                key_weight[layer], value_weight[layer], query_weight[layer], output_weight[layer].T
            )
        )
        for layer in range(layers)
    ]
    vectors = (first_gain, first_shift, output_bias, second_gain, second_shift, down_bias)
    x, gradient, grad_rows, vectors, bias, up_bias, mixed = entry(
        tokens.T, cotangent.T, value_bias, query_bias, up_bias, mixed_parts[0], vectors, count, used_cols
    )

    halves = [(place, place ^ 1) for place in range(count)]
    lines = [[place * 2 + low for place in range(count // 2)] for low in range(2)]

    def swap(part):
        return lax.ppermute(part, "tok", halves)

    def both_halves(own, other):
        first = tok % 2 == 0
        return jnp.stack([jnp.where(first, own, other), jnp.where(first, other, own)])

    def along(part):
        return lax.all_gather(part, "tok", axis=0, tiled=True, axis_index_groups=lines)

    def along_first(part):
        own = along(part)
        other = swap(own)
        parts = [rows_of.reshape(count // 2, shard, part.shape[1]) for rows_of in (own, other)]
        if shard % 16 == 0:
            return parts
        return [both_halves(*parts).transpose(1, 0, 2, 3).reshape(width, part.shape[1])]

    def hold(*values):
        return lax.optimization_barrier(values)

    def pair_rows(part, other):
        return both_halves(part, other).reshape(2 * shard, part.shape[1])

    def up_part(layer):
        return padded(up_weight[layer])

    def down_part(layer):
        return padded(down_weight[layer].T)

    ups, weights = [along_first(up_part(0))], [[joined(mixed)]]
    early = down_part(0)
    early, early_other, x = hold(early, swap(early), x)
    downs = [[along(pair_rows(early, early_other))]]
    for layer in range(1, layers):
        weights.append(along_first(mixed_parts[layer][:shard]))
        coming = up_part(layer)
        ups.append([along(pair_rows(coming, swap(coming)))])
    saved = []
    for layer in range(layers):
        mixed, up = weights[layer], ups[layer]
        more = layer + 1 < layers
        normed, queries, own_pairs, far_pairs = project(layer, x, vectors, bias, mixed, head_cols)
        if layer > 0:
            queries, coming, coming_other = hold(queries, coming, coming_other)
            downs.append([along(pair_rows(coming, coming_other))])
        mixture, logsum = attend(
            meta, queries, own_pairs, far_pairs, query_marks, key_marks, lead
        )
        if more:
            coming, mixture = hold(down_part(layer + 1), mixture)
            coming_other = swap(coming)
        after, normed_two, active, slope, *x_next = mlp(
            layer, mixture, x, vectors, up_bias, mixed, up, downs[layer], not more
        )
        saved.append(
            (x, normed, queries, own_pairs, far_pairs, mixture, logsum, after, normed_two, active, slope)
        )
        x = x_next[0] if x_next else None

    def by_halves(part):
        own = lax.dynamic_index_in_dim(part, tok % 2, 1, keepdims=False)
        other = lax.dynamic_index_in_dim(part, 1 - tok % 2, 1, keepdims=False)
        return own, other

    def sum_along(part):
        return lax.psum_scatter(
            part, "tok", scatter_dimension=0, tiled=True, axis_index_groups=lines
        )

    def halves_of(parts):
        if len(parts) == 1:
            part = parts[0].reshape(-1, 2, shard, parts[0].shape[1])
            parts = by_halves(part)
        return parts[0], swap(parts[1])

    def by_half(part):
        return jnp.pad(part.reshape(2, shard, part.shape[1]), ((0, 0), (0, shard_pad), (0, 0)))

    def added(own, other):
        return (own.astype(F32) + other.astype(F32)).astype(BF)

    def in_rows(part):
        return part.reshape(-1, part.shape[-1])

    split = shard if shard % 16 == 0 else 0
    mixed_grads, up_grads, down_grads = [None] * layers, [None] * layers, [None] * layers
    layer_sums = [None] * layers
    grads = final = None
    for layer in reversed(range(layers)):
        x, normed, queries, own_pairs, far_pairs, mixture, logsum, after, normed_two, active, slope = saved[layer]
        mixed, up, down = weights[layer], ups[layer], downs[layer]
        last = layer + 1
        crossing = ()
        if last < layers:
            gradient, down_grads[last] = hold(gradient, down_grads[last])
            crossing = (by_half(down_grads[last]),)
        grad_after, grad_mixture, grad_down, grad_out, sums_two, hidden_sums, *grad_up = mlp_back(
            layer, gradient, after, vectors, mixed, up, down, mixture, normed_two, active, slope,
            () if last < layers else (grad_rows,), split, crossing,
        )
        if last < layers:
            down_grads[last] = grad_up.pop()
            grad_down, up_grads[last] = hold(grad_down, up_grads[last])
        down_grads[layer] = sum_along(grad_down)
        up_own, up_other = halves_of(grad_up)
        grad_queries, grad_own, grad_far = attend_back(
            meta, queries, own_pairs, far_pairs, query_marks, key_marks, grad_mixture, logsum
        )
        up_other, grad_far = hold(up_other, grad_far)
        up_grad = added(up_own, up_other)
        crossing = ()
        if last < layers:
            grad_after, mixed_grads[last] = hold(grad_after, mixed_grads[last])
            crossing = (by_half(mixed_grads[last]),)
        grad_after, up_grad = hold(grad_after, up_grad)
        up_grads[layer] = sum_along(in_rows(up_grad))
        gradient, sums_one, column_sums, grads, *closed = project_back(
            layer, grad_after, x, vectors, mixed, normed, grad_queries, grad_own, grad_far,
            grad_out, used_cols, () if last < layers else (active, after, *down), crossing,
        )
        if last < layers:
            mixed_grads[last] = closed.pop()
        final = closed[0] if closed else final
        if layer > 0:
            mixed_grads[layer] = sum_along(grads)
        layer_sums[layer] = (sums_one, sums_two, column_sums, hidden_sums)
    gradient, down_grads[0] = hold(gradient, down_grads[0])
    final, gradient, mixed_grads[0], *small = finish(
        final, gradient, separate(grads), by_half(down_grads[0]), layer_sums, head_cols, feed
    )
    up_grads[0], final, gradient, mixed_grads[0], *small = hold(
        up_grads[0], final, gradient, mixed_grads[0], *small
    )
    down_grads[0] = small.pop()
    first_gain, first_shift, output_bias, second_gain, second_shift, down_bias = small[:6]
    query_bias, value_bias, up_bias = small[6:]

    def mixed_columns(start):
        columns = slice(start * head_cols, (start + 1) * head_cols)
        return jnp.stack([part[:shard, columns].astype(F32) for part in mixed_grads])

    def hidden_columns(parts):
        return jnp.stack([part[:shard, :feed].astype(F32) for part in parts])

    return (
        final.T,
        gradient.T,
        first_gain,
        first_shift,
        mixed_columns(2),
        query_bias,
        mixed_columns(0),
        mixed_columns(1),
        value_bias,
        mixed_columns(3).transpose(0, 2, 1),
        output_bias,
        second_gain,
        second_shift,
        hidden_columns(up_grads),
        up_bias,
        hidden_columns(down_grads).transpose(0, 2, 1),
        down_bias,
    )


def solution(mesh):
    rows = P("tok", "hid")
    vector = P(None, "hid")
    inward = P(None, "tok", "hid")
    outward = P(None, "hid", "tok")
    in_specs = (
        rows, P(), rows, vector, vector, inward, vector, inward, inward, vector, outward, vector,
        vector, vector, inward, vector, outward, vector,
    )
    out_specs = (
        rows, rows, vector, vector, inward, vector, inward, inward, vector, outward, vector,
        vector, vector, inward, vector, outward, vector,
    )
    return jax.shard_map(body, mesh=mesh, in_specs=in_specs, out_specs=out_specs, check_vma=False)
```

```python
import functools

import jax
import jax.numpy as jnp
from jax import lax
from jax.experimental import pallas as pl
from jax.experimental.pallas import tpu as pltpu
from jax.sharding import PartitionSpec as P

HEAD_DIM = 72
LANES = 128
KEYS = 512
EPS = 1e-06
GELU = 0.7978845608028654
CUBE = 0.044715
MASKED = -1e30
LOG2E = 1.4426950408889634
LN2 = 0.6931471805599453
NN = (((1,), (0,)), ((), ()))
NT = (((1,), (1,)), ((), ()))
TN = (((0,), (0,)), ((), ()))
MESH = pl.DeviceIdType.MESH
BF = jnp.bfloat16
F32 = jnp.float32
VMEM_LIMIT = 60 * 1024 * 1024


def dot(left, right, dims=NN):
    return lax.dot_general(left, right, dims, preferred_element_type=F32)


def micros(duration):
    return pl.CostEstimate(flops=duration * 10**9, bytes_accessed=0, transcendentals=0)


def flat(value):
    return value.reshape(value.shape[0] * value.shape[1], value.shape[2])


class Net:
    def __init__(self, send_sems, recv_sems):
        tok, hid = lax.axis_index("tok"), lax.axis_index("hid")
        near = hid + 1 - 2 * lax.rem(hid, 2)
        self.tok, self.hid = tok, hid
        self.core = (tok, near)
        self.far = (tok, lax.rem(hid + 2, 4))
        self.far_core = (tok, lax.rem(near + 2, 4))
        self.half = (tok + 1 - 2 * lax.rem(tok, 2), hid)
        self.low, self.high = lax.rem(tok, 2), lax.div(tok, 2)
        self.send_sems, self.recv_sems = send_sems, recv_sems
        self.copies, self.count = [], 0

    def row(self, high):
        return (high * 2 + self.low, self.hid)

    def line(self, count):
        self.before, self.has_before = self.row(lax.max(self.high - 1, 0)), self.high > 0
        self.after = self.row(lax.min(self.high + 1, count - 1))
        self.has_after, self.last = self.high + 1 < count, count - 1

    def barrier(self, devices, line=False):
        sem = pltpu.get_barrier_semaphore()

        def signal(device):
            pl.semaphore_signal(sem, inc=1, device_id=device, device_id_type=MESH)

        for device in devices:
            signal(device)
        peers = len(devices)
        if line:
            pl.when(self.has_before)(lambda: signal(self.before))
            pl.when(self.has_after)(lambda: signal(self.after))
            peers = peers + lax.min(self.high, 1) + lax.min(self.last - self.high, 1)
        pl.semaphore_wait(sem, peers)

    def take(self, count):
        first = self.count
        self.count += count
        return first

    def make(self, index, source, target, device):
        return pltpu.make_async_remote_copy(
            src_ref=source,
            dst_ref=target,
            send_sem=self.send_sems.at[index],
            recv_sem=self.recv_sems.at[index],
            device_id=device,
            device_id_type=MESH,
        )

    def copy(self, source, target, device):
        made = self.make(self.take(1), source, target, device)
        self.copies.append(made)
        made.start()
        return made

    def finish(self, waited=()):
        done = [id(made) for made in waited]
        for made in self.copies:
            if id(made) not in done:
                made.wait_send()


class Moves:
    def __init__(self, sems):
        self.sems, self.count, self.stores = sems, 0, []

    def take(self, count):
        first = self.count
        self.count += count
        return first

    def make(self, index, source, target):
        return pltpu.make_async_copy(source, target, self.sems.at[index])

    def load(self, source, target):
        made = self.make(self.take(1), source, target)
        made.start()
        return made

    def store(self, source, target):
        self.stores.append(self.load(source, target))

    def finish(self):
        for made in self.stores:
            made.wait()


class Several:
    def __init__(self, copies):
        self.copies = copies

    def wait(self):
        for one in self.copies:
            one.wait()


def weight_loads(parts):
    return 1 if len(parts) == 1 else 2 * parts[0].shape[0]


def load_weight(net, moves, parts, columns, target):
    if len(parts) == 1:
        return moves.load(parts[0].at[:, columns], target)
    copies = []
    for part, low in zip(parts, (net.low, 1 - net.low)):
        shard = part.shape[1]
        for high in range(part.shape[0]):
            start = pl.multiple_of((high * 2 + low) * shard, 16)
            copies.append(moves.load(part.at[high, :, columns], target.at[pl.ds(start, shard)]))
    return Several(copies)


def store_halves(net, moves, grad, outs, shard):
    if not shard:
        moves.store(grad, outs[0])
        return
    for out, low in zip(outs, (net.low, 1 - net.low)):
        for place in range(out.shape[0]):
            start = pl.multiple_of((place * 2 + low) * shard, 16)
            moves.store(grad.at[pl.ds(start, shard)], out.at[place])


def half_outputs(rows, columns, shard):
    if not shard:
        return [((rows, columns), BF, False)]
    return [((rows // (2 * shard), shard, columns), BF, False)] * 2


def spaced(arrays):
    return [(array, False) for array in arrays]


def job_copies(count):
    return 2 * count + 1


class GatherJob:
    def __init__(self, net, moves, shard, weights):
        self.net, self.weights = net, weights
        self.count = weights.shape[0] // 2
        self.across = net.take(2 * self.count - 1)
        self.up, self.down = net.take(self.count), net.take(self.count)
        own = weights.at[net.tok]
        moves.store(shard, own)
        first = self.swap(0, shard, own)
        pl.when(net.has_after)(lambda: net.make(self.up, shard, own, net.after).start())
        pl.when(net.has_before)(lambda: net.make(self.down, shard, own, net.before).start())
        first.start()

    def swap(self, index, source, target):
        return self.net.make(self.across + index, source, target, self.net.half)

    def arrive(self, step, above):
        net = self.net
        place = net.high + step if above else net.high - step
        block = self.weights.at[place * 2 + net.low]
        base, onward = (self.down, net.before) if above else (self.up, net.after)
        net.make(base + step - 1, block, block, onward).wait_recv()
        if step + 1 < self.count:
            go_on = net.has_before if above else net.has_after
            pl.when(go_on)(lambda: net.make(base + step, block, block, onward).start())
        self.swap(2 * step - int(above), block, block).start()

    def forward(self, point, points):
        net = self.net
        for step in range(1, self.count):
            if (step - 1) * points // (self.count - 1) == point:
                pl.when(net.high - step >= 0)(functools.partial(self.arrive, step, False))
                pl.when(net.high + step < self.count)(functools.partial(self.arrive, step, True))

    def finish(self):
        net = self.net
        own = self.weights.at[net.tok]
        self.swap(0, own, own).wait()
        for step in range(1, self.count):
            below, above = net.high - step >= 0, net.high + step < self.count
            pl.when(below)(lambda step=step: self.swap(2 * step, own, own).wait())
            pl.when(above)(lambda step=step: self.swap(2 * step - 1, own, own).wait())
        for step in range(self.count - 1):
            for base, device, has, there in (
                (self.up, net.after, net.has_after, net.high - step >= 0),
                (self.down, net.before, net.has_before, net.high + step < self.count),
            ):
                sent = net.make(base + step, own, own, device)
                pl.when(jnp.logical_and(has, there))(sent.wait_send)


class Line:
    def __init__(self, net, count, value, passing, arrived):
        self.net, self.count, self.value = net, count, value
        self.passing, self.arrived = passing, arrived
        self.up, self.down = net.take(count), net.take(count)

    def upward(self, place):
        source, target = self.passing.at[place], self.arrived.at[place + 1]
        return self.net.make(self.up + place, source, target, self.net.after)

    def downward(self, place):
        source, target = self.passing.at[place], self.arrived.at[place]
        return self.net.make(self.down + place, source, target, self.net.before)

    def send(self, place, above):
        net = self.net
        value = self.value(place)
        self.passing[place] = value.astype(BF)
        move = self.upward(place) if above else self.downward(place)

        def add():
            move.wait_recv()
            landed = self.arrived[place + 1 if above else place]
            self.passing[place] = (value + landed.astype(F32)).astype(BF)

        pl.when(net.has_before if above else net.has_after)(add)
        move.start()

    def forward(self, point, points):
        high, last = self.net.high, self.count - 1
        for slot in range(last):
            if slot * points // last == point:
                pl.when(high <= slot)(functools.partial(self.send, last - slot + high, True))
                pl.when(last - high <= slot)(functools.partial(self.send, slot - last + high, False))

    def finish(self, total):
        net = self.net
        total[...] = self.value(net.high)

        def add(move, place):
            move.wait_recv()
            total[...] += self.arrived[place].astype(F32)

        pl.when(net.has_before)(lambda: add(self.upward(net.high), net.high + 1))
        pl.when(net.has_after)(lambda: add(self.downward(net.high), net.high))

    def drain(self):
        for place in range(self.count):
            pl.when(self.net.high < place)(self.upward(place).wait_send)
            pl.when(self.net.high > place)(self.downward(place).wait_send)


def part_scratch(count, shard, width):
    half = count // 2
    return [pltpu.VMEM((half, shard, width), BF)] * 3 + [pltpu.VMEM((half + 1, shard, width), BF)]


class ScatterParts:
    def __init__(self, net, moves, grads, scratch):
        self.net, self.moves = net, moves
        self.own, self.landed, passing, arrived = scratch
        self.count = count = grads.shape[0] // 2
        self.across, self.loads = net.take(count), moves.take(count)
        high, last = net.high, count - 1

        def start(place):
            self.swap(place, grads.at[place * 2 + 1 - net.low]).start()

        for slot in range(last):
            pl.when(high <= slot)(functools.partial(start, last - slot + high))
            pl.when(last - high <= slot)(functools.partial(start, slot - last + high))
        start(high)
        for place in range(count):
            source = grads.at[place * 2 + net.low]
            moves.make(self.loads + place, source, self.own.at[place]).start()
        self.line = Line(net, count, self.pair, passing, arrived)
        self.forward = self.line.forward

    def swap(self, place, source=None):
        target = self.landed.at[place]
        source = target if source is None else source
        return self.net.make(self.across + place, source, target, self.net.half)

    def pair(self, place):
        own = self.own.at[place]
        self.moves.make(self.loads + place, own, own).wait()
        self.swap(place).wait_recv()
        return self.own[place].astype(F32) + self.landed[place].astype(F32)

    def finish(self, total):
        self.line.finish(total)
        self.line.drain()
        for place in range(self.count):
            self.swap(place).wait_send()


class Across:
    def __init__(self, net, moves, part, scratch):
        self.net, self.part = net, part
        self.own, self.landed = scratch
        self.load = moves.load(part.at[net.low], self.own)

    def start(self):
        self.copy = self.net.copy(self.part.at[1 - self.net.low], self.landed, self.net.half)

    def finish(self, total):
        self.load.wait()
        self.copy.wait_recv()
        total[...] = self.own[...].astype(F32) + self.landed[...].astype(F32)


def across_scratch(part):
    return [pltpu.VMEM(part.shape[1:], BF)] * 2


def run(kernel, name, duration, inputs, outputs, scratch, identity, copies, moves):
    def space(near):
        return pl.BlockSpec(memory_space=pltpu.VMEM if near else pl.ANY)

    return pl.pallas_call(
        kernel,
        name=name,
        cost_estimate=micros(duration),
        out_shape=[jax.ShapeDtypeStruct(shape, dtype) for shape, dtype, _ in outputs],
        in_specs=[space(near) for _, near in inputs],
        out_specs=[space(near) for _, _, near in outputs],
        scratch_shapes=list(scratch)
        + [
            pltpu.SemaphoreType.DMA((copies,)),
            pltpu.SemaphoreType.DMA((copies,)),
            pltpu.SemaphoreType.DMA((moves,)),
        ],
        compiler_params=pltpu.CompilerParams(
            collective_id=identity, has_side_effects=True, vmem_limit_bytes=VMEM_LIMIT
        ),
    )(*[array for array, _ in inputs])


def split_refs(refs, inputs, outputs):
    return refs[:inputs], refs[inputs : inputs + outputs], refs[inputs + outputs :]


def norm_parts(rows):
    centred = rows - jnp.mean(rows, axis=1, keepdims=True)
    inverse = lax.rsqrt(jnp.mean(centred * centred, axis=1, keepdims=True) + EPS)
    return centred * inverse, inverse


def norm_back(rows, gain, grad):
    scaled, inverse = norm_parts(rows)
    inner = grad * gain
    first = jnp.mean(inner, axis=1, keepdims=True)
    second = jnp.mean(inner * scaled, axis=1, keepdims=True)
    return (
        inverse * (inner - first - scaled * second),
        jnp.sum(grad * scaled, axis=0, keepdims=True),
        jnp.sum(grad, axis=0, keepdims=True),
    )


def gather_send(net, full, chunk):
    near = net.copy(full.at[0, chunk], full.at[1, chunk], net.core)
    far = net.copy(full.at[0, chunk], full.at[2, chunk], net.far)
    return near, far


def gather_pass(net, full, chunk, far):
    far.wait_recv()
    return net.copy(full.at[2, chunk], full.at[3, chunk], net.core)


def scatter_scratch(rows, width):
    return [
        pltpu.VMEM((rows, width), F32),
        pltpu.VMEM((rows, width), F32),
    ] + [pltpu.VMEM((rows, width), BF)] * 6


class Scatter:
    def __init__(self, net, scratch):
        self.net = net
        self.hold, self.total, self.cs0, self.cr0, self.ys, self.yr, self.cs1, self.cr1 = scratch
        self.first, self.second = {}, {}

    def far_part(self, key, chunk, partial):
        rows = partial.shape[0] // 2
        self.hold[chunk] = partial[:rows]
        self.cs0[chunk] = partial[rows:].astype(BF)
        self.first[key] = self.net.copy(self.cs0.at[chunk], self.cr0.at[chunk], self.net.core)

    def far_send(self, key, chunk):
        self.first[key].wait_recv()
        self.ys[chunk] = (self.hold[chunk] + self.cr0[chunk].astype(F32)).astype(BF)
        self.second[key] = self.net.copy(self.ys.at[chunk], self.yr.at[chunk], self.net.far)

    def near_part(self, partial):
        rows = partial.shape[0] // 2
        self.total[...] = partial[:rows]
        self.cs1[...] = partial[rows:].astype(BF)
        self.near = self.net.copy(self.cs1, self.cr1, self.net.core)

    def near_done(self):
        self.near.wait_recv()
        self.total[...] += self.cr1[...].astype(F32)

    def result(self, key, chunk):
        self.second[key].wait_recv()
        return self.total[chunk] + self.yr[chunk].astype(F32)


def blocked(value):
    return value.astype(BF).reshape(2, value.shape[0] // 2, value.shape[1])


def chunks_of(rows, count):
    step = rows // count
    return [pl.ds(index * step, step) for index in range(count)]


def weight_grad(left, right, out, extra=None):
    width = left.shape[2]
    tile = 384

    def one(index, carry):
        columns = pl.ds(pl.multiple_of(index * tile, tile), tile)
        result = dot(flat(left[:, :, columns]), flat(right[...]), TN)
        if extra is None:
            out[columns, :] = result.astype(out.dtype)
        else:
            start = out.shape[1] - extra.shape[1]
            join = result.shape[1] - start
            added = extra[columns, :]
            out[columns, :start] = result[:, :start].astype(out.dtype)
            both = result[:, start:] + added[:, :join].astype(F32)
            out[columns, start : start + join] = both.astype(out.dtype)
            out[columns, start + join :] = added[:, join:]
        return carry

    lax.fori_loop(0, width // tile, one, 0)


def packed_shape(rows, columns):
    return (2, rows // 2 * columns // LANES, LANES)


def pack_half(tiles, target):
    rows = tiles[0].shape[0]
    for index, tile in enumerate(tiles[:-1]):
        target[index * rows : (index + 1) * rows, :] = tile.astype(BF)
    tail = tiles[-1][:, : LANES // 2]
    both = jnp.concatenate([tail[: rows // 2], tail[rows // 2 :]], axis=1)
    target[(len(tiles) - 1) * rows :, :] = both.astype(BF)


def unpack_half(packed, rows):
    full = packed.shape[0] // rows
    tiles = [packed[index * rows : (index + 1) * rows] for index in range(full)]
    tail = packed[full * rows :]
    return tiles + [jnp.concatenate([tail[:, : LANES // 2], tail[:, LANES // 2 :]], axis=0)]


def project_kernel(*refs, layer, head_cols, factor, parts):
    (x_hbm, vec, bias, *mixed_hbm), outs, scratch = split_refs(refs, 3 + parts, 4)
    normed_out, queries_out, pairs_out, far_out = outs
    x, weight, normed, queries, pairs, far_pairs, send_sems, recv_sems, move_sems = scratch
    net, moves = Net(send_sems, recv_sems), Moves(move_sems)
    rows = x.shape[0]
    pair_cols = 2 * head_cols
    chunks = chunks_of(rows, 2)
    x_load = moves.load(x_hbm, x)
    columns = pl.ds(0, weight.shape[1])
    weight_load = load_weight(net, moves, mixed_hbm, columns, weight)
    net.barrier([net.core, net.far, net.half])
    x_load.wait()
    sent = []
    for chunk in chunks:
        scaled, _ = norm_parts(x[chunk, :])
        normed[0, chunk, :] = (scaled * vec[layer, 0:1] + vec[layer, 1:2]).astype(BF)
        sent.append(gather_send(net, normed, chunk))
    arrived = []
    weight_load.wait()

    def project(slots, chunk):
        result = dot(flat(normed[slots, chunk, :]), weight[...]) + bias[layer : layer + 1]
        shape = (slots.size, chunk.size, -1)
        halves = range(len(chunks)) if chunk.size == rows else [chunk.start // chunk.size]
        step = rows // len(chunks)
        for index in range(slots.size):
            for place, half in enumerate(halves):
                start = (index * len(halves) + place) * step
                part = result[start : start + step]
                tiles = [part[:, lane : lane + LANES] for lane in range(0, pair_cols, LANES)]
                pack_half(tiles, pairs.at[slots.start + index, half])
        halves = pl.ds(halves[0], len(halves))
        own = result[:, pair_cols : pair_cols + head_cols] * factor
        queries[slots, chunk, :] = own.astype(BF).reshape(shape)
        source, target = pairs.at[slots, halves], far_pairs.at[slots, halves]
        arrived.append(net.copy(source, target, net.half))

    whole = pl.ds(0, rows)
    project(pl.ds(0, 1), whole)
    for near, _ in sent:
        near.wait_recv()
    project(pl.ds(1, 1), whole)
    for chunk, (_, far) in zip(chunks, sent):
        gather_pass(net, normed, chunk, far).wait_recv()
        project(pl.ds(2, 2), chunk)
    moves.store(normed, normed_out)
    moves.store(queries, queries_out)
    moves.store(pairs, pairs_out)
    for one in arrived:
        one.wait_recv()
    moves.store(far_pairs, far_out)
    net.finish()
    moves.finish()


def project(layer, x, vec, bias, mixed, head_cols):
    rows, width = x.shape
    used = bias.shape[1]
    outputs = [
        ((4, rows, width), BF, False),
        ((4, rows, head_cols), BF, False),
        ((4,) + packed_shape(rows, 2 * head_cols), BF, False),
        ((4,) + packed_shape(rows, 2 * head_cols), BF, False),
    ]
    scratch = [pltpu.VMEM((rows, width), F32), pltpu.VMEM((width, used), BF)]
    scratch += [pltpu.VMEM(shape, dtype) for shape, dtype, _ in outputs]
    kernel = functools.partial(
        project_kernel,
        layer=layer,
        head_cols=head_cols,
        factor=HEAD_DIM ** (-0.5) * LOG2E,
        parts=len(mixed),
    )
    inputs = [(x, False), (vec, True), (bias, True)] + spaced(mixed)
    return run(kernel, "project", 40, inputs, outputs, scratch, 8 * layer, 12, 6 + weight_loads(mixed))


def pair_windows(width, lead=0):
    windows = []
    for first in range(lead, width - HEAD_DIM, 2 * HEAD_DIM):
        start = first // LANES * LANES
        size = min(2 * LANES, width - start)
        row = lax.broadcasted_iota(jnp.int32, (size, 2 * LANES), 0) + (start - first)
        lane = lax.broadcasted_iota(jnp.int32, (size, 2 * LANES), 1)
        second = lane >= LANES
        lane = jnp.where(second, lane - LANES, lane)
        match = row == jnp.where(second, lane + HEAD_DIM, lane)
        windows.append((start, size, jnp.logical_and(match, lane < HEAD_DIM).astype(BF)))
    return windows


def spread_heads(value, windows):
    heads = []
    for start, size, pick in windows:
        both = dot(value[:, start : start + size], pick).astype(BF)
        heads += [both[:, :LANES], both[:, LANES:]]
    return heads


def join_heads(heads, windows, width):
    tiles = [None] * (-(-width // LANES))
    for index, (start, size, pick) in enumerate(windows):
        both = jnp.concatenate(heads[2 * index : 2 * index + 2], axis=1)
        part = dot(both, pick, NT)
        for lane in range(0, size, LANES):
            tile, piece = (start + lane) // LANES, part[:, lane : lane + LANES]
            tiles[tile] = piece if tiles[tile] is None else tiles[tile] + piece
    return jnp.concatenate(tiles, axis=1)


def as_rows(columns):
    rows = columns[0].shape[0]
    lane = lax.broadcasted_iota(jnp.int32, (rows, LANES), 1)
    together = jnp.zeros((rows, LANES), F32)
    for head, column in enumerate(columns):
        together = jnp.where(lane == head, column, together)
    return together.T[:8]


def load_pairs(meta, own_pairs, far_pairs, key_marks, key_scratch, value_scratch, heads):
    rows = 2 * (own_pairs.shape[2] * LANES // (2 * heads * HEAD_DIM))
    hid, half = meta[0], meta[1]
    windows = pair_windows(2 * heads * HEAD_DIM)
    lowest, highest = meta[2], meta[3]
    for block in range(1, 4):
        lowest = jnp.minimum(lowest, meta[2 + 2 * block])
        highest = jnp.maximum(highest, meta[3 + 2 * block])
    for which, source in ((0, own_pairs), (1, far_pairs)):
        for slot in range(4):
            place = jnp.bitwise_xor(half, which) * 4 + jnp.bitwise_xor(hid, slot)
            step = place * rows // KEYS

            @pl.when(jnp.logical_and(step >= lowest, step < highest))
            def load(source=source, slot=slot, place=place):
                start = pl.ds(pl.multiple_of(place * rows, rows), rows)
                marks = key_marks[start, :]
                halves = [unpack_half(source[slot, index], rows // 2) for index in range(2)]
                tiles = [jnp.concatenate(both, axis=0) for both in zip(*halves)]
                spread = spread_heads(jnp.concatenate(tiles, axis=1), windows)
                for head in range(heads):
                    key_scratch[head, start, :] = spread[head] + marks
                    value_scratch[head, start, :] = spread[heads + head]


def attend_kernel(
    meta, queries, own_pairs, far_pairs, query_marks, key_marks, mixture, logsum,
    key_scratch, value_scratch, score_scratch, high_scratch, total_scratch, sum_scratch, query_scratch,
    *, heads
):
    rows = queries.shape[1]
    head_cols = heads * HEAD_DIM
    load_pairs(meta, own_pairs, far_pairs, key_marks, key_scratch, value_scratch, heads)
    query_windows = pair_windows(head_cols)
    mixed_windows = pair_windows(mixture.shape[2], mixture.shape[2] - head_cols)

    def one_block(block, carry):
        slot = jnp.bitwise_xor(meta[0], block)
        first, last = meta[2 + 2 * block], meta[3 + 2 * block]
        own = pl.ds(pl.multiple_of(block * rows, rows), rows)
        marks = query_marks[own, :]
        for head, query in enumerate(spread_heads(queries[slot], query_windows)):
            query_scratch[head] = query + marks
        high_scratch[...] = jnp.full_like(high_scratch, -3e38)
        sum_scratch[...] = jnp.zeros_like(sum_scratch)
        total_scratch[...] = jnp.zeros_like(total_scratch)

        def scores_of(key_block, inner):
            keys = pl.ds(pl.multiple_of(key_block * KEYS, KEYS), KEYS)
            for head in range(heads):
                scores = dot(query_scratch[head], key_scratch[head, keys, :], NT)
                score_scratch[head, :, keys] = scores
                high = high_scratch[head]
                for lane in range(0, KEYS, LANES):
                    high = jnp.maximum(high, scores[:, lane : lane + LANES])
                high_scratch[head] = high
            return inner

        lax.fori_loop(first, last, scores_of, 0)
        for head in range(heads):
            high_scratch[head] = jnp.broadcast_to(
                jnp.max(high_scratch[head], axis=1, keepdims=True), (rows, LANES)
            )

        def sums_of(key_block, inner):
            keys = pl.ds(pl.multiple_of(key_block * KEYS, KEYS), KEYS)
            for head in range(heads):
                high = high_scratch[head]
                high = jnp.concatenate([high] * (KEYS // LANES), axis=1)
                powers = jnp.exp2(score_scratch[head, :, keys] - high)
                total = total_scratch[head]
                for lane in range(0, KEYS, LANES):
                    total += powers[:, lane : lane + LANES]
                total_scratch[head] = total
                sum_scratch[head] += dot(powers.astype(BF), value_scratch[head, keys, :])
            return inner

        lax.fori_loop(first, last, sums_of, 0)
        mixed, columns = [], []
        for head in range(heads):
            total = jnp.sum(total_scratch[head], axis=1, keepdims=True)
            columns.append(high_scratch[head][:, :1] + jnp.log2(total))
            mixed.append((sum_scratch[head] / total).astype(BF))
        mixture[slot] = join_heads(mixed, mixed_windows, mixture.shape[2]).astype(BF)
        logsum[:, own] = as_rows(columns)
        return carry

    lax.fori_loop(0, 4, one_block, 0)


def attend(meta, queries, own_pairs, far_pairs, query_marks, key_marks, lead):
    _, rows, head_cols = queries.shape
    heads = head_cols // HEAD_DIM
    own, count = 4 * rows, 8 * rows
    space = pl.BlockSpec(memory_space=pltpu.VMEM)
    return pl.pallas_call(
        functools.partial(attend_kernel, heads=heads),
        name="attend",
        cost_estimate=micros(22),
        out_shape=[
            jax.ShapeDtypeStruct((4, rows, lead + head_cols), BF),
            jax.ShapeDtypeStruct((8, own), F32),
        ],
        in_specs=[pl.BlockSpec(memory_space=pltpu.SMEM)] + [space] * 5,
        out_specs=[space] * 2,
        scratch_shapes=[
            pltpu.VMEM((heads, count, LANES), BF),
            pltpu.VMEM((heads, count, LANES), BF),
            pltpu.VMEM((heads, rows, count), F32),
            pltpu.VMEM((heads, rows, LANES), F32),
            pltpu.VMEM((heads, rows, LANES), F32),
            pltpu.VMEM((heads, rows, LANES), F32),
            pltpu.VMEM((heads, rows, LANES), BF),
        ],
        compiler_params=pltpu.CompilerParams(vmem_limit_bytes=VMEM_LIMIT),
    )(meta, queries, own_pairs, far_pairs, query_marks, key_marks)


def attend_back_kernel(
    meta, queries, own_pairs, far_pairs, query_marks, key_marks, grad_mixture, logsum,
    grad_queries, grad_own, grad_far,
    key_scratch, value_scratch, grad_key, grad_value, grad_query, query_scratch, grad_scratch,
    prob_scratch, grad_prob_scratch, delta_scratch,
    *, heads
):
    rows = queries.shape[1]
    head_cols = heads * HEAD_DIM
    load_pairs(meta, own_pairs, far_pairs, key_marks, key_scratch, value_scratch, heads)
    query_windows = pair_windows(head_cols)
    mixed_windows = pair_windows(grad_mixture.shape[2], grad_mixture.shape[2] - head_cols)
    grad_key[...] = jnp.zeros_like(grad_key)
    grad_value[...] = jnp.zeros_like(grad_value)

    def one_block(block, carry):
        slot = jnp.bitwise_xor(meta[0], block)
        first, last = meta[2 + 2 * block], meta[3 + 2 * block]
        own = pl.ds(pl.multiple_of(block * rows, rows), rows)
        marks = query_marks[own, :]
        for head, query in enumerate(spread_heads(queries[slot], query_windows)):
            query_scratch[head] = query + marks
        for head, grad in enumerate(spread_heads(grad_mixture[slot], mixed_windows)):
            grad_scratch[head] = grad
        logs = logsum[:, own]
        grad_query[...] = jnp.zeros_like(grad_query)
        delta_scratch[...] = jnp.zeros_like(delta_scratch)

        def probs_of(key_block, inner):
            keys = pl.ds(pl.multiple_of(key_block * KEYS, KEYS), KEYS)
            for head in range(heads):
                grad = grad_scratch[head]
                scores = dot(key_scratch[head, keys, :], query_scratch[head], NT)
                probs = jnp.exp2(scores - logs[head : head + 1])
                grad_probs = dot(value_scratch[head, keys, :], grad, NT)
                prob_scratch[head, keys, :] = probs
                grad_prob_scratch[head, keys, :] = grad_probs
                delta_scratch[head] += jnp.sum((probs * grad_probs).reshape(KEYS // 8, 8, rows), axis=0)
                grad_value[head, keys, :] += dot(probs.astype(BF), grad)
            return inner

        lax.fori_loop(first, last, probs_of, 0)
        for head in range(heads):
            delta_scratch[head, 0:1] = jnp.sum(delta_scratch[head], axis=0, keepdims=True)

        def one_key(key_block, inner):
            keys = pl.ds(pl.multiple_of(key_block * KEYS, KEYS), KEYS)
            for head in range(heads):
                delta = delta_scratch[head, 0:1]
                grad_scores = prob_scratch[head, keys, :] * (grad_prob_scratch[head, keys, :] - delta)
                grad_scores = grad_scores.astype(BF)
                grad_key[head, keys, :] += dot(grad_scores, query_scratch[head])
                grad_query[head] += dot(grad_scores, key_scratch[head, keys, :], TN)
            return inner

        lax.fori_loop(first, last, one_key, 0)
        real = lax.broadcasted_iota(jnp.int32, (rows, LANES), 1) < HEAD_DIM
        scaled = [
            jnp.where(real, grad_query[head] * HEAD_DIM ** (-0.5), 0.0).astype(BF)
            for head in range(heads)
        ]
        grad_queries[slot] = join_heads(scaled, query_windows, head_cols).astype(BF)
        return carry

    lax.fori_loop(0, 4, one_block, 0)
    hid, half = meta[0], meta[1]
    for which, target in ((0, grad_own), (1, grad_far)):
        for slot in range(4):
            place = jnp.bitwise_xor(half, which) * 4 + jnp.bitwise_xor(hid, slot)
            start = pl.ds(pl.multiple_of(place * rows, rows), rows)
            parts = [(grad_key[head, start, :] * LN2).astype(BF) for head in range(heads)]
            parts += [grad_value[head, start, :].astype(BF) for head in range(heads)]
            joined = join_heads(parts, pair_windows(2 * head_cols), 2 * head_cols)
            for index in range(2):
                part = joined[index * (rows // 2) : (index + 1) * (rows // 2)]
                tiles = [part[:, lane : lane + LANES] for lane in range(0, 2 * head_cols, LANES)]
                pack_half(tiles, target.at[slot, index])


def attend_back(
    meta, queries, own_pairs, far_pairs, query_marks, key_marks, grad_mixture, logsum
):
    _, rows, head_cols = queries.shape
    heads = head_cols // HEAD_DIM
    count = 8 * rows
    space = pl.BlockSpec(memory_space=pltpu.VMEM)
    return pl.pallas_call(
        functools.partial(attend_back_kernel, heads=heads),
        name="attend_back",
        cost_estimate=micros(37),
        out_shape=[
            jax.ShapeDtypeStruct((4, rows, head_cols), BF),
            jax.ShapeDtypeStruct(own_pairs.shape, BF),
            jax.ShapeDtypeStruct(own_pairs.shape, BF),
        ],
        in_specs=[pl.BlockSpec(memory_space=pltpu.SMEM)] + [space] * 7,
        out_specs=[space] * 3,
        scratch_shapes=[
            pltpu.VMEM((heads, count, LANES), BF),
            pltpu.VMEM((heads, count, LANES), BF),
            pltpu.VMEM((heads, count, LANES), F32),
            pltpu.VMEM((heads, count, LANES), F32),
            pltpu.VMEM((heads, rows, LANES), F32),
            pltpu.VMEM((heads, rows, LANES), BF),
            pltpu.VMEM((heads, rows, LANES), BF),
            pltpu.VMEM((heads, count, rows), F32),
            pltpu.VMEM((heads, count, rows), F32),
            pltpu.VMEM((heads, 8, rows), F32),
        ],
        compiler_params=pltpu.CompilerParams(vmem_limit_bytes=VMEM_LIMIT),
    )(meta, queries, own_pairs, far_pairs, query_marks, key_marks, grad_mixture, logsum)


def mlp_kernel(*refs, layer, parts, last):
    ins, outs, scratch = split_refs(refs, 4 + sum(parts), 5 - last)
    mixture_hbm, x_hbm, vec, up_bias = ins[:4]
    mixed_hbm, up_hbm, down_hbm = split_refs(ins[4:], parts[0], parts[1])
    after_out, normed_out, active_out, slope_out = outs[:4]
    mixture, x, out_weight, up_weight, down_weight, after, normed, active, slope, x_next = scratch[:10]
    first_scratch, second_scratch = scratch[10:18], scratch[18:26]
    send_sems, recv_sems, move_sems = scratch[26:]
    net, moves = Net(send_sems, recv_sems), Moves(move_sems)
    rows = x.shape[0]
    hidden_cols = up_weight.shape[1]
    out_cols = out_weight.shape[1]
    chunks = chunks_of(rows, 4)
    out_part = pl.ds(x.shape[1] - out_cols, out_cols)
    loads = [
        moves.load(mixture_hbm, mixture), load_weight(net, moves, mixed_hbm, out_part, out_weight),
    ]
    x_load = moves.load(x_hbm, x)
    up_load = load_weight(net, moves, up_hbm, pl.ds(0, hidden_cols), up_weight)
    if not last:
        down_load = load_weight(net, moves, down_hbm, pl.ds(0, hidden_cols), down_weight)
    net.barrier([net.core, net.far])
    out_bias, gain = vec[layer, 2:3], vec[layer, 3:4]
    shift, down_bias = vec[layer, 4:5], vec[layer, 5:6]

    def mixed(slots, chunk):
        return dot(flat(mixture[slots, chunk, :]), out_weight[...], NT)

    def up(slots, chunk):
        hidden = dot(flat(normed[slots, chunk, :]), up_weight[...]) + up_bias[layer : layer + 1]
        square = hidden * hidden
        bend = jnp.tanh(GELU * hidden * (1.0 + CUBE * square))
        half = 0.5 * (1.0 + bend)
        value = hidden * half
        rise = half + 0.5 * hidden * (1.0 - bend * bend) * GELU * (1.0 + 3.0 * CUBE * square)
        active[slots, chunk, :] = blocked(value)
        slope[slots, chunk, :] = blocked(rise)

    def down(slots, chunk):
        return dot(flat(active[slots, chunk, :]), down_weight[...], NT)

    near, far, whole = pl.ds(0, 2), pl.ds(2, 2), pl.ds(0, rows)
    for load in loads:
        load.wait()
    first = Scatter(net, first_scratch)
    for key, chunk in enumerate(chunks):
        first.far_part(key, chunk, mixed(far, chunk))
    for key, chunk in enumerate(chunks):
        first.far_send(key, chunk)
    first.near_part(mixed(near, whole))
    first.near_done()
    x_load.wait()
    sent = []
    for key, chunk in enumerate(chunks):
        residual = first.result(key, chunk) + x[chunk, :] + out_bias
        after[chunk, :] = residual
        normed[0, chunk, :] = (norm_parts(residual)[0] * gain + shift).astype(BF)
        sent.append(gather_send(net, normed, chunk))
    moves.store(after, after_out)
    for one, _ in sent:
        one.wait_recv()
    up_load.wait()
    up(near, whole)
    if not last:
        down_load.wait()
    second = Scatter(net, second_scratch)
    for key, chunk in enumerate(chunks):
        passed = gather_pass(net, normed, chunk, sent[key][1])
        passed.wait_recv()
        up(far, chunk)
        if not last:
            second.far_part(key, chunk, down(far, chunk))
            second.far_send(key, chunk)
    moves.store(normed, normed_out)
    moves.store(active, active_out)
    moves.store(slope, slope_out)
    if not last:
        second.near_part(down(near, whole))
        second.near_done()
        for key, chunk in enumerate(chunks):
            x_next[chunk, :] = second.result(key, chunk) + after[chunk, :] + down_bias
        moves.store(x_next, outs[4])
    net.finish()
    moves.finish()


def mlp(layer, mixture, x, vec, up_bias, mixed, up, down, last):
    rows, width = x.shape
    hidden = up_bias.shape[1]
    outputs = [
        ((rows, width), F32, False),
        ((4, rows, width), BF, False),
        ((4, rows, hidden), BF, False),
        ((4, rows, hidden), BF, False),
        ((rows, width), F32, False),
    ]
    scratch = [
        pltpu.VMEM(mixture.shape, BF),
        pltpu.VMEM((rows, width), F32),
        pltpu.VMEM((width, mixture.shape[2]), BF),
        pltpu.VMEM((width, hidden), BF),
        pltpu.VMEM((width, hidden), BF),
    ]
    scratch += [pltpu.VMEM(shape, dtype) for shape, dtype, _ in outputs]
    scratch += scatter_scratch(rows, width) * 2
    outputs = outputs[: 5 - last]
    down = () if last else down
    inputs = [(mixture, False), (x, False), (vec, True), (up_bias, True)]
    inputs += spaced([*mixed, *up, *down])
    parts = (len(mixed), len(up), len(down))
    kernel = functools.partial(mlp_kernel, layer=layer, parts=parts, last=last)
    moves = 8 + sum(weight_loads(part) for part in (mixed, up, down) if part)
    return run(kernel, "mlp", 48, inputs, outputs, scratch, 8 * layer + 1, 32, moves)


def mlp_back_kernel(*refs, layer, parts, given, shard, crossing):
    ins, outs, scratch = split_refs(
        refs, 7 + given + sum(parts) + crossing, 7 + (shard > 0) + crossing
    )
    gradient_hbm, after_hbm, vec, mixture_hbm, normed_hbm, active_hbm, slope_hbm = ins[:7]
    weights = ins[7 + given : 7 + given + sum(parts)]
    mixed_hbm, up_hbm, down_hbm = split_refs(weights, parts[0], parts[1])
    after_out, mixture_out, down_out, out_out, sums, hidden_sums = outs[:6]
    up_outs = outs[6 : 7 + (shard > 0)]
    gradient, after, out_weight, up_weight, down_weight, mixture, normed, active, slope = scratch[:9]
    grad_after, grad_mixture, grad_down, grad_up, grad_out = scratch[9:14]
    grad_rows, grad_hidden, grad_mid = scratch[14:17]
    scatter_refs, across_refs = scratch[17:25], scratch[25:-3]
    send_sems, recv_sems, move_sems = scratch[-3:]
    net, moves = Net(send_sems, recv_sems), Moves(move_sems)
    rows, width = gradient.shape
    hidden_cols = up_weight.shape[1]
    out_cols = out_weight.shape[1]
    chunks = chunks_of(rows, 2)
    out_part = pl.ds(width - out_cols, out_cols)
    load_gradient = moves.load(ins[7] if given else gradient_hbm, grad_rows if given else gradient)
    load_down = load_weight(net, moves, down_hbm, pl.ds(0, hidden_cols), down_weight)
    load_slope = moves.load(slope_hbm, slope)
    load_up = load_weight(net, moves, up_hbm, pl.ds(0, hidden_cols), up_weight)
    load_active = moves.load(active_hbm, active)
    load_after = moves.load(after_hbm, after)
    load_normed = moves.load(normed_hbm, normed)
    load_out = load_weight(net, moves, mixed_hbm, out_part, out_weight)
    load_mixture = moves.load(mixture_hbm, mixture)
    if given:
        load_own = moves.load(gradient_hbm, gradient)
    across = Across(net, moves, ins[-1], across_refs) if crossing else None
    net.barrier([net.core, net.far] + ([net.half] if crossing else []))
    if crossing:
        across.start()
    gain = vec[layer, 3:4]
    near, far, whole = pl.ds(0, 2), pl.ds(2, 2), pl.ds(0, rows)
    load_gradient.wait()
    if not given:
        grad_rows[0] = gradient[...].astype(BF)
        sent = [gather_send(net, grad_rows, chunk) for chunk in chunks]
    sums[...] = jnp.zeros_like(sums)
    sums[5:6] = jnp.sum(grad_rows[0].astype(F32), axis=0, keepdims=True)

    def hidden_grad(slots, chunk):
        value = dot(flat(grad_rows[slots, chunk, :]), down_weight[...])
        value = value * flat(slope[slots, chunk, :]).astype(F32)
        grad_hidden[slots, chunk, :] = blocked(value)

    def up_back(slots, chunk):
        return dot(flat(grad_hidden[slots, chunk, :]), up_weight[...], NT)

    if not given:
        for one, _ in sent:
            one.wait_recv()
    load_down.wait()
    load_slope.wait()
    scatter = Scatter(net, scatter_refs)
    if given:
        for key, chunk in enumerate(chunks):
            hidden_grad(far, chunk)
            if key == 0:
                load_up.wait()
            scatter.far_part(key, chunk, up_back(far, chunk))
        for key, chunk in enumerate(chunks):
            scatter.far_send(key, chunk)
        hidden_grad(near, whole)
    else:
        hidden_grad(near, whole)
        load_up.wait()
        for key, chunk in enumerate(chunks):
            passed = gather_pass(net, grad_rows, chunk, sent[key][1])
            passed.wait_recv()
            hidden_grad(far, chunk)
            scatter.far_part(key, chunk, up_back(far, chunk))
            scatter.far_send(key, chunk)
    scatter.near_part(up_back(near, whole))
    load_active.wait()
    weight_grad(grad_rows, active, grad_down)
    moves.store(grad_down, down_out)
    scatter.near_done()
    load_after.wait()
    if given:
        load_own.wait()
    sent = []
    for key, chunk in enumerate(chunks):
        back, gain_sum, shift_sum = norm_back(after[chunk, :], gain, scatter.result(key, chunk))
        total = gradient[chunk, :] + back
        grad_after[chunk, :] = total
        rounded = total.astype(BF)
        grad_mid[0, chunk, :] = rounded
        sent.append(gather_send(net, grad_mid, chunk))
        sums[3:4] += gain_sum
        sums[4:5] += shift_sum
        sums[2:3] += jnp.sum(rounded.astype(F32), axis=0, keepdims=True)
    moves.store(grad_after, after_out)
    load_normed.wait()
    weight_grad(normed, grad_hidden, grad_up)
    store_halves(net, moves, grad_up, up_outs, shard)
    column = jnp.zeros((1, hidden_cols), F32)
    for slot in range(4):
        column += jnp.sum(grad_hidden[slot].astype(F32), axis=0, keepdims=True)
    hidden_sums[...] = column

    def mix_back(slots, chunk):
        value = dot(flat(grad_mid[slots, chunk, :]), out_weight[...])
        grad_mixture[slots, chunk, :] = blocked(value)

    for one, _ in sent:
        one.wait_recv()
    load_out.wait()
    mix_back(near, whole)
    for key, chunk in enumerate(chunks):
        gather_pass(net, grad_mid, chunk, sent[key][1]).wait_recv()
    mix_back(far, whole)
    moves.store(grad_mixture, mixture_out)
    load_mixture.wait()
    weight_grad(grad_mid, mixture, grad_out)
    moves.store(grad_out, out_out)
    if crossing:
        across.finish(outs[-1])
    net.finish()
    moves.finish()


def mlp_back(
    layer, gradient, after, vec, mixed, up, down, mixture, normed, active, slope, given=(),
    shard=0, crossing=(),
):
    rows, width = gradient.shape
    hidden = active.shape[2]
    out_cols = mixture.shape[2]
    outputs = [
        ((rows, width), F32, False),
        ((4, rows, out_cols), BF, False),
        ((width, hidden), BF, False),
        ((width, out_cols), BF, False),
        ((8, width), F32, True),
        ((1, hidden), F32, True),
    ]
    shapes = [
        ((rows, width), F32),
        ((rows, width), F32),
        ((width, out_cols), BF),
        ((width, hidden), BF),
        ((width, hidden), BF),
        ((4, rows, out_cols), BF),
        ((4, rows, width), BF),
        ((4, rows, hidden), BF),
        ((4, rows, hidden), BF),
        ((rows, width), F32),
        ((4, rows, out_cols), BF),
        ((width, hidden), BF),
        ((width, hidden), BF),
        ((width, out_cols), BF),
        ((4, rows, width), BF),
        ((4, rows, hidden), BF),
        ((4, rows, width), BF),
    ]
    outputs += half_outputs(width, hidden, shard)
    scratch = [pltpu.VMEM(shape, dtype) for shape, dtype in shapes] + scatter_scratch(rows, width)
    for part in crossing:
        outputs.append((part.shape[1:], F32, True))
        scratch += across_scratch(part)
    inputs = [
        (gradient, False), (after, False), (vec, True), (mixture, False), (normed, False),
        (active, False), (slope, False),
    ] + spaced([*given, *mixed, *up, *down, *crossing])
    parts = (len(mixed), len(up), len(down))
    kernel = functools.partial(
        mlp_back_kernel,
        layer=layer,
        parts=parts,
        given=len(given),
        shard=shard,
        crossing=len(crossing),
    )
    moves = 14 + (3 * width // (2 * shard) if shard else 0)
    moves += weight_loads(mixed) + weight_loads(up) + weight_loads(down)
    return run(kernel, "mlp_back", 48, inputs, outputs, scratch, 8 * layer + 2, 21, moves)


def project_back_kernel(*refs, layer, parts, closing, crossing):
    ins, outs, scratch = split_refs(
        refs, 8 + parts + closing + crossing, 4 + (closing > 0) + crossing
    )
    after_hbm, x_hbm, vec, normed_hbm, queries_hbm, own_hbm, far_hbm, out_hbm = ins[:8]
    mixed_hbm, closing_ins = ins[8 : 8 + parts], ins[8 + parts : 8 + parts + closing]
    gradient_out, sums, column_sums, weight_out = outs[:4]
    grad_after, x, weight, normed, grad_queries, grad_own, grad_out = scratch[:7]
    landed, together, gradient, grad_weight = scratch[7:11]
    scatter_refs, closing_refs = scratch[11:19], scratch[19 : -3 - 2 * crossing]
    across_refs = scratch[-3 - 2 * crossing : -3]
    send_sems, recv_sems, move_sems = scratch[-3:]
    net, moves = Net(send_sems, recv_sems), Moves(move_sems)
    rows, width = x.shape
    pair_cols = 2 * grad_queries.shape[2]
    used_cols = pair_cols + grad_queries.shape[2]
    all_cols = together.shape[2]
    chunks = chunks_of(rows, 2)
    near, far, whole = pl.ds(0, 2), pl.ds(2, 2), pl.ds(0, rows)
    load_own = moves.load(own_hbm, grad_own)
    load_queries = moves.load(queries_hbm, grad_queries)
    loading = load_weight(net, moves, mixed_hbm, pl.ds(0, all_cols), weight)
    load_normed = moves.load(normed_hbm, normed)
    load_out = moves.load(out_hbm, grad_out)
    load_x = moves.load(x_hbm, x)
    load_after = moves.load(after_hbm, grad_after)
    if closing:
        active, down_weight, after, final = closing_refs[:4]
        load_active = moves.load(closing_ins[0], active)
        load_after_two = moves.load(closing_ins[1], after)
        columns = pl.ds(0, down_weight.shape[1])
        load_down = load_weight(net, moves, closing_ins[2:], columns, down_weight)
    across = Across(net, moves, ins[-1], across_refs) if crossing else None
    net.barrier([net.core, net.far, net.half])
    arriving = {
        slot: net.copy(far_hbm.at[slot], landed.at[slot], net.half) for slot in (3, 2, 1, 0)
    }
    load_queries.wait()
    together[:, :, pair_cols:used_cols] = grad_queries[...]
    together[:, :, used_cols:] = jnp.zeros((4, rows, all_cols - used_cols), BF)
    load_own.wait()
    loading.wait()

    def join(slot):
        arriving[slot].wait_recv()
        for index in range(2):
            pair = grad_own[slot, index].astype(F32) + landed[slot, index].astype(F32)
            part = pl.ds(index * (rows // 2), rows // 2)
            for place, tile in enumerate(unpack_half(pair.astype(BF), rows // 2)):
                columns = pl.ds(place * LANES, tile.shape[1])
                together[slot, part, columns] = tile

    def back(slots, chunk):
        return dot(flat(together[slots, chunk, :]), weight[...], NT)

    if closing:

        def down(slots, chunk):
            return dot(flat(active[slots, chunk, :]), down_weight[...], NT)

        load_active.wait()
        load_down.wait()
        last = Scatter(net, closing_refs[4:])
        for key, chunk in enumerate(chunks):
            last.far_part(key, chunk, down(far, chunk))
        for key, chunk in enumerate(chunks):
            last.far_send(key, chunk)
        last.near_part(down(near, whole))
        last.near_done()
    scatter = Scatter(net, scatter_refs)
    join(3)
    join(2)
    for key, chunk in enumerate(chunks):
        scatter.far_part(key, chunk, back(far, chunk))
    for key, chunk in enumerate(chunks):
        scatter.far_send(key, chunk)
    join(1)
    join(0)
    if crossing:
        across.start()
    scatter.near_part(back(near, whole))
    load_normed.wait()
    load_out.wait()
    weight_grad(normed, together, grad_weight, grad_out)
    moves.store(grad_weight, weight_out)
    column = jnp.zeros((1, all_cols), F32)
    for slot in range(4):
        column += jnp.sum(together[slot].astype(F32), axis=0, keepdims=True)
    column_sums[...] = column
    scatter.near_done()
    sums[...] = jnp.zeros_like(sums)
    load_x.wait()
    load_after.wait()
    for key, chunk in enumerate(chunks):
        grad, gain_sum, shift_sum = norm_back(
            x[chunk, :], vec[layer, 0:1], scatter.result(key, chunk)
        )
        gradient[chunk, :] = grad_after[chunk, :] + grad
        sums[0:1] += gain_sum
        sums[1:2] += shift_sum
    moves.store(gradient, gradient_out)
    if closing:
        load_after_two.wait()
        for key, chunk in enumerate(chunks):
            final[chunk, :] = last.result(key, chunk) + after[chunk, :] + vec[layer, 5:6]
        moves.store(final, outs[4])
    if crossing:
        across.finish(outs[-1])
    net.finish()
    moves.finish()


def project_back(
    layer, grad_after, x, vec, mixed, normed, grad_queries, grad_own, grad_far, grad_out, all_cols,
    closing=(), crossing=(),
):
    rows, width = x.shape
    outputs = [
        ((rows, width), F32, False),
        ((8, width), F32, True),
        ((1, all_cols), F32, True),
        ((width, width), BF, False),
    ]
    shapes = [
        ((rows, width), F32),
        ((rows, width), F32),
        ((width, all_cols), BF),
        (normed.shape, BF),
        (grad_queries.shape, BF),
        (grad_own.shape, BF),
        (grad_out.shape, BF),
        (grad_far.shape, BF),
        ((4, rows, all_cols), BF),
        ((rows, width), F32),
        ((width, width), BF),
    ]
    scratch = [pltpu.VMEM(shape, dtype) for shape, dtype in shapes] + scatter_scratch(rows, width)
    copies, moves = 12, 9 + weight_loads(mixed)
    if closing:
        active, after, *down = closing
        outputs.append(((rows, width), F32, False))
        shapes = [
            (active.shape, BF), ((width, active.shape[2]), BF), ((rows, width), F32), ((rows, width), F32),
        ]
        scratch += [pltpu.VMEM(shape, dtype) for shape, dtype in shapes] + scatter_scratch(rows, width)
        copies, moves = 18, moves + 3 + weight_loads(down)
    for part in crossing:
        outputs.append((part.shape[1:], F32, True))
        scratch += across_scratch(part)
        copies, moves = copies + 1, moves + 1
    inputs = [
        (grad_after, False), (x, False), (vec, True), (normed, False), (grad_queries, False),
        (grad_own, False), (grad_far, False), (grad_out, False),
    ] + spaced([*mixed, *closing, *crossing])
    kernel = functools.partial(
        project_back_kernel, layer=layer, parts=len(mixed), closing=len(closing),
        crossing=len(crossing),
    )
    return run(kernel, "project_back", 42, inputs, outputs, scratch, 8 * layer + 3, copies, moves)


def entry_kernel(*refs):
    ins, outs, scratch = split_refs(refs, 12, 7)
    tokens, cotangent, value_bias, query_bias, up_bias, shard = ins[:6]
    x, gradient, grad_rows, vec, bias, hidden_bias, weights = outs
    vectors, token_land, cotangent_land, vector_land, send_sems, recv_sems, move_sems = scratch
    net, moves = Net(send_sems, recv_sems), Moves(move_sems)
    rows, cols = x.shape[0], tokens.shape[0]
    layers = vec.shape[0]
    others = [net.core, net.far, net.far_core]
    vectors[...] = jnp.zeros_like(vectors)
    for index, one in enumerate(ins[6:]):
        for layer in range(layers):
            vectors[layer * 8 + index : layer * 8 + index + 1] = one[layer : layer + 1]
    net.line(weights.shape[0] // 2)
    net.barrier(others + [net.half], True)
    gathering = GatherJob(net, moves, shard, weights)

    def block(hid):
        return pl.ds(pl.multiple_of(hid * rows, rows), rows)

    moved = [
        net.copy(tokens.at[:, block(device[1])], token_land.at[net.hid], device)
        for device in reversed(others)
    ]
    moved += [net.copy(vectors, vector_land.at[net.hid], device) for device in others]
    sent = []
    for chunk in chunks_of(4 * rows, 2):
        source, own = cotangent.at[:, chunk], cotangent_land.at[net.hid, :, chunk]
        moved.append(net.copy(source, own, net.core))
        sent.append((net.copy(source, own, net.far), cotangent_land.at[net.far[1], :, chunk]))
    token_land[net.hid] = tokens[:, block(net.hid)]
    cotangent_land[net.hid] = cotangent[...]
    vector_land[net.hid] = vectors[...]
    bias[...] = jnp.zeros_like(bias)
    bias[:, cols : 2 * cols] = value_bias[...]
    bias[:, 2 * cols : 3 * cols] = query_bias[...]
    hidden_bias[...] = jnp.zeros_like(hidden_bias)
    hidden_bias[:, : up_bias.shape[1]] = up_bias[...]
    gathering.forward(0, 3)
    for point, (one, landed) in enumerate(sent):
        one.wait_recv()
        moved.append(net.copy(landed, landed, net.core))
        gathering.forward(point + 1, 3)
    for one in moved:
        one.wait_recv()
    for place in range(4):
        columns = slice(place * cols, (place + 1) * cols)
        for layer in range(layers):
            vec[layer, :, columns] = vector_land[place, layer * 8 : layer * 8 + 8]
    x[...] = flat(token_land[...]).astype(F32).T
    for slot, device in enumerate([(net.tok, net.hid)] + others):
        whole = flat(cotangent_land[:, :, block(device[1])])
        grad_rows[slot] = whole.astype(F32).T.astype(BF)
    gradient[...] = grad_rows[0].astype(F32)
    gathering.finish()
    net.finish()
    moves.finish()


def entry(tokens, cotangent, value_bias, query_bias, up_bias, shard, vectors, count, used_cols):
    cols, rows = tokens.shape[0], tokens.shape[1] // 4
    layers, feed = up_bias.shape
    inputs = [
        (tokens, True), (cotangent, True), (value_bias, True), (query_bias, True), (up_bias, True),
        (shard, False),
    ] + [(one, True) for one in vectors]
    outputs = [
        ((rows, 4 * cols), F32, True),
        ((rows, 4 * cols), F32, True),
        ((4, rows, 4 * cols), BF, True),
        ((layers, 8, 4 * cols), F32, True),
        ((layers, used_cols), F32, True),
        ((layers, feed + -feed % LANES), F32, True),
        ((count,) + shard.shape, BF, False),
    ]
    scratch = [
        pltpu.VMEM((layers * 8, cols), F32),
        pltpu.VMEM((4, cols, rows), BF),
        pltpu.VMEM((4,) + cotangent.shape, BF),
        pltpu.VMEM((4, layers * 8, cols), F32),
    ]
    return run(entry_kernel, "entry", 50, inputs, outputs, scratch, 4, 12 + job_copies(count), 1)


def finish_kernel(*refs, layers):
    ins, outs, scratch = split_refs(refs, 4 + 4 * layers, 13)
    final_rows, gradient_rows, grads, down_grads = ins[:4]
    layer_sums = [ins[4 + 4 * layer : 8 + 4 * layer] for layer in range(layers)]
    final_out, gradient_out, total = outs[:3]
    wide_outs, query_out, value_out, hidden_out = outs[3:9], outs[9], outs[10], outs[11]
    down_total = outs[12]
    final, gradient, final_land, gradient_land = scratch[:4]
    sums, across_land, along, wide, wide_land = scratch[4:9]
    job_refs, across_refs = scratch[9:13], scratch[13:15]
    send_sems, recv_sems, move_sems = scratch[15:]
    net, moves = Net(send_sems, recv_sems), Moves(move_sems)
    count = grads.shape[0] // 2
    rows, cols, last = final_rows.shape[0], wide.shape[2], count - 1
    others = [net.core, net.far, net.far_core]
    top = layers * 8
    sums[top:] = jnp.zeros((sums.shape[0] - top, sums.shape[1]), F32)
    for layer, (one, two, column_sums, hidden) in enumerate(layer_sums):
        sums[layer * 8 : layer * 8 + 8] = one[...] + two[...]
        sums[top + layer : top + layer + 1, : column_sums.shape[1]] = column_sums[...]
        sums[top + layers + layer : top + layers + layer + 1, : hidden.shape[1]] = hidden[...]
    net.line(count)
    net.barrier(others + [net.half], True)
    swap = net.copy(sums, across_land, net.half)
    scattering = ScatterParts(net, moves, grads, job_refs)
    across = Across(net, moves, down_grads, across_refs)
    for target, source in ((final, final_rows), (gradient, gradient_rows)):
        target[...] = source[...].T.astype(BF).reshape(target.shape)
    moved = []
    for source, target in ((final, final_land), (gradient, gradient_land)):
        for device in reversed(others):
            moved.append(net.copy(source.at[device[1]], target.at[net.hid], device))
        target[net.hid] = source[net.hid]
    up, down = net.take(count), net.take(count)
    own = along.at[net.high]
    swap.wait()
    along[net.high] = sums[...] + across_land[...]
    pl.when(net.has_after)(net.make(up, own, own, net.after).start)
    pl.when(net.has_before)(net.make(down, own, own, net.before).start)

    def pass_on(step, place, base, device, has):
        block = along.at[place]
        net.make(base + step - 1, block, block, device).wait_recv()
        if step < last:
            pl.when(has)(net.make(base + step, block, block, device).start)

    def pass_sums(step):
        pl.when(net.high >= step)(
            functools.partial(pass_on, step, net.high - step, up, net.after, net.has_after)
        )
        pl.when(net.high + step < count)(
            functools.partial(pass_on, step, net.high + step, down, net.before, net.has_before)
        )

    for point in range(3):
        scattering.forward(point, 3)
        for step in range(1, count):
            if (step - 1) * 3 // last == point:
                pass_sums(step)
    across.start()
    reduced = along[0]
    for place in range(1, count):
        reduced += along[place]
    sums[...] = reduced
    for place in range(4):
        wide[place] = sums[:top, place * cols : (place + 1) * cols]
    wide_land[net.hid] = wide[net.hid]
    summed = [net.copy(wide.at[device[1]], wide_land.at[net.hid], device) for device in others]
    for one in moved:
        one.wait_recv()
    for source, target in ((final_land, final_out), (gradient_land, gradient_out)):
        for place in range(4):
            target[:, place * rows : (place + 1) * rows] = source[place].astype(F32)
    for one in summed:
        one.wait_recv()
    narrow = wide_land[0] + wide_land[1] + wide_land[2] + wide_land[3]
    for layer in range(layers):
        one = slice(layer, layer + 1)
        for index, out in enumerate(wide_outs):
            out[one, :] = narrow[layer * 8 + index : layer * 8 + index + 1]
        row = slice(top + layer, top + layer + 1)
        value_out[one, :] = sums[row, cols : 2 * cols]
        query_out[one, :] = sums[row, 2 * cols : 3 * cols]
        row = slice(top + layers + layer, top + layers + layer + 1)
        hidden_out[one, :] = sums[row, : hidden_out.shape[1]]
    for step in range(last):
        sent_up = jnp.logical_and(net.has_after, net.high >= step)
        sent_down = jnp.logical_and(net.has_before, net.high + step < count)
        pl.when(sent_up)(net.make(up + step, own, own, net.after).wait_send)
        pl.when(sent_down)(net.make(down + step, own, own, net.before).wait_send)
    scattering.finish(total)
    across.finish(down_total)
    net.finish([swap])


def finish(final, gradient, grads, down_grads, layer_sums, head_cols, feed):
    count, layers = grads.shape[0] // 2, len(layer_sums)
    rows, width = final.shape
    sum_cols = max(width, layer_sums[0][2].shape[1], layer_sums[0][3].shape[1])
    sums = (layers * 10 + -layers * 10 % 8, sum_cols)
    vector = ((layers, head_cols), F32, True)
    outputs = [
        ((head_cols, 4 * rows), F32, True),
        ((head_cols, 4 * rows), F32, True),
        (grads.shape[1:], F32, True),
    ] + [vector] * 8
    outputs += [((layers, feed), F32, True), (down_grads.shape[1:], F32, True)]
    blocks, wide = (4, head_cols, rows), (4, layers * 8, head_cols)
    scratch = [pltpu.VMEM(blocks, BF)] * 4 + [
        pltpu.VMEM(sums, F32),
        pltpu.VMEM(sums, F32),
        pltpu.VMEM((count,) + sums, F32),
        pltpu.VMEM(wide, F32),
        pltpu.VMEM(wide, F32),
    ]
    scratch += part_scratch(*grads.shape) + across_scratch(down_grads)
    inputs = [(final, True), (gradient, True), (grads, False), (down_grads, False)]
    inputs += [(one, True) for four in layer_sums for one in four]
    kernel = functools.partial(finish_kernel, layers=layers)
    return run(kernel, "finish", 2, inputs, outputs, scratch, 5, 13 + 5 * count, 2 + count)


def key_ranges(own_ids, row_ids, rows):
    blocks = own_ids.reshape(-1, rows)
    position = jnp.arange(row_ids.shape[0], dtype=jnp.int32)
    low = jnp.min(jnp.where(row_ids == blocks[:, :1], position, row_ids.shape[0]), axis=1)
    high = jnp.max(jnp.where(row_ids == blocks[:, -1:], position, -1), axis=1)
    return jnp.stack([low // KEYS, high // KEYS + 1], axis=1).reshape(-1)


def body(
    tokens, picture, cotangent, first_gain, first_shift, query_weight, query_bias, key_weight,
    value_weight, value_bias, output_weight, output_bias, second_gain, second_shift, up_weight,
    up_bias, down_weight, down_bias,
):
    token_count = tokens.shape[0]
    rows = token_count // 4
    layers = query_weight.shape[0]
    head_cols = query_bias.shape[1]
    feed = up_bias.shape[1]
    feed_pad = -feed % LANES
    feed_cols = feed + feed_pad
    hid = lax.axis_index("hid")
    tok = lax.axis_index("tok")
    count = lax.axis_size("tok")
    shard = query_weight.shape[1]
    shard_pad = -shard % 16
    width = count * shard
    lead = 3 * head_cols % LANES
    used_cols = 3 * head_cols + -3 * head_cols % LANES

    own_ids = lax.dynamic_slice_in_dim(picture, tok * token_count, token_count)
    row_ids = lax.dynamic_slice_in_dim(picture, (tok // 2) * 2 * token_count, 2 * token_count)
    place = jnp.stack([hid, tok % 2]).astype(jnp.int32)
    meta = jnp.concatenate([place, key_ranges(own_ids, row_ids, rows)])

    starts = jnp.concatenate([jnp.zeros(1, jnp.int32), (row_ids[1:] != row_ids[:-1]).astype(jnp.int32)])
    number = jnp.cumsum(starts)[:, None] + HEAD_DIM
    lane = lax.broadcasted_iota(jnp.int32, (row_ids.shape[0], LANES), 1)
    key_marks = jnp.where((lane == number) | (lane < HEAD_DIM), 0.0, MASKED).astype(BF)
    own_number = lax.dynamic_slice_in_dim(number, tok % 2 * token_count, token_count)
    query_marks = (lane[:token_count] == own_number).astype(BF)

    def side_by_side(*parts):
        return jnp.concatenate(parts, axis=1)

    def padded(part):
        return jnp.pad(part, ((0, 0), (0, feed_pad)))

    def shards(part):
        return jnp.pad(part, ((0, shard_pad), (0, 0)))

    def joined(gathered):
        return gathered[:, :shard].reshape(width, gathered.shape[2])

    def separate(grads):
        grads = grads.reshape(count, shard, grads.shape[1])
        return jnp.pad(grads, ((0, 0), (0, shard_pad), (0, 0)))

    mixed_parts = [
        shards(
            side_by_side(
                key_weight[layer], value_weight[layer], query_weight[layer], output_weight[layer].T
            )
        )
        for layer in range(layers)
    ]
    vectors = (first_gain, first_shift, output_bias, second_gain, second_shift, down_bias)
    x, gradient, grad_rows, vectors, bias, up_bias, mixed = entry(
        tokens.T, cotangent.T, value_bias, query_bias, up_bias, mixed_parts[0], vectors, count, used_cols
    )

    halves = [(place, place ^ 1) for place in range(count)]
    lines = [[place * 2 + low for place in range(count // 2)] for low in range(2)]

    def swap(part):
        return lax.ppermute(part, "tok", halves)

    def both_halves(own, other):
        first = tok % 2 == 0
        return jnp.stack([jnp.where(first, own, other), jnp.where(first, other, own)])

    def along(part):
        return lax.all_gather(part, "tok", axis=0, tiled=True, axis_index_groups=lines)

    def along_first(part):
        own = along(part)
        other = swap(own)
        parts = [rows_of.reshape(count // 2, shard, part.shape[1]) for rows_of in (own, other)]
        if shard % 16 == 0:
            return parts
        return [both_halves(*parts).transpose(1, 0, 2, 3).reshape(width, part.shape[1])]

    def hold(*values):
        return lax.optimization_barrier(values)

    def pair_rows(part, other):
        return both_halves(part, other).reshape(2 * shard, part.shape[1])

    def up_part(layer):
        return padded(up_weight[layer])

    def down_part(layer):
        return padded(down_weight[layer].T)

    ups, weights = [along_first(up_part(0))], [[joined(mixed)]]
    early = down_part(0)
    early, early_other, x = hold(early, swap(early), x)
    downs = [[along(pair_rows(early, early_other))]]
    for layer in range(1, layers):
        weights.append(along_first(mixed_parts[layer][:shard]))
        coming = up_part(layer)
        ups.append([along(pair_rows(coming, swap(coming)))])
    saved = []
    for layer in range(layers):
        mixed, up = weights[layer], ups[layer]
        more = layer + 1 < layers
        normed, queries, own_pairs, far_pairs = project(layer, x, vectors, bias, mixed, head_cols)
        if layer > 0:
            queries, coming, coming_other = hold(queries, coming, coming_other)
            downs.append([along(pair_rows(coming, coming_other))])
        mixture, logsum = attend(
            meta, queries, own_pairs, far_pairs, query_marks, key_marks, lead
        )
        if more:
            coming, mixture = hold(down_part(layer + 1), mixture)
            coming_other = swap(coming)
        after, normed_two, active, slope, *x_next = mlp(
            layer, mixture, x, vectors, up_bias, mixed, up, downs[layer], not more
        )
        saved.append(
            (x, normed, queries, own_pairs, far_pairs, mixture, logsum, after, normed_two, active, slope)
        )
        x = x_next[0] if x_next else None

    def by_halves(part):
        own = lax.dynamic_index_in_dim(part, tok % 2, 1, keepdims=False)
        other = lax.dynamic_index_in_dim(part, 1 - tok % 2, 1, keepdims=False)
        return own, other

    def sum_along(part):
        return lax.psum_scatter(
            part, "tok", scatter_dimension=0, tiled=True, axis_index_groups=lines
        )

    def halves_of(parts):
        if len(parts) == 1:
            part = parts[0].reshape(-1, 2, shard, parts[0].shape[1])
            parts = by_halves(part)
        return parts[0], swap(parts[1])

    def by_half(part):
        return jnp.pad(part.reshape(2, shard, part.shape[1]), ((0, 0), (0, shard_pad), (0, 0)))

    def added(own, other):
        return (own.astype(F32) + other.astype(F32)).astype(BF)

    def in_rows(part):
        return part.reshape(-1, part.shape[-1])

    split = shard if shard % 16 == 0 else 0
    mixed_grads, up_grads, down_grads = [None] * layers, [None] * layers, [None] * layers
    layer_sums = [None] * layers
    grads = final = None
    for layer in reversed(range(layers)):
        x, normed, queries, own_pairs, far_pairs, mixture, logsum, after, normed_two, active, slope = saved[layer]
        mixed, up, down = weights[layer], ups[layer], downs[layer]
        last = layer + 1
        crossing = ()
        if last < layers:
            gradient, down_grads[last] = hold(gradient, down_grads[last])
            crossing = (by_half(down_grads[last]),)
        grad_after, grad_mixture, grad_down, grad_out, sums_two, hidden_sums, *grad_up = mlp_back(
            layer, gradient, after, vectors, mixed, up, down, mixture, normed_two, active, slope,
            () if last < layers else (grad_rows,), split, crossing,
        )
        if last < layers:
            down_grads[last] = grad_up.pop()
            grad_down, up_grads[last] = hold(grad_down, up_grads[last])
        down_grads[layer] = sum_along(grad_down)
        up_own, up_other = halves_of(grad_up)
        grad_queries, grad_own, grad_far = attend_back(
            meta, queries, own_pairs, far_pairs, query_marks, key_marks, grad_mixture, logsum
        )
        up_other, grad_far = hold(up_other, grad_far)
        up_grad = added(up_own, up_other)
        crossing = ()
        if last < layers:
            grad_after, mixed_grads[last] = hold(grad_after, mixed_grads[last])
            crossing = (by_half(mixed_grads[last]),)
        grad_after, up_grad = hold(grad_after, up_grad)
        up_grads[layer] = sum_along(in_rows(up_grad))
        gradient, sums_one, column_sums, grads, *closed = project_back(
            layer, grad_after, x, vectors, mixed, normed, grad_queries, grad_own, grad_far,
            grad_out, used_cols, () if last < layers else (active, after, *down), crossing,
        )
        if last < layers:
            mixed_grads[last] = closed.pop()
        final = closed[0] if closed else final
        if layer > 0:
            mixed_grads[layer] = sum_along(grads)
        layer_sums[layer] = (sums_one, sums_two, column_sums, hidden_sums)
    gradient, down_grads[0] = hold(gradient, down_grads[0])
    final, gradient, mixed_grads[0], *small = finish(
        final, gradient, separate(grads), by_half(down_grads[0]), layer_sums, head_cols, feed
    )
    up_grads[0], final, gradient, mixed_grads[0], *small = hold(
        up_grads[0], final, gradient, mixed_grads[0], *small
    )
    down_grads[0] = small.pop()
    first_gain, first_shift, output_bias, second_gain, second_shift, down_bias = small[:6]
    query_bias, value_bias, up_bias = small[6:]

    def mixed_columns(start):
        columns = slice(start * head_cols, (start + 1) * head_cols)
        return jnp.stack([part[:shard, columns].astype(F32) for part in mixed_grads])

    def hidden_columns(parts):
        return jnp.stack([part[:shard, :feed].astype(F32) for part in parts])

    return (
        final.T,
        gradient.T,
        first_gain,
        first_shift,
        mixed_columns(2),
        query_bias,
        mixed_columns(0),
        mixed_columns(1),
        value_bias,
        mixed_columns(3).transpose(0, 2, 1),
        output_bias,
        second_gain,
        second_shift,
        hidden_columns(up_grads),
        up_bias,
        hidden_columns(down_grads).transpose(0, 2, 1),
        down_bias,
    )


def solution(mesh):
    rows = P("tok", "hid")
    vector = P(None, "hid")
    inward = P(None, "tok", "hid")
    outward = P(None, "hid", "tok")
    in_specs = (
        rows, P(), rows, vector, vector, inward, vector, inward, inward, vector, outward, vector,
        vector, vector, inward, vector, outward, vector,
    )
    out_specs = (
        rows, rows, vector, vector, inward, vector, inward, inward, vector, outward, vector,
        vector, vector, inward, vector, outward, vector,
    )
    return jax.shard_map(body, mesh=mesh, in_specs=in_specs, out_specs=out_specs, check_vma=False)
```
